32 devices in a mesh: blk: 8 (over y, x, core), dp: 4 (over z).
Axes of the slice: x: 2, y: 2, z: 4, core: 2. Of those that a mesh axis runs over, the one named last changes fastest.
Arguments:
- embeds: bfloat16 [128, 2, 64, 768], P(('blk', 'dp')), may hold values from -6 to 6
- token_mask: int32 [128, 2, 64], P(('blk', 'dp')), may hold values from 0 to 1, as said below
- groups: int32 [128], P(('blk', 'dp')), may hold values from 0 to 108
- counts: int32 [32], P(('blk', 'dp')), may hold values from 1 to 4, as said below
- rows_master: float32 [768, 6144], P(('blk', 'dp')), may hold values from -0.21875 to 0.21875
- rows_mean: float32 [768, 6144], P(('blk', 'dp')), may hold values from -0.0014648438 to 0.0014648438
- rows_square: float32 [768, 6144], P(('blk', 'dp')), may hold values from 5.2981908e-09 to 2.1192763e-08
- down_master: float32 [3072, 768], P(('blk', 'dp')), may hold values from -0.109375 to 0.109375
- down_mean: float32 [3072, 768], P(('blk', 'dp')), may hold values from -0.0014648438 to 0.0014648438
- down_square: float32 [3072, 768], P(('blk', 'dp')), may hold values from 5.2981908e-09 to 2.1192763e-08
- vector_master: float32 [9216], P(('blk', 'dp')), may hold values from -0.6 to 0.6
- vector_mean: float32 [9216], P(('blk', 'dp')), may hold values from -0.0014648438 to 0.0014648438
- vector_square: float32 [9216], P(('blk', 'dp')), may hold values from 5.2981908e-09 to 2.1192763e-08
Outputs:
- pair_loss: float32 [], replicated
- embeds_grad: float32 [128, 2, 64, 768], P(('blk', 'dp'))
- rows_updated: float32 [768, 6144], P(('blk', 'dp'))
- rows_mean_new: float32 [768, 6144], P(('blk', 'dp'))
- rows_square_new: float32 [768, 6144], P(('blk', 'dp'))
- down_updated: float32 [3072, 768], P(('blk', 'dp'))
- down_mean_new: float32 [3072, 768], P(('blk', 'dp'))
- down_square_new: float32 [3072, 768], P(('blk', 'dp'))
- vector_updated: float32 [9216], P(('blk', 'dp'))
- vector_mean_new: float32 [9216], P(('blk', 'dp'))
- vector_square_new: float32 [9216], P(('blk', 'dp'))
The draws below stay inside these ranges and needn't reach their ends.
Inputs may be any that keep to these rules, and one draw needn't show every extreme that they name: `token_mask`: every sentence is a run of ones followed by zeros, 16 to 64 ones; position 0 is always 1. Entry r counts the valid slots of the r-th device of blk+dp (slots below it are valid); some device holds 4.
All inputs are finite; a program needn't handle non-finite values.
Results may differ from the reference program's by a relative error of at most 0.0075.
Values may be sent and summed in bfloat16 or wider, within the bound.
A program may use at most 192 MiB of HBM per device.

```python
import math
import jax
import jax.numpy as jnp
from jax import lax

D = 768
HEADS = 12
HEAD = 64
FF = 3072
SEQ = 64
SLOTS = 4
GROUPS = 109
STEP = 10
RANKS = 32
PAIRS = 128
VEC = 9216


def draw_token_mask(key, part):
    key = jax.random.fold_in(key, 5)
    lengths = jax.random.randint(key, (PAIRS, 2), max(SEQ // 4, 1), SEQ + 1)
    first = (jnp.arange(PAIRS)[:, None] == 0) & (jnp.arange(2)[None, :] == 0)
    lengths = jnp.where(first, SEQ, lengths)
    return (jnp.arange(SEQ)[None, None, :] < lengths[:, :, None]).astype(jnp.int32)


def draw_counts(key, part):
    key = jax.random.fold_in(key, 7)
    places = jnp.arange(RANKS)
    base = 2 + (SLOTS - 2) * places // max(RANKS - 1, 1)
    jitter = jax.random.randint(key, (RANKS,), -1, 2)
    filled = jnp.clip(base + jitter, 1, SLOTS)
    return jnp.where(places == RANKS - 1, SLOTS, filled).astype(jnp.int32)


def set_ends(result, rng, smallest, high):
    index_at = [jax.random.randint(jax.random.fold_in(rng, axis), (), 0, length) for axis, length in enumerate(result.shape)]
    widest = result.shape.index(max(result.shape))
    neighbour = index_at[:widest] + [(index_at[widest] + 1) % result.shape[widest]] + index_at[widest + 1:]
    return result.at[tuple(index_at)].set(smallest).at[tuple(neighbour)].set(high)


def level_of(own_key, shape, split, smallest, top_value):
    def one(axis_at, blocks):
        steps = jax.random.uniform(jax.random.fold_in(jax.random.fold_in(own_key, 6), axis_at), (blocks,), jnp.float32, smallest / len(split), top_value / len(split))
        return jnp.repeat(jnp.exp(steps), shape[axis_at] // blocks).reshape((-1,) + (1,) * (len(shape) - axis_at - 1))

    gain = one(*split[0])
    for cut in split[1:]:
        gain = gain * one(*cut)
    return gain


def gaussian(rng, dims, scale, most, pieces=(), kind=jnp.bfloat16):
    factor_of = level_of(rng, dims, pieces, -0.22, 0.18) if pieces else 1.0
    array = jax.random.normal(rng, dims, jnp.float32) * scale * factor_of
    return jnp.minimum(jnp.maximum(array, -most), most).astype(kind)


def setup_inputs(seed: int = 0) -> dict:
    streams_of = jax.random.split(jax.random.key(seed), 14)
    return {
        "embeds": gaussian(streams_of[0], (PAIRS, 2, SEQ, D), 1.0, 6.0, ((0, 32),)),
        "token_mask": draw_token_mask(jax.random.fold_in(streams_of[13], 71), 0),
        "groups": set_ends(jax.random.randint(streams_of[2], (PAIRS,), 0, GROUPS), jax.random.fold_in(streams_of[2], 1), 0, GROUPS - 1).astype(jnp.int32),
        "counts": draw_counts(jax.random.fold_in(streams_of[13], 71), 0),
        "rows_master": gaussian(streams_of[4], (D, 4 * D + FF), D ** -0.5, 0.21875, ((0, 32),), jnp.float32),
        "rows_mean": gaussian(streams_of[5], (D, 4 * D + FF), (2.2 / (D * PAIRS ** 0.5)), 0.0014648438, ((0, 32),), jnp.float32),
        "rows_square": jnp.clip(jnp.exp(math.log(2.119276309997531e-08) - 1.3862944 * jax.random.uniform(streams_of[6], (D, 4 * D + FF), jnp.float32) ** level_of(streams_of[6], (D, 4 * D + FF), ((0, 32),), -0.2, 0.2)), 5.298190774993827e-09, 2.119276309997531e-08),
        "down_master": gaussian(streams_of[7], (FF, D), FF ** -0.5, 0.109375, ((0, 32),), jnp.float32),
        "down_mean": gaussian(streams_of[8], (FF, D), (2.2 / (D * PAIRS ** 0.5)), 0.0014648438, ((0, 32),), jnp.float32),
        "down_square": jnp.clip(jnp.exp(math.log(2.119276309997531e-08) - 1.3862944 * jax.random.uniform(streams_of[9], (FF, D), jnp.float32) ** level_of(streams_of[9], (FF, D), ((0, 32),), -0.2, 0.2)), 5.298190774993827e-09, 2.119276309997531e-08),
        "vector_master": gaussian(streams_of[10], (VEC,), 0.1, 0.6, ((0, 32),), jnp.float32),
        "vector_mean": gaussian(streams_of[11], (VEC,), (2.2 / (D * PAIRS ** 0.5)), 0.0014648438, ((0, 32),), jnp.float32),
        "vector_square": jnp.clip(jnp.exp(math.log(2.119276309997531e-08) - 1.3862944 * jax.random.uniform(streams_of[12], (VEC,), jnp.float32) ** level_of(streams_of[12], (VEC,), ((0, 32),), -0.2, 0.2)), 5.298190774993827e-09, 2.119276309997531e-08),
    }


score_scale = 32.0
margin = 0.3
beta_one = 0.9
beta_two = 0.999
learn_rate = 0.03
vector_rate = 0.06
decay_rate = 0.01
adam_epsilon = 1e-08
norm_epsilon = 1e-12
unit_epsilon = 1e-06
highest = lax.Precision.HIGHEST

@jax.custom_vjp
def low(v):
    return lax.optimization_barrier(v.astype(jnp.bfloat16)).astype(jnp.float32)

@jax.custom_vjp
def low_back(v):
    return v

def low_keep(v):
    return (low(v), None)

def low_pass(kept, grad):
    return (grad,)

def back_keep(v):
    return (v, None)

def back_low(kept, grad):
    return (low(grad),)
low.defvjp(low_keep, low_pass)
low_back.defvjp(back_keep, back_low)

def rounded(values):
    return low(low_back(values))

def layer_norm(values, scale_vec, shift_vec):
    centre = values - lax.optimization_barrier(jnp.mean(values, axis=-1, keepdims=True))
    spread = lax.optimization_barrier(jnp.mean(centre * centre, axis=-1, keepdims=True))
    return centre * lax.rsqrt(spread + norm_epsilon) * scale_vec + shift_vec

def pool_unit(output, weights):
    summed = lax.optimization_barrier(jnp.sum(output * weights[:, :, None], axis=1)) / lax.optimization_barrier(jnp.sum(weights, axis=1, keepdims=True))
    return summed * lax.rsqrt(lax.optimization_barrier(jnp.sum(summed * summed, axis=1, keepdims=True)) + unit_epsilon)

def split_vectors(vectors, model_width, hidden):
    extents = [model_width] * 5 + [hidden] + [model_width] * 3
    pieces_out = []
    offset = 0
    for extent in extents:
        pieces_out.append(vectors[offset:offset + extent])
        offset = offset + extent
    return pieces_out

def encode_block(params, block_data):
    row_weights, down_weights, vectors = params
    embed_rows, mask_rows = block_data
    pair_rows = embed_rows.shape[0]
    seq_count = 2 * pair_rows
    tokens = seq_count * SEQ
    bias_q, bias_v, bias_o, gain_one, shift_one, bias_up, bias_down, gain_two, shift_two = split_vectors(vectors, D, FF)
    inputs = embed_rows.reshape(tokens, D)
    weights = mask_rows.reshape(seq_count, SEQ).astype(jnp.float32)
    key_valid = mask_rows.reshape(seq_count, SEQ) > 0
    joined = jnp.concatenate([bias_q, jnp.zeros_like(bias_q), bias_v])
    projected = rounded(jnp.dot(inputs, row_weights[:, :3 * D], precision=highest) + joined)
    queries = projected[:, :D].reshape(seq_count, SEQ, HEADS, HEAD)
    key_part = projected[:, D:2 * D].reshape(seq_count, SEQ, HEADS, HEAD)
    values = projected[:, 2 * D:].reshape(seq_count, SEQ, HEADS, HEAD)
    scores = jnp.einsum('nihe,njhe->nhij', queries, key_part, precision=highest) * HEAD ** (-0.5)
    scores = low_back(jnp.where(key_valid[:, None, None, :], scores, -1e+30))
    attention = low(jax.nn.softmax(scores, axis=-1))
    context = rounded(jnp.einsum('nhij,njhe->nihe', attention, values, precision=highest).reshape(tokens, D))
    resid_one = inputs + low_back(jnp.dot(context, row_weights[:, 3 * D:4 * D], precision=highest) + bias_o)
    normed_one = low(layer_norm(resid_one, 1.0 + gain_one, shift_one))
    up_pre = low_back(jnp.dot(normed_one, row_weights[:, 4 * D:], precision=highest) + bias_up)
    activated = low(jax.nn.gelu(up_pre, approximate=False))
    resid_two = normed_one + low_back(jnp.dot(activated, down_weights, precision=highest) + bias_down)
    output = layer_norm(resid_two, 1.0 + gain_two, shift_two)
    pooled = pool_unit(output.reshape(seq_count, SEQ, D), weights)
    return pooled.reshape(pair_rows, 2, D)

def contrast(sources, targets, groups, counts):
    valid_slot = jnp.arange(PAIRS) % SLOTS < jnp.repeat(counts, SLOTS)
    group_ids = jnp.where(valid_slot, groups, -1)
    diagonal = jnp.eye(PAIRS, dtype=jnp.float32)
    scores = score_scale * jnp.dot(sources, targets.T, precision=highest) - score_scale * margin * diagonal
    same = (group_ids[:, None] == group_ids[None, :]) & (group_ids[:, None] >= 0)
    exp_terms = jnp.where(same, jnp.exp(scores), 0.0)
    row_sum = jnp.where(valid_slot, lax.optimization_barrier(jnp.sum(exp_terms, axis=1)), 1.0)
    col_sum = jnp.where(valid_slot, lax.optimization_barrier(jnp.sum(exp_terms, axis=0)), 1.0)
    positive = jnp.diagonal(scores)
    pair_total = jnp.sum(valid_slot.astype(jnp.float32))
    terms = jnp.where(valid_slot, jnp.log(row_sum) + jnp.log(col_sum) - 2.0 * positive, 0.0)
    return jnp.sum(terms) / (2.0 * pair_total)

def adam_step(master, gradient, moment_one, moment_two, decay, rate):
    mean_new = beta_one * moment_one + (1.0 - beta_one) * gradient
    square_new = beta_two * moment_two + (1.0 - beta_two) * gradient * gradient
    mean_hat = mean_new / (1.0 - beta_one ** STEP)
    square_hat = square_new / (1.0 - beta_two ** STEP)
    updated = master - rate * (mean_hat / (jnp.sqrt(square_hat) + adam_epsilon) + decay * master)
    return (updated, mean_new, square_new)

def reference(embeds, token_mask, groups, counts, rows_master, rows_mean, rows_square, down_master, down_mean, down_square, vector_master, vector_mean, vector_square):
    block_pairs = math.gcd(PAIRS, max(1, 4096 // (2 * SEQ)))
    block_count = PAIRS // block_pairs
    mask_blocks = token_mask.reshape(block_count, block_pairs, 2, SEQ)
    checkpointed = jax.checkpoint(encode_block)

    def forward(embed_values, row_weights, down_weights, vectors):
        params = (low(row_weights), low(down_weights), low(vectors))
        blocks = embed_values.reshape(block_count, block_pairs, 2, SEQ, D)

        def mapped(block_data):
            return checkpointed(params, block_data)
        pooled = lax.map(mapped, (blocks, mask_blocks)).reshape(PAIRS, 2, D)
        return contrast(pooled[:, 0], pooled[:, 1], groups, counts)
    pair_loss, backward = jax.vjp(forward, embeds.astype(jnp.float32), rows_master, down_master, vector_master)
    embed_grad, row_grad, down_grad, vector_grad = backward(jnp.ones_like(pair_loss))
    rows_new = adam_step(rows_master, row_grad, rows_mean, rows_square, decay_rate, learn_rate)
    down_new = adam_step(down_master, down_grad, down_mean, down_square, decay_rate, learn_rate)
    vector_new = adam_step(vector_master, vector_grad, vector_mean, vector_square, 0.0, vector_rate)
    return (pair_loss, embed_grad, rows_new[0], rows_new[1], rows_new[2], down_new[0], down_new[1], down_new[2], vector_new[0], vector_new[1], vector_new[2])
```

```python
from functools import partial

import jax
import jax.numpy as jnp
from jax import lax
from jax.experimental import pallas as pl
from jax.experimental.pallas import tpu as pltpu
from jax.sharding import PartitionSpec as P

HEAD = 64
STEP = 10


score_scale = 32.0
margin = 0.3
beta_one = 0.9
beta_two = 0.999
learn_rate = 0.03
vector_rate = 0.06
decay_rate = 0.01
adam_epsilon = 1e-08
norm_epsilon = 1e-12
unit_epsilon = 1e-06
highest = lax.Precision.HIGHEST

f32 = jnp.float32
bf16 = jnp.bfloat16


def dot_nn(a, b, precision=None):
    return lax.dot_general(a, b, (((1,), (0,)), ((), ())), precision=precision, preferred_element_type=f32)


def dot_nt(a, b, precision=None):
    return lax.dot_general(a, b, (((1,), (1,)), ((), ())), precision=precision, preferred_element_type=f32)


def dot_tn(a, b):
    return lax.dot_general(a, b, (((0,), (0,)), ((), ())), preferred_element_type=f32)


Z_FIRST, Z_MID = 0, 1
GATHER_MODE = (Z_FIRST, Z_MID, Z_MID)


class Comm:
    def __init__(self, depth):
        self.depth = depth
        self.b = lax.axis_index("blk")
        self.z = lax.axis_index("dp")
        b, z = self.b, self.z
        self.X, self.Y, self.C = (b ^ 2, z), (b ^ 4, z), (b ^ 1, z)
        self.Z = [(b, z ^ k) for k in range(depth)]
        self.up, self.down = (b, z + 1), (b, z - 1)

    def barrier(self):
        sem = pltpu.get_barrier_semaphore()
        friends = [self.X, self.Y, self.C] + self.Z[1:]
        for friend in friends:
            pl.semaphore_signal(sem, inc=1, device_id=friend, device_id_type=pl.DeviceIdType.MESH)
        pl.semaphore_wait(sem, len(friends))


def remote(src, dst, send_sem, recv_sem, device):
    return pltpu.make_async_remote_copy(
        src_ref=src,
        dst_ref=dst,
        send_sem=send_sem,
        recv_sem=recv_sem,
        device_id=device,
        device_id_type=pl.DeviceIdType.MESH,
    )


def layer_kernel(
    x_ref, tok_ref, group_ref, rows_ref, down_ref, vec_ref,
    loss_ref, dx_ref, grad_attn_ref, grad_up_ref, grad_down_ref, grad_vec_ref,
    raw_a, raw_u, w_down, w_attn, w_up, g_up, g_down,
    qkv, probs, ctx, ctx_t, x_t, y_low, y_t, act, act_t, slope, xhat1, xhat2, work,
    rstd1, rstd2, tok_w, vec_all, vec_row, pairs, pooled_hat, unit_rs, pair_k, vec_grad, vec_out, vec_in,
    zsem, xsem, ysem, dsem, csem, ssem,
    small_recv, small_send,
    rc_sem, r1_sem, r2_sem, rz_sem, rs_send,
    vr_sem, vs_sem,
):
    comm = Comm(4)
    b, z = comm.b, comm.z
    bx, by, bd = b ^ 2, b ^ 4, b ^ 6
    width = 768
    raw = (raw_a, raw_u, w_down)

    def unit(ref, s):
        return ref.at[s // 16, pl.ds((s % 16) * 48, 48), :]

    def quad(ref, s):
        return ref.at[s // 16, pl.ds((s % 16) * 48, 192), :]

    def slot(p, bb, zz, h):
        if p == 2:
            return (bb * 4 + zz) * 2 + h
        return h * 32 + bb * 4 + zz

    def span(ref, n):
        return ref.at[pl.ds(0, n // 16)] if n % 16 == 0 else ref.at[0, pl.ds(0, 48 * n), :]

    def send(p, s, device, way, rsem):
        remote(unit(raw[p], s), unit(raw[p], s), ssem.at[p, way], rsem, device).start()

    def arrived(p, s, rsem):
        remote(unit(raw[p], s), unit(raw[p], s), ssem.at[p, 0], rsem, comm.X).wait_recv()

    def cast(p):
        for h in range(2):
            if p < 2:
                base = p * 4 * width + h * 2 * width
                both = jnp.concatenate([rows_ref[:, base : base + width], rows_ref[:, base + width : base + 2 * width]], axis=0)
            else:
                both = down_ref[h * 48 : h * 48 + 48, :]
            s = slot(p, b, z, h)
            raw[p][s // 16, pl.ds((s % 16) * 48, 48), :] = both.astype(bf16)

    def along_z(p, s, k, upward, c):
        if upward:
            send(p, s, comm.up, 3, zsem.at[p, 0, k - 1, c])
        else:
            send(p, s, comm.down, 4, zsem.at[p, 1, k - 1, c])

    def both_ways(p, s, c):
        @pl.when(z < 3)
        def _():
            along_z(p, s, 1, True, c)

        @pl.when(z > 0)
        def _():
            along_z(p, s, 1, False, c)

    def column(p, zs):
        a, c = slot(p, b, zs, 0), slot(p, b, zs, 1)
        send(p, a, comm.X, 0, xsem.at[p, zs, 0])
        send(p, c, comm.Y, 1, ysem.at[p, zs, 1])
        send(p, c, comm.X, 0, xsem.at[p, zs, 1])
        send(p, a, comm.Y, 1, ysem.at[p, zs, 0])
        send(p, a, comm.C, 2, csem.at[p])
        send(p, c, comm.C, 2, csem.at[p])

    def final(p, s, h, zs, j):
        if h == 0:
            send(p, s, comm.Y, 1, ysem.at[p, zs, j])
        else:
            send(p, s, comm.X, 0, xsem.at[p, zs, j])
        send(p, s, comm.C, 2, csem.at[p])

    def own(p):
        cast(p)
        a, c = slot(p, b, z, 0), slot(p, b, z, 1)
        if GATHER_MODE[p] == Z_FIRST:
            both_ways(p, a, 0)
            both_ways(p, c, 1)
            column(p, z)
        else:
            send(p, a, comm.X, 0, dsem.at[p, 0, 0])
            send(p, c, comm.Y, 1, dsem.at[p, 0, 1])
            both_ways(p, a, 0)
            both_ways(p, c, 1)
            final(p, a, 0, z, 0)
            final(p, c, 1, z, 0)

    def first(p):
        for h, bb in ((0, bx), (1, by)):
            s = slot(p, bb, z, h)
            arrived(p, s, dsem.at[p, 0, h])
            both_ways(p, s, 2 + h)
            final(p, s, h, z, 1)

    def from_z(p, k):
        for upward in (True, False):
            @pl.when((z >= k) if upward else (z + k <= 3))
            def _():
                zs = z - k if upward else z + k
                more = (z < 3) if upward else (z > 0)
                way = 0 if upward else 1
                if GATHER_MODE[p] == Z_FIRST:
                    kinds = [(b, 0, 0), (b, 1, 1)]
                else:
                    kinds = [(b, 0, 0), (b, 1, 1), (bx, 0, 2), (by, 1, 3)]
                for bb, h, c in kinds:
                    s = slot(p, bb, zs, h)
                    arrived(p, s, zsem.at[p, way, k - 1, c])
                    if k < 3:
                        @pl.when(more)
                        def _():
                            along_z(p, s, k + 1, upward, c)
                    if GATHER_MODE[p] == Z_MID:
                        final(p, s, h, zs, c // 2)
                if GATHER_MODE[p] == Z_FIRST:
                    column(p, zs)

    def near(f, p, k):
        if k == 0:
            f(p, z)
            return

        @pl.when(z >= k)
        def _():
            f(p, z - k)

        @pl.when(z + k <= 3)
        def _():
            f(p, z + k)

    def across(p, zs):
        s = slot(p, bx, zs, 0)
        arrived(p, s, xsem.at[p, zs, 0])
        send(p, s, comm.Y, 1, dsem.at[p, zs, 0])
        send(p, s, comm.C, 2, csem.at[p])
        s = slot(p, by, zs, 1)
        arrived(p, s, ysem.at[p, zs, 1])
        send(p, s, comm.X, 0, dsem.at[p, zs, 1])
        send(p, s, comm.C, 2, csem.at[p])
        s = slot(p, bx, zs, 1)
        arrived(p, s, xsem.at[p, zs, 1])
        send(p, s, comm.C, 2, csem.at[p])
        s = slot(p, by, zs, 0)
        arrived(p, s, ysem.at[p, zs, 0])
        send(p, s, comm.C, 2, csem.at[p])

    def last(p, zs):
        if GATHER_MODE[p] == Z_FIRST:
            for h in range(2):
                s = slot(p, bd, zs, h)
                arrived(p, s, dsem.at[p, zs, h])
                send(p, s, comm.C, 2, csem.at[p])
        else:
            for j in range(2):
                s = slot(p, by if j == 0 else bd, zs, 0)
                arrived(p, s, ysem.at[p, zs, j])
                send(p, s, comm.C, 2, csem.at[p])
                s = slot(p, bx if j == 0 else bd, zs, 1)
                arrived(p, s, xsem.at[p, zs, j])
                send(p, s, comm.C, 2, csem.at[p])

    def gathered(p):
        whole = span(raw[p], 32)
        remote(whole, whole, ssem.at[p, 0], csem.at[p], comm.X).wait_recv()

    def sent(p):
        def wait(n, way):
            part = span(raw[p], n)
            remote(part, part, ssem.at[p, way], csem.at[p], comm.X).wait_send()

        z_first = GATHER_MODE[p] == Z_FIRST
        wait(12 if z_first else 9, 0)
        wait(12 if z_first else 9, 1)
        wait(32, 2)
        per = 2 if z_first else 4
        for zz in range(3):
            @pl.when(z == zz)
            def _():
                wait((zz + 1) * per, 3)

            @pl.when(z == 3 - zz)
            def _():
                wait((zz + 1) * per, 4)

    def small_z(ref, n):
        mine = ref.at[pl.ds(b * 4 + z, 1)]
        for k in (3, 1, 2):
            remote(mine, mine, small_send.at[n, 0], small_recv.at[n, z], comm.Z[k]).start()

    def small_plane(ref, n):
        for k in (1, 2, 3):
            theirs = ref.at[pl.ds(b * 4 + (z ^ k), 1)]
            remote(theirs, theirs, small_send.at[n, 0], small_recv.at[n, z ^ k], comm.X).wait_recv()
        mine = ref.at[pl.ds(b * 4, 4)]
        remote(mine, mine, small_send.at[n, 1], small_recv.at[n, 4], comm.X).start()
        remote(mine, mine, small_send.at[n, 2], small_recv.at[n, 5], comm.Y).start()
        remote(mine, mine, small_send.at[n, 3], small_recv.at[n, 7], comm.C).start()

    def small_cross(ref, n):
        theirs = ref.at[pl.ds(bx * 4, 4)]
        remote(theirs, theirs, small_send.at[n, 1], small_recv.at[n, 4], comm.X).wait_recv()
        remote(theirs, theirs, small_send.at[n, 4], small_recv.at[n, 6], comm.Y).start()
        remote(theirs, theirs, small_send.at[n, 5], small_recv.at[n, 8], comm.C).start()
        theirs = ref.at[pl.ds(by * 4, 4)]
        remote(theirs, theirs, small_send.at[n, 1], small_recv.at[n, 5], comm.X).wait_recv()
        remote(theirs, theirs, small_send.at[n, 6], small_recv.at[n, 9], comm.C).start()

    def small_end(ref, n):
        theirs = ref.at[pl.ds(bd * 4, 4)]
        remote(theirs, theirs, small_send.at[n, 1], small_recv.at[n, 6], comm.X).wait_recv()
        remote(theirs, theirs, small_send.at[n, 7], small_recv.at[n, 10], comm.C).start()
        for j in range(4):
            theirs = ref.at[pl.ds((b ^ (1 + 2 * j)) * 4, 4)]
            remote(theirs, theirs, small_send.at[n, 1], small_recv.at[n, 7 + j], comm.X).wait_recv()
        three = ref.at[pl.ds(0, 3)]
        remote(three, three, small_send.at[n, 0], small_recv.at[n, 0], comm.X).wait_send()
        four = ref.at[pl.ds(0, 4)]
        for j in range(1, 8):
            remote(four, four, small_send.at[n, j], small_recv.at[n, 0], comm.X).wait_send()

    def vec(offset, size=width):
        return vec_row[0:1, offset : offset + size]

    bias_q, bias_v, bias_o, gain1_at, shift1_at, bias_up_at = 0, width, 2 * width, 3 * width, 4 * width, 5 * width
    bias_down_at, gain2_at, shift2_at = 9 * width, 10 * width, 11 * width

    def spread_vectors():
        for blk in range(8):
            tile = vec_all[4 * blk].astype(f32)
            for k in range(1, 4):
                tile = tile + vec_all[4 * blk + k].astype(f32)
            for r in range(9):
                at = (blk * 9 + r) * 128
                vec_row[0:1, at : at + 128] = tile[r : r + 1, :]

    def relayout(p, target):
        source = raw[p]

        def body(j, carry):
            for h in range(2):
                even, odd = h * 32 + 2 * j, h * 32 + 2 * j + 1
                first_dev = source[even // 16, pl.ds((even % 16) * 48, 48), :].astype(f32)
                second_dev = source[odd // 16, pl.ds((odd % 16) * 48, 48), :].astype(f32)
                for q in range(2):
                    rows = jnp.concatenate([first_dev[24 * q : 24 * q + 24], second_dev[24 * q : 24 * q + 24]], axis=0)
                    target[2 * h + q, pl.ds(j * 48, 48), :] = rows.astype(bf16)
            return carry

        lax.fori_loop(0, 16, body, 0)

    def transpose_into(source, target):
        def body(j, carry):
            at = pl.multiple_of(j * 256, 256)
            target[pl.ds(at, 256), :] = jnp.transpose(source[:, pl.ds(at, 256)])
            return carry

        lax.fori_loop(0, source.shape[1] // 256, body, 0)

    def token_weights():
        lane = lax.broadcasted_iota(jnp.int32, (1, 128), 1)
        left = (lane < 64).astype(f32)
        for p in range(4):
            m = tok_ref[p : p + 1, :]
            n0 = jnp.sum(m * left, axis=1, keepdims=True)
            n1 = jnp.sum(m * (1.0 - left), axis=1, keepdims=True)
            w = m / (left * n0 + (1.0 - left) * n1)
            tok_w[128 * p : 128 * p + 128, :] = jnp.transpose(jnp.broadcast_to(w, (128, 128)))

    def project():
        def body(t, carry):
            c, n = t // 3, t % 3
            at = pl.multiple_of(n * 256, 256)
            bias = vec_row[0:1, pl.ds(pl.multiple_of(jnp.where(c == 2, bias_v, bias_q) + at, 256), 256)]
            bias = bias * jnp.where(c == 1, 0.0, 1.0)
            out = dot_nn(x_ref[...], w_attn[c, :, pl.ds(at, 256)]) + bias
            qkv[c, :, pl.ds(at, 256)] = out.astype(bf16)
            return carry

        lax.fori_loop(0, 9, body, 0)

    lane128 = lax.broadcasted_iota(jnp.int32, (128, 128), 1)
    row128 = lax.broadcasted_iota(jnp.int32, (128, 128), 0)
    even_half = lane128 < 64

    def split_heads(v):
        zero = jnp.zeros_like(v)
        return jnp.concatenate([jnp.where(even_half, v, zero), jnp.where(even_half, zero, v)], axis=0)

    def attend(p):
        rows = pl.ds(pl.multiple_of(p * 128, 128), 128)
        m = tok_ref[pl.ds(p, 1), :]
        same = (row128 < 64) == (lane128 < 64)
        open_one = same & (jnp.broadcast_to(m, (128, 128)) > 0.0)
        block = jnp.where(open_one, 0.0, -1e30)
        block = jnp.concatenate([block, block], axis=0)
        for hp in range(6):
            lanes = slice(128 * hp, 128 * hp + 128)
            q2, k2, v2 = qkv[0, rows, lanes], qkv[1, rows, lanes], qkv[2, rows, lanes]
            s = dot_nt(split_heads(q2), k2) * HEAD ** (-0.5) + block
            e = jnp.exp(s - jnp.max(s, axis=1, keepdims=True))
            a = (e * (1.0 / jnp.sum(e, axis=1, keepdims=True))).astype(bf16)
            probs[p * 6 + hp] = a
            wide = jnp.concatenate([a[:128], a[128:]], axis=1)
            ctx[rows, lanes] = dot_nn(wide, split_heads(v2)).astype(bf16)

    def attend_some(lo, hi):
        def body(p, carry):
            attend(p)
            return carry

        lax.fori_loop(lo, hi, body, 0)

    def norm_rows(i, source_fn, hat, rstd, emit):
        rows = pl.ds(pl.multiple_of(i * 64, 64), 64)
        h = source_fn(rows)
        centre = h - jnp.mean(h, axis=1, keepdims=True)
        r = lax.rsqrt(jnp.mean(centre * centre, axis=1, keepdims=True) + norm_epsilon)
        xh = centre * r
        hat[rows, :] = xh
        rstd[rows, :] = jnp.broadcast_to(r, (64, 128))
        if emit is not None:
            emit(rows, xh)

    def attn_out():
        def body(n, carry):
            at = pl.multiple_of(n * 256, 256)
            work[:, pl.ds(at, 256)] = dot_nn(ctx[...], w_attn[3, :, pl.ds(at, 256)])
            return carry

        lax.fori_loop(0, 3, body, 0)

        def source(rows):
            return x_ref[rows, :].astype(f32) + work[rows, :] + vec(bias_o)

        def emit(rows, xh):
            y_low[rows, :] = (xh * (1.0 + vec(gain1_at)) + vec(shift1_at)).astype(bf16)

        def norm(i, carry):
            norm_rows(i, source, xhat1, rstd1, emit)
            return carry

        lax.fori_loop(0, 8, norm, 0)

    def feed_up(lo, hi):
        def body(t, carry):
            c, n = t // 3, t % 3
            at = pl.multiple_of(n * 256, 256)
            to = pl.multiple_of(t * 256, 256)
            work[:, pl.ds(0, 256)] = dot_nn(y_low[...], w_up[c, :, pl.ds(at, 256)])
            bias = vec_row[0:1, pl.ds(pl.multiple_of(bias_up_at + to, 256), 256)]

            def rows_of(i, inner):
                rows = pl.ds(pl.multiple_of(i * 32, 32), 32)
                v = work[rows, 0:256] + bias
                cdf = 0.5 * (1.0 + lax.erf(v * 0.7071067811865476))
                dens = jnp.exp(v * v * -0.5) * 0.3989422804014327
                act[rows, pl.ds(to, 256)] = (v * cdf).astype(bf16)
                slope[rows, pl.ds(to, 256)] = (cdf + v * dens).astype(bf16)
                return inner

            lax.fori_loop(0, 16, rows_of, 0)
            act_t[pl.ds(to, 256), :] = jnp.transpose(act[:, pl.ds(to, 256)])
            return carry

        lax.fori_loop(lo, hi, body, 0)

    def feed_down():
        def body(n, carry):
            at = pl.multiple_of(n * 256, 256)
            total = dot_nn(act[:, 0:width], w_down[0, :, pl.ds(at, 256)])
            for c in range(1, 4):
                total = total + dot_nn(act[:, c * width : (c + 1) * width], w_down[c, :, pl.ds(at, 256)])
            work[:, pl.ds(at, 256)] = total
            return carry

        lax.fori_loop(0, 3, body, 0)

        def source(rows):
            return y_low[rows, :].astype(f32) + work[rows, :] + vec(bias_down_at)

        def norm(i, carry):
            norm_rows(i, source, xhat2, rstd2, None)
            rows = pl.ds(pl.multiple_of(i * 64, 64), 64)
            got = jnp.sum(xhat2[rows, :] * tok_w[rows, 0:1], axis=0, keepdims=True)
            at = i // 2 + 4 * (i % 2)
            pooled_hat[pl.ds(at, 1), :] = got
            return carry

        lax.fori_loop(0, 8, norm, 0)

    me = b * 4 + z

    def pool():
        e = pooled_hat[...] * (1.0 + vec(gain2_at)) + vec(shift2_at)
        r = lax.rsqrt(jnp.sum(e * e, axis=1, keepdims=True) + unit_epsilon)
        unit_rs[...] = jnp.broadcast_to(r, (8, 128))
        pairs[me, :, 0:width] = e * r
        pairs[me, :, width : width + 128] = group_ref[...]

    def contrast():
        total = 256
        every = pairs[...].reshape(total, width + 128)
        v = every[:, 0:width]
        tag = every[:, width : width + 128]
        tag_row = jnp.concatenate([jnp.transpose(tag[0:128])[0:1], jnp.transpose(tag[128:256])[0:1]], axis=1)
        s = dot_nt(v, v, precision=highest) * score_scale
        i = lax.broadcasted_iota(jnp.int32, (total, total), 0)
        j = lax.broadcasted_iota(jnp.int32, (total, total), 1)
        opposite = (i & 4) != (j & 4)
        diagonal = (i ^ j) == 4
        s = s - jnp.where(diagonal, score_scale * margin, 0.0)
        same = (tag[:, 0:1] == tag_row) & (tag_row >= 0.0) & opposite
        e = jnp.where(same, jnp.exp(jnp.where(same, s, 0.0)), 0.0)
        sums = jnp.sum(e, axis=0, keepdims=True)
        valid = (tag_row >= 0.0).astype(f32)
        sums = jnp.where(tag_row >= 0.0, sums, 1.0)
        doubled = jnp.sum(valid)
        coef = 1.0 / doubled
        positive = jnp.sum(jnp.where(diagonal & same, s, 0.0))
        loss = (jnp.sum(jnp.log(sums) * valid) - positive) * coef
        loss_ref[...] = jnp.full((8, 128), loss, f32)
        pair_k[0] = e
        pair_k[1] = jnp.where(diagonal & same, 2.0, 0.0)
        own_rows = pl.ds(pl.multiple_of(me * 8, 8), 8)
        e_own = pair_k[0, own_rows, :]
        r_own = jnp.sum(e_own, axis=1, keepdims=True)
        r_own = jnp.where(group_ref[:, 0:1] >= 0.0, r_own, 1.0)
        k = (e_own / r_own + e_own / sums - pair_k[1, own_rows, :]) * coef
        dn = score_scale * dot_nn(k, v, precision=highest)
        n = pairs[me, :, 0:width]
        de = unit_rs[:, 0:1] * (dn - n * jnp.sum(n * dn, axis=1, keepdims=True))
        pooled_grad = de
        vec_grad[0:1, gain2_at : gain2_at + width] = jnp.sum(de * pooled_hat[...], axis=0, keepdims=True)
        vec_grad[0:1, shift2_at : shift2_at + width] = jnp.sum(de, axis=0, keepdims=True)
        pooled_hat[...] = pooled_grad

    def norm_two_back():
        def body(i, carry):
            rows = pl.ds(pl.multiple_of(i * 64, 64), 64)
            de = pooled_hat[pl.ds(i // 2 + 4 * (i % 2), 1), :]
            dg = de * (1.0 + vec(gain2_at))
            xh = xhat2[rows, :]
            m1 = jnp.mean(dg, axis=1, keepdims=True)
            m2 = jnp.mean(dg * xh, axis=1, keepdims=True)
            dz = (rstd2[rows, 0:1] * tok_w[rows, 0:1]) * (dg - m1 - xh * m2)
            low = dz.astype(bf16)
            xhat2[rows, :] = dz
            y_low[rows, :] = low
            return carry + jnp.sum(low.astype(f32), axis=0, keepdims=True)

        vec_grad[0:1, bias_down_at : bias_down_at + width] = lax.fori_loop(0, 8, body, jnp.zeros((1, width), f32))

    def grad_w_down():
        def body(m, carry):
            out = dot_nn(act_t[pl.ds(pl.multiple_of(m * 384, 128), 384), :], y_low[...])
            for zz in range(4):
                for h in range(2):
                    s = h * 32 + m * 4 + zz
                    g_down[s // 16, pl.ds((s % 16) * 48, 48), :] = out[96 * zz + 48 * h : 96 * zz + 48 * h + 48].astype(bf16)
            return carry

        lax.fori_loop(0, 8, body, 0)

    def grad_act(lo, hi):
        def body(t, carry):
            c, n = t // 3, t % 3
            to = pl.multiple_of(t * 256, 256)
            work[:, 0:256] = dot_nt(y_low[...], w_down[c, pl.ds(pl.multiple_of(n * 256, 256), 256), :])

            def rows_of(i, total):
                rows = pl.ds(pl.multiple_of(i * 64, 64), 64)
                low = (work[rows, 0:256] * slope[rows, pl.ds(to, 256)].astype(f32)).astype(bf16)
                act[rows, pl.ds(to, 256)] = low
                return total + jnp.sum(low.astype(f32), axis=0, keepdims=True)

            sums = lax.fori_loop(0, 8, rows_of, jnp.zeros((1, 256), f32))
            vec_grad[0:1, pl.ds(pl.multiple_of(bias_up_at + to, 256), 256)] = sums
            return carry

        lax.fori_loop(lo, hi, body, 0)

    def store_pairs(target, h, m, first_chunk, second_chunk):
        for d in range(16):
            both = jnp.concatenate([first_chunk[24 * d : 24 * d + 24], second_chunk[24 * d : 24 * d + 24]], axis=0)
            s = h * 32 + m * 16 + d
            target[s // 16, pl.ds((s % 16) * 48, 48), :] = both.astype(bf16)

    def grad_w_up():
        def body(t, carry):
            h, m = t // 2, t % 2
            rows = pl.ds(pl.multiple_of(m * 384, 128), 384)
            at = pl.multiple_of(h * 2 * width, 256)
            one = dot_nn(y_t[rows, :], act[:, pl.ds(at, width)])
            two = dot_nn(y_t[rows, :], act[:, pl.ds(at + width, width)])
            store_pairs(g_up, h, m, one, two)
            return carry

        lax.fori_loop(0, 4, body, 0)

    def grad_y():
        def body(n, carry):
            at = pl.multiple_of(n * 256, 256)
            total = xhat2[:, pl.ds(at, 256)]
            for c in range(4):
                total = total + dot_nt(act[:, c * width : (c + 1) * width], w_up[c, pl.ds(at, 256), :])
            work[:, pl.ds(at, 256)] = total
            return carry

        lax.fori_loop(0, 3, body, 0)

    def norm_one_back():
        def body(i, carry):
            rows = pl.ds(pl.multiple_of(i * 64, 64), 64)
            dy = work[rows, :]
            xh = xhat1[rows, :]
            dg = dy * (1.0 + vec(gain1_at))
            m1 = jnp.mean(dg, axis=1, keepdims=True)
            m2 = jnp.mean(dg * xh, axis=1, keepdims=True)
            dh = rstd1[rows, 0:1] * (dg - m1 - xh * m2)
            low = dh.astype(bf16)
            work[rows, :] = dh
            y_low[rows, :] = low
            gain, shift, bias = carry
            return (
                gain + jnp.sum(dy * xh, axis=0, keepdims=True),
                shift + jnp.sum(dy, axis=0, keepdims=True),
                bias + jnp.sum(low.astype(f32), axis=0, keepdims=True),
            )

        zero = jnp.zeros((1, width), f32)
        gain, shift, bias = lax.fori_loop(0, 8, body, (zero, zero, zero))
        vec_grad[0:1, gain1_at : gain1_at + width] = gain
        vec_grad[0:1, shift1_at : shift1_at + width] = shift
        vec_grad[0:1, bias_o : bias_o + width] = bias

    def grad_ctx():
        def body(n, carry):
            at = pl.multiple_of(n * 256, 256)
            ctx[:, pl.ds(at, 256)] = dot_nt(y_low[...], w_attn[3, pl.ds(at, 256), :]).astype(bf16)
            return carry

        lax.fori_loop(0, 3, body, 0)

    def attend_back(p):
        rows = pl.ds(pl.multiple_of(p * 128, 128), 128)
        for hp in range(6):
            lanes = slice(128 * hp, 128 * hp + 128)
            q2, k2, v2 = qkv[0, rows, lanes], qkv[1, rows, lanes], qkv[2, rows, lanes]
            dc = split_heads(ctx[rows, lanes])
            a = probs[p * 6 + hp]
            af = a.astype(f32)
            da = dot_nt(dc, v2)
            ds = (af * (da - jnp.sum(af * da, axis=1, keepdims=True))).astype(bf16)
            dv = dot_tn(a, dc)
            wide = jnp.concatenate([ds[:128], ds[128:]], axis=1)
            dq = dot_nn(wide, split_heads(k2)) * HEAD ** (-0.5)
            dk = dot_tn(ds, split_heads(q2)) * HEAD ** (-0.5)
            qkv[0, rows, lanes] = dq.astype(bf16)
            qkv[1, rows, lanes] = dk.astype(bf16)
            qkv[2, rows, lanes] = dv.astype(bf16)

    def attend_back_some(lo, hi):
        def body(p, carry):
            attend_back(p)
            return carry

        lax.fori_loop(lo, hi, body, 0)

    def grad_bias_in():
        def body(i, carry):
            rows = pl.ds(pl.multiple_of(i * 64, 64), 64)
            one, two = carry
            return (
                one + jnp.sum(qkv[0, rows, :].astype(f32), axis=0, keepdims=True),
                two + jnp.sum(qkv[2, rows, :].astype(f32), axis=0, keepdims=True),
            )

        zero = jnp.zeros((1, width), f32)
        one, two = lax.fori_loop(0, 8, body, (zero, zero))
        vec_grad[0:1, bias_q : bias_q + width] = one
        vec_grad[0:1, bias_v : bias_v + width] = two

    g_attn = w_up

    def grad_w_attn():
        def body(m, carry):
            rows = pl.ds(pl.multiple_of(m * 384, 128), 384)
            one = dot_nn(x_t[rows, :], qkv[0])
            two = dot_nn(x_t[rows, :], qkv[1])
            store_pairs(g_attn, 0, m, one, two)
            one = dot_nn(x_t[rows, :], qkv[2])
            two = dot_nn(ctx_t[rows, :], y_low[...])
            store_pairs(g_attn, 1, m, one, two)
            return carry

        lax.fori_loop(0, 2, body, 0)

    def grad_x():
        def body(n, carry):
            at = pl.multiple_of(n * 256, 256)
            total = work[:, pl.ds(at, 256)]
            for c in range(3):
                total = total + dot_nt(qkv[c], w_attn[c, pl.ds(at, 256), :])
            dx_ref[:, pl.ds(at, 256)] = total
            return carry

        lax.fori_loop(0, 3, body, 0)

    grads = (g_attn, g_up, g_down)
    boxes = (w_down, raw_u, raw_a)
    outs = (grad_attn_ref, grad_up_ref, grad_down_ref)

    def at_q(q):
        return b ^ (2 * q)

    def c_slot(h, q):
        return h * 16 + q * 4

    def one_slot(h, own_side):
        return 32 + (h * 2 + own_side) * 4

    def two_slot(h):
        return 48 + h * 4

    def z_slot(h, zs):
        return 56 + h * 4 + zs

    def core_send(p):
        for h, q in ((0, 3), (1, 3), (0, 2), (1, 1), (0, 1), (1, 2), (0, 0), (1, 0)):
            s = h * 32 + (at_q(q) ^ 1) * 4
            remote(quad(grads[p], s), quad(boxes[p], c_slot(h, q)), rs_send.at[p, 0], rc_sem.at[p, h, q], comm.C).start()

    def quad_wait(p, s, sem):
        remote(quad(boxes[p], s), quad(boxes[p], s), rs_send.at[p, 0], sem, comm.C).wait_recv()

    def add_in(p, h, q, slots):
        mine = h * 32 + at_q(q) * 4
        target, box = grads[p], boxes[p]

        def body(i, carry):
            at = pl.multiple_of((mine % 16) * 48 + i * 48, 16)
            total = target[mine // 16, pl.ds(at, 48), :].astype(f32)
            for s in slots:
                from_at = pl.multiple_of((s % 16) * 48 + i * 48, 16)
                total = total + box[s // 16, pl.ds(from_at, 48), :].astype(f32)
            target[mine // 16, pl.ds(at, 48), :] = total.astype(bf16)
            return carry

        lax.fori_loop(0, 4, body, 0)

    def pass_on(p, h, q, device, way, to_slot, sem):
        s = h * 32 + at_q(q) * 4
        remote(quad(grads[p], s), quad(boxes[p], to_slot), rs_send.at[p, way], sem, device).start()

    def stage_one(p):
        for h, q in ((0, 3), (1, 3), (0, 2), (1, 1)):
            quad_wait(p, c_slot(h, q), rc_sem.at[p, h, q])
            add_in(p, h, q, (c_slot(h, q),))
            side = 1 if q == 3 else 0
            pass_on(p, h, q, comm.Y if h == 0 else comm.X, 2 if h == 0 else 1, one_slot(h, side), r1_sem.at[p, h, side])

    def stage_two(p):
        for h, q in ((0, 1), (1, 2)):
            quad_wait(p, c_slot(h, q), rc_sem.at[p, h, q])
            quad_wait(p, one_slot(h, 1), r1_sem.at[p, h, 1])
            add_in(p, h, q, (c_slot(h, q), one_slot(h, 1)))
            pass_on(p, h, q, comm.X if h == 0 else comm.Y, 1 if h == 0 else 2, two_slot(h), r2_sem.at[p, h])

    def stage_three(p):
        for h in range(2):
            quad_wait(p, c_slot(h, 0), rc_sem.at[p, h, 0])
            quad_wait(p, one_slot(h, 0), r1_sem.at[p, h, 0])
            quad_wait(p, two_slot(h), r2_sem.at[p, h])
            add_in(p, h, 0, (c_slot(h, 0), one_slot(h, 0), two_slot(h)))
            for k in (1, 2, 3):
                s = h * 32 + b * 4 + (z ^ k)
                remote(unit(grads[p], s), unit(boxes[p], z_slot(h, z)), rs_send.at[p, 3], rz_sem.at[p, h, z], comm.Z[k]).start()

    def stage_end(p):
        for h in range(2):
            s = h * 32 + b * 4 + z
            total = grads[p][s // 16, pl.ds((s % 16) * 48, 48), :].astype(f32)
            for k in (1, 2, 3):
                t = z_slot(h, z ^ k)
                remote(unit(boxes[p], t), unit(boxes[p], t), rs_send.at[p, 3], rz_sem.at[p, h, z ^ k], comm.C).wait_recv()
                total = total + boxes[p][t // 16, pl.ds((t % 16) * 48, 48), :].astype(f32)
            if p == 2:
                outs[p][48 * h : 48 * h + 48, :] = total
            else:
                outs[p][:, 2 * h * width : (2 * h + 1) * width] = total[0:24]
                outs[p][:, (2 * h + 1) * width : (2 * h + 2) * width] = total[24:48]

    def sums_sent(p):
        for way, n in ((0, 32), (1, 12), (2, 12), (3, 6)):
            part = span(grads[p], n)
            remote(part, part, rs_send.at[p, way], rc_sem.at[p, 0, 0], comm.C).wait_send()

    def vec_pack():
        for blk in range(8):
            for r in range(9):
                at = (blk * 9 + r) * 128
                vec_out[blk, r : r + 1, :] = vec_grad[0:1, at : at + 128]
            vec_out[blk, 9:16, :] = jnp.zeros((7, 128), f32)

    def vec_copy(src, dst, n, device):
        return remote(vec_out.at[src], vec_in.at[dst], vs_sem.at[n], vr_sem.at[dst], device)

    def vec_core():
        for q in range(4):
            vec_copy(at_q(q) ^ 1, q, q, comm.C).start()

    def vec_take(dst, target):
        vec_copy(target, dst, 0, comm.C).wait_recv()
        vec_out[target] = vec_out[target] + vec_in[dst]

    def vec_y():
        for q in range(4):
            vec_take(q, at_q(q))
        vec_copy(at_q(3), 5, 4, comm.Y).start()
        vec_copy(at_q(2), 4, 5, comm.Y).start()

    def vec_x():
        vec_take(5, at_q(1))
        vec_copy(at_q(1), 6, 6, comm.X).start()

    def vec_z():
        vec_take(4, b)
        vec_take(6, b)
        for k in (1, 2, 3):
            vec_copy(b, 8 + z, 6 + k, comm.Z[k]).start()

    def vec_end():
        total = vec_out[b]
        for k in (1, 2, 3):
            vec_copy(b, 8 + (z ^ k), 0, comm.C).wait_recv()
            total = total + vec_in[8 + (z ^ k)]
        grad_vec_ref[...] = total
        for n in range(10):
            vec_copy(b, 0, n, comm.C).wait_send()

    comm.barrier()
    vec_all[pl.ds(me, 1)] = vec_ref[...].astype(bf16).reshape(1, 16, 128)
    own(0)
    small_z(vec_all, 0)
    own(1)
    token_weights()
    from_z(0, 1)
    from_z(0, 2)
    first(1)
    small_plane(vec_all, 0)
    near(across, 0, 0)
    from_z(0, 3)
    near(across, 0, 1)
    own(2)
    small_cross(vec_all, 0)
    from_z(1, 1)
    near(across, 0, 2)
    near(last, 0, 0)
    from_z(1, 2)
    small_end(vec_all, 0)
    spread_vectors()
    transpose_into(x_ref, x_t)
    near(across, 0, 3)
    first(2)
    near(last, 0, 1)
    from_z(1, 3)
    near(last, 0, 2)
    near(last, 0, 3)
    gathered(0)
    from_z(2, 1)
    near(last, 1, 0)
    relayout(0, w_attn)
    project()
    from_z(2, 2)
    near(last, 1, 1)
    attend_some(0, 2)
    from_z(2, 3)
    near(last, 1, 2)
    attend_some(2, 4)
    near(last, 1, 3)
    near(last, 2, 0)
    attn_out()
    near(last, 2, 1)
    gathered(1)
    relayout(1, w_up)
    feed_up(0, 6)
    near(last, 2, 2)
    near(last, 2, 3)
    feed_up(6, 12)
    transpose_into(y_low, y_t)
    transpose_into(ctx, ctx_t)
    gathered(2)
    feed_down()
    pool()
    for p in range(3):
        sent(p)
    small_z(pairs, 1)
    small_plane(pairs, 1)
    small_cross(pairs, 1)
    small_end(pairs, 1)
    contrast()
    norm_two_back()
    grad_w_down()
    core_send(2)
    grad_act(0, 6)
    stage_one(2)
    grad_act(6, 12)
    grad_w_up()
    core_send(1)
    stage_two(2)
    grad_y()
    stage_one(1)
    norm_one_back()
    grad_ctx()
    stage_three(2)
    attend_back_some(0, 2)
    stage_two(1)
    attend_back_some(2, 4)
    stage_end(2)
    grad_w_attn()
    core_send(0)
    grad_bias_in()
    vec_pack()
    vec_core()
    stage_three(1)
    stage_one(0)
    vec_y()
    grad_x()
    vec_x()
    stage_end(1)
    stage_two(0)
    vec_z()
    stage_three(0)
    vec_end()
    stage_end(0)
    for p in range(3):
        sums_sent(p)


def fused_layer(x, tok, group, rows, down, vec):
    big = (4, 768, 768)
    scratch = [pltpu.VMEM(big, bf16)] * 7
    scratch += [
        pltpu.VMEM((3, 512, 768), bf16),
        pltpu.VMEM((24, 256, 128), bf16),
        pltpu.VMEM((512, 768), bf16),
        pltpu.VMEM((768, 512), bf16),
        pltpu.VMEM((768, 512), bf16),
        pltpu.VMEM((512, 768), bf16),
        pltpu.VMEM((768, 512), bf16),
        pltpu.VMEM((512, 3072), bf16),
        pltpu.VMEM((3072, 512), bf16),
        pltpu.VMEM((512, 3072), bf16),
        pltpu.VMEM((512, 768), f32),
        pltpu.VMEM((512, 768), f32),
        pltpu.VMEM((512, 768), f32),
        pltpu.VMEM((512, 128), f32),
        pltpu.VMEM((512, 128), f32),
        pltpu.VMEM((512, 128), f32),
        pltpu.VMEM((32, 16, 128), bf16),
        pltpu.VMEM((8, 9216), f32),
        pltpu.VMEM((32, 8, 896), f32),
        pltpu.VMEM((8, 768), f32),
        pltpu.VMEM((8, 128), f32),
        pltpu.VMEM((2, 256, 256), f32),
        pltpu.VMEM((8, 9216), f32),
        pltpu.VMEM((8, 16, 128), f32),
        pltpu.VMEM((12, 16, 128), f32),
    ]
    dma = pltpu.SemaphoreType.DMA
    scratch += [
        dma((3, 2, 3, 4)), dma((3, 4, 2)), dma((3, 4, 2)), dma((3, 4, 2)), dma((3,)), dma((3, 5)),
        dma((2, 11)), dma((2, 8)),
        dma((3, 2, 4)), dma((3, 2, 2)), dma((3, 2)), dma((3, 2, 4)), dma((3, 4)),
        dma((12,)), dma((10,)),
    ]
    vmem = pl.BlockSpec(memory_space=pltpu.VMEM)
    return pl.pallas_call(
        layer_kernel,
        out_shape=(
            jax.ShapeDtypeStruct((8, 128), f32),
            jax.ShapeDtypeStruct((512, 768), f32),
            jax.ShapeDtypeStruct((24, 3072), f32),
            jax.ShapeDtypeStruct((24, 3072), f32),
            jax.ShapeDtypeStruct((96, 768), f32),
            jax.ShapeDtypeStruct((16, 128), f32),
        ),
        in_specs=[vmem] * 6,
        out_specs=(vmem,) * 6,
        scratch_shapes=scratch,
        compiler_params=pltpu.CompilerParams(collective_id=0, has_side_effects=True, vmem_limit_bytes=64 * 1024 * 1024 - 65536),
    )(x, tok, group, rows, down, vec)


def adam_step(master, gradient, moment_one, moment_two, decay, rate):
    mean_new = beta_one * moment_one + (1.0 - beta_one) * gradient
    square_new = beta_two * moment_two + (1.0 - beta_two) * gradient * gradient
    mean_hat = mean_new / (1.0 - beta_one**STEP)
    square_hat = square_new / (1.0 - beta_two**STEP)
    updated = master - rate * (mean_hat / (jnp.sqrt(square_hat) + adam_epsilon) + decay * master)
    return (updated, mean_new, square_new)


def on_device_fused(
    embeds, token_mask, groups, counts,
    rows_master, rows_mean, rows_square, down_master, down_mean, down_square,
    vector_master, vector_mean, vector_square,
):
    slots, sides, length, width = embeds.shape
    z = lax.axis_index("dp")
    share = vector_master.shape[0]
    x = embeds.reshape(slots * sides * length, width)
    tok = token_mask.reshape(slots, sides * length).astype(f32)
    tags = jnp.where(jnp.arange(slots) < counts[0], groups, -1).astype(f32)
    tags = jnp.broadcast_to(jnp.concatenate([tags, tags])[:, None], (2 * slots, 128))
    tile = lax.dynamic_update_slice(jnp.zeros((4 * share,), f32), vector_master, (z * share,))
    tile = jnp.pad(tile.reshape(9, 128), ((0, 7), (0, 0)))
    loss, dx, g_attn, g_up, g_down, g_vec = fused_layer(x, tok, tags, rows_master, down_master, tile)
    rows_grad = jnp.concatenate([g_attn, g_up], axis=1)
    vec_grad = lax.dynamic_slice(g_vec[:9].reshape(-1), (z * share,), (share,))
    rows_new = adam_step(rows_master, rows_grad, rows_mean, rows_square, decay_rate, learn_rate)
    down_new = adam_step(down_master, g_down, down_mean, down_square, decay_rate, learn_rate)
    vector_new = adam_step(vector_master, vec_grad, vector_mean, vector_square, 0.0, vector_rate)
    return (loss[0, 0], dx.reshape(embeds.shape)) + rows_new + down_new + vector_new


def layer_norm(values, scale_vec, shift_vec):
    centre = values - jnp.mean(values, axis=-1, keepdims=True)
    spread = jnp.mean(centre * centre, axis=-1, keepdims=True)
    return centre * lax.rsqrt(spread + norm_epsilon) * scale_vec + shift_vec


def pool_unit(weights, output):
    summed = jnp.sum(output * weights[:, :, None], axis=1) / jnp.sum(weights, axis=1, keepdims=True)
    return summed * lax.rsqrt(jnp.sum(summed * summed, axis=1, keepdims=True) + unit_epsilon)


def exact_gelu(values):
    return jax.nn.gelu(values, approximate=False)


def softmax_last(values):
    return jax.nn.softmax(values, axis=-1)


def split_vectors(vectors, model_width, hidden):
    extents = [model_width] * 5 + [hidden] + [model_width] * 3
    pieces_out = []
    offset = 0
    for extent in extents:
        pieces_out.append(vectors[offset : offset + extent])
        offset = offset + extent
    return pieces_out


def pair_exps(left_rows, right_rows, left_group, right_group, left_start, right_start):
    scores = score_scale * jnp.dot(left_rows, right_rows.T, precision=highest)
    left_index = left_start + jnp.arange(left_rows.shape[0])
    right_index = right_start + jnp.arange(right_rows.shape[0])
    diagonal = left_index[:, None] == right_index[None, :]
    scores = scores - score_scale * margin * diagonal.astype(jnp.float32)
    same = (left_group[:, None] == right_group[None, :]) & (left_group[:, None] >= 0.0)
    return (jnp.where(same, jnp.exp(scores), 0.0), (diagonal & same).astype(jnp.float32))


def add_sums(own_data, arrived, offset):
    sources, targets, group_own, own_start = own_data
    other_src, other_tgt, other_group = arrived
    row_exp, unused_row = pair_exps(sources, other_tgt, group_own, other_group, own_start, offset)
    col_exp, unused_col = pair_exps(other_src, targets, other_group, group_own, offset, own_start)
    return (jnp.sum(row_exp, axis=1), jnp.sum(col_exp, axis=0))


def add_grads(own_data, loss_coef, arrived, offset):
    sources, targets, group_own, own_start, row_own, col_own = own_data
    other_src, other_tgt, other_group, other_row, other_col = arrived
    row_exp, row_diag = pair_exps(sources, other_tgt, group_own, other_group, own_start, offset)
    row_coef = (
        row_exp / row_own[:, None] + row_exp / other_col[None, :] - 2.0 * row_diag
    ) * loss_coef
    col_exp, col_diag = pair_exps(other_src, targets, other_group, group_own, offset, own_start)
    col_coef = (
        col_exp / other_row[:, None] + col_exp / col_own[None, :] - 2.0 * col_diag
    ) * loss_coef
    grad_src = score_scale * jnp.dot(row_coef, other_tgt, precision=highest)
    grad_tgt = score_scale * jnp.dot(col_coef.T, other_src, precision=highest)
    return (grad_src, grad_tgt)


def on_device_general(
    embeds,
    token_mask,
    groups,
    counts,
    rows_master,
    rows_mean,
    rows_square,
    down_master,
    down_mean,
    down_square,
    vector_master,
    vector_mean,
    vector_square,
):
    slot_count = embeds.shape[0]
    length = embeds.shape[2]
    model_width = embeds.shape[3]
    row_all, down_all, vector_all = (
        lax.all_gather(rows_master.astype(jnp.bfloat16), ("blk", "dp"), axis=0, tiled=True),
        lax.all_gather(down_master.astype(jnp.bfloat16), ("blk", "dp"), axis=0, tiled=True),
        lax.all_gather(vector_master.astype(jnp.bfloat16), ("blk", "dp"), axis=0, tiled=True),
    )
    hidden = down_all.shape[0]
    vectors = vector_all.astype(jnp.float32)
    bias_q, bias_v, bias_o, gain_one, shift_one, bias_up, bias_down, gain_two, shift_two = (
        split_vectors(vectors, model_width, hidden)
    )
    w_attn_in = row_all[:, : 3 * model_width]
    w_attn_out = row_all[:, 3 * model_width : 4 * model_width]
    w_up = row_all[:, 4 * model_width :]
    seq_count = 2 * slot_count
    tokens = seq_count * length
    head_count = model_width // HEAD
    inputs = embeds.reshape(tokens, model_width)
    weights = token_mask.reshape(seq_count, length).astype(jnp.float32)
    key_valid = token_mask.reshape(seq_count, length) > 0
    joined = jnp.concatenate([bias_q, jnp.zeros_like(bias_q), bias_v])
    projected = (jnp.dot(inputs, w_attn_in, preferred_element_type=jnp.float32) + joined).astype(
        jnp.bfloat16
    )
    queries = projected[:, :model_width].reshape(seq_count, length, head_count, HEAD)
    key_part = projected[:, model_width : 2 * model_width].reshape(
        seq_count, length, head_count, HEAD
    )
    values = projected[:, 2 * model_width :].reshape(seq_count, length, head_count, HEAD)
    scores = jnp.einsum(
        "nihe,njhe->nhij", queries, key_part, preferred_element_type=jnp.float32
    ) * HEAD ** (-0.5)
    scores = jnp.where(key_valid[:, None, None, :], scores, -1e30)
    attention, soft_back = jax.vjp(softmax_last, scores)
    attention_low = attention.astype(jnp.bfloat16)
    context = (
        jnp.einsum("nhij,njhe->nihe", attention_low, values, preferred_element_type=jnp.float32)
        .astype(jnp.bfloat16)
        .reshape(tokens, model_width)
    )
    resid_one = (
        inputs.astype(jnp.float32)
        + jnp.dot(context, w_attn_out, preferred_element_type=jnp.float32)
        + bias_o
    )
    normed_full, norm_one_back = jax.vjp(layer_norm, resid_one, 1.0 + gain_one, shift_one)
    normed_one = normed_full.astype(jnp.bfloat16)
    up_pre = jnp.dot(normed_one, w_up, preferred_element_type=jnp.float32) + bias_up
    activated_full, gelu_back = jax.vjp(exact_gelu, up_pre)
    activated = activated_full.astype(jnp.bfloat16)
    resid_two = (
        normed_one.astype(jnp.float32)
        + jnp.dot(activated, down_all, preferred_element_type=jnp.float32)
        + bias_down
    )
    output, norm_two_back = jax.vjp(layer_norm, resid_two, 1.0 + gain_two, shift_two)
    pooled, pool_back = jax.vjp(
        partial(pool_unit, weights), output.reshape(seq_count, length, model_width)
    )
    pooled = pooled.reshape(slot_count, 2, model_width)
    sources = pooled[:, 0]
    targets = pooled[:, 1]
    own_start = lax.axis_index(("blk", "dp")) * slot_count
    valid_slot = jnp.arange(slot_count) < counts[0]
    group_own = jnp.where(valid_slot, groups, -1).astype(jnp.float32)
    pair_total = lax.psum(counts[0].astype(jnp.float32), ("blk", "dp"))
    loss_coef = 0.5 / pair_total
    own_sums = (sources, targets, group_own, own_start)
    row_sum, col_sum = add_sums(
        own_sums,
        (
            lax.all_gather(sources, ("blk", "dp"), axis=0, tiled=True),
            lax.all_gather(targets, ("blk", "dp"), axis=0, tiled=True),
            lax.all_gather(group_own, ("blk", "dp"), axis=0, tiled=True),
        ),
        jnp.int32(0),
    )
    row_safe = jnp.where(valid_slot, row_sum, 1.0)
    col_safe = jnp.where(valid_slot, col_sum, 1.0)
    own_grads = (sources, targets, group_own, own_start, row_safe, col_safe)
    grad_src, grad_tgt = add_grads(
        own_grads,
        loss_coef,
        (
            lax.all_gather(sources, ("blk", "dp"), axis=0, tiled=True),
            lax.all_gather(targets, ("blk", "dp"), axis=0, tiled=True),
            lax.all_gather(group_own, ("blk", "dp"), axis=0, tiled=True),
            lax.all_gather(row_safe, ("blk", "dp"), axis=0, tiled=True),
            lax.all_gather(col_safe, ("blk", "dp"), axis=0, tiled=True),
        ),
        jnp.int32(0),
    )
    positive = score_scale * jnp.sum(sources * targets, axis=1) - score_scale * margin
    loss_terms = jnp.sum(
        jnp.where(valid_slot, jnp.log(row_safe) + jnp.log(col_safe) - 2.0 * positive, 0.0)
    )
    pair_loss = lax.psum(loss_terms, ("blk", "dp")) * loss_coef
    grad_pooled = jnp.stack([grad_src, grad_tgt], axis=1).reshape(seq_count, model_width)
    grad_output = pool_back(grad_pooled)[0].reshape(tokens, model_width)
    grad_resid_two, grad_gain_two, grad_shift_two = norm_two_back(grad_output)
    grad_down_low = grad_resid_two.astype(jnp.bfloat16)
    grad_w_down = jnp.einsum(
        "tf,td->fd", activated, grad_down_low, preferred_element_type=jnp.float32
    )
    grad_bias_down = jnp.sum(grad_down_low.astype(jnp.float32), axis=0)
    grad_act = jnp.einsum("td,fd->tf", grad_down_low, down_all, preferred_element_type=jnp.float32)
    grad_up = gelu_back(grad_act)[0].astype(jnp.bfloat16)
    grad_w_up = jnp.einsum("td,tf->df", normed_one, grad_up, preferred_element_type=jnp.float32)
    grad_bias_up = jnp.sum(grad_up.astype(jnp.float32), axis=0)
    grad_normed = grad_resid_two + jnp.einsum(
        "tf,df->td", grad_up, w_up, preferred_element_type=jnp.float32
    )
    grad_resid_one, grad_gain_one, grad_shift_one = norm_one_back(grad_normed)
    grad_attn_low = grad_resid_one.astype(jnp.bfloat16)
    grad_w_out = jnp.einsum("td,te->de", context, grad_attn_low, preferred_element_type=jnp.float32)
    grad_bias_out = jnp.sum(grad_attn_low.astype(jnp.float32), axis=0)
    grad_context = jnp.einsum(
        "te,de->td", grad_attn_low, w_attn_out, preferred_element_type=jnp.float32
    ).astype(jnp.bfloat16)
    grad_context = grad_context.reshape(seq_count, length, head_count, HEAD)
    grad_attention = jnp.einsum(
        "nihe,njhe->nhij", grad_context, values, preferred_element_type=jnp.float32
    )
    grad_values = jnp.einsum(
        "nhij,nihe->njhe", attention_low, grad_context, preferred_element_type=jnp.float32
    )
    grad_scores = soft_back(grad_attention)[0].astype(jnp.bfloat16)
    grad_queries = jnp.einsum(
        "nhij,njhe->nihe", grad_scores, key_part, preferred_element_type=jnp.float32
    ) * HEAD ** (-0.5)
    grad_keys = jnp.einsum(
        "nhij,nihe->njhe", grad_scores, queries, preferred_element_type=jnp.float32
    ) * HEAD ** (-0.5)
    grad_projected = jnp.concatenate(
        [
            grad_queries.reshape(tokens, model_width),
            grad_keys.reshape(tokens, model_width),
            grad_values.reshape(tokens, model_width),
        ],
        axis=1,
    ).astype(jnp.bfloat16)
    grad_w_in = jnp.einsum("td,te->de", inputs, grad_projected, preferred_element_type=jnp.float32)
    grad_bias_q = jnp.sum(grad_projected[:, :model_width].astype(jnp.float32), axis=0)
    grad_bias_v = jnp.sum(grad_projected[:, 2 * model_width :].astype(jnp.float32), axis=0)
    grad_inputs = grad_resid_one + jnp.einsum(
        "te,de->td", grad_projected, w_attn_in, preferred_element_type=jnp.float32
    )
    grad_vector = jnp.concatenate(
        [
            grad_bias_q,
            grad_bias_v,
            grad_bias_out,
            grad_gain_one,
            grad_shift_one,
            grad_bias_up,
            grad_bias_down,
            grad_gain_two,
            grad_shift_two,
        ]
    )
    rows_share, down_share, vector_share = (
        lax.psum_scatter(
            jnp.concatenate([grad_w_in, grad_w_out, grad_w_up], axis=1),
            ("blk", "dp"),
            scatter_dimension=0,
            tiled=True,
        ),
        lax.psum_scatter(grad_w_down, ("blk", "dp"), scatter_dimension=0, tiled=True),
        lax.psum_scatter(grad_vector, ("blk", "dp"), scatter_dimension=0, tiled=True),
    )
    rows_new = adam_step(rows_master, rows_share, rows_mean, rows_square, decay_rate, learn_rate)
    down_new = adam_step(down_master, down_share, down_mean, down_square, decay_rate, learn_rate)
    vector_new = adam_step(
        vector_master, vector_share, vector_mean, vector_square, 0.0, vector_rate
    )
    embeds_grad = grad_inputs.reshape(slot_count, 2, length, model_width)
    return (
        pair_loss,
        embeds_grad,
        rows_new[0],
        rows_new[1],
        rows_new[2],
        down_new[0],
        down_new[1],
        down_new[2],
        vector_new[0],
        vector_new[1],
        vector_new[2],
    )


def solution(mesh):
    in_specs = (
        P(("blk", "dp"), None, None, None),
        P(("blk", "dp"), None, None),
        P(("blk", "dp")),
        P(("blk", "dp")),
        P(("blk", "dp"), None),
        P(("blk", "dp"), None),
        P(("blk", "dp"), None),
        P(("blk", "dp"), None),
        P(("blk", "dp"), None),
        P(("blk", "dp"), None),
        P(("blk", "dp")),
        P(("blk", "dp")),
        P(("blk", "dp")),
    )
    out_specs = (
        P(),
        P(("blk", "dp"), None, None, None),
        P(("blk", "dp"), None),
        P(("blk", "dp"), None),
        P(("blk", "dp"), None),
        P(("blk", "dp"), None),
        P(("blk", "dp"), None),
        P(("blk", "dp"), None),
        P(("blk", "dp")),
        P(("blk", "dp")),
        P(("blk", "dp")),
    )
    fits = dict(mesh.shape) == {"blk": 8, "dp": 4}
    return jax.shard_map(
        on_device_fused if fits else on_device_general, mesh=mesh, in_specs=in_specs, out_specs=out_specs, check_vma=False
    )
```

```python
from functools import partial

import jax
import jax.numpy as jnp
from jax import lax
from jax.experimental import pallas as pl
from jax.experimental.pallas import tpu as pltpu
from jax.sharding import PartitionSpec as P

HEAD = 64
STEP = 10


score_scale = 32.0
margin = 0.3
beta_one = 0.9
beta_two = 0.999
learn_rate = 0.03
vector_rate = 0.06
decay_rate = 0.01
adam_epsilon = 1e-08
norm_epsilon = 1e-12
unit_epsilon = 1e-06
highest = lax.Precision.HIGHEST

f32 = jnp.float32
bf16 = jnp.bfloat16


def dot_nn(a, b, precision=None):
    return lax.dot_general(a, b, (((1,), (0,)), ((), ())), precision=precision, preferred_element_type=f32)


def dot_nt(a, b, precision=None):
    return lax.dot_general(a, b, (((1,), (1,)), ((), ())), precision=precision, preferred_element_type=f32)


def dot_tn(a, b):
    return lax.dot_general(a, b, (((0,), (0,)), ((), ())), preferred_element_type=f32)


Z_FIRST, Z_MID = 0, 1
GATHER_MODE = (Z_FIRST, Z_MID, Z_MID, Z_FIRST, Z_MID, Z_FIRST)
REDUCE_MODE = (Z_FIRST, Z_FIRST, Z_MID, Z_MID, Z_MID, Z_FIRST)

PIECES = (
    (((0, 512), (768, 256)), ((1024, 256), (1536, 512))),
    (((512, 256), (1280, 256), (2048, 256)), ((2304, 768),)),
    (((3072, 768),), ((3840, 768),)),
    (((4608, 768),), ((5376, 768),)),
)

PLAN = (
    ("start",), ("vectors", 0), ("cast", 0), ("ownz", 0), ("col", 0, 0), ("cast", 1), ("own1", 1), ("ownz", 1), ("fin", 1, 0, 0),
    ("cast", 2), ("vectors", 1), ("cast", 3), ("load", 1), ("cast", 4), ("cast", 5), ("own1", 2), ("load", 2), ("x_t",),
    ("fin", 2, 0, 0), ("vectors", 2), ("across", 0, 0), ("col", 5, 0), ("first", 1), ("fin", 1, 0, 1), ("col", 0, 1),
    ("last", 0, 0), ("across", 5, 0), ("fold", 0), ("vectors", 3), ("col", 0, 3), ("fold", 1, 0), ("fin", 1, 3, 0),
    ("fin", 1, 1, 0), ("last", 1, 0), ("across", 0, 1), ("fold", 1, 1), ("fin", 1, 3, 1), ("last", 5, 0), ("fin", 1, 1, 1),
    ("across", 0, 3), ("ownz", 2), ("col", 0, 2), ("fin", 1, 2, 0), ("fin", 1, 2, 1), ("last", 0, 1), ("last", 1, 3),
    ("first", 2), ("last", 1, 1), ("fin", 2, 0, 1), ("last", 0, 3), ("across", 0, 2), ("col", 3, 0), ("fold", 2, 0),
    ("fin", 2, 1, 0), ("last", 1, 2), ("fin", 2, 3, 0), ("ownz", 5), ("last", 2, 0), ("gathered", 1), ("last", 0, 2), ("own1", 4),
    ("gathered", 0), ("fin", 2, 1, 1), ("relayout", 0), ("spread",), ("project", 0, 3), ("fold", 2, 1), ("fin", 2, 3, 1),
    ("fin", 2, 2, 0), ("project", 3, 6), ("across", 3, 0), ("attend", 0, 0, 2), ("last", 2, 1), ("last", 2, 3), ("ownz", 3),
    ("fin", 4, 0, 0), ("col", 5, 1), ("attend", 0, 2, 4), ("fin", 2, 2, 1), ("last", 3, 0), ("relayout", 1), ("project", 6, 9),
    ("fold", 5), ("col", 5, 3), ("across", 5, 1), ("attend", 1, 0, 4), ("last", 2, 2), ("fold", 3), ("col", 3, 3), ("attn_out",),
    ("gathered", 2), ("col", 3, 1), ("ownz", 4), ("attn_norm",), ("across", 3, 3), ("across", 5, 3), ("last", 5, 1),
    ("col", 5, 2), ("relayout", 2), ("feed_up", 0, 3), ("col", 3, 2), ("last", 3, 3), ("first", 4), ("last", 5, 3),
    ("across", 3, 1), ("across", 5, 2), ("feed_up", 3, 6), ("across", 3, 2), ("fin", 4, 0, 1), ("last", 3, 1), ("fold", 4, 0),
    ("fin", 4, 3, 0), ("last", 5, 2), ("fin", 4, 1, 0), ("fold", 4, 1), ("gathered", 5), ("fin", 4, 3, 1), ("last", 3, 2),
    ("fin", 4, 1, 1), ("last", 4, 0), ("gathered", 3), ("relayout", 3), ("feed_up", 6, 9), ("fin", 4, 2, 0), ("last", 4, 3),
    ("fin", 4, 2, 1), ("last", 4, 1), ("feed_up", 9, 12), ("last", 4, 2), ("tr",), ("gathered", 4), ("feed_down", 0),
    ("feed_down", 1), ("norm2",), ("pool",), ("pair_gather",), ("contrast",), ("n2",), ("dw2a",), ("dw2b",), ("s1", 4, 1),
    ("df", 0, 4), ("s1", 4, 0), ("df", 4, 8), ("s1", 5, 1), ("df", 8, 12), ("s2", 4), ("s1", 5, 0), ("dw", 2), ("s2", 5),
    ("dw", 3), ("dy",), ("s1", 2, 1), ("s3", 4), ("n1",), ("s1", 2, 0), ("dc",), ("attb", 0, 0, 2), ("s3", 5), ("s1", 3, 1),
    ("attb", 0, 2, 4), ("s2", 2), ("s4", 4), ("dw", 0), ("s1", 3, 0), ("attb", 1, 0, 4), ("s5", 4), ("s1", 0, 1), ("s4", 5),
    ("dw", 1), ("s1", 0, 0), ("bias",), ("vec_pack",), ("vec_core",), ("s2", 3), ("gx", 0, 1), ("vec_y",), ("gx", 1, 2),
    ("vec_x",), ("s2", 0), ("gx", 2, 3), ("vec_z",), ("s5", 5), ("s3", 2), ("s1", 1, 1), ("s3", 0), ("s1", 1, 0), ("s3", 3),
    ("s2", 1), ("s4", 2), ("s4", 0), ("s5", 2), ("s3", 1), ("s4", 3), ("s5", 3), ("s5", 0), ("s4", 1), ("vec_end",), ("s5", 1),
    ("finish",),
)


class Comm:
    def __init__(self, depth):
        self.depth = depth
        self.b = lax.axis_index("blk")
        self.z = lax.axis_index("dp")
        b, z = self.b, self.z
        self.X, self.Y, self.C = (b ^ 2, z), (b ^ 4, z), (b ^ 1, z)
        self.Z = [(b, z ^ k) for k in range(depth)]
        self.up, self.down = (b, z + 1), (b, z - 1)

    def barrier(self):
        sem = pltpu.get_barrier_semaphore()
        friends = [self.X, self.Y, self.C] + self.Z[1:]
        for friend in friends:
            pl.semaphore_signal(sem, inc=1, device_id=friend, device_id_type=pl.DeviceIdType.MESH)
        pl.semaphore_wait(sem, len(friends))


def remote(src, dst, send_sem, recv_sem, device):
    return pltpu.make_async_remote_copy(
        src_ref=src,
        dst_ref=dst,
        send_sem=send_sem,
        recv_sem=recv_sem,
        device_id=device,
        device_id_type=pl.DeviceIdType.MESH,
    )


def layer_kernel(
    x_hbm, tok_ref, group_ref, count_ref, rows_hbm, down_hbm, vec_ref,
    loss_ref, dx_hbm, grad_rows_ref, grad_down_ref, grad_vec_ref,
    x_ref, rows_ref, down_ref,
    raw, w_attn, w_up, w_down, g_rest,
    qkv, probs, ctx, ctx_t, x_t, y_low, y_t, act, act_t, slope, xhat1, xhat2, work,
    rstd1, rstd2, tok_w, tok_f, tags, vec_all, vec_row, bias_in, pairs, pooled_hat, unit_rs, pair_k, vec_grad, vec_out, vec_in,
    local_sem, zsem, xsem, ysem, dsem, csem, ssem,
    small_recv, small_send,
    rc_sem, r1_sem, r2_sem, rz_sem, ry_sem, rf_sem, rs_send,
    vr_sem, vs_sem,
):
    comm = Comm(4)
    b, z = comm.b, comm.z
    me = b * 4 + z
    width = 768
    half = 384
    def at_q(q):
        return b ^ (2 * q)

    def lanes(h):
        return pl.ds(half * h, half)

    def unit(place, i, h):
        ref, base = place
        return ref.at[base + i // 16, pl.ds((i % 16) * 48, 48), lanes(h)]

    def quad(place, n, h):
        ref, base = place
        return ref.at[base + n // 4, pl.ds((n % 4) * 192, 192), lanes(h)]

    def share(p, i, h):
        if p < 4:
            return unit((raw, 2 * p), i, h)
        return w_down.at[i // 8, pl.ds((i % 8) * 96 + 48 * h, 48), lanes(p - 4)]

    def bulk(n):
        return raw.at[0] if n == 32 else raw.at[0, pl.ds(0, 48 * n), pl.ds(0, half)]

    def send(p, i, h, device, way, rsem):
        ref = share(p, i, h)
        remote(ref, ref, ssem.at[p, way], rsem, device).start()

    def arrived(p, i, h, rsem):
        ref = share(p, i, h)
        remote(ref, ref, ssem.at[p, 0], rsem, comm.X).wait_recv()

    def to_core(p, i, h):
        send(p, i, h, comm.C, 2, csem.at[p])

    def dev(q, k):
        return at_q(q) * 4 + (z ^ k)

    def cast(p):
        for h in range(2):
            if p < 4:
                row = jnp.concatenate([rows_ref[:, c : c + n] for c, n in PIECES[p][h]], axis=1)
                both = jnp.concatenate([row[:, :half], row[:, half:]], axis=0)
            else:
                both = down_ref[48 * h : 48 * h + 48, half * (p - 4) : half * (p - 3)]
            if p < 4:
                raw[2 * p + me // 16, pl.ds((me % 16) * 48, 48), lanes(h)] = both.astype(bf16)
            else:
                w_down[me // 8, pl.ds((me % 8) * 96 + 48 * h, 48), lanes(p - 4)] = both.astype(bf16)

    def along_z(p, q, k, j, h):
        i = dev(q, k)
        if k == 0:
            send(p, i, h, comm.Z[3], 3, zsem.at[p, 3, 2 * j + h])
            send(p, i, h, comm.Z[1], 3, zsem.at[p, 1, 2 * j + h])
        else:
            send(p, i, h, comm.Z[1], 3, zsem.at[p, 2, 2 * j + h])

    def place(j, h):
        return 0 if j == 0 else (1 if h == 0 else 2)

    def ownz(p):
        for h in range(2):
            along_z(p, 0, 0, 0, h)

    def own1(p):
        send(p, dev(0, 0), 0, comm.X, 0, dsem.at[p, 0, 0])
        send(p, dev(0, 0), 1, comm.Y, 1, dsem.at[p, 0, 1])

    def first(p):
        for h in range(2):
            q = place(1, h)
            arrived(p, dev(q, 0), h, dsem.at[p, 0, h])
            along_z(p, q, 0, 1, h)

    def fold(p, j=0):
        for h in range(2):
            q = place(j, h)
            arrived(p, dev(q, 3), h, zsem.at[p, 3, 2 * j + h])
            along_z(p, q, 3, j, h)

    def z_wait(p, k, j):
        if k in (1, 2):
            for h in range(2):
                arrived(p, dev(place(j, h), k), h, zsem.at[p, k, 2 * j + h])

    def col(p, k):
        z_wait(p, k, 0)
        i = dev(0, k)
        send(p, i, 0, comm.X, 0, xsem.at[p, k, 0])
        send(p, i, 1, comm.Y, 1, ysem.at[p, k, 1])
        send(p, i, 1, comm.X, 0, xsem.at[p, k, 1])
        send(p, i, 0, comm.Y, 1, ysem.at[p, k, 0])
        to_core(p, i, 0)
        to_core(p, i, 1)

    def across(p, k):
        i = dev(1, k)
        arrived(p, i, 0, xsem.at[p, k, 0])
        send(p, i, 0, comm.Y, 1, dsem.at[p, k, 0])
        to_core(p, i, 0)
        i = dev(2, k)
        arrived(p, i, 1, ysem.at[p, k, 1])
        send(p, i, 1, comm.X, 0, dsem.at[p, k, 1])
        to_core(p, i, 1)

    def fin(p, k, j):
        z_wait(p, k, j)
        i = dev(place(j, 0), k)
        send(p, i, 0, comm.Y, 1, ysem.at[p, k, j])
        to_core(p, i, 0)
        i = dev(place(j, 1), k)
        send(p, i, 1, comm.X, 0, xsem.at[p, k, j])
        to_core(p, i, 1)

    def last(p, k):
        if GATHER_MODE[p] == Z_FIRST:
            rest = ((1, 1, xsem.at[p, k, 1]), (2, 0, ysem.at[p, k, 0]), (3, 0, dsem.at[p, k, 0]), (3, 1, dsem.at[p, k, 1]))
        else:
            rest = ((2, 0, ysem.at[p, k, 0]), (1, 1, xsem.at[p, k, 0]), (3, 0, ysem.at[p, k, 1]), (3, 1, xsem.at[p, k, 1]))
        for q, h, sem in rest:
            arrived(p, dev(q, k), h, sem)
            to_core(p, dev(q, k), h)

    def gathered(p):
        remote(bulk(32), bulk(32), ssem.at[p, 0], csem.at[p], comm.X).wait_recv()

    def sent(p):
        z_first = GATHER_MODE[p] == Z_FIRST
        for way, n in ((0, 12 if z_first else 9), (1, 12 if z_first else 9), (2, 32), (3, 6 if z_first else 12)):
            remote(bulk(n), bulk(n), ssem.at[p, way], csem.at[p], comm.X).wait_send()

    def small_z(ref, n):
        mine = ref.at[pl.ds(b * 4 + z, 1)]
        for k in (3, 1, 2):
            remote(mine, mine, small_send.at[n, 0], small_recv.at[n, z], comm.Z[k]).start()

    def small_plane(ref, n):
        for k in (1, 2, 3):
            theirs = ref.at[pl.ds(b * 4 + (z ^ k), 1)]
            remote(theirs, theirs, small_send.at[n, 0], small_recv.at[n, z ^ k], comm.X).wait_recv()
        mine = ref.at[pl.ds(b * 4, 4)]
        remote(mine, mine, small_send.at[n, 1], small_recv.at[n, 4], comm.X).start()
        remote(mine, mine, small_send.at[n, 2], small_recv.at[n, 5], comm.Y).start()
        remote(mine, mine, small_send.at[n, 3], small_recv.at[n, 7], comm.C).start()

    def small_cross(ref, n):
        theirs = ref.at[pl.ds(at_q(1) * 4, 4)]
        remote(theirs, theirs, small_send.at[n, 1], small_recv.at[n, 4], comm.X).wait_recv()
        remote(theirs, theirs, small_send.at[n, 4], small_recv.at[n, 6], comm.Y).start()
        remote(theirs, theirs, small_send.at[n, 5], small_recv.at[n, 8], comm.C).start()
        theirs = ref.at[pl.ds(at_q(2) * 4, 4)]
        remote(theirs, theirs, small_send.at[n, 1], small_recv.at[n, 5], comm.X).wait_recv()
        remote(theirs, theirs, small_send.at[n, 6], small_recv.at[n, 9], comm.C).start()

    def small_end(ref, n):
        theirs = ref.at[pl.ds(at_q(3) * 4, 4)]
        remote(theirs, theirs, small_send.at[n, 1], small_recv.at[n, 6], comm.X).wait_recv()
        remote(theirs, theirs, small_send.at[n, 7], small_recv.at[n, 10], comm.C).start()
        for j in range(4):
            theirs = ref.at[pl.ds((b ^ (1 + 2 * j)) * 4, 4)]
            remote(theirs, theirs, small_send.at[n, 1], small_recv.at[n, 7 + j], comm.X).wait_recv()
        three = ref.at[pl.ds(0, 3)]
        remote(three, three, small_send.at[n, 0], small_recv.at[n, 0], comm.X).wait_send()
        four = ref.at[pl.ds(0, 4)]
        for j in range(1, 8):
            remote(four, four, small_send.at[n, j], small_recv.at[n, 0], comm.X).wait_send()

    def vec(offset, size=width):
        return vec_row[0:1, offset : offset + size]

    bias_q, bias_v, bias_o, gain1_at, shift1_at, bias_up_at = 0, width, 2 * width, 3 * width, 4 * width, 5 * width
    bias_down_at, gain2_at, shift2_at = 9 * width, 10 * width, 11 * width

    share_v = 288

    def place_vectors():
        v = vec_ref[...].reshape(1, share_v)
        tail = jnp.concatenate([v[:, 256:share_v], jnp.zeros((1, 384 - share_v), f32)], axis=1)
        tile = jnp.concatenate([v[:, 0:128], v[:, 128:256], tail, jnp.zeros((13, 128), f32)], axis=0)
        vec_all[pl.ds(me, 1)] = tile.astype(bf16).reshape(1, 16, 128)

    def spread_vectors():
        for i in range(32):
            tile = vec_all[i].astype(f32)
            for r, n in ((0, 128), (1, 128), (2, share_v - 256)):
                at = share_v * i + 128 * r
                vec_row[0:1, at : at + n] = tile[r : r + 1, 0:n]
        bias_in[...] = jnp.zeros_like(bias_in)
        bias_in[0:1, 0:512] = vec(bias_q, 512)
        bias_in[0:1, 1024:1536] = vec(bias_v, 512)
        bias_in[0:1, 1536:1792] = vec(bias_q + 512, 256)
        bias_in[0:1, 2048:2304] = vec(bias_v + 512, 256)

    def relayout(p):
        target, chunk = (w_attn, 2 * p) if p < 2 else (w_up, 2 * p - 4)

        def body(j, carry):
            for h in range(2):
                even = raw[2 * p + j // 8, pl.ds((j % 8) * 96, 48), lanes(h)].astype(f32)
                odd = raw[2 * p + j // 8, pl.ds((j % 8) * 96 + 48, 48), lanes(h)].astype(f32)
                for q in range(2):
                    rows = jnp.concatenate([even[24 * q : 24 * q + 24], odd[24 * q : 24 * q + 24]], axis=0)
                    target[chunk + h, pl.ds(j * 48, 48), lanes(q)] = rows.astype(bf16)
            return carry

        lax.fori_loop(0, 16, body, 0)

    def transpose_into(source, target):
        def body(j, carry):
            at = pl.multiple_of(j * 256, 256)
            target[pl.ds(at, 256), :] = jnp.transpose(source[:, pl.ds(at, 256)])
            return carry

        lax.fori_loop(0, source.shape[1] // 256, body, 0)

    def token_weights():
        lane = lax.broadcasted_iota(jnp.int32, (1, 128), 1)
        left = (lane < 64).astype(f32)
        tok = tok_ref[...].astype(f32)
        tok_f[0:4, :] = jnp.concatenate([tok[:, 0, :], tok[:, 1, :]], axis=1)
        for p in range(4):
            m = tok_f[p : p + 1, :]
            n0 = jnp.sum(m * left, axis=1, keepdims=True)
            n1 = jnp.sum(m * (1.0 - left), axis=1, keepdims=True)
            w = m / (left * n0 + (1.0 - left) * n1)
            tok_w[128 * p : 128 * p + 128, :] = jnp.transpose(jnp.broadcast_to(w, (128, 128)))
        row = lax.broadcasted_iota(jnp.int32, (8, 128), 0) % 4
        tag = jnp.full((8, 128), -1.0, f32)
        for s in range(4):
            tag = jnp.where((row == s) & (count_ref[0] > s), group_ref[s].astype(f32), tag)
        tags[...] = tag

    def project(lo, hi):
        def body(t, carry):
            c, n = t // 3, t % 3
            at = pl.multiple_of(n * 256, 256)
            bias = bias_in[0:1, pl.ds(pl.multiple_of(t * 256, 256), 256)]
            out = dot_nn(x_ref[...], w_attn[c, :, pl.ds(at, 256)]) + bias
            qkv[c, :, pl.ds(at, 256)] = out.astype(bf16)
            return carry

        lax.fori_loop(lo, hi, body, 0)

    def head_places(hp):
        if hp < 4:
            key = (0, 512 + 128 * hp) if hp < 2 else (1, 128 * hp - 256)
            return (0, 128 * hp), key, (1, 256 + 128 * hp)
        return (2, 128 * hp - 512), (2, 128 * hp - 256), (2, 128 * hp)

    lane128 = lax.broadcasted_iota(jnp.int32, (128, 128), 1)
    row128 = lax.broadcasted_iota(jnp.int32, (128, 128), 0)
    even_half = lane128 < 64

    def split_heads(v):
        zero = jnp.zeros_like(v)
        return jnp.concatenate([jnp.where(even_half, v, zero), jnp.where(even_half, zero, v)], axis=0)

    def attend(group, lo, hi):
        def body(p, carry):
            rows = pl.ds(pl.multiple_of(p * 128, 128), 128)
            m = tok_f[pl.ds(p, 1), :]
            same = (row128 < 64) == (lane128 < 64)
            open_one = same & (jnp.broadcast_to(m, (128, 128)) > 0.0)
            block = jnp.where(open_one, 0.0, -1e30)
            block = jnp.concatenate([block, block], axis=0)
            for hp in range(4) if group == 0 else range(4, 6):
                q2, k2, v2 = [qkv[c, rows, at : at + 128] for c, at in head_places(hp)]
                s = dot_nt(split_heads(q2), k2) * HEAD ** (-0.5) + block
                e = jnp.exp(s - jnp.max(s, axis=1, keepdims=True))
                a = (e * (1.0 / jnp.sum(e, axis=1, keepdims=True))).astype(bf16)
                probs[p * 6 + hp] = a
                wide = jnp.concatenate([a[:128], a[128:]], axis=1)
                ctx[rows, 128 * hp : 128 * hp + 128] = dot_nn(wide, split_heads(v2)).astype(bf16)
            return carry

        lax.fori_loop(lo, hi, body, 0)

    def norm_rows(i, source_fn, hat, rstd, emit):
        rows = pl.ds(pl.multiple_of(i * 64, 64), 64)
        h = source_fn(rows)
        centre = h - jnp.mean(h, axis=1, keepdims=True)
        r = lax.rsqrt(jnp.mean(centre * centre, axis=1, keepdims=True) + norm_epsilon)
        xh = centre * r
        hat[rows, :] = xh
        rstd[rows, :] = jnp.broadcast_to(r, (64, 128))
        if emit is not None:
            emit(rows, xh)

    def attn_out():
        def body(n, carry):
            at = pl.multiple_of(n * 256, 256)
            work[:, pl.ds(at, 256)] = dot_nn(ctx[...], w_attn[3, :, pl.ds(at, 256)])
            return carry

        lax.fori_loop(0, 3, body, 0)

    def attn_norm():
        def source(rows):
            return x_ref[rows, :].astype(f32) + work[rows, :] + vec(bias_o)

        def emit(rows, xh):
            y_low[rows, :] = (xh * (1.0 + vec(gain1_at)) + vec(shift1_at)).astype(bf16)

        def norm(i, carry):
            norm_rows(i, source, xhat1, rstd1, emit)
            return carry

        lax.fori_loop(0, 8, norm, 0)

    def feed_up(lo, hi):
        def body(t, carry):
            c, n = t // 3, t % 3
            at = pl.multiple_of(n * 256, 256)
            to = pl.multiple_of(t * 256, 256)
            work[:, pl.ds(0, 256)] = dot_nn(y_low[...], w_up[c, :, pl.ds(at, 256)])
            bias = vec_row[0:1, pl.ds(pl.multiple_of(bias_up_at + to, 256), 256)]

            def rows_of(i, inner):
                rows = pl.ds(pl.multiple_of(i * 32, 32), 32)
                v = work[rows, 0:256] + bias
                cdf = 0.5 * (1.0 + lax.erf(v * 0.7071067811865476))
                dens = jnp.exp(v * v * -0.5) * 0.3989422804014327
                act[rows, pl.ds(to, 256)] = (v * cdf).astype(bf16)
                slope[rows, pl.ds(to, 256)] = (cdf + v * dens).astype(bf16)
                return inner

            lax.fori_loop(0, 16, rows_of, 0)
            act_t[pl.ds(to, 256), :] = jnp.transpose(act[:, pl.ds(to, 256)])
            return carry

        lax.fori_loop(lo, hi, body, 0)

    def feed_down(s):
        total = dot_nn(act[:, 0:width], w_down[0, :, lanes(s)])
        for c in range(1, 4):
            total = total + dot_nn(act[:, c * width : (c + 1) * width], w_down[c, :, lanes(s)])
        work[:, lanes(s)] = total

    def down_norm():
        def source(rows):
            return y_low[rows, :].astype(f32) + work[rows, :] + vec(bias_down_at)

        def norm(i, carry):
            norm_rows(i, source, xhat2, rstd2, None)
            rows = pl.ds(pl.multiple_of(i * 64, 64), 64)
            got = jnp.sum(xhat2[rows, :] * tok_w[rows, 0:1], axis=0, keepdims=True)
            at = i // 2 + 4 * (i % 2)
            pooled_hat[pl.ds(at, 1), :] = got
            return carry

        lax.fori_loop(0, 8, norm, 0)

    def transposes():
        transpose_into(y_low, y_t)
        transpose_into(ctx, ctx_t)

    def pool():
        e = pooled_hat[...] * (1.0 + vec(gain2_at)) + vec(shift2_at)
        r = lax.rsqrt(jnp.sum(e * e, axis=1, keepdims=True) + unit_epsilon)
        unit_rs[...] = jnp.broadcast_to(r, (8, 128))
        pairs[me, :, 0:width] = e * r
        pairs[me, :, width : width + 128] = tags[...]

    def contrast():
        total = 256
        every = pairs[...].reshape(total, width + 128)
        v = every[:, 0:width]
        tag = every[:, width : width + 128]
        tag_row = jnp.concatenate([jnp.transpose(tag[0:128])[0:1], jnp.transpose(tag[128:256])[0:1]], axis=1)
        s = dot_nt(v, v, precision=highest) * score_scale
        i = lax.broadcasted_iota(jnp.int32, (total, total), 0)
        j = lax.broadcasted_iota(jnp.int32, (total, total), 1)
        opposite = (i & 4) != (j & 4)
        diagonal = (i ^ j) == 4
        s = s - jnp.where(diagonal, score_scale * margin, 0.0)
        same = (tag[:, 0:1] == tag_row) & (tag_row >= 0.0) & opposite
        e = jnp.where(same, jnp.exp(jnp.where(same, s, 0.0)), 0.0)
        sums = jnp.sum(e, axis=0, keepdims=True)
        valid = (tag_row >= 0.0).astype(f32)
        sums = jnp.where(tag_row >= 0.0, sums, 1.0)
        doubled = jnp.sum(valid)
        coef = 1.0 / doubled
        positive = jnp.sum(jnp.where(diagonal & same, s, 0.0))
        loss = (jnp.sum(jnp.log(sums) * valid) - positive) * coef
        loss_ref[0, 0] = loss
        pair_k[0] = e
        pair_k[1] = jnp.where(diagonal & same, 2.0, 0.0)
        own_rows = pl.ds(pl.multiple_of(me * 8, 8), 8)
        e_own = pair_k[0, own_rows, :]
        r_own = jnp.sum(e_own, axis=1, keepdims=True)
        r_own = jnp.where(tags[:, 0:1] >= 0.0, r_own, 1.0)
        k = (e_own / r_own + e_own / sums - pair_k[1, own_rows, :]) * coef
        dn = score_scale * dot_nn(k, v, precision=highest)
        n = pairs[me, :, 0:width]
        de = unit_rs[:, 0:1] * (dn - n * jnp.sum(n * dn, axis=1, keepdims=True))
        pooled_grad = de
        vec_grad[0:1, gain2_at : gain2_at + width] = jnp.sum(de * pooled_hat[...], axis=0, keepdims=True)
        vec_grad[0:1, shift2_at : shift2_at + width] = jnp.sum(de, axis=0, keepdims=True)
        pooled_hat[...] = pooled_grad

    def norm_two_back():
        def body(i, carry):
            rows = pl.ds(pl.multiple_of(i * 64, 64), 64)
            de = pooled_hat[pl.ds(i // 2 + 4 * (i % 2), 1), :]
            dg = de * (1.0 + vec(gain2_at))
            xh = xhat2[rows, :]
            m1 = jnp.mean(dg, axis=1, keepdims=True)
            m2 = jnp.mean(dg * xh, axis=1, keepdims=True)
            dz = (rstd2[rows, 0:1] * tok_w[rows, 0:1]) * (dg - m1 - xh * m2)
            low = dz.astype(bf16)
            xhat2[rows, :] = dz
            y_low[rows, :] = low
            return carry + jnp.sum(low.astype(f32), axis=0, keepdims=True)

        vec_grad[0:1, bias_down_at : bias_down_at + width] = lax.fori_loop(0, 8, body, jnp.zeros((1, width), f32))

    g_places = ((w_up, 0), (w_up, 2), (g_rest, 4), (g_rest, 6), (g_rest, 0), (g_rest, 2))
    box_places = ((w_down, 0), (w_down, 2), (raw, 4), (raw, 6), (raw, 0), (raw, 2))

    def grad_w_down(blk):
        out = dot_nn(act_t[pl.ds(pl.multiple_of(blk * 384, 128), 384), :], y_low[...])
        for part in range(2):
            for zz in range(4):
                for h in range(2):
                    rows = out[96 * zz + 48 * h : 96 * zz + 48 * h + 48, half * part : half * part + half]
                    at = pl.multiple_of((blk % 4) * 192 + 48 * zz, 16)
                    g_rest[2 * part + blk // 4, pl.ds(at, 48), lanes(h)] = rows.astype(bf16)

    def down_sibling():
        def body(n, carry):
            blk = at_q(3 - n) ^ 1
            grad_w_down(blk)
            for p in (4, 5):
                for h in range(2):
                    core_send(p, h, 3 - n)
            return carry

        lax.fori_loop(0, 4, body, 0)

    def down_own():
        def body(n, carry):
            grad_w_down(at_q(3 - n))
            return carry

        lax.fori_loop(0, 4, body, 0)

    def grad_act(lo, hi):
        def body(t, carry):
            c, n = t // 3, t % 3
            to = pl.multiple_of(t * 256, 256)
            work[:, 0:256] = dot_nt(y_low[...], w_down[c, pl.ds(pl.multiple_of(n * 256, 256), 256), :])

            def rows_of(i, total):
                rows = pl.ds(pl.multiple_of(i * 64, 64), 64)
                low = (work[rows, 0:256] * slope[rows, pl.ds(to, 256)].astype(f32)).astype(bf16)
                act[rows, pl.ds(to, 256)] = low
                return total + jnp.sum(low.astype(f32), axis=0, keepdims=True)

            sums = lax.fori_loop(0, 8, rows_of, jnp.zeros((1, 256), f32))
            vec_grad[0:1, pl.ds(pl.multiple_of(bias_up_at + to, 256), 256)] = sums
            return carry

        lax.fori_loop(lo, hi, body, 0)

    def store_units(p, h, m, out):
        ref, base = g_places[p]
        for d in range(16):
            rows = out[24 * d : 24 * d + 24]
            both = jnp.concatenate([rows[:, :half], rows[:, half:]], axis=0)
            ref[base + m, 48 * d : 48 * d + 48, lanes(h)] = both.astype(bf16)

    def grad_w_rows(p):
        def body(n, carry):
            m = (b // 4) ^ (1 - n)
            rows = pl.ds(pl.multiple_of(m * 384, 128), 384)
            for h in range(2):
                if p >= 2:
                    out = dot_nn(y_t[rows, :], act[:, (2 * p - 4 + h) * width : (2 * p - 3 + h) * width])
                elif (p, h) == (1, 1):
                    out = dot_nn(ctx_t[rows, :], y_low[...])
                else:
                    out = dot_nn(x_t[rows, :], qkv[2 * p + h])
                store_units(p, h, m, out)
                for q in (1, 0):
                    core_send(p, h, 2 * (1 - n) + q)
            return carry

        lax.fori_loop(0, 2, body, 0)

    def grad_y():
        def body(n, carry):
            at = pl.multiple_of(n * 256, 256)
            total = xhat2[:, pl.ds(at, 256)]
            for c in range(4):
                total = total + dot_nt(act[:, c * width : (c + 1) * width], w_up[c, pl.ds(at, 256), :])
            work[:, pl.ds(at, 256)] = total
            return carry

        lax.fori_loop(0, 3, body, 0)

    def norm_one_back():
        def body(i, carry):
            rows = pl.ds(pl.multiple_of(i * 64, 64), 64)
            dy = work[rows, :]
            xh = xhat1[rows, :]
            dg = dy * (1.0 + vec(gain1_at))
            m1 = jnp.mean(dg, axis=1, keepdims=True)
            m2 = jnp.mean(dg * xh, axis=1, keepdims=True)
            dh = rstd1[rows, 0:1] * (dg - m1 - xh * m2)
            low = dh.astype(bf16)
            work[rows, :] = dh
            y_low[rows, :] = low
            gain, shift, bias = carry
            return (
                gain + jnp.sum(dy * xh, axis=0, keepdims=True),
                shift + jnp.sum(dy, axis=0, keepdims=True),
                bias + jnp.sum(low.astype(f32), axis=0, keepdims=True),
            )

        zero = jnp.zeros((1, width), f32)
        gain, shift, bias = lax.fori_loop(0, 8, body, (zero, zero, zero))
        vec_grad[0:1, gain1_at : gain1_at + width] = gain
        vec_grad[0:1, shift1_at : shift1_at + width] = shift
        vec_grad[0:1, bias_o : bias_o + width] = bias

    def grad_ctx():
        def body(n, carry):
            at = pl.multiple_of(n * 256, 256)
            ctx[:, pl.ds(at, 256)] = dot_nt(y_low[...], w_attn[3, pl.ds(at, 256), :]).astype(bf16)
            return carry

        lax.fori_loop(0, 3, body, 0)

    def attend_back(group, lo, hi):
        def body(p, carry):
            rows = pl.ds(pl.multiple_of(p * 128, 128), 128)
            for hp in range(4) if group == 0 else range(4, 6):
                places = head_places(hp)
                q2, k2, v2 = [qkv[c, rows, at : at + 128] for c, at in places]
                dc = split_heads(ctx[rows, 128 * hp : 128 * hp + 128])
                a = probs[p * 6 + hp]
                af = a.astype(f32)
                da = dot_nt(dc, v2)
                ds = (af * (da - jnp.sum(af * da, axis=1, keepdims=True))).astype(bf16)
                dv = dot_tn(a, dc)
                wide = jnp.concatenate([ds[:128], ds[128:]], axis=1)
                dq = dot_nn(wide, split_heads(k2)) * HEAD ** (-0.5)
                dk = dot_tn(ds, split_heads(q2)) * HEAD ** (-0.5)
                for (c, at), d in zip(places, (dq, dk, dv)):
                    qkv[c, rows, at : at + 128] = d.astype(bf16)
            return carry

        lax.fori_loop(lo, hi, body, 0)

    def grad_bias_in():
        def body(i, carry):
            rows = pl.ds(pl.multiple_of(i * 64, 64), 64)
            return tuple(have + jnp.sum(qkv[c, rows, :].astype(f32), axis=0, keepdims=True) for c, have in enumerate(carry))

        zero = jnp.zeros((1, width), f32)
        first_sum, second_sum, third_sum = lax.fori_loop(0, 8, body, (zero, zero, zero))
        vec_grad[0:1, bias_q : bias_q + 512] = first_sum[:, 0:512]
        vec_grad[0:1, bias_q + 512 : bias_q + 768] = third_sum[:, 0:256]
        vec_grad[0:1, bias_v : bias_v + 512] = second_sum[:, 256:768]
        vec_grad[0:1, bias_v + 512 : bias_v + 768] = third_sum[:, 512:768]

    def dx_copy(n):
        at = pl.ds(pl.multiple_of(n * 256, 256), 256)
        return pltpu.make_async_copy(work.at[:, at], dx_hbm.at[:, at], local_sem.at[3])

    def grad_x(lo, hi):
        def body(n, carry):
            at = pl.multiple_of(n * 256, 256)
            total = work[:, pl.ds(at, 256)]
            for c in range(3):
                total = total + dot_nt(qkv[c], w_attn[c, pl.ds(at, 256), :])
            work[:, pl.ds(at, 256)] = total
            return carry

        lax.fori_loop(lo, hi, body, 0)
        for n in range(lo, hi):
            dx_copy(n).start()

    def spot(p, run, u, h):
        ref, base = box_places[p]
        return ref.at[base + run // 4, pl.ds((run % 4) * 192 + 48 * u, 48), lanes(h)]

    def core_send(p, h, q):
        remote(
            quad(g_places[p], at_q(q) ^ 1, h), quad(box_places[p], q, h), rs_send.at[p, 0], rc_sem.at[p, h, q], comm.C
        ).start()

    def run_wait(p, run, h, sem):
        ref = quad(box_places[p], run, h)
        remote(ref, ref, rs_send.at[p, 0], sem, comm.C).wait_recv()

    def spot_wait(p, run, u, h, sem):
        ref = spot(p, run, u, h)
        remote(ref, ref, rs_send.at[p, 0], sem, comm.C).wait_recv()

    def add_in(p, h, q, runs):
        target, base = g_places[p]
        box, box_base = box_places[p]
        blk = at_q(q)

        def body(i, carry):
            at = pl.multiple_of((blk % 4) * 192 + i * 48, 16)
            total = target[base + blk // 4, pl.ds(at, 48), lanes(h)].astype(f32)
            for run in runs:
                from_at = pl.multiple_of((run % 4) * 192 + i * 48, 16)
                total = total + box[box_base + run // 4, pl.ds(from_at, 48), lanes(h)].astype(f32)
            target[base + blk // 4, pl.ds(at, 48), lanes(h)] = total.astype(bf16)
            return carry

        lax.fori_loop(0, 4, body, 0)

    def read_unit(p, i, h):
        ref, base = g_places[p]
        return ref[base + i // 16, pl.ds((i % 16) * 48, 48), lanes(h)].astype(f32)

    def read_spot(p, run, u, h):
        ref, base = box_places[p]
        return ref[base + run // 4, (run % 4) * 192 + 48 * u : (run % 4) * 192 + 48 * u + 48, lanes(h)].astype(f32)

    def write_unit(p, i, h, total):
        ref, base = g_places[p]
        ref[base + i // 16, pl.ds((i % 16) * 48, 48), lanes(h)] = total.astype(bf16)

    def pass_run(p, h, q, run, sem):
        along_y = (run < 6) == (h == 0)
        device, way = (comm.Y, 2) if along_y else (comm.X, 1)
        remote(quad(g_places[p], at_q(q), h), quad(box_places[p], run, h), rs_send.at[p, way], sem, device).start()

    def pass_unit(p, i, run, u, h, device, way, sem):
        remote(unit(g_places[p], i, h), spot(p, run, u, h), rs_send.at[p, way], sem, device).start()

    def s1(p, side):
        for h in range(2):
            q = 3 if side == 1 else 2 - h
            run_wait(p, q, h, rc_sem.at[p, h, q])
            add_in(p, h, q, (q,))
            pass_run(p, h, q, 4 + side, r1_sem.at[p, h, side])

    def s2(p):
        if REDUCE_MODE[p] == Z_FIRST:
            for h in range(2):
                q = 1 + h
                run_wait(p, q, h, rc_sem.at[p, h, q])
                run_wait(p, 5, h, r1_sem.at[p, h, 1])
                add_in(p, h, q, (q, 5))
                pass_run(p, h, q, 6, r2_sem.at[p, h])
            return
        for h in range(2):
            for j, q in enumerate((0, 1 + h)):
                run_wait(p, q, h, rc_sem.at[p, h, q])
                run_wait(p, 4 + j, h, r1_sem.at[p, h, j])
                add_in(p, h, q, (q, 4 + j))
                pass_unit(p, dev(q, 1), 6, 2 * j, h, comm.Z[1], 3, rz_sem.at[p, h, 2 * j])
                pass_unit(p, dev(q, 2), 6, 2 * j + 1, h, comm.Z[1], 3, rz_sem.at[p, h, 2 * j + 1])

    def s3(p):
        if REDUCE_MODE[p] == Z_FIRST:
            for h in range(2):
                run_wait(p, 0, h, rc_sem.at[p, h, 0])
                run_wait(p, 4, h, r1_sem.at[p, h, 0])
                run_wait(p, 6, h, r2_sem.at[p, h])
                add_in(p, h, 0, (0, 4, 6))
                pass_unit(p, dev(0, 1), 7, 0, h, comm.Z[1], 3, rz_sem.at[p, h, 0])
                pass_unit(p, dev(0, 2), 7, 1, h, comm.Z[1], 3, rz_sem.at[p, h, 1])
            return
        for h in range(2):
            for j, q in enumerate((0, 1 + h)):
                spot_wait(p, 6, 2 * j + 1, h, rz_sem.at[p, h, 2 * j + 1])
                write_unit(p, dev(q, 3), h, read_unit(p, dev(q, 3), h) + read_spot(p, 6, 2 * j + 1, h))
                pass_unit(p, dev(q, 3), 7, j, h, comm.Z[3], 3, ry_sem.at[p, h, j])

    def s4(p):
        if REDUCE_MODE[p] == Z_FIRST:
            for h in range(2):
                spot_wait(p, 7, 1, h, rz_sem.at[p, h, 1])
                write_unit(p, dev(0, 3), h, read_unit(p, dev(0, 3), h) + read_spot(p, 7, 1, h))
                pass_unit(p, dev(0, 3), 7, 2, h, comm.Z[3], 3, ry_sem.at[p, h, 0])
            return
        for h in range(2):
            q = 1 + h
            spot_wait(p, 6, 2, h, rz_sem.at[p, h, 2])
            spot_wait(p, 7, 1, h, ry_sem.at[p, h, 1])
            write_unit(p, dev(q, 0), h, read_unit(p, dev(q, 0), h) + read_spot(p, 6, 2, h) + read_spot(p, 7, 1, h))
            device, way = (comm.X, 1) if h == 0 else (comm.Y, 2)
            pass_unit(p, dev(q, 0), 7, 2, h, device, way, rf_sem.at[p, h])

    def s5(p):
        for h in range(2):
            total = read_unit(p, me, h)
            if REDUCE_MODE[p] == Z_FIRST:
                spot_wait(p, 7, 0, h, rz_sem.at[p, h, 0])
                spot_wait(p, 7, 2, h, ry_sem.at[p, h, 0])
                total = total + read_spot(p, 7, 0, h) + read_spot(p, 7, 2, h)
            else:
                spot_wait(p, 6, 0, h, rz_sem.at[p, h, 0])
                spot_wait(p, 7, 0, h, ry_sem.at[p, h, 0])
                spot_wait(p, 7, 2, h, rf_sem.at[p, h])
                total = total + read_spot(p, 6, 0, h) + read_spot(p, 7, 0, h) + read_spot(p, 7, 2, h)
            if p >= 4:
                grad_down_ref[48 * h : 48 * h + 48, half * (p - 4) : half * (p - 3)] = total
            else:
                row = jnp.concatenate([total[0:24], total[24:48]], axis=1)
                at = 0
                for c, n in PIECES[p][h]:
                    grad_rows_ref[:, c : c + n] = row[:, at : at + n]
                    at = at + n

    def sums_sent(p):
        z_first = REDUCE_MODE[p] == Z_FIRST
        for way, n in ((0, 32), (1, 12 if z_first else 9), (2, 12 if z_first else 9), (3, 6 if z_first else 12)):
            remote(bulk(n), bulk(n), rs_send.at[p, way], rc_sem.at[p, 0, 0], comm.C).wait_send()

    def vec_pack():
        vec_out[...] = jnp.zeros_like(vec_out)
        for i in range(32):
            for r, n in ((0, 128), (1, 128), (2, share_v - 256)):
                at = share_v * i + 128 * r
                vec_out[i // 4, 3 * (i % 4) + r : 3 * (i % 4) + r + 1, 0:n] = vec_grad[0:1, at : at + n]

    def vec_copy(src, dst, n, device):
        return remote(vec_out.at[src], vec_in.at[dst], vs_sem.at[n], vr_sem.at[dst], device)

    def vec_core():
        for q in range(4):
            vec_copy(at_q(q) ^ 1, q, q, comm.C).start()

    def vec_take(dst, target):
        vec_copy(target, dst, 0, comm.C).wait_recv()
        vec_out[target] = vec_out[target] + vec_in[dst]

    def vec_y():
        for q in range(4):
            vec_take(q, at_q(q))
        vec_copy(at_q(3), 5, 4, comm.Y).start()
        vec_copy(at_q(2), 4, 5, comm.Y).start()

    def vec_x():
        vec_take(5, at_q(1))
        vec_copy(at_q(1), 6, 6, comm.X).start()

    def vec_z():
        vec_take(4, b)
        vec_take(6, b)
        for k in (1, 2, 3):
            vec_copy(b, 8 + z, 6 + k, comm.Z[k]).start()

    def vec_end():
        total = vec_out[b]
        for k in (1, 2, 3):
            vec_copy(b, 8 + (z ^ k), 0, comm.C).wait_recv()
            total = total + vec_in[8 + (z ^ k)]
        mine = total[0:3]
        for zz in range(1, 4):
            mine = jnp.where(z == zz, total[3 * zz : 3 * zz + 3], mine)
        grad_vec_ref[...] = jnp.concatenate([mine[0:1], mine[1:2], mine[2:3, 0 : share_v - 256]], axis=1)
        for n in range(10):
            vec_copy(b, 0, n, comm.C).wait_send()

    def load(n):
        src, dst = ((rows_hbm, rows_ref), (down_hbm, down_ref), (x_hbm, x_ref))[n]
        return pltpu.make_async_copy(src, dst, local_sem.at[n])

    def start():
        for n in range(3):
            load(n).start()
        place_vectors()
        token_weights()
        comm.barrier()
        load(0).wait()

    def load_rest(n):
        load(n).wait()

    def pair_gather():
        for p in range(6):
            sent(p)
        small_z(pairs, 1)
        small_plane(pairs, 1)
        small_cross(pairs, 1)
        small_end(pairs, 1)

    def finish():
        for p in range(6):
            sums_sent(p)
        pltpu.make_async_copy(work, dx_hbm, local_sem.at[3]).wait()

    def vectors(n):
        (small_z, small_plane, small_cross, small_end)[n](vec_all, 0)

    actions = {
        name: f
        for name, f in (
            ("start", start), ("load", load_rest), ("vectors", vectors), ("spread", spread_vectors),
            ("x_t", lambda: transpose_into(x_ref, x_t)),
            ("cast", cast), ("ownz", ownz), ("own1", own1), ("first", first), ("fold", fold), ("col", col), ("across", across),
            ("fin", fin), ("last", last), ("gathered", gathered),
            ("relayout", relayout), ("project", project), ("attend", attend), ("attn_out", attn_out), ("attn_norm", attn_norm),
            ("feed_up", feed_up), ("tr", transposes), ("feed_down", feed_down), ("norm2", down_norm),
            ("pool", pool), ("pair_gather", pair_gather), ("contrast", contrast),
            ("n2", norm_two_back), ("dw2a", down_sibling), ("dw2b", down_own), ("df", grad_act), ("dw", grad_w_rows),
            ("dy", grad_y), ("n1", norm_one_back), ("dc", grad_ctx), ("attb", attend_back), ("bias", grad_bias_in), ("gx", grad_x),
            ("s1", s1), ("s2", s2), ("s3", s3), ("s4", s4), ("s5", s5),
            ("vec_pack", vec_pack), ("vec_core", vec_core), ("vec_y", vec_y), ("vec_x", vec_x), ("vec_z", vec_z), ("vec_end", vec_end),
            ("finish", finish),
        )
    }
    for step in PLAN:
        actions[step[0]](*step[1:])


def fused_layer(x, tok, groups, counts, rows, down, vec):
    def big(n):
        return pltpu.VMEM((n, 768, 768), bf16)

    scratch = [
        pltpu.VMEM((512, 768), bf16),
        pltpu.VMEM((24, 6144), f32),
        pltpu.VMEM((96, 768), f32),
        big(8),
        big(4),
        big(4),
        big(4),
        big(8),
        pltpu.VMEM((3, 512, 768), bf16),
        pltpu.VMEM((24, 256, 128), bf16),
        pltpu.VMEM((512, 768), bf16),
        pltpu.VMEM((768, 512), bf16),
        pltpu.VMEM((768, 512), bf16),
        pltpu.VMEM((512, 768), bf16),
        pltpu.VMEM((768, 512), bf16),
        pltpu.VMEM((512, 3072), bf16),
        pltpu.VMEM((3072, 512), bf16),
        pltpu.VMEM((512, 3072), bf16),
        pltpu.VMEM((512, 768), f32),
        pltpu.VMEM((512, 768), f32),
        pltpu.VMEM((512, 768), f32),
        pltpu.VMEM((512, 128), f32),
        pltpu.VMEM((512, 128), f32),
        pltpu.VMEM((512, 128), f32),
        pltpu.VMEM((8, 128), f32),
        pltpu.VMEM((8, 128), f32),
        pltpu.VMEM((32, 16, 128), bf16),
        pltpu.VMEM((8, 9216), f32),
        pltpu.VMEM((8, 2304), f32),
        pltpu.VMEM((32, 8, 896), f32),
        pltpu.VMEM((8, 768), f32),
        pltpu.VMEM((8, 128), f32),
        pltpu.VMEM((2, 256, 256), f32),
        pltpu.VMEM((8, 9216), f32),
        pltpu.VMEM((8, 16, 128), f32),
        pltpu.VMEM((12, 16, 128), f32),
    ]
    dma = pltpu.SemaphoreType.DMA
    scratch += [
        dma((4,)), dma((6, 4, 4)), dma((6, 4, 2)), dma((6, 4, 2)), dma((6, 4, 2)), dma((6,)), dma((6, 4)),
        dma((2, 11)), dma((2, 8)),
        dma((6, 2, 4)), dma((6, 2, 2)), dma((6, 2)), dma((6, 2, 4)), dma((6, 2, 2)), dma((6, 2)), dma((6, 4)),
        dma((12,)), dma((10,)),
    ]
    vmem = pl.BlockSpec(memory_space=pltpu.VMEM)
    smem = pl.BlockSpec(memory_space=pltpu.SMEM)
    anywhere = pl.BlockSpec(memory_space=pl.ANY)
    return pl.pallas_call(
        layer_kernel,
        out_shape=(
            jax.ShapeDtypeStruct((1, 1), f32),
            jax.ShapeDtypeStruct(x.shape, f32),
            jax.ShapeDtypeStruct(rows.shape, f32),
            jax.ShapeDtypeStruct(down.shape, f32),
            jax.ShapeDtypeStruct((1,) + vec.shape, f32),
        ),
        in_specs=[anywhere, vmem, smem, smem, anywhere, anywhere, vmem],
        out_specs=(smem, anywhere, vmem, vmem, vmem),
        scratch_shapes=scratch,
        compiler_params=pltpu.CompilerParams(collective_id=0, has_side_effects=True, vmem_limit_bytes=64 * 1024 * 1024 - 65536),
    )(x, tok, groups, counts, rows, down, vec)


def adam_step(master, gradient, moment_one, moment_two, decay, rate):
    mean_new = beta_one * moment_one + (1.0 - beta_one) * gradient
    square_new = beta_two * moment_two + (1.0 - beta_two) * gradient * gradient
    mean_hat = mean_new / (1.0 - beta_one**STEP)
    square_hat = square_new / (1.0 - beta_two**STEP)
    updated = master - rate * (mean_hat / (jnp.sqrt(square_hat) + adam_epsilon) + decay * master)
    return (updated, mean_new, square_new)


def on_device_fused(
    embeds, token_mask, groups, counts,
    rows_master, rows_mean, rows_square, down_master, down_mean, down_square,
    vector_master, vector_mean, vector_square,
):
    x = embeds.reshape(-1, embeds.shape[-1])
    loss, dx, rows_grad, down_grad, vec_grad = fused_layer(x, token_mask, groups, counts, rows_master, down_master, vector_master)
    rows_new = adam_step(rows_master, rows_grad, rows_mean, rows_square, decay_rate, learn_rate)
    down_new = adam_step(down_master, down_grad, down_mean, down_square, decay_rate, learn_rate)
    vector_new = adam_step(vector_master, vec_grad.reshape(-1), vector_mean, vector_square, 0.0, vector_rate)
    return (loss[0, 0], dx.reshape(embeds.shape)) + rows_new + down_new + vector_new


def layer_norm(values, scale_vec, shift_vec):
    centre = values - jnp.mean(values, axis=-1, keepdims=True)
    spread = jnp.mean(centre * centre, axis=-1, keepdims=True)
    return centre * lax.rsqrt(spread + norm_epsilon) * scale_vec + shift_vec


def pool_unit(weights, output):
    summed = jnp.sum(output * weights[:, :, None], axis=1) / jnp.sum(weights, axis=1, keepdims=True)
    return summed * lax.rsqrt(jnp.sum(summed * summed, axis=1, keepdims=True) + unit_epsilon)


def exact_gelu(values):
    return jax.nn.gelu(values, approximate=False)


def softmax_last(values):
    return jax.nn.softmax(values, axis=-1)


def split_vectors(vectors, model_width, hidden):
    extents = [model_width] * 5 + [hidden] + [model_width] * 3
    pieces_out = []
    offset = 0
    for extent in extents:
        pieces_out.append(vectors[offset : offset + extent])
        offset = offset + extent
    return pieces_out


def pair_exps(left_rows, right_rows, left_group, right_group, left_start, right_start):
    scores = score_scale * jnp.dot(left_rows, right_rows.T, precision=highest)
    left_index = left_start + jnp.arange(left_rows.shape[0])
    right_index = right_start + jnp.arange(right_rows.shape[0])
    diagonal = left_index[:, None] == right_index[None, :]
    scores = scores - score_scale * margin * diagonal.astype(jnp.float32)
    same = (left_group[:, None] == right_group[None, :]) & (left_group[:, None] >= 0.0)
    return (jnp.where(same, jnp.exp(scores), 0.0), (diagonal & same).astype(jnp.float32))


def add_sums(own_data, arrived, offset):
    sources, targets, group_own, own_start = own_data
    other_src, other_tgt, other_group = arrived
    row_exp, unused_row = pair_exps(sources, other_tgt, group_own, other_group, own_start, offset)
    col_exp, unused_col = pair_exps(other_src, targets, other_group, group_own, offset, own_start)
    return (jnp.sum(row_exp, axis=1), jnp.sum(col_exp, axis=0))


def add_grads(own_data, loss_coef, arrived, offset):
    sources, targets, group_own, own_start, row_own, col_own = own_data
    other_src, other_tgt, other_group, other_row, other_col = arrived
    row_exp, row_diag = pair_exps(sources, other_tgt, group_own, other_group, own_start, offset)
    row_coef = (
        row_exp / row_own[:, None] + row_exp / other_col[None, :] - 2.0 * row_diag
    ) * loss_coef
    col_exp, col_diag = pair_exps(other_src, targets, other_group, group_own, offset, own_start)
    col_coef = (
        col_exp / other_row[:, None] + col_exp / col_own[None, :] - 2.0 * col_diag
    ) * loss_coef
    grad_src = score_scale * jnp.dot(row_coef, other_tgt, precision=highest)
    grad_tgt = score_scale * jnp.dot(col_coef.T, other_src, precision=highest)
    return (grad_src, grad_tgt)


def on_device_general(
    embeds,
    token_mask,
    groups,
    counts,
    rows_master,
    rows_mean,
    rows_square,
    down_master,
    down_mean,
    down_square,
    vector_master,
    vector_mean,
    vector_square,
):
    slot_count = embeds.shape[0]
    length = embeds.shape[2]
    model_width = embeds.shape[3]
    row_all, down_all, vector_all = (
        lax.all_gather(rows_master.astype(jnp.bfloat16), ("blk", "dp"), axis=0, tiled=True),
        lax.all_gather(down_master.astype(jnp.bfloat16), ("blk", "dp"), axis=0, tiled=True),
        lax.all_gather(vector_master.astype(jnp.bfloat16), ("blk", "dp"), axis=0, tiled=True),
    )
    hidden = down_all.shape[0]
    vectors = vector_all.astype(jnp.float32)
    bias_q, bias_v, bias_o, gain_one, shift_one, bias_up, bias_down, gain_two, shift_two = (
        split_vectors(vectors, model_width, hidden)
    )
    w_attn_in = row_all[:, : 3 * model_width]
    w_attn_out = row_all[:, 3 * model_width : 4 * model_width]
    w_up = row_all[:, 4 * model_width :]
    seq_count = 2 * slot_count
    tokens = seq_count * length
    head_count = model_width // HEAD
    inputs = embeds.reshape(tokens, model_width)
    weights = token_mask.reshape(seq_count, length).astype(jnp.float32)
    key_valid = token_mask.reshape(seq_count, length) > 0
    joined = jnp.concatenate([bias_q, jnp.zeros_like(bias_q), bias_v])
    projected = (jnp.dot(inputs, w_attn_in, preferred_element_type=jnp.float32) + joined).astype(
        jnp.bfloat16
    )
    queries = projected[:, :model_width].reshape(seq_count, length, head_count, HEAD)
    key_part = projected[:, model_width : 2 * model_width].reshape(
        seq_count, length, head_count, HEAD
    )
    values = projected[:, 2 * model_width :].reshape(seq_count, length, head_count, HEAD)
    scores = jnp.einsum(
        "nihe,njhe->nhij", queries, key_part, preferred_element_type=jnp.float32
    ) * HEAD ** (-0.5)
    scores = jnp.where(key_valid[:, None, None, :], scores, -1e30)
    attention, soft_back = jax.vjp(softmax_last, scores)
    attention_low = attention.astype(jnp.bfloat16)
    context = (
        jnp.einsum("nhij,njhe->nihe", attention_low, values, preferred_element_type=jnp.float32)
        .astype(jnp.bfloat16)
        .reshape(tokens, model_width)
    )
    resid_one = (
        inputs.astype(jnp.float32)
        + jnp.dot(context, w_attn_out, preferred_element_type=jnp.float32)
        + bias_o
    )
    normed_full, norm_one_back = jax.vjp(layer_norm, resid_one, 1.0 + gain_one, shift_one)
    normed_one = normed_full.astype(jnp.bfloat16)
    up_pre = jnp.dot(normed_one, w_up, preferred_element_type=jnp.float32) + bias_up
    activated_full, gelu_back = jax.vjp(exact_gelu, up_pre)
    activated = activated_full.astype(jnp.bfloat16)
    resid_two = (
        normed_one.astype(jnp.float32)
        + jnp.dot(activated, down_all, preferred_element_type=jnp.float32)
        + bias_down
    )
    output, norm_two_back = jax.vjp(layer_norm, resid_two, 1.0 + gain_two, shift_two)
    pooled, pool_back = jax.vjp(
        partial(pool_unit, weights), output.reshape(seq_count, length, model_width)
    )
    pooled = pooled.reshape(slot_count, 2, model_width)
    sources = pooled[:, 0]
    targets = pooled[:, 1]
    own_start = lax.axis_index(("blk", "dp")) * slot_count
    valid_slot = jnp.arange(slot_count) < counts[0]
    group_own = jnp.where(valid_slot, groups, -1).astype(jnp.float32)
    pair_total = lax.psum(counts[0].astype(jnp.float32), ("blk", "dp"))
    loss_coef = 0.5 / pair_total
    own_sums = (sources, targets, group_own, own_start)
    row_sum, col_sum = add_sums(
        own_sums,
        (
            lax.all_gather(sources, ("blk", "dp"), axis=0, tiled=True),
            lax.all_gather(targets, ("blk", "dp"), axis=0, tiled=True),
            lax.all_gather(group_own, ("blk", "dp"), axis=0, tiled=True),
        ),
        jnp.int32(0),
    )
    row_safe = jnp.where(valid_slot, row_sum, 1.0)
    col_safe = jnp.where(valid_slot, col_sum, 1.0)
    own_grads = (sources, targets, group_own, own_start, row_safe, col_safe)
    grad_src, grad_tgt = add_grads(
        own_grads,
        loss_coef,
        (
            lax.all_gather(sources, ("blk", "dp"), axis=0, tiled=True),
            lax.all_gather(targets, ("blk", "dp"), axis=0, tiled=True),
            lax.all_gather(group_own, ("blk", "dp"), axis=0, tiled=True),
            lax.all_gather(row_safe, ("blk", "dp"), axis=0, tiled=True),
            lax.all_gather(col_safe, ("blk", "dp"), axis=0, tiled=True),
        ),
        jnp.int32(0),
    )
    positive = score_scale * jnp.sum(sources * targets, axis=1) - score_scale * margin
    loss_terms = jnp.sum(
        jnp.where(valid_slot, jnp.log(row_safe) + jnp.log(col_safe) - 2.0 * positive, 0.0)
    )
    pair_loss = lax.psum(loss_terms, ("blk", "dp")) * loss_coef
    grad_pooled = jnp.stack([grad_src, grad_tgt], axis=1).reshape(seq_count, model_width)
    grad_output = pool_back(grad_pooled)[0].reshape(tokens, model_width)
    grad_resid_two, grad_gain_two, grad_shift_two = norm_two_back(grad_output)
    grad_down_low = grad_resid_two.astype(jnp.bfloat16)
    grad_w_down = jnp.einsum(
        "tf,td->fd", activated, grad_down_low, preferred_element_type=jnp.float32
    )
    grad_bias_down = jnp.sum(grad_down_low.astype(jnp.float32), axis=0)
    grad_act = jnp.einsum("td,fd->tf", grad_down_low, down_all, preferred_element_type=jnp.float32)
    grad_up = gelu_back(grad_act)[0].astype(jnp.bfloat16)
    grad_w_up = jnp.einsum("td,tf->df", normed_one, grad_up, preferred_element_type=jnp.float32)
    grad_bias_up = jnp.sum(grad_up.astype(jnp.float32), axis=0)
    grad_normed = grad_resid_two + jnp.einsum(
        "tf,df->td", grad_up, w_up, preferred_element_type=jnp.float32
    )
    grad_resid_one, grad_gain_one, grad_shift_one = norm_one_back(grad_normed)
    grad_attn_low = grad_resid_one.astype(jnp.bfloat16)
    grad_w_out = jnp.einsum("td,te->de", context, grad_attn_low, preferred_element_type=jnp.float32)
    grad_bias_out = jnp.sum(grad_attn_low.astype(jnp.float32), axis=0)
    grad_context = jnp.einsum(
        "te,de->td", grad_attn_low, w_attn_out, preferred_element_type=jnp.float32
    ).astype(jnp.bfloat16)
    grad_context = grad_context.reshape(seq_count, length, head_count, HEAD)
    grad_attention = jnp.einsum(
        "nihe,njhe->nhij", grad_context, values, preferred_element_type=jnp.float32
    )
    grad_values = jnp.einsum(
        "nhij,nihe->njhe", attention_low, grad_context, preferred_element_type=jnp.float32
    )
    grad_scores = soft_back(grad_attention)[0].astype(jnp.bfloat16)
    grad_queries = jnp.einsum(
        "nhij,njhe->nihe", grad_scores, key_part, preferred_element_type=jnp.float32
    ) * HEAD ** (-0.5)
    grad_keys = jnp.einsum(
        "nhij,nihe->njhe", grad_scores, queries, preferred_element_type=jnp.float32
    ) * HEAD ** (-0.5)
    grad_projected = jnp.concatenate(
        [
            grad_queries.reshape(tokens, model_width),
            grad_keys.reshape(tokens, model_width),
            grad_values.reshape(tokens, model_width),
        ],
        axis=1,
    ).astype(jnp.bfloat16)
    grad_w_in = jnp.einsum("td,te->de", inputs, grad_projected, preferred_element_type=jnp.float32)
    grad_bias_q = jnp.sum(grad_projected[:, :model_width].astype(jnp.float32), axis=0)
    grad_bias_v = jnp.sum(grad_projected[:, 2 * model_width :].astype(jnp.float32), axis=0)
    grad_inputs = grad_resid_one + jnp.einsum(
        "te,de->td", grad_projected, w_attn_in, preferred_element_type=jnp.float32
    )
    grad_vector = jnp.concatenate(
        [
            grad_bias_q,
            grad_bias_v,
            grad_bias_out,
            grad_gain_one,
            grad_shift_one,
            grad_bias_up,
            grad_bias_down,
            grad_gain_two,
            grad_shift_two,
        ]
    )
    rows_share, down_share, vector_share = (
        lax.psum_scatter(
            jnp.concatenate([grad_w_in, grad_w_out, grad_w_up], axis=1),
            ("blk", "dp"),
            scatter_dimension=0,
            tiled=True,
        ),
        lax.psum_scatter(grad_w_down, ("blk", "dp"), scatter_dimension=0, tiled=True),
        lax.psum_scatter(grad_vector, ("blk", "dp"), scatter_dimension=0, tiled=True),
    )
    rows_new = adam_step(rows_master, rows_share, rows_mean, rows_square, decay_rate, learn_rate)
    down_new = adam_step(down_master, down_share, down_mean, down_square, decay_rate, learn_rate)
    vector_new = adam_step(
        vector_master, vector_share, vector_mean, vector_square, 0.0, vector_rate
    )
    embeds_grad = grad_inputs.reshape(slot_count, 2, length, model_width)
    return (
        pair_loss,
        embeds_grad,
        rows_new[0],
        rows_new[1],
        rows_new[2],
        down_new[0],
        down_new[1],
        down_new[2],
        vector_new[0],
        vector_new[1],
        vector_new[2],
    )


def solution(mesh):
    in_specs = (
        P(("blk", "dp"), None, None, None),
        P(("blk", "dp"), None, None),
        P(("blk", "dp")),
        P(("blk", "dp")),
        P(("blk", "dp"), None),
        P(("blk", "dp"), None),
        P(("blk", "dp"), None),
        P(("blk", "dp"), None),
        P(("blk", "dp"), None),
        P(("blk", "dp"), None),
        P(("blk", "dp")),
        P(("blk", "dp")),
        P(("blk", "dp")),
    )
    out_specs = (
        P(),
        P(("blk", "dp"), None, None, None),
        P(("blk", "dp"), None),
        P(("blk", "dp"), None),
        P(("blk", "dp"), None),
        P(("blk", "dp"), None),
        P(("blk", "dp"), None),
        P(("blk", "dp"), None),
        P(("blk", "dp")),
        P(("blk", "dp")),
        P(("blk", "dp")),
    )
    fits = dict(mesh.shape) == {"blk": 8, "dp": 4}
    return jax.shard_map(
        on_device_fused if fits else on_device_general, mesh=mesh, in_specs=in_specs, out_specs=out_specs, check_vma=False
    )
```

```python
from functools import partial

import jax
import jax.numpy as jnp
from jax import lax
from jax.experimental import pallas as pl
from jax.experimental.pallas import tpu as pltpu
from jax.sharding import PartitionSpec as P

HEAD = 64
STEP = 10


score_scale = 32.0
margin = 0.3
beta_one = 0.9
beta_two = 0.999
learn_rate = 0.03
vector_rate = 0.06
decay_rate = 0.01
adam_epsilon = 1e-08
norm_epsilon = 1e-12
unit_epsilon = 1e-06
highest = lax.Precision.HIGHEST

vmem_bytes = 64 * 1024 * 1024 - 65536

f32 = jnp.float32
bf16 = jnp.bfloat16


def dot_nn(a, b, precision=None):
    return lax.dot_general(a, b, (((1,), (0,)), ((), ())), precision=precision, preferred_element_type=f32)


def dot_nt(a, b, precision=None):
    return lax.dot_general(a, b, (((1,), (1,)), ((), ())), precision=precision, preferred_element_type=f32)


def dot_tn(a, b):
    return lax.dot_general(a, b, (((0,), (0,)), ((), ())), preferred_element_type=f32)


Z_FIRST, Z_MID = 0, 1
GATHER_MODE = (Z_FIRST, Z_MID, Z_FIRST, Z_FIRST, Z_MID, Z_MID)
REDUCE_MODE = (Z_FIRST, Z_FIRST, Z_FIRST, Z_MID, Z_MID, Z_FIRST)

PIECES = (
    (((0, 512), (768, 256)), ((1024, 256), (1536, 512))),
    (((512, 256), (1280, 256), (2048, 256)), ((2304, 768),)),
    (((3072, 768),), ((3840, 768),)),
    (((4608, 768),), ((5376, 768),)),
)


class Comm:
    def __init__(self, depth):
        self.depth = depth
        self.b = lax.axis_index("blk")
        self.z = lax.axis_index("dp")
        b, z = self.b, self.z
        self.X, self.Y, self.C = (b ^ 2, z), (b ^ 4, z), (b ^ 1, z)
        self.Z = [(b, z ^ k) for k in range(depth)]
        self.up, self.down = (b, z + 1), (b, z - 1)

    def barrier(self):
        sem = pltpu.get_barrier_semaphore()
        friends = [self.X, self.Y, self.C] + self.Z[1:3]
        for friend in friends:
            pl.semaphore_signal(sem, inc=1, device_id=friend, device_id_type=pl.DeviceIdType.MESH)
        pl.semaphore_wait(sem, len(friends))


def remote(src, dst, send_sem, recv_sem, device):
    return pltpu.make_async_remote_copy(
        src_ref=src,
        dst_ref=dst,
        send_sem=send_sem,
        recv_sem=recv_sem,
        device_id=device,
        device_id_type=pl.DeviceIdType.MESH,
    )


def layer_kernel(
    x_hbm, tok_ref, group_ref, count_ref, rows_hbm, down_hbm, vec_ref,
    loss_ref, dx_hbm, grad_rows_ref, grad_down_ref, grad_vec_ref,
    x_ref, rows_ref, down_ref,
    raw, w_attn, w_up, w_down, g_rest,
    qkv, probs, ctx, ctx_t, x_t, y_low, y_t, act, act_t, slope, xhat1, xhat2, work,
    rstd1, rstd2, tok_w, tok_f, tags, vec_all, vec_row, bias_in, pairs, pooled_hat, own_unit, unit_rs, pair_k, vec_grad, vec_out, vec_in,
    local_sem, zsem, xsem, ysem, dsem, csem, ssem,
    small_recv, small_send,
    rc_sem, r1_sem, r2_sem, rz_sem, ry_sem, rf_sem, rs_send,
    vr_sem, vs_sem,
):
    comm = Comm(4)
    b, z = comm.b, comm.z
    me = b * 4 + z
    width = 768
    half = 384
    def at_q(q):
        return b ^ (2 * q)

    def lanes(h):
        return pl.ds(half * h, half)

    def unit(place, i, h):
        ref, base = place
        return ref.at[base + i // 16, pl.ds((i % 16) * 48, 48), lanes(h)]

    def quad(place, n, h):
        ref, base = place
        return ref.at[base + n // 4, pl.ds((n % 4) * 192, 192), lanes(h)]

    def share(p, i, h):
        if p < 4:
            return unit((raw, 2 * p), i, h)
        return w_down.at[i // 8, pl.ds((i % 8) * 96 + 48 * h, 48), lanes(p - 4)]

    def bulk(n):
        return raw.at[0] if n == 32 else raw.at[0, pl.ds(0, 48 * n), pl.ds(0, half)]

    def send(p, i, h, device, way, rsem):
        ref = share(p, i, h)
        remote(ref, ref, ssem.at[p, way], rsem, device).start()

    def arrived(p, i, h, rsem):
        ref = share(p, i, h)
        remote(ref, ref, ssem.at[p, 0], rsem, comm.X).wait_recv()

    def to_core(p, i, h):
        send(p, i, h, comm.C, 2, csem.at[p])

    def both_to_core(p, i):
        if p < 4:
            ref = raw.at[2 * p + i // 16, pl.ds((i % 16) * 48, 48), :]
        else:
            ref = w_down.at[i // 8, pl.ds((i % 8) * 96, 96), lanes(p - 4)]
        remote(ref, ref, ssem.at[p, 2], csem.at[p], comm.C).start()

    def dev(q, k):
        return at_q(q) * 4 + (z ^ k)

    def cast(p):
        for h in range(2):
            if p < 4:
                row = jnp.concatenate([rows_ref[:, c : c + n] for c, n in PIECES[p][h]], axis=1)
                both = jnp.concatenate([row[:, :half], row[:, half:]], axis=0)
            else:
                both = down_ref[48 * h : 48 * h + 48, half * (p - 4) : half * (p - 3)]
            if p < 4:
                raw[2 * p + me // 16, pl.ds((me % 16) * 48, 48), lanes(h)] = both.astype(bf16)
            else:
                w_down[me // 8, pl.ds((me % 8) * 96 + 48 * h, 48), lanes(p - 4)] = both.astype(bf16)

    def along_z(p, q, k, j, h):
        i = dev(q, k)
        if k == 0:
            send(p, i, h, comm.Z[2], 3, zsem.at[p, 2, 2 * j + h])
            send(p, i, h, comm.Z[1], 3, zsem.at[p, 1, 2 * j + h])
        else:
            send(p, i, h, comm.Z[1], 3, zsem.at[p, 3, 2 * j + h])

    def place(j, h):
        return 0 if j == 0 else (1 if h == 0 else 2)

    def ownz(p):
        for h in range(2):
            along_z(p, 0, 0, 0, h)

    def own1(p):
        send(p, dev(0, 0), 0, comm.X, 0, dsem.at[p, 0, 0])
        send(p, dev(0, 0), 1, comm.Y, 1, dsem.at[p, 0, 1])

    def first(p):
        for h in range(2):
            q = place(1, h)
            arrived(p, dev(q, 0), h, dsem.at[p, 0, h])
            along_z(p, q, 0, 1, h)

    def fold(p, j=0):
        for h in range(2):
            q = place(j, h)
            arrived(p, dev(q, 2), h, zsem.at[p, 2, 2 * j + h])
            along_z(p, q, 2, j, h)

    def z_wait(p, k, j):
        if k in (1, 3):
            for h in range(2):
                arrived(p, dev(place(j, h), k), h, zsem.at[p, k, 2 * j + h])

    def col(p, k):
        z_wait(p, k, 0)
        i = dev(0, k)
        send(p, i, 0, comm.X, 0, xsem.at[p, k, 0])
        send(p, i, 1, comm.Y, 1, ysem.at[p, k, 1])
        send(p, i, 1, comm.X, 0, xsem.at[p, k, 1])
        send(p, i, 0, comm.Y, 1, ysem.at[p, k, 0])
        both_to_core(p, i)

    def across(p, k):
        i = dev(1, k)
        arrived(p, i, 0, xsem.at[p, k, 0])
        send(p, i, 0, comm.Y, 1, dsem.at[p, k, 0])
        to_core(p, i, 0)
        i = dev(2, k)
        arrived(p, i, 1, ysem.at[p, k, 1])
        send(p, i, 1, comm.X, 0, dsem.at[p, k, 1])
        to_core(p, i, 1)

    def fin(p, k, j):
        z_wait(p, k, j)
        i = dev(place(j, 0), k)
        send(p, i, 0, comm.Y, 1, ysem.at[p, k, j])
        to_core(p, i, 0)
        i = dev(place(j, 1), k)
        send(p, i, 1, comm.X, 0, xsem.at[p, k, j])
        to_core(p, i, 1)

    def last(p, k):
        if GATHER_MODE[p] == Z_FIRST:
            rest = ((1, 1, xsem.at[p, k, 1]), (2, 0, ysem.at[p, k, 0]), (3, 0, dsem.at[p, k, 0]), (3, 1, dsem.at[p, k, 1]))
        else:
            rest = ((2, 0, ysem.at[p, k, 0]), (1, 1, xsem.at[p, k, 0]), (3, 0, ysem.at[p, k, 1]), (3, 1, xsem.at[p, k, 1]))
        for q, h, sem in rest:
            arrived(p, dev(q, k), h, sem)
            if q < 3:
                to_core(p, dev(q, k), h)
        both_to_core(p, dev(3, k))

    def gathered(p):
        remote(bulk(32), bulk(32), ssem.at[p, 0], csem.at[p], comm.X).wait_recv()

    def sent(p):
        z_first = GATHER_MODE[p] == Z_FIRST
        for way, n in ((0, 12 if z_first else 9), (1, 12 if z_first else 9), (2, 32), (3, 6 if z_first else 12)):
            remote(bulk(n), bulk(n), ssem.at[p, way], csem.at[p], comm.X).wait_send()

    def small_send_one(ref, n, i, device, rsem):
        block = ref.at[pl.ds(i, 1)]
        remote(block, block, small_send.at[n], rsem, device).start()

    def small_wait(ref, n, i, rsem):
        block = ref.at[pl.ds(i, 1)]
        remote(block, block, small_send.at[n], rsem, comm.X).wait_recv()

    def small_plane(ref, n, k):
        i = dev(0, k)
        small_send_one(ref, n, i, comm.X, small_recv.at[n, 4 + k])
        small_send_one(ref, n, i, comm.Y, small_recv.at[n, 8 + k])
        small_send_one(ref, n, i, comm.C, small_recv.at[n, 0])

    def small_own(ref, n):
        small_send_one(ref, n, me, comm.Z[2], small_recv.at[n, 2])
        small_send_one(ref, n, me, comm.Z[1], small_recv.at[n, 1])
        small_plane(ref, n, 0)

    def small_z(ref, n):
        small_wait(ref, n, dev(0, 1), small_recv.at[n, 1])
        small_plane(ref, n, 1)
        small_wait(ref, n, dev(0, 2), small_recv.at[n, 2])
        small_send_one(ref, n, dev(0, 2), comm.Z[1], small_recv.at[n, 3])
        small_plane(ref, n, 2)
        small_wait(ref, n, dev(0, 3), small_recv.at[n, 3])
        small_plane(ref, n, 3)

    def small_cross(ref, n):
        for k in range(4):
            small_wait(ref, n, dev(1, k), small_recv.at[n, 4 + k])
            if k % 2 == 0:
                small_send_one(ref, n, dev(1, k), comm.Y, small_recv.at[n, 12 + k])
            small_send_one(ref, n, dev(1, k), comm.C, small_recv.at[n, 0])
            small_wait(ref, n, dev(2, k), small_recv.at[n, 8 + k])
            if k % 2 == 1:
                small_send_one(ref, n, dev(2, k), comm.X, small_recv.at[n, 12 + k])
            small_send_one(ref, n, dev(2, k), comm.C, small_recv.at[n, 0])

    def small_end(ref, n):
        for k in range(4):
            small_wait(ref, n, dev(3, k), small_recv.at[n, 12 + k])
            small_send_one(ref, n, dev(3, k), comm.C, small_recv.at[n, 0])
        many = ref.at[pl.ds(0, 16)]
        remote(many, many, small_send.at[n], small_recv.at[n, 0], comm.X).wait_recv()
        many = ref.at[pl.ds(0, 31)]
        remote(many, many, small_send.at[n], small_recv.at[n, 0], comm.X).wait_send()

    def vec(offset, size=width):
        return vec_row[0:1, offset : offset + size]

    bias_q, bias_v, bias_o, gain1_at, shift1_at, bias_up_at = 0, width, 2 * width, 3 * width, 4 * width, 5 * width
    bias_down_at, gain2_at, shift2_at = 9 * width, 10 * width, 11 * width

    share_v = 288

    def place_vectors():
        v = vec_ref[...].reshape(1, share_v)
        tail = jnp.concatenate([v[:, 256:share_v], jnp.zeros((1, 384 - share_v), f32)], axis=1)
        tile = jnp.concatenate([v[:, 0:128], v[:, 128:256], tail, jnp.zeros((13, 128), f32)], axis=0)
        vec_all[pl.ds(me, 1)] = tile.astype(bf16).reshape(1, 16, 128)

    def spread_vectors():
        for i in range(32):
            tile = vec_all[i].astype(f32)
            for r, n in ((0, 128), (1, 128), (2, share_v - 256)):
                at = share_v * i + 128 * r
                vec_row[0:1, at : at + n] = tile[r : r + 1, 0:n]
        bias_in[...] = jnp.zeros_like(bias_in)
        bias_in[0:1, 0:512] = vec(bias_q, 512)
        bias_in[0:1, 1024:1536] = vec(bias_v, 512)
        bias_in[0:1, 1536:1792] = vec(bias_q + 512, 256)
        bias_in[0:1, 2048:2304] = vec(bias_v + 512, 256)

    def relayout(p):
        target, chunk = (w_attn, 2 * p) if p < 2 else (w_up, 2 * p - 4)

        def body(j, carry):
            for h in range(2):
                even = raw[2 * p + j // 8, pl.ds((j % 8) * 96, 48), lanes(h)].astype(f32)
                odd = raw[2 * p + j // 8, pl.ds((j % 8) * 96 + 48, 48), lanes(h)].astype(f32)
                for q in range(2):
                    rows = jnp.concatenate([even[24 * q : 24 * q + 24], odd[24 * q : 24 * q + 24]], axis=0)
                    target[chunk + h, pl.ds(j * 48, 48), lanes(q)] = rows.astype(bf16)
            return carry

        lax.fori_loop(0, 16, body, 0)

    def transpose_into(source, target):
        def body(j, carry):
            at = pl.multiple_of(j * 256, 256)
            target[pl.ds(at, 256), :] = jnp.transpose(source[:, pl.ds(at, 256)])
            return carry

        lax.fori_loop(0, source.shape[1] // 256, body, 0)

    def token_weights():
        lane = lax.broadcasted_iota(jnp.int32, (1, 128), 1)
        left = (lane < 64).astype(f32)
        tok = tok_ref[...].astype(f32)
        tok_f[0:4, :] = jnp.concatenate([tok[:, 0, :], tok[:, 1, :]], axis=1)
        for p in range(4):
            m = tok_f[p : p + 1, :]
            n0 = jnp.sum(m * left, axis=1, keepdims=True)
            n1 = jnp.sum(m * (1.0 - left), axis=1, keepdims=True)
            w = m / (left * n0 + (1.0 - left) * n1)
            tok_w[128 * p : 128 * p + 128, :] = jnp.transpose(jnp.broadcast_to(w, (128, 128)))
        row = lax.broadcasted_iota(jnp.int32, (8, 128), 0) % 4
        tag = jnp.full((8, 128), -1.0, f32)
        for s in range(4):
            tag = jnp.where((row == s) & (count_ref[0] > s), group_ref[s].astype(f32), tag)
        tags[...] = tag

    def project(lo, hi):
        def body(t, carry):
            c, n = t // 3, t % 3
            at = pl.multiple_of(n * 256, 256)
            bias = bias_in[0:1, pl.ds(pl.multiple_of(t * 256, 256), 256)]
            out = dot_nn(x_ref[...], w_attn[c, :, pl.ds(at, 256)]) + bias
            qkv[c, :, pl.ds(at, 256)] = out.astype(bf16)
            return carry

        lax.fori_loop(lo, hi, body, 0)

    def head_places(hp):
        if hp < 4:
            key = (0, 512 + 128 * hp) if hp < 2 else (1, 128 * hp - 256)
            return (0, 128 * hp), key, (1, 256 + 128 * hp)
        return (2, 128 * hp - 512), (2, 128 * hp - 256), (2, 128 * hp)

    lane128 = lax.broadcasted_iota(jnp.int32, (128, 128), 1)
    row128 = lax.broadcasted_iota(jnp.int32, (128, 128), 0)
    even_half = lane128 < 64

    def split_heads(v):
        zero = jnp.zeros_like(v)
        return jnp.concatenate([jnp.where(even_half, v, zero), jnp.where(even_half, zero, v)], axis=0)

    def attend(group, lo, hi):
        def body(p, carry):
            rows = pl.ds(pl.multiple_of(p * 128, 128), 128)
            m = tok_f[pl.ds(p, 1), :]
            same = (row128 < 64) == (lane128 < 64)
            open_one = same & (jnp.broadcast_to(m, (128, 128)) > 0.0)
            block = jnp.where(open_one, 0.0, -1e30)
            block = jnp.concatenate([block, block], axis=0)
            for hp in range(4) if group == 0 else range(4, 6):
                q2, k2, v2 = [qkv[c, rows, at : at + 128] for c, at in head_places(hp)]
                s = dot_nt(split_heads(q2), k2) * HEAD ** (-0.5) + block
                e = jnp.exp(s - jnp.max(s, axis=1, keepdims=True))
                a = (e * (1.0 / jnp.sum(e, axis=1, keepdims=True))).astype(bf16)
                probs[p * 6 + hp] = a
                wide = jnp.concatenate([a[:128], a[128:]], axis=1)
                ctx[rows, 128 * hp : 128 * hp + 128] = dot_nn(wide, split_heads(v2)).astype(bf16)
            return carry

        lax.fori_loop(lo, hi, body, 0, unroll=1 + group)

    def norm_rows(i, source_fn, hat, rstd, emit):
        rows = pl.ds(pl.multiple_of(i * 64, 64), 64)
        h = source_fn(rows)
        centre = h - jnp.mean(h, axis=1, keepdims=True)
        r = lax.rsqrt(jnp.mean(centre * centre, axis=1, keepdims=True) + norm_epsilon)
        xh = centre * r
        hat[rows, :] = xh
        rstd[rows, :] = jnp.broadcast_to(r, (64, 128))
        if emit is not None:
            emit(rows, xh)

    def attn_out():
        def body(n, carry):
            at = pl.multiple_of(n * 256, 256)
            work[:, pl.ds(at, 256)] = dot_nn(ctx[...], w_attn[3, :, pl.ds(at, 256)])
            return carry

        lax.fori_loop(0, 3, body, 0)

    def attn_norm():
        def source(rows):
            return x_ref[rows, :].astype(f32) + work[rows, :] + vec(bias_o)

        def emit(rows, xh):
            y_low[rows, :] = (xh * (1.0 + vec(gain1_at)) + vec(shift1_at)).astype(bf16)

        def norm(i, carry):
            norm_rows(i, source, xhat1, rstd1, emit)
            return carry

        lax.fori_loop(0, 8, norm, 0, unroll=2)

    def feed_up(lo, hi):
        def body(t, carry):
            c, n = t // 3, t % 3
            at = pl.multiple_of(n * 256, 256)
            to = pl.multiple_of(t * 256, 256)
            work[:, pl.ds(0, 256)] = dot_nn(y_low[...], w_up[c, :, pl.ds(at, 256)])
            bias = vec_row[0:1, pl.ds(pl.multiple_of(bias_up_at + to, 256), 256)]

            def rows_of(i, inner):
                rows = pl.ds(pl.multiple_of(i * 32, 32), 32)
                v = work[rows, 0:256] + bias
                cdf = 0.5 * (1.0 + lax.erf(v * 0.7071067811865476))
                dens = jnp.exp(v * v * -0.5) * 0.3989422804014327
                act[rows, pl.ds(to, 256)] = (v * cdf).astype(bf16)
                slope[rows, pl.ds(to, 256)] = (cdf + v * dens).astype(bf16)
                return inner

            lax.fori_loop(0, 16, rows_of, 0, unroll=4)
            act_t[pl.ds(to, 256), :] = jnp.transpose(act[:, pl.ds(to, 256)])
            return carry

        lax.fori_loop(lo, hi, body, 0)

    def feed_down(s):
        def body(n, carry):
            at = pl.multiple_of(n * 256, 256)
            total = dot_nn(act[:, 0:width], w_down[0, :, pl.ds(at, 256)])
            for c in range(1, 4):
                total = total + dot_nn(act[:, c * width : (c + 1) * width], w_down[c, :, pl.ds(at, 256)])
            work[:, pl.ds(at, 256)] = total
            return carry

        lax.fori_loop(s, 2 * s + 1, body, 0)

    def down_norm():
        def source(rows):
            return y_low[rows, :].astype(f32) + work[rows, :] + vec(bias_down_at)

        def norm(i, carry):
            norm_rows(i, source, xhat2, rstd2, None)
            rows = pl.ds(pl.multiple_of(i * 64, 64), 64)
            got = jnp.sum(xhat2[rows, :] * tok_w[rows, 0:1], axis=0, keepdims=True)
            at = i // 2 + 4 * (i % 2)
            pooled_hat[pl.ds(at, 1), :] = got
            return carry

        lax.fori_loop(0, 8, norm, 0, unroll=2)

    def transposes():
        transpose_into(y_low, y_t)
        transpose_into(ctx, ctx_t)

    def pool():
        e = pooled_hat[...] * (1.0 + vec(gain2_at)) + vec(shift2_at)
        r = lax.rsqrt(jnp.sum(e * e, axis=1, keepdims=True) + unit_epsilon)
        unit_rs[...] = jnp.broadcast_to(r, (8, 128))
        n = e * r
        own_unit[...] = n
        packed = jnp.concatenate([n[:, :half], n[:, half:]], axis=0)
        tag = jnp.concatenate([tags[...], tags[...]], axis=0)
        pairs[pl.ds(me, 1)] = jnp.concatenate([packed, tag], axis=1).astype(bf16).reshape(1, 16, 512)

    def contrast():
        total = 256
        every = pairs[...].astype(f32)
        left = every[:, 0:8, 0:half].reshape(total, half).astype(bf16)
        right = every[:, 8:16, 0:half].reshape(total, half).astype(bf16)
        tag = every[:, 0:8, half : half + 128].reshape(total, 128)
        tag_row = jnp.concatenate([jnp.transpose(tag[0:128])[0:1], jnp.transpose(tag[128:256])[0:1]], axis=1)
        s = (dot_nt(left, left) + dot_nt(right, right)) * score_scale
        i = lax.broadcasted_iota(jnp.int32, (total, total), 0)
        j = lax.broadcasted_iota(jnp.int32, (total, total), 1)
        opposite = (i & 4) != (j & 4)
        diagonal = (i ^ j) == 4
        s = s - jnp.where(diagonal, score_scale * margin, 0.0)
        same = (tag[:, 0:1] == tag_row) & (tag_row >= 0.0) & opposite
        e = jnp.where(same, jnp.exp(jnp.where(same, s, 0.0)), 0.0)
        valid = tag_row >= 0.0
        sums = jnp.where(valid, jnp.sum(e, axis=0, keepdims=True), 1.0)
        coef = 1.0 / jnp.sum(valid.astype(f32))
        positive = jnp.sum(jnp.where(diagonal & same, s, 0.0))
        loss = (jnp.sum(jnp.where(valid, jnp.log(sums), 0.0)) - positive) * coef
        loss_ref[0, 0] = loss
        pair_k[0] = e
        pair_k[1] = jnp.where(diagonal & same, 2.0, 0.0)
        own_rows = pl.ds(pl.multiple_of(me * 8, 8), 8)
        e_own = pair_k[0, own_rows, :]
        r_own = jnp.sum(e_own, axis=1, keepdims=True)
        r_own = jnp.where(tags[:, 0:1] >= 0.0, r_own, 1.0)
        k = (e_own / r_own + e_own / sums - pair_k[1, own_rows, :]) * (coef * score_scale)
        high = k.astype(bf16)
        low = (k - high.astype(f32)).astype(bf16)
        both = jnp.concatenate([high, low], axis=0)
        dn = jnp.concatenate([dot_nn(both, left), dot_nn(both, right)], axis=1)
        dn = dn[0:8] + dn[8:16]
        n = own_unit[...]
        de = unit_rs[:, 0:1] * (dn - n * jnp.sum(n * dn, axis=1, keepdims=True))
        vec_grad[0:1, gain2_at : gain2_at + width] = jnp.sum(de * pooled_hat[...], axis=0, keepdims=True)
        vec_grad[0:1, shift2_at : shift2_at + width] = jnp.sum(de, axis=0, keepdims=True)
        pooled_hat[...] = de

    def norm_two_back():
        def body(i, carry):
            rows = pl.ds(pl.multiple_of(i * 64, 64), 64)
            de = pooled_hat[pl.ds(i // 2 + 4 * (i % 2), 1), :]
            dg = de * (1.0 + vec(gain2_at))
            xh = xhat2[rows, :]
            m1 = jnp.mean(dg, axis=1, keepdims=True)
            m2 = jnp.mean(dg * xh, axis=1, keepdims=True)
            dz = (rstd2[rows, 0:1] * tok_w[rows, 0:1]) * (dg - m1 - xh * m2)
            low = dz.astype(bf16)
            xhat2[rows, :] = dz
            y_low[rows, :] = low
            return carry + jnp.sum(low.astype(f32), axis=0, keepdims=True)

        vec_grad[0:1, bias_down_at : bias_down_at + width] = lax.fori_loop(0, 8, body, jnp.zeros((1, width), f32), unroll=2)

    g_places = ((w_up, 0), (w_up, 2), (g_rest, 4), (g_rest, 6), (g_rest, 0), (g_rest, 2))
    box_places = ((w_down, 0), (w_down, 2), (raw, 4), (raw, 6), (raw, 0), (raw, 2))

    def grad_w_down(blk):
        out = dot_nn(act_t[pl.ds(pl.multiple_of(blk * 384, 128), 384), :], y_low[...])
        for part in range(2):
            for zz in range(4):
                for h in range(2):
                    rows = out[96 * zz + 48 * h : 96 * zz + 48 * h + 48, half * part : half * part + half]
                    at = pl.multiple_of((blk % 4) * 192 + 48 * zz, 16)
                    g_rest[2 * part + blk // 4, pl.ds(at, 48), lanes(h)] = rows.astype(bf16)

    def down_sibling():
        def body(n, carry):
            blk = at_q(3 - n) ^ 1
            grad_w_down(blk)
            for p in (4, 5):
                for h in range(2):
                    core_send(p, h, 3 - n)
            return carry

        lax.fori_loop(0, 4, body, 0)

    def down_own():
        def body(n, carry):
            grad_w_down(at_q(3 - n))
            return carry

        lax.fori_loop(0, 4, body, 0)

    def grad_act(lo, hi):
        def body(t, carry):
            c, n = t // 3, t % 3
            to = pl.multiple_of(t * 256, 256)
            work[:, 0:256] = dot_nt(y_low[...], w_down[c, pl.ds(pl.multiple_of(n * 256, 256), 256), :])

            def rows_of(i, total):
                rows = pl.ds(pl.multiple_of(i * 64, 64), 64)
                low = (work[rows, 0:256] * slope[rows, pl.ds(to, 256)].astype(f32)).astype(bf16)
                act[rows, pl.ds(to, 256)] = low
                return total + jnp.sum(low.astype(f32), axis=0, keepdims=True)

            sums = lax.fori_loop(0, 8, rows_of, jnp.zeros((1, 256), f32))
            vec_grad[0:1, pl.ds(pl.multiple_of(bias_up_at + to, 256), 256)] = sums
            return carry

        lax.fori_loop(lo, hi, body, 0)

    def store_units(p, h, m, out):
        ref, base = g_places[p]
        for d in range(16):
            rows = out[24 * d : 24 * d + 24]
            both = jnp.concatenate([rows[:, :half], rows[:, half:]], axis=0)
            ref[base + m, 48 * d : 48 * d + 48, lanes(h)] = both.astype(bf16)

    def grad_w_rows(p):
        def body(n, carry):
            m = (b // 4) ^ (1 - n)
            rows = pl.ds(pl.multiple_of(m * 384, 128), 384)
            for h in range(2):
                if p >= 2:
                    out = dot_nn(y_t[rows, :], act[:, (2 * p - 4 + h) * width : (2 * p - 3 + h) * width])
                elif (p, h) == (1, 1):
                    out = dot_nn(ctx_t[rows, :], y_low[...])
                else:
                    out = dot_nn(x_t[rows, :], qkv[2 * p + h])
                store_units(p, h, m, out)
                for q in (1, 0):
                    core_send(p, h, 2 * (1 - n) + q)
            return carry

        lax.fori_loop(0, 2, body, 0)

    def grad_y():
        def body(n, carry):
            at = pl.multiple_of(n * 256, 256)
            total = xhat2[:, pl.ds(at, 256)]
            for c in range(4):
                total = total + dot_nt(act[:, c * width : (c + 1) * width], w_up[c, pl.ds(at, 256), :])
            work[:, pl.ds(at, 256)] = total
            return carry

        lax.fori_loop(0, 3, body, 0)

    def norm_one_back():
        def body(i, carry):
            rows = pl.ds(pl.multiple_of(i * 64, 64), 64)
            dy = work[rows, :]
            xh = xhat1[rows, :]
            dg = dy * (1.0 + vec(gain1_at))
            m1 = jnp.mean(dg, axis=1, keepdims=True)
            m2 = jnp.mean(dg * xh, axis=1, keepdims=True)
            dh = rstd1[rows, 0:1] * (dg - m1 - xh * m2)
            low = dh.astype(bf16)
            work[rows, :] = dh
            y_low[rows, :] = low
            gain, shift, bias = carry
            return (
                gain + jnp.sum(dy * xh, axis=0, keepdims=True),
                shift + jnp.sum(dy, axis=0, keepdims=True),
                bias + jnp.sum(low.astype(f32), axis=0, keepdims=True),
            )

        zero = jnp.zeros((1, width), f32)
        gain, shift, bias = lax.fori_loop(0, 8, body, (zero, zero, zero), unroll=2)
        vec_grad[0:1, gain1_at : gain1_at + width] = gain
        vec_grad[0:1, shift1_at : shift1_at + width] = shift
        vec_grad[0:1, bias_o : bias_o + width] = bias

    def grad_ctx():
        def body(n, carry):
            at = pl.multiple_of(n * 256, 256)
            ctx[:, pl.ds(at, 256)] = dot_nt(y_low[...], w_attn[3, pl.ds(at, 256), :]).astype(bf16)
            return carry

        lax.fori_loop(0, 3, body, 0)

    def attend_back(group, lo, hi):
        def body(p, carry):
            rows = pl.ds(pl.multiple_of(p * 128, 128), 128)
            for hp in range(4) if group == 0 else range(4, 6):
                places = head_places(hp)
                q2, k2, v2 = [qkv[c, rows, at : at + 128] for c, at in places]
                dc = split_heads(ctx[rows, 128 * hp : 128 * hp + 128])
                a = probs[p * 6 + hp]
                af = a.astype(f32)
                da = dot_nt(dc, v2)
                ds = (af * (da - jnp.sum(af * da, axis=1, keepdims=True))).astype(bf16)
                dv = dot_tn(a, dc)
                wide = jnp.concatenate([ds[:128], ds[128:]], axis=1)
                dq = dot_nn(wide, split_heads(k2)) * HEAD ** (-0.5)
                dk = dot_tn(ds, split_heads(q2)) * HEAD ** (-0.5)
                for (c, at), d in zip(places, (dq, dk, dv)):
                    qkv[c, rows, at : at + 128] = d.astype(bf16)
            return carry

        lax.fori_loop(lo, hi, body, 0, unroll=1 + group)

    def grad_bias_in():
        def body(i, carry):
            rows = pl.ds(pl.multiple_of(i * 64, 64), 64)
            return tuple(have + jnp.sum(qkv[c, rows, :].astype(f32), axis=0, keepdims=True) for c, have in enumerate(carry))

        zero = jnp.zeros((1, width), f32)
        first_sum, second_sum, third_sum = lax.fori_loop(0, 8, body, (zero, zero, zero))
        vec_grad[0:1, bias_q : bias_q + 512] = first_sum[:, 0:512]
        vec_grad[0:1, bias_q + 512 : bias_q + 768] = third_sum[:, 0:256]
        vec_grad[0:1, bias_v : bias_v + 512] = second_sum[:, 256:768]
        vec_grad[0:1, bias_v + 512 : bias_v + 768] = third_sum[:, 512:768]

    def dx_copy(n):
        at = pl.ds(pl.multiple_of(n * 256, 256), 256)
        return pltpu.make_async_copy(work.at[:, at], dx_hbm.at[:, at], local_sem.at[3])

    def grad_x(lo, hi):
        def body(n, carry):
            at = pl.multiple_of(n * 256, 256)
            total = work[:, pl.ds(at, 256)]
            for c in range(3):
                total = total + dot_nt(qkv[c], w_attn[c, pl.ds(at, 256), :])
            work[:, pl.ds(at, 256)] = total
            return carry

        lax.fori_loop(lo, hi, body, 0)
        for n in range(lo, hi):
            dx_copy(n).start()

    def spot(p, run, u, h):
        ref, base = box_places[p]
        return ref.at[base + run // 4, pl.ds((run % 4) * 192 + 48 * u, 48), lanes(h)]

    def core_send(p, h, q):
        remote(
            quad(g_places[p], at_q(q) ^ 1, h), quad(box_places[p], q, h), rs_send.at[p, 0], rc_sem.at[p, h, q], comm.C
        ).start()

    def run_wait(p, run, h, sem):
        ref = quad(box_places[p], run, h)
        remote(ref, ref, rs_send.at[p, 0], sem, comm.C).wait_recv()

    def spot_wait(p, run, u, h, sem):
        ref = spot(p, run, u, h)
        remote(ref, ref, rs_send.at[p, 0], sem, comm.C).wait_recv()

    def add_in(p, h, q, runs):
        target, base = g_places[p]
        box, box_base = box_places[p]
        blk = at_q(q)

        def body(i, carry):
            at = pl.multiple_of((blk % 4) * 192 + i * 48, 16)
            total = target[base + blk // 4, pl.ds(at, 48), lanes(h)].astype(f32)
            for run in runs:
                from_at = pl.multiple_of((run % 4) * 192 + i * 48, 16)
                total = total + box[box_base + run // 4, pl.ds(from_at, 48), lanes(h)].astype(f32)
            target[base + blk // 4, pl.ds(at, 48), lanes(h)] = total.astype(bf16)
            return carry

        lax.fori_loop(0, 4, body, 0)

    def read_unit(p, i, h):
        ref, base = g_places[p]
        return ref[base + i // 16, pl.ds((i % 16) * 48, 48), lanes(h)].astype(f32)

    def read_spot(p, run, u, h):
        ref, base = box_places[p]
        return ref[base + run // 4, (run % 4) * 192 + 48 * u : (run % 4) * 192 + 48 * u + 48, lanes(h)].astype(f32)

    def write_unit(p, i, h, total):
        ref, base = g_places[p]
        ref[base + i // 16, pl.ds((i % 16) * 48, 48), lanes(h)] = total.astype(bf16)

    def pass_run(p, h, q, run, sem):
        along_y = (run < 6) == (h == 0)
        device, way = (comm.Y, 2) if along_y else (comm.X, 1)
        remote(quad(g_places[p], at_q(q), h), quad(box_places[p], run, h), rs_send.at[p, way], sem, device).start()

    def pass_unit(p, i, run, u, h, device, way, sem):
        remote(unit(g_places[p], i, h), spot(p, run, u, h), rs_send.at[p, way], sem, device).start()

    def s1(p, side):
        for h in range(2):
            q = 3 if side == 1 else 2 - h
            run_wait(p, q, h, rc_sem.at[p, h, q])
            add_in(p, h, q, (q,))
            pass_run(p, h, q, 4 + side, r1_sem.at[p, h, side])

    def s2(p):
        if REDUCE_MODE[p] == Z_FIRST:
            for h in range(2):
                q = 1 + h
                run_wait(p, q, h, rc_sem.at[p, h, q])
                run_wait(p, 5, h, r1_sem.at[p, h, 1])
                add_in(p, h, q, (q, 5))
                pass_run(p, h, q, 6, r2_sem.at[p, h])
            return
        for h in range(2):
            for j, q in enumerate((0, 1 + h)):
                run_wait(p, q, h, rc_sem.at[p, h, q])
                run_wait(p, 4 + j, h, r1_sem.at[p, h, j])
                add_in(p, h, q, (q, 4 + j))
                pass_unit(p, dev(q, 1), 6, 2 * j, h, comm.Z[1], 3, rz_sem.at[p, h, 2 * j])
                pass_unit(p, dev(q, 3), 6, 2 * j + 1, h, comm.Z[1], 3, rz_sem.at[p, h, 2 * j + 1])

    def s3(p):
        if REDUCE_MODE[p] == Z_FIRST:
            for h in range(2):
                run_wait(p, 0, h, rc_sem.at[p, h, 0])
                run_wait(p, 4, h, r1_sem.at[p, h, 0])
                run_wait(p, 6, h, r2_sem.at[p, h])
                add_in(p, h, 0, (0, 4, 6))
                pass_unit(p, dev(0, 1), 7, 0, h, comm.Z[1], 3, rz_sem.at[p, h, 0])
                pass_unit(p, dev(0, 3), 7, 1, h, comm.Z[1], 3, rz_sem.at[p, h, 1])
            return
        for h in range(2):
            for j, q in enumerate((0, 1 + h)):
                spot_wait(p, 6, 2 * j + 1, h, rz_sem.at[p, h, 2 * j + 1])
                write_unit(p, dev(q, 2), h, read_unit(p, dev(q, 2), h) + read_spot(p, 6, 2 * j + 1, h))
                pass_unit(p, dev(q, 2), 7, j, h, comm.Z[2], 3, ry_sem.at[p, h, j])

    def s4(p):
        if REDUCE_MODE[p] == Z_FIRST:
            for h in range(2):
                spot_wait(p, 7, 1, h, rz_sem.at[p, h, 1])
                write_unit(p, dev(0, 2), h, read_unit(p, dev(0, 2), h) + read_spot(p, 7, 1, h))
                pass_unit(p, dev(0, 2), 7, 2, h, comm.Z[2], 3, ry_sem.at[p, h, 0])
            return
        for h in range(2):
            q = 1 + h
            spot_wait(p, 6, 2, h, rz_sem.at[p, h, 2])
            spot_wait(p, 7, 1, h, ry_sem.at[p, h, 1])
            write_unit(p, dev(q, 0), h, read_unit(p, dev(q, 0), h) + read_spot(p, 6, 2, h) + read_spot(p, 7, 1, h))
            device, way = (comm.X, 1) if h == 0 else (comm.Y, 2)
            pass_unit(p, dev(q, 0), 7, 2, h, device, way, rf_sem.at[p, h])

    def s5(p):
        for h in range(2):
            total = read_unit(p, me, h)
            if REDUCE_MODE[p] == Z_FIRST:
                spot_wait(p, 7, 0, h, rz_sem.at[p, h, 0])
                spot_wait(p, 7, 2, h, ry_sem.at[p, h, 0])
                total = total + read_spot(p, 7, 0, h) + read_spot(p, 7, 2, h)
            else:
                spot_wait(p, 6, 0, h, rz_sem.at[p, h, 0])
                spot_wait(p, 7, 0, h, ry_sem.at[p, h, 0])
                spot_wait(p, 7, 2, h, rf_sem.at[p, h])
                total = total + read_spot(p, 6, 0, h) + read_spot(p, 7, 0, h) + read_spot(p, 7, 2, h)
            if p >= 4:
                grad_down_ref[48 * h : 48 * h + 48, half * (p - 4) : half * (p - 3)] = total
            else:
                row = jnp.concatenate([total[0:24], total[24:48]], axis=1)
                at = 0
                for c, n in PIECES[p][h]:
                    grad_rows_ref[:, c : c + n] = row[:, at : at + n]
                    at = at + n

    def sums_sent(p):
        z_first = REDUCE_MODE[p] == Z_FIRST
        for way, n in ((0, 32), (1, 12 if z_first else 9), (2, 12 if z_first else 9), (3, 6 if z_first else 12)):
            remote(bulk(n), bulk(n), rs_send.at[p, way], rc_sem.at[p, 0, 0], comm.C).wait_send()

    def vec_pack():
        vec_out[...] = jnp.zeros_like(vec_out)
        for i in range(32):
            for r, n in ((0, 128), (1, 128), (2, share_v - 256)):
                at = share_v * i + 128 * r
                vec_out[i // 4, 3 * (i % 4) + r : 3 * (i % 4) + r + 1, 0:n] = vec_grad[0:1, at : at + n]

    def vec_copy(src, dst, n, device):
        return remote(vec_out.at[src], vec_in.at[dst], vs_sem.at[n], vr_sem.at[dst], device)

    def vec_core():
        for q in range(4):
            vec_copy(at_q(q) ^ 1, q, q, comm.C).start()

    def vec_take(dst, target):
        vec_copy(target, dst, 0, comm.C).wait_recv()
        vec_out[target] = vec_out[target] + vec_in[dst]

    def vec_y():
        for q in range(4):
            vec_take(q, at_q(q))
        vec_copy(at_q(3), 5, 4, comm.Y).start()
        vec_copy(at_q(2), 4, 5, comm.Y).start()

    def vec_x():
        vec_take(5, at_q(1))
        vec_copy(at_q(1), 6, 6, comm.X).start()

    def vec_z():
        vec_take(4, b)
        vec_take(6, b)
        vec_copy(b, 8, 7, comm.Z[2]).start()

    def vec_w():
        vec_copy(b, 8, 0, comm.C).wait_recv()
        vec_in[10] = vec_out[b] + vec_in[8]
        remote(vec_in.at[10], vec_in.at[9], vs_sem.at[8], vr_sem.at[9], comm.Z[1]).start()

    def vec_end():
        vec_copy(b, 9, 0, comm.C).wait_recv()
        total = vec_in[9] + vec_in[10]
        mine = total[0:3]
        for zz in range(1, 4):
            mine = jnp.where(z == zz, total[3 * zz : 3 * zz + 3], mine)
        whole = jnp.concatenate([mine[0:1], mine[1:2], mine[2:3, 0 : share_v - 256]], axis=1)
        grad_vec_ref[...] = whole.reshape(share_v)
        for n in range(9):
            vec_copy(b, 0, n, comm.C).wait_send()

    def load(n):
        src, dst = ((rows_hbm, rows_ref), (down_hbm, down_ref), (x_hbm, x_ref))[n]
        return pltpu.make_async_copy(src, dst, local_sem.at[n])

    def start():
        for n in range(3):
            load(n).start()
        place_vectors()
        token_weights()
        comm.barrier()
        load(0).wait()

    def loaded(n):
        load(n).wait()

    def pair_gather():
        for p in range(6):
            sent(p)
        small_own(pairs, 1)
        small_z(pairs, 1)
        small_cross(pairs, 1)
        small_end(pairs, 1)

    def finish():
        for p in range(6):
            sums_sent(p)
        pltpu.make_async_copy(work, dx_hbm, local_sem.at[3]).wait()

    def vectors(n):
        (small_own, small_z, small_cross, small_end)[n](vec_all, 0)

    start()
    vectors(0)
    cast(2)
    cast(0)
    ownz(0)
    cast(3)
    loaded(2)
    transpose_into(x_ref, x_t)
    col(2, 0)
    cast(1)
    own1(1)
    vectors(1)
    ownz(1)
    col(0, 0)
    across(2, 0)
    fin(1, 0, 0)
    first(1)
    fold(0)
    vectors(2)
    ownz(2)
    col(0, 1)
    loaded(1)
    cast(5)
    cast(4)
    col(0, 2)
    own1(5)
    ownz(3)
    across(0, 2)
    vectors(3)
    fold(1, 0)
    fin(1, 2, 0)
    fin(1, 0, 1)
    fin(1, 1, 1)
    across(0, 0)
    col(0, 3)
    across(0, 1)
    col(3, 0)
    across(0, 3)
    fin(5, 0, 0)
    last(0, 1)
    fold(1, 1)
    last(0, 2)
    fold(2)
    last(0, 0)
    fin(1, 1, 0)
    last(1, 0)
    fold(3)
    ownz(5)
    col(3, 2)
    last(0, 3)
    col(3, 1)
    gathered(0)
    first(5)
    ownz(4)
    across(3, 0)
    fin(1, 3, 0)
    fin(1, 3, 1)
    fin(5, 0, 1)
    last(1, 1)
    col(2, 1)
    relayout(0)
    spread_vectors()
    fin(1, 2, 1)
    project(0, 3)
    project(3, 6)
    col(2, 2)
    col(2, 3)
    last(1, 3)
    col(3, 3)
    attend(0, 0, 2)
    last(1, 2)
    fold(5, 0)
    attend(0, 2, 4)
    across(3, 1)
    gathered(1)
    relayout(1)
    across(2, 2)
    across(2, 1)
    across(2, 3)
    own1(4)
    project(6, 9)
    across(3, 3)
    fold(5, 1)
    attend(1, 0, 4)
    fin(4, 1, 0)
    last(2, 2)
    last(2, 0)
    fin(5, 1, 1)
    fold(4, 0)
    last(3, 0)
    attn_out()
    last(2, 3)
    last(2, 1)
    fin(4, 2, 0)
    last(3, 1)
    last(5, 0)
    first(4)
    across(3, 2)
    fin(5, 1, 0)
    attn_norm()
    last(3, 3)
    fin(4, 0, 1)
    fin(5, 3, 1)
    gathered(2)
    fin(5, 3, 0)
    relayout(2)
    feed_up(0, 3)
    fin(4, 0, 0)
    last(3, 2)
    last(5, 1)
    feed_up(3, 6)
    fin(5, 2, 1)
    fold(4, 1)
    fin(4, 3, 0)
    fin(4, 1, 1)
    gathered(3)
    relayout(3)
    fin(5, 2, 0)
    last(4, 0)
    fin(4, 2, 1)
    last(5, 3)
    feed_up(6, 9)
    fin(4, 3, 1)
    feed_up(9, 12)
    last(4, 1)
    last(4, 2)
    transposes()
    last(5, 2)
    last(4, 3)
    gathered(5)
    gathered(4)
    feed_down(0)
    feed_down(1)
    down_norm()
    pool()
    pair_gather()
    contrast()
    norm_two_back()
    down_sibling()
    down_own()
    s1(4, 1)
    grad_act(0, 4)
    s1(4, 0)
    grad_act(4, 8)
    s1(5, 1)
    s1(5, 0)
    grad_act(8, 12)
    s2(4)
    grad_w_rows(2)
    s2(5)
    grad_w_rows(3)
    s1(2, 1)
    grad_y()
    norm_one_back()
    s1(3, 1)
    s3(4)
    grad_ctx()
    s1(2, 0)
    s3(5)
    attend_back(0, 0, 2)
    s2(2)
    s1(3, 0)
    attend_back(0, 2, 4)
    grad_w_rows(0)
    attend_back(1, 0, 4)
    s4(5)
    s1(0, 0)
    s3(2)
    grad_w_rows(1)
    grad_bias_in()
    vec_pack()
    vec_core()
    s1(0, 1)
    s2(3)
    s1(1, 1)
    s5(5)
    grad_x(0, 1)
    vec_y()
    s4(2)
    s2(0)
    s1(1, 0)
    s2(1)
    s3(3)
    s3(0)
    grad_x(1, 2)
    vec_x()
    s3(1)
    s4(4)
    s5(2)
    s4(0)
    s5(4)
    grad_x(2, 3)
    vec_z()
    s4(3)
    s4(1)
    vec_w()
    s5(3)
    s5(0)
    vec_end()
    s5(1)
    finish()


def fused_layer(x, tok, groups, counts, rows, down, vec):
    def big(n):
        return pltpu.VMEM((n, 768, 768), bf16)

    scratch = [
        pltpu.VMEM((512, 768), bf16),
        pltpu.VMEM((24, 6144), f32),
        pltpu.VMEM((96, 768), f32),
        big(8),
        big(4),
        big(4),
        big(4),
        big(8),
        pltpu.VMEM((3, 512, 768), bf16),
        pltpu.VMEM((24, 256, 128), bf16),
        pltpu.VMEM((512, 768), bf16),
        pltpu.VMEM((768, 512), bf16),
        pltpu.VMEM((768, 512), bf16),
        pltpu.VMEM((512, 768), bf16),
        pltpu.VMEM((768, 512), bf16),
        pltpu.VMEM((512, 3072), bf16),
        pltpu.VMEM((3072, 512), bf16),
        pltpu.VMEM((512, 3072), bf16),
        pltpu.VMEM((512, 768), f32),
        pltpu.VMEM((512, 768), f32),
        pltpu.VMEM((512, 768), f32),
        pltpu.VMEM((512, 128), f32),
        pltpu.VMEM((512, 128), f32),
        pltpu.VMEM((512, 128), f32),
        pltpu.VMEM((8, 128), f32),
        pltpu.VMEM((8, 128), f32),
        pltpu.VMEM((32, 16, 128), bf16),
        pltpu.VMEM((8, 9216), f32),
        pltpu.VMEM((8, 2304), f32),
        pltpu.VMEM((32, 16, 512), bf16),
        pltpu.VMEM((8, 768), f32),
        pltpu.VMEM((8, 768), f32),
        pltpu.VMEM((8, 128), f32),
        pltpu.VMEM((2, 256, 256), f32),
        pltpu.VMEM((8, 9216), f32),
        pltpu.VMEM((8, 16, 128), f32),
        pltpu.VMEM((12, 16, 128), f32),
    ]
    dma = pltpu.SemaphoreType.DMA
    scratch += [
        dma((4,)), dma((6, 4, 4)), dma((6, 4, 2)), dma((6, 4, 2)), dma((6, 4, 2)), dma((6,)), dma((6, 4)),
        dma((2, 16)), dma((2,)),
        dma((6, 2, 4)), dma((6, 2, 2)), dma((6, 2)), dma((6, 2, 4)), dma((6, 2, 2)), dma((6, 2)), dma((6, 4)),
        dma((12,)), dma((9,)),
    ]
    vmem = pl.BlockSpec(memory_space=pltpu.VMEM)
    smem = pl.BlockSpec(memory_space=pltpu.SMEM)
    anywhere = pl.BlockSpec(memory_space=pl.ANY)
    return pl.pallas_call(
        layer_kernel,
        out_shape=(
            jax.ShapeDtypeStruct((1, 1), f32),
            jax.ShapeDtypeStruct(x.shape, f32),
            jax.ShapeDtypeStruct(rows.shape, f32),
            jax.ShapeDtypeStruct(down.shape, f32),
            jax.ShapeDtypeStruct(vec.shape, f32),
        ),
        in_specs=[anywhere, vmem, smem, smem, anywhere, anywhere, vmem],
        out_specs=(smem, anywhere, vmem, vmem, vmem),
        scratch_shapes=scratch,
        compiler_params=pltpu.CompilerParams(collective_id=0, has_side_effects=True, vmem_limit_bytes=vmem_bytes),
    )(x, tok, groups, counts, rows, down, vec)


def adam_step(master, gradient, moment_one, moment_two, decay, rate):
    mean_new = beta_one * moment_one + (1.0 - beta_one) * gradient
    square_new = beta_two * moment_two + (1.0 - beta_two) * gradient * gradient
    mean_hat = mean_new / (1.0 - beta_one**STEP)
    square_hat = square_new / (1.0 - beta_two**STEP)
    updated = master - rate * (mean_hat / (jnp.sqrt(square_hat) + adam_epsilon) + decay * master)
    return (updated, mean_new, square_new)


def update_kernel(*refs):
    ins, outs, in_bufs, out_bufs = refs[:13], refs[13:23], refs[23:36], refs[36:45]
    in_sem, out_sem = refs[45:]
    loads = [pltpu.make_async_copy(ref, buf, in_sem.at[n]) for n, (ref, buf) in enumerate(zip(ins, in_bufs))]
    stores = [pltpu.make_async_copy(buf, ref, out_sem.at[n]) for n, (buf, ref) in enumerate(zip(in_bufs[:1] + out_bufs, outs))]
    for load in loads:
        load.start()
    loads[0].wait()
    stores[0].start()
    for group, (decay, rate) in enumerate(((decay_rate, learn_rate), (decay_rate, learn_rate), (0.0, vector_rate))):
        for load in loads[1 + 4 * group : 5 + 4 * group]:
            load.wait()
        sources = in_bufs[1 + 4 * group : 5 + 4 * group]
        targets = out_bufs[3 * group : 3 * group + 3]
        if len(sources[0].shape) == 1:
            for target, value in zip(targets, adam_step(*[ref[...] for ref in sources], decay, rate)):
                target[...] = value
        else:

            def body(n, carry, sources=sources, targets=targets, decay=decay, rate=rate):
                part = pl.ds(pl.multiple_of(n * 8, 8), 8)
                for target, value in zip(targets, adam_step(*[ref[part, :] for ref in sources], decay, rate)):
                    target[part, :] = value
                return carry

            lax.fori_loop(0, sources[0].shape[0] // 8, body, 0)
        for store in stores[1 + 3 * group : 4 + 3 * group]:
            store.start()
    for store in stores:
        store.wait()


def update(dx, rows, down, vec):
    news = [jax.ShapeDtypeStruct(dx.shape, f32)]
    for group in (rows, down, vec):
        news += [jax.ShapeDtypeStruct(group[0].shape, f32)] * 3
    anywhere = pl.BlockSpec(memory_space=pl.ANY)
    return pl.pallas_call(
        update_kernel,
        out_shape=tuple(news),
        in_specs=[anywhere] * 13,
        out_specs=(anywhere,) * 10,
        scratch_shapes=[pltpu.VMEM(a.shape, f32) for a in (dx, *rows, *down, *vec)]
        + [pltpu.VMEM(a.shape, f32) for a in news[1:]]
        + [pltpu.SemaphoreType.DMA((13,)), pltpu.SemaphoreType.DMA((10,))],
        compiler_params=pltpu.CompilerParams(vmem_limit_bytes=vmem_bytes),
    )(dx, *rows, *down, *vec)


def on_device_fused(
    embeds, token_mask, groups, counts,
    rows_master, rows_mean, rows_square, down_master, down_mean, down_square,
    vector_master, vector_mean, vector_square,
):
    x = embeds.reshape(-1, embeds.shape[-1])
    loss, dx, rows_grad, down_grad, vec_grad = fused_layer(x, token_mask, groups, counts, rows_master, down_master, vector_master)
    dx, *new = update(
        dx,
        (rows_master, rows_grad, rows_mean, rows_square),
        (down_master, down_grad, down_mean, down_square),
        (vector_master, vec_grad, vector_mean, vector_square),
    )
    return (loss[0, 0], dx.reshape(embeds.shape), *new)


def layer_norm(values, scale_vec, shift_vec):
    centre = values - jnp.mean(values, axis=-1, keepdims=True)
    spread = jnp.mean(centre * centre, axis=-1, keepdims=True)
    return centre * lax.rsqrt(spread + norm_epsilon) * scale_vec + shift_vec


def pool_unit(weights, output):
    summed = jnp.sum(output * weights[:, :, None], axis=1) / jnp.sum(weights, axis=1, keepdims=True)
    return summed * lax.rsqrt(jnp.sum(summed * summed, axis=1, keepdims=True) + unit_epsilon)


def exact_gelu(values):
    return jax.nn.gelu(values, approximate=False)


def softmax_last(values):
    return jax.nn.softmax(values, axis=-1)


def split_vectors(vectors, model_width, hidden):
    extents = [model_width] * 5 + [hidden] + [model_width] * 3
    pieces_out = []
    offset = 0
    for extent in extents:
        pieces_out.append(vectors[offset : offset + extent])
        offset = offset + extent
    return pieces_out


def pair_exps(left_rows, right_rows, left_group, right_group, left_start, right_start):
    scores = score_scale * jnp.dot(left_rows, right_rows.T, precision=highest)
    left_index = left_start + jnp.arange(left_rows.shape[0])
    right_index = right_start + jnp.arange(right_rows.shape[0])
    diagonal = left_index[:, None] == right_index[None, :]
    scores = scores - score_scale * margin * diagonal.astype(jnp.float32)
    same = (left_group[:, None] == right_group[None, :]) & (left_group[:, None] >= 0.0)
    return (jnp.where(same, jnp.exp(scores), 0.0), (diagonal & same).astype(jnp.float32))


def add_sums(own_data, arrived, offset):
    sources, targets, group_own, own_start = own_data
    other_src, other_tgt, other_group = arrived
    row_exp, unused_row = pair_exps(sources, other_tgt, group_own, other_group, own_start, offset)
    col_exp, unused_col = pair_exps(other_src, targets, other_group, group_own, offset, own_start)
    return (jnp.sum(row_exp, axis=1), jnp.sum(col_exp, axis=0))


def add_grads(own_data, loss_coef, arrived, offset):
    sources, targets, group_own, own_start, row_own, col_own = own_data
    other_src, other_tgt, other_group, other_row, other_col = arrived
    row_exp, row_diag = pair_exps(sources, other_tgt, group_own, other_group, own_start, offset)
    row_coef = (
        row_exp / row_own[:, None] + row_exp / other_col[None, :] - 2.0 * row_diag
    ) * loss_coef
    col_exp, col_diag = pair_exps(other_src, targets, other_group, group_own, offset, own_start)
    col_coef = (
        col_exp / other_row[:, None] + col_exp / col_own[None, :] - 2.0 * col_diag
    ) * loss_coef
    grad_src = score_scale * jnp.dot(row_coef, other_tgt, precision=highest)
    grad_tgt = score_scale * jnp.dot(col_coef.T, other_src, precision=highest)
    return (grad_src, grad_tgt)


def on_device_general(
    embeds,
    token_mask,
    groups,
    counts,
    rows_master,
    rows_mean,
    rows_square,
    down_master,
    down_mean,
    down_square,
    vector_master,
    vector_mean,
    vector_square,
):
    slot_count = embeds.shape[0]
    length = embeds.shape[2]
    model_width = embeds.shape[3]
    row_all, down_all, vector_all = (
        lax.all_gather(rows_master.astype(jnp.bfloat16), ("blk", "dp"), axis=0, tiled=True),
        lax.all_gather(down_master.astype(jnp.bfloat16), ("blk", "dp"), axis=0, tiled=True),
        lax.all_gather(vector_master.astype(jnp.bfloat16), ("blk", "dp"), axis=0, tiled=True),
    )
    hidden = down_all.shape[0]
    vectors = vector_all.astype(jnp.float32)
    bias_q, bias_v, bias_o, gain_one, shift_one, bias_up, bias_down, gain_two, shift_two = (
        split_vectors(vectors, model_width, hidden)
    )
    w_attn_in = row_all[:, : 3 * model_width]
    w_attn_out = row_all[:, 3 * model_width : 4 * model_width]
    w_up = row_all[:, 4 * model_width :]
    seq_count = 2 * slot_count
    tokens = seq_count * length
    head_count = model_width // HEAD
    inputs = embeds.reshape(tokens, model_width)
    weights = token_mask.reshape(seq_count, length).astype(jnp.float32)
    key_valid = token_mask.reshape(seq_count, length) > 0
    joined = jnp.concatenate([bias_q, jnp.zeros_like(bias_q), bias_v])
    projected = (jnp.dot(inputs, w_attn_in, preferred_element_type=jnp.float32) + joined).astype(
        jnp.bfloat16
    )
    queries = projected[:, :model_width].reshape(seq_count, length, head_count, HEAD)
    key_part = projected[:, model_width : 2 * model_width].reshape(
        seq_count, length, head_count, HEAD
    )
    values = projected[:, 2 * model_width :].reshape(seq_count, length, head_count, HEAD)
    scores = jnp.einsum(
        "nihe,njhe->nhij", queries, key_part, preferred_element_type=jnp.float32
    ) * HEAD ** (-0.5)
    scores = jnp.where(key_valid[:, None, None, :], scores, -1e30)
    attention, soft_back = jax.vjp(softmax_last, scores)
    attention_low = attention.astype(jnp.bfloat16)
    context = (
        jnp.einsum("nhij,njhe->nihe", attention_low, values, preferred_element_type=jnp.float32)
        .astype(jnp.bfloat16)
        .reshape(tokens, model_width)
    )
    resid_one = (
        inputs.astype(jnp.float32)
        + jnp.dot(context, w_attn_out, preferred_element_type=jnp.float32)
        + bias_o
    )
    normed_full, norm_one_back = jax.vjp(layer_norm, resid_one, 1.0 + gain_one, shift_one)
    normed_one = normed_full.astype(jnp.bfloat16)
    up_pre = jnp.dot(normed_one, w_up, preferred_element_type=jnp.float32) + bias_up
    activated_full, gelu_back = jax.vjp(exact_gelu, up_pre)
    activated = activated_full.astype(jnp.bfloat16)
    resid_two = (
        normed_one.astype(jnp.float32)
        + jnp.dot(activated, down_all, preferred_element_type=jnp.float32)
        + bias_down
    )
    output, norm_two_back = jax.vjp(layer_norm, resid_two, 1.0 + gain_two, shift_two)
    pooled, pool_back = jax.vjp(
        partial(pool_unit, weights), output.reshape(seq_count, length, model_width)
    )
    pooled = pooled.reshape(slot_count, 2, model_width)
    sources = pooled[:, 0]
    targets = pooled[:, 1]
    own_start = lax.axis_index(("blk", "dp")) * slot_count
    valid_slot = jnp.arange(slot_count) < counts[0]
    group_own = jnp.where(valid_slot, groups, -1).astype(jnp.float32)
    pair_total = lax.psum(counts[0].astype(jnp.float32), ("blk", "dp"))
    loss_coef = 0.5 / pair_total
    own_sums = (sources, targets, group_own, own_start)
    row_sum, col_sum = add_sums(
        own_sums,
        (
            lax.all_gather(sources, ("blk", "dp"), axis=0, tiled=True),
            lax.all_gather(targets, ("blk", "dp"), axis=0, tiled=True),
            lax.all_gather(group_own, ("blk", "dp"), axis=0, tiled=True),
        ),
        jnp.int32(0),
    )
    row_safe = jnp.where(valid_slot, row_sum, 1.0)
    col_safe = jnp.where(valid_slot, col_sum, 1.0)
    own_grads = (sources, targets, group_own, own_start, row_safe, col_safe)
    grad_src, grad_tgt = add_grads(
        own_grads,
        loss_coef,
        (
            lax.all_gather(sources, ("blk", "dp"), axis=0, tiled=True),
            lax.all_gather(targets, ("blk", "dp"), axis=0, tiled=True),
            lax.all_gather(group_own, ("blk", "dp"), axis=0, tiled=True),
            lax.all_gather(row_safe, ("blk", "dp"), axis=0, tiled=True),
            lax.all_gather(col_safe, ("blk", "dp"), axis=0, tiled=True),
        ),
        jnp.int32(0),
    )
    positive = score_scale * jnp.sum(sources * targets, axis=1) - score_scale * margin
    loss_terms = jnp.sum(
        jnp.where(valid_slot, jnp.log(row_safe) + jnp.log(col_safe) - 2.0 * positive, 0.0)
    )
    pair_loss = lax.psum(loss_terms, ("blk", "dp")) * loss_coef
    grad_pooled = jnp.stack([grad_src, grad_tgt], axis=1).reshape(seq_count, model_width)
    grad_output = pool_back(grad_pooled)[0].reshape(tokens, model_width)
    grad_resid_two, grad_gain_two, grad_shift_two = norm_two_back(grad_output)
    grad_down_low = grad_resid_two.astype(jnp.bfloat16)
    grad_w_down = jnp.einsum(
        "tf,td->fd", activated, grad_down_low, preferred_element_type=jnp.float32
    )
    grad_bias_down = jnp.sum(grad_down_low.astype(jnp.float32), axis=0)
    grad_act = jnp.einsum("td,fd->tf", grad_down_low, down_all, preferred_element_type=jnp.float32)
    grad_up = gelu_back(grad_act)[0].astype(jnp.bfloat16)
    grad_w_up = jnp.einsum("td,tf->df", normed_one, grad_up, preferred_element_type=jnp.float32)
    grad_bias_up = jnp.sum(grad_up.astype(jnp.float32), axis=0)
    grad_normed = grad_resid_two + jnp.einsum(
        "tf,df->td", grad_up, w_up, preferred_element_type=jnp.float32
    )
    grad_resid_one, grad_gain_one, grad_shift_one = norm_one_back(grad_normed)
    grad_attn_low = grad_resid_one.astype(jnp.bfloat16)
    grad_w_out = jnp.einsum("td,te->de", context, grad_attn_low, preferred_element_type=jnp.float32)
    grad_bias_out = jnp.sum(grad_attn_low.astype(jnp.float32), axis=0)
    grad_context = jnp.einsum(
        "te,de->td", grad_attn_low, w_attn_out, preferred_element_type=jnp.float32
    ).astype(jnp.bfloat16)
    grad_context = grad_context.reshape(seq_count, length, head_count, HEAD)
    grad_attention = jnp.einsum(
        "nihe,njhe->nhij", grad_context, values, preferred_element_type=jnp.float32
    )
    grad_values = jnp.einsum(
        "nhij,nihe->njhe", attention_low, grad_context, preferred_element_type=jnp.float32
    )
    grad_scores = soft_back(grad_attention)[0].astype(jnp.bfloat16)
    grad_queries = jnp.einsum(
        "nhij,njhe->nihe", grad_scores, key_part, preferred_element_type=jnp.float32
    ) * HEAD ** (-0.5)
    grad_keys = jnp.einsum(
        "nhij,nihe->njhe", grad_scores, queries, preferred_element_type=jnp.float32
    ) * HEAD ** (-0.5)
    grad_projected = jnp.concatenate(
        [
            grad_queries.reshape(tokens, model_width),
            grad_keys.reshape(tokens, model_width),
            grad_values.reshape(tokens, model_width),
        ],
        axis=1,
    ).astype(jnp.bfloat16)
    grad_w_in = jnp.einsum("td,te->de", inputs, grad_projected, preferred_element_type=jnp.float32)
    grad_bias_q = jnp.sum(grad_projected[:, :model_width].astype(jnp.float32), axis=0)
    grad_bias_v = jnp.sum(grad_projected[:, 2 * model_width :].astype(jnp.float32), axis=0)
    grad_inputs = grad_resid_one + jnp.einsum(
        "te,de->td", grad_projected, w_attn_in, preferred_element_type=jnp.float32
    )
    grad_vector = jnp.concatenate(
        [
            grad_bias_q,
            grad_bias_v,
            grad_bias_out,
            grad_gain_one,
            grad_shift_one,
            grad_bias_up,
            grad_bias_down,
            grad_gain_two,
            grad_shift_two,
        ]
    )
    rows_share, down_share, vector_share = (
        lax.psum_scatter(
            jnp.concatenate([grad_w_in, grad_w_out, grad_w_up], axis=1),
            ("blk", "dp"),
            scatter_dimension=0,
            tiled=True,
        ),
        lax.psum_scatter(grad_w_down, ("blk", "dp"), scatter_dimension=0, tiled=True),
        lax.psum_scatter(grad_vector, ("blk", "dp"), scatter_dimension=0, tiled=True),
    )
    rows_new = adam_step(rows_master, rows_share, rows_mean, rows_square, decay_rate, learn_rate)
    down_new = adam_step(down_master, down_share, down_mean, down_square, decay_rate, learn_rate)
    vector_new = adam_step(
        vector_master, vector_share, vector_mean, vector_square, 0.0, vector_rate
    )
    embeds_grad = grad_inputs.reshape(slot_count, 2, length, model_width)
    return (
        pair_loss,
        embeds_grad,
        rows_new[0],
        rows_new[1],
        rows_new[2],
        down_new[0],
        down_new[1],
        down_new[2],
        vector_new[0],
        vector_new[1],
        vector_new[2],
    )


def solution(mesh):
    in_specs = (
        P(("blk", "dp"), None, None, None),
        P(("blk", "dp"), None, None),
        P(("blk", "dp")),
        P(("blk", "dp")),
        P(("blk", "dp"), None),
        P(("blk", "dp"), None),
        P(("blk", "dp"), None),
        P(("blk", "dp"), None),
        P(("blk", "dp"), None),
        P(("blk", "dp"), None),
        P(("blk", "dp")),
        P(("blk", "dp")),
        P(("blk", "dp")),
    )
    out_specs = (
        P(),
        P(("blk", "dp"), None, None, None),
        P(("blk", "dp"), None),
        P(("blk", "dp"), None),
        P(("blk", "dp"), None),
        P(("blk", "dp"), None),
        P(("blk", "dp"), None),
        P(("blk", "dp"), None),
        P(("blk", "dp")),
        P(("blk", "dp")),
        P(("blk", "dp")),
    )
    fits = dict(mesh.shape) == {"blk": 8, "dp": 4}
    return jax.shard_map(
        on_device_fused if fits else on_device_general, mesh=mesh, in_specs=in_specs, out_specs=out_specs, check_vma=False
    )
```

```python
from functools import partial

import jax
import jax.numpy as jnp
from jax import lax
from jax.experimental import pallas as pl
from jax.experimental.pallas import tpu as pltpu
from jax.sharding import PartitionSpec as P

HEAD = 64
STEP = 10


score_scale = 32.0
margin = 0.3
beta_one = 0.9
beta_two = 0.999
learn_rate = 0.03
vector_rate = 0.06
decay_rate = 0.01
adam_epsilon = 1e-08
norm_epsilon = 1e-12
unit_epsilon = 1e-06
highest = lax.Precision.HIGHEST

vmem_bytes = 64 * 1024 * 1024 - 65536

f32 = jnp.float32
bf16 = jnp.bfloat16


def dot_nn(a, b, precision=None):
    return lax.dot_general(a, b, (((1,), (0,)), ((), ())), precision=precision, preferred_element_type=f32)


def dot_nt(a, b, precision=None):
    return lax.dot_general(a, b, (((1,), (1,)), ((), ())), precision=precision, preferred_element_type=f32)


def dot_tn(a, b):
    return lax.dot_general(a, b, (((0,), (0,)), ((), ())), preferred_element_type=f32)


Z_FIRST, Z_MID = 0, 1
GATHER_MODE = (Z_FIRST, Z_FIRST, Z_MID, Z_FIRST, Z_MID, Z_FIRST)
REDUCE_MODE = (Z_FIRST, Z_FIRST, Z_FIRST, Z_MID, Z_MID, Z_MID)

PIECES = (
    (((0, 512), (768, 256)), ((1024, 256), (1536, 512))),
    (((512, 256), (1280, 256), (2048, 256)), ((2304, 768),)),
    (((3072, 768),), ((3840, 768),)),
    (((4608, 768),), ((5376, 768),)),
)


class Comm:
    def __init__(self, depth):
        self.depth = depth
        self.b = lax.axis_index("blk")
        self.z = lax.axis_index("dp")
        b, z = self.b, self.z
        self.X, self.Y, self.C, self.D = (b ^ 2, z), (b ^ 4, z), (b ^ 1, z), (b ^ 6, z)
        self.Z = [(b, z ^ k) for k in range(depth)]
        self.up, self.down = (b, z + 1), (b, z - 1)

    def barrier(self):
        sem = pltpu.get_barrier_semaphore()
        friends = [self.X, self.Y, self.C] + self.Z[1:3]
        for friend in friends:
            pl.semaphore_signal(sem, inc=1, device_id=friend, device_id_type=pl.DeviceIdType.MESH)
        pl.semaphore_wait(sem, len(friends))


def remote(src, dst, send_sem, recv_sem, device):
    return pltpu.make_async_remote_copy(
        src_ref=src,
        dst_ref=dst,
        send_sem=send_sem,
        recv_sem=recv_sem,
        device_id=device,
        device_id_type=pl.DeviceIdType.MESH,
    )


def layer_kernel(
    x_hbm, tok_ref, group_ref, count_ref, rows_hbm, down_hbm, vec_ref,
    loss_ref, dx_hbm, grad_rows_ref, grad_down_ref, grad_vec_ref,
    x_ref, rows_ref, down_ref,
    raw, w_attn, w_up, w_down, g_rest,
    qkv, probs, ctx, ctx_t, x_t, y_low, y_t, act, act_t, slope, xhat1, xhat2, work,
    rstd1, rstd2, tok_w, tok_f, tags, vec_all, vec_row, bias_in, pairs, pooled_hat, own_unit, unit_rs, pair_k, vec_grad, vec_out, vec_in,
    local_sem, zsem, xsem, ysem, dsem, csem, ssem,
    small_recv, small_send,
    rc_sem, r1_sem, r2_sem, rz_sem, ry_sem, rf_sem, rs_send,
    vr_sem, vs_sem,
):
    comm = Comm(4)
    b, z = comm.b, comm.z
    me = b * 4 + z
    width = 768
    half = 384
    def at_q(q):
        return b ^ (2 * q)

    def lanes(h):
        return pl.ds(half * h, half)

    def unit(place, i, h):
        ref, base = place
        return ref.at[base + i // 16, pl.ds((i % 16) * 48, 48), lanes(h)]

    def quad(place, n, h):
        ref, base = place
        return ref.at[base + n // 4, pl.ds((n % 4) * 192, 192), lanes(h)]

    def share(p, i, h):
        if p < 4:
            return unit((raw, 2 * p), i, h)
        return w_down.at[i // 8, pl.ds((i % 8) * 96 + 48 * h, 48), lanes(p - 4)]

    def bulk(n):
        return raw.at[0] if n == 32 else raw.at[0, pl.ds(0, 48 * n), pl.ds(0, half)]

    def send(p, i, h, device, way, rsem):
        ref = share(p, i, h)
        remote(ref, ref, ssem.at[p, way], rsem, device).start()

    def arrived(p, i, h, rsem):
        ref = share(p, i, h)
        remote(ref, ref, ssem.at[p, 0], rsem, comm.X).wait_recv()

    def to_core(p, i, h):
        send(p, i, h, comm.C, 2, csem.at[p])

    def both_to_core(p, i):
        if p < 4:
            ref = raw.at[2 * p + i // 16, pl.ds((i % 16) * 48, 48), :]
        else:
            ref = w_down.at[i // 8, pl.ds((i % 8) * 96, 96), lanes(p - 4)]
        remote(ref, ref, ssem.at[p, 2], csem.at[p], comm.C).start()

    def dev(q, k):
        return at_q(q) * 4 + (z ^ k)

    def cast(p):
        for h in range(2):
            if p < 4:
                row = jnp.concatenate([rows_ref[:, c : c + n] for c, n in PIECES[p][h]], axis=1)
                both = jnp.concatenate([row[:, :half], row[:, half:]], axis=0)
            else:
                both = down_ref[48 * h : 48 * h + 48, half * (p - 4) : half * (p - 3)]
            if p < 4:
                raw[2 * p + me // 16, pl.ds((me % 16) * 48, 48), lanes(h)] = both.astype(bf16)
            else:
                w_down[me // 8, pl.ds((me % 8) * 96 + 48 * h, 48), lanes(p - 4)] = both.astype(bf16)

    def along_z(p, q, k, j, h):
        i = dev(q, k)
        if k == 0:
            send(p, i, h, comm.Z[2], 3, zsem.at[p, 2, 2 * j + h])
            send(p, i, h, comm.Z[1], 3, zsem.at[p, 1, 2 * j + h])
        else:
            send(p, i, h, comm.Z[1], 3, zsem.at[p, 3, 2 * j + h])

    def place(j, h):
        return 0 if j == 0 else (1 if h == 0 else 2)

    def ownz(p):
        for h in range(2):
            along_z(p, 0, 0, 0, h)

    def own1(p):
        send(p, dev(0, 0), 0, comm.X, 0, dsem.at[p, 0, 0])
        send(p, dev(0, 0), 1, comm.Y, 1, dsem.at[p, 0, 1])

    def first(p):
        for h in range(2):
            q = place(1, h)
            arrived(p, dev(q, 0), h, dsem.at[p, 0, h])
            along_z(p, q, 0, 1, h)

    def fold(p, j=0):
        for h in range(2):
            q = place(j, h)
            arrived(p, dev(q, 2), h, zsem.at[p, 2, 2 * j + h])
            along_z(p, q, 2, j, h)

    def z_wait(p, k, j):
        if k in (1, 3):
            for h in range(2):
                arrived(p, dev(place(j, h), k), h, zsem.at[p, k, 2 * j + h])

    def col(p, k):
        z_wait(p, k, 0)
        i = dev(0, k)
        send(p, i, 0, comm.X, 0, xsem.at[p, k, 0])
        send(p, i, 1, comm.Y, 1, ysem.at[p, k, 1])
        send(p, i, 1, comm.X, 0, xsem.at[p, k, 1])
        send(p, i, 0, comm.Y, 1, ysem.at[p, k, 0])
        both_to_core(p, i)

    def across(p, k):
        i = dev(1, k)
        arrived(p, i, 0, xsem.at[p, k, 0])
        send(p, i, 0, comm.Y, 1, dsem.at[p, k, 0])
        to_core(p, i, 0)
        i = dev(2, k)
        arrived(p, i, 1, ysem.at[p, k, 1])
        send(p, i, 1, comm.X, 0, dsem.at[p, k, 1])
        to_core(p, i, 1)

    def fin(p, k, j):
        z_wait(p, k, j)
        i = dev(place(j, 0), k)
        send(p, i, 0, comm.Y, 1, ysem.at[p, k, j])
        to_core(p, i, 0)
        i = dev(place(j, 1), k)
        send(p, i, 1, comm.X, 0, xsem.at[p, k, j])
        to_core(p, i, 1)

    def last(p, k):
        if GATHER_MODE[p] == Z_FIRST:
            rest = ((1, 1, xsem.at[p, k, 1]), (2, 0, ysem.at[p, k, 0]), (3, 0, dsem.at[p, k, 0]), (3, 1, dsem.at[p, k, 1]))
        else:
            rest = ((2, 0, ysem.at[p, k, 0]), (1, 1, xsem.at[p, k, 0]), (3, 0, ysem.at[p, k, 1]), (3, 1, xsem.at[p, k, 1]))
        for q, h, sem in rest:
            arrived(p, dev(q, k), h, sem)
            if q < 3:
                to_core(p, dev(q, k), h)
        both_to_core(p, dev(3, k))

    def gathered(p):
        remote(bulk(32), bulk(32), ssem.at[p, 0], csem.at[p], comm.X).wait_recv()

    def sent(p):
        z_first = GATHER_MODE[p] == Z_FIRST
        for way, n in ((0, 12 if z_first else 9), (1, 12 if z_first else 9), (2, 32), (3, 6 if z_first else 12)):
            remote(bulk(n), bulk(n), ssem.at[p, way], csem.at[p], comm.X).wait_send()

    def small_send_one(ref, n, i, device, rsem):
        block = ref.at[pl.ds(i, 1)]
        remote(block, block, small_send.at[n], rsem, device).start()

    def small_wait(ref, n, i, rsem):
        block = ref.at[pl.ds(i, 1)]
        remote(block, block, small_send.at[n], rsem, comm.X).wait_recv()

    def small_plane(ref, n, k):
        i = dev(0, k)
        small_send_one(ref, n, i, comm.D, small_recv.at[n, 12 + k])
        small_send_one(ref, n, i, comm.X, small_recv.at[n, 4 + k])
        small_send_one(ref, n, i, comm.Y, small_recv.at[n, 8 + k])
        small_send_one(ref, n, i, comm.C, small_recv.at[n, 0])

    def small_own(ref, n):
        for k in (3, 2, 1):
            small_send_one(ref, n, me, comm.Z[k], small_recv.at[n, k])
        small_plane(ref, n, 0)

    def small_z(ref, n):
        for k in (1, 2, 3):
            small_wait(ref, n, dev(0, k), small_recv.at[n, k])
            small_plane(ref, n, k)

    def small_cross(ref, n):
        for k in range(4):
            for q in (1, 2, 3):
                small_wait(ref, n, dev(q, k), small_recv.at[n, 4 * q + k])
                small_send_one(ref, n, dev(q, k), comm.C, small_recv.at[n, 0])

    def small_end(ref, n):
        many = ref.at[pl.ds(0, 16)]
        remote(many, many, small_send.at[n], small_recv.at[n, 0], comm.X).wait_recv()
        many = ref.at[pl.ds(0, 31)]
        remote(many, many, small_send.at[n], small_recv.at[n, 0], comm.X).wait_send()

    def vec(offset, size=width):
        return vec_row[0:1, offset : offset + size]

    bias_q, bias_v, bias_o, gain1_at, shift1_at, bias_up_at = 0, width, 2 * width, 3 * width, 4 * width, 5 * width
    bias_down_at, gain2_at, shift2_at = 9 * width, 10 * width, 11 * width

    share_v = 288

    def place_vectors():
        v = vec_ref[...].reshape(1, share_v)
        tail = jnp.concatenate([v[:, 256:share_v], jnp.zeros((1, 384 - share_v), f32)], axis=1)
        tile = jnp.concatenate([v[:, 0:128], v[:, 128:256], tail, jnp.zeros((13, 128), f32)], axis=0)
        vec_all[pl.ds(me, 1)] = tile.astype(bf16).reshape(1, 16, 128)

    def spread_vectors():
        for i in range(32):
            tile = vec_all[i].astype(f32)
            for r, n in ((0, 128), (1, 128), (2, share_v - 256)):
                at = share_v * i + 128 * r
                vec_row[0:1, at : at + n] = tile[r : r + 1, 0:n]
        bias_in[...] = jnp.zeros_like(bias_in)
        bias_in[0:1, 0:512] = vec(bias_q, 512)
        bias_in[0:1, 1024:1536] = vec(bias_v, 512)
        bias_in[0:1, 1536:1792] = vec(bias_q + 512, 256)
        bias_in[0:1, 2048:2304] = vec(bias_v + 512, 256)

    def relayout(p):
        target, chunk = (w_attn, 2 * p) if p < 2 else (w_up, 2 * p - 4)

        def body(j, carry):
            for h in range(2):
                even = raw[2 * p + j // 8, pl.ds((j % 8) * 96, 48), lanes(h)].astype(f32)
                odd = raw[2 * p + j // 8, pl.ds((j % 8) * 96 + 48, 48), lanes(h)].astype(f32)
                for q in range(2):
                    rows = jnp.concatenate([even[24 * q : 24 * q + 24], odd[24 * q : 24 * q + 24]], axis=0)
                    target[chunk + h, pl.ds(j * 48, 48), lanes(q)] = rows.astype(bf16)
            return carry

        lax.fori_loop(0, 16, body, 0)

    def transpose_into(source, target, lo=0, hi=3):
        def body(j, carry):
            at = pl.multiple_of(j * 256, 256)
            target[pl.ds(at, 256), :] = jnp.transpose(source[:, pl.ds(at, 256)])
            return carry

        lax.fori_loop(lo, hi, body, 0)

    def token_weights():
        lane = lax.broadcasted_iota(jnp.int32, (1, 128), 1)
        left = (lane < 64).astype(f32)
        tok = tok_ref[...].astype(f32)
        tok_f[0:4, :] = jnp.concatenate([tok[:, 0, :], tok[:, 1, :]], axis=1)
        for p in range(4):
            m = tok_f[p : p + 1, :]
            n0 = jnp.sum(m * left, axis=1, keepdims=True)
            n1 = jnp.sum(m * (1.0 - left), axis=1, keepdims=True)
            w = m / (left * n0 + (1.0 - left) * n1)
            tok_w[128 * p : 128 * p + 128, :] = jnp.transpose(jnp.broadcast_to(w, (128, 128)))
        row = lax.broadcasted_iota(jnp.int32, (8, 128), 0) % 4
        tag = jnp.full((8, 128), -1.0, f32)
        for s in range(4):
            tag = jnp.where((row == s) & (count_ref[0] > s), group_ref[s].astype(f32), tag)
        tags[...] = tag

    def project(lo, hi):
        def body(t, carry):
            c, n = t // 3, t % 3
            at = pl.multiple_of(n * 256, 256)
            bias = bias_in[0:1, pl.ds(pl.multiple_of(t * 256, 256), 256)]
            out = dot_nn(x_ref[...], w_attn[c, :, pl.ds(at, 256)]) + bias
            qkv[c, :, pl.ds(at, 256)] = out.astype(bf16)
            return carry

        lax.fori_loop(lo, hi, body, 0)

    def head_places(hp):
        if hp < 4:
            key = (0, 512 + 128 * hp) if hp < 2 else (1, 128 * hp - 256)
            return (0, 128 * hp), key, (1, 256 + 128 * hp)
        return (2, 128 * hp - 512), (2, 128 * hp - 256), (2, 128 * hp)

    lane128 = lax.broadcasted_iota(jnp.int32, (128, 128), 1)
    row128 = lax.broadcasted_iota(jnp.int32, (128, 128), 0)
    even_half = lane128 < 64

    def split_heads(v):
        zero = jnp.zeros_like(v)
        return jnp.concatenate([jnp.where(even_half, v, zero), jnp.where(even_half, zero, v)], axis=0)

    def attend(group, lo, hi):
        def body(p, carry):
            rows = pl.ds(pl.multiple_of(p * 128, 128), 128)
            m = tok_f[pl.ds(p, 1), :]
            same = (row128 < 64) == (lane128 < 64)
            open_one = same & (jnp.broadcast_to(m, (128, 128)) > 0.0)
            block = jnp.where(open_one, 0.0, -1e30)
            block = jnp.concatenate([block, block], axis=0)
            for hp in range(4) if group == 0 else range(4, 6):
                q2, k2, v2 = [qkv[c, rows, at : at + 128] for c, at in head_places(hp)]
                s = dot_nt(split_heads(q2), k2) * HEAD ** (-0.5) + block
                e = jnp.exp(s - jnp.max(s, axis=1, keepdims=True))
                a = (e * (1.0 / jnp.sum(e, axis=1, keepdims=True))).astype(bf16)
                probs[p * 6 + hp] = a
                wide = jnp.concatenate([a[:128], a[128:]], axis=1)
                ctx[rows, 128 * hp : 128 * hp + 128] = dot_nn(wide, split_heads(v2)).astype(bf16)
            return carry

        lax.fori_loop(lo, hi, body, 0, unroll=1 + group)

    def norm_rows(i, source_fn, hat, rstd, emit):
        rows = pl.ds(pl.multiple_of(i * 64, 64), 64)
        h = source_fn(rows)
        centre = h - jnp.mean(h, axis=1, keepdims=True)
        r = lax.rsqrt(jnp.mean(centre * centre, axis=1, keepdims=True) + norm_epsilon)
        xh = centre * r
        hat[rows, :] = xh
        rstd[rows, :] = jnp.broadcast_to(r, (64, 128))
        if emit is not None:
            emit(rows, xh)

    def attn_out():
        def body(n, carry):
            at = pl.multiple_of(n * 256, 256)
            work[:, pl.ds(at, 256)] = dot_nn(ctx[...], w_attn[3, :, pl.ds(at, 256)])
            return carry

        lax.fori_loop(0, 3, body, 0)

    def attn_norm():
        def source(rows):
            return x_ref[rows, :].astype(f32) + work[rows, :] + vec(bias_o)

        def emit(rows, xh):
            y_low[rows, :] = (xh * (1.0 + vec(gain1_at)) + vec(shift1_at)).astype(bf16)

        def norm(i, carry):
            norm_rows(i, source, xhat1, rstd1, emit)
            return carry

        lax.fori_loop(0, 8, norm, 0, unroll=2)

    def feed_up(lo, hi):
        def body(t, carry):
            c, n = t // 3, t % 3
            at = pl.multiple_of(n * 256, 256)
            to = pl.multiple_of(t * 256, 256)
            work[:, pl.ds(0, 256)] = dot_nn(y_low[...], w_up[c, :, pl.ds(at, 256)])
            bias = vec_row[0:1, pl.ds(pl.multiple_of(bias_up_at + to, 256), 256)]

            def rows_of(i, inner):
                rows = pl.ds(pl.multiple_of(i * 32, 32), 32)
                v = work[rows, 0:256] + bias
                cdf = 0.5 * (1.0 + lax.erf(v * 0.7071067811865476))
                dens = jnp.exp(v * v * -0.5) * 0.3989422804014327
                act[rows, pl.ds(to, 256)] = (v * cdf).astype(bf16)
                slope[rows, pl.ds(to, 256)] = (cdf + v * dens).astype(bf16)
                return inner

            lax.fori_loop(0, 16, rows_of, 0, unroll=4)
            return carry

        lax.fori_loop(lo, hi, body, 0)

    def feed_down(s):
        def body(n, carry):
            at = pl.multiple_of(n * 256, 256)
            total = dot_nn(act[:, 0:width], w_down[0, :, pl.ds(at, 256)])
            for c in range(1, 4):
                total = total + dot_nn(act[:, c * width : (c + 1) * width], w_down[c, :, pl.ds(at, 256)])
            work[:, pl.ds(at, 256)] = total
            return carry

        lax.fori_loop(s, 2 * s + 1, body, 0)

    def down_norm():
        def source(rows):
            return y_low[rows, :].astype(f32) + work[rows, :] + vec(bias_down_at)

        def norm(i, carry):
            norm_rows(i, source, xhat2, rstd2, None)
            rows = pl.ds(pl.multiple_of(i * 64, 64), 64)
            got = jnp.sum(xhat2[rows, :] * tok_w[rows, 0:1], axis=0, keepdims=True)
            at = i // 2 + 4 * (i % 2)
            pooled_hat[pl.ds(at, 1), :] = got
            return carry

        lax.fori_loop(0, 8, norm, 0, unroll=2)

    def pool():
        e = pooled_hat[...] * (1.0 + vec(gain2_at)) + vec(shift2_at)
        r = lax.rsqrt(jnp.sum(e * e, axis=1, keepdims=True) + unit_epsilon)
        unit_rs[...] = jnp.broadcast_to(r, (8, 128))
        n = e * r
        own_unit[...] = n
        packed = jnp.concatenate([n[:, :half], n[:, half:]], axis=0)
        tag = jnp.concatenate([tags[...], tags[...]], axis=0)
        pairs[pl.ds(me, 1)] = jnp.concatenate([packed, tag], axis=1).astype(bf16).reshape(1, 16, 512)

    def contrast():
        total = 256
        every = pairs[...].astype(f32)
        left = every[:, 0:8, 0:half].reshape(total, half).astype(bf16)
        right = every[:, 8:16, 0:half].reshape(total, half).astype(bf16)
        tag = every[:, 0:8, half : half + 128].reshape(total, 128)
        tag_row = jnp.concatenate([jnp.transpose(tag[0:128])[0:1], jnp.transpose(tag[128:256])[0:1]], axis=1)
        s = (dot_nt(left, left) + dot_nt(right, right)) * score_scale
        i = lax.broadcasted_iota(jnp.int32, (total, total), 0)
        j = lax.broadcasted_iota(jnp.int32, (total, total), 1)
        opposite = (i & 4) != (j & 4)
        diagonal = (i ^ j) == 4
        s = s - jnp.where(diagonal, score_scale * margin, 0.0)
        same = (tag[:, 0:1] == tag_row) & (tag_row >= 0.0) & opposite
        e = jnp.where(same, jnp.exp(jnp.where(same, s, 0.0)), 0.0)
        valid = tag_row >= 0.0
        sums = jnp.where(valid, jnp.sum(e, axis=0, keepdims=True), 1.0)
        coef = 1.0 / jnp.sum(valid.astype(f32))
        positive = jnp.sum(jnp.where(diagonal & same, s, 0.0))
        loss = (jnp.sum(jnp.where(valid, jnp.log(sums), 0.0)) - positive) * coef
        loss_ref[0, 0] = loss
        pair_k[0] = e
        pair_k[1] = jnp.where(diagonal & same, 2.0, 0.0)
        own_rows = pl.ds(pl.multiple_of(me * 8, 8), 8)
        e_own = pair_k[0, own_rows, :]
        r_own = jnp.sum(e_own, axis=1, keepdims=True)
        r_own = jnp.where(tags[:, 0:1] >= 0.0, r_own, 1.0)
        k = (e_own / r_own + e_own / sums - pair_k[1, own_rows, :]) * (coef * score_scale)
        high = k.astype(bf16)
        low = (k - high.astype(f32)).astype(bf16)
        both = jnp.concatenate([high, low], axis=0)
        dn = jnp.concatenate([dot_nn(both, left), dot_nn(both, right)], axis=1)
        dn = dn[0:8] + dn[8:16]
        n = own_unit[...]
        de = unit_rs[:, 0:1] * (dn - n * jnp.sum(n * dn, axis=1, keepdims=True))
        vec_grad[0:1, gain2_at : gain2_at + width] = jnp.sum(de * pooled_hat[...], axis=0, keepdims=True)
        vec_grad[0:1, shift2_at : shift2_at + width] = jnp.sum(de, axis=0, keepdims=True)
        pooled_hat[...] = de

    def norm_two_back():
        def body(i, carry):
            rows = pl.ds(pl.multiple_of(i * 64, 64), 64)
            de = pooled_hat[pl.ds(i // 2 + 4 * (i % 2), 1), :]
            dg = de * (1.0 + vec(gain2_at))
            xh = xhat2[rows, :]
            m1 = jnp.mean(dg, axis=1, keepdims=True)
            m2 = jnp.mean(dg * xh, axis=1, keepdims=True)
            dz = (rstd2[rows, 0:1] * tok_w[rows, 0:1]) * (dg - m1 - xh * m2)
            low = dz.astype(bf16)
            xhat2[rows, :] = dz
            y_low[rows, :] = low
            return carry + jnp.sum(low.astype(f32), axis=0, keepdims=True)

        vec_grad[0:1, bias_down_at : bias_down_at + width] = lax.fori_loop(0, 8, body, jnp.zeros((1, width), f32), unroll=2)

    g_places = ((w_up, 0), (w_up, 2), (g_rest, 4), (g_rest, 6), (g_rest, 0), (g_rest, 2))
    box_places = ((w_down, 0), (w_down, 2), (raw, 4), (raw, 6), (raw, 0), (raw, 2))

    def grad_w_down(blk):
        out = dot_nn(act_t[pl.ds(pl.multiple_of(blk * 384, 128), 384), :], y_low[...])
        for part in range(2):
            for zz in range(4):
                for h in range(2):
                    rows = out[96 * zz + 48 * h : 96 * zz + 48 * h + 48, half * part : half * part + half]
                    at = pl.multiple_of((blk % 4) * 192 + 48 * zz, 16)
                    g_rest[2 * part + blk // 4, pl.ds(at, 48), lanes(h)] = rows.astype(bf16)

    def down_grads(lo, hi):
        def body(n, carry):
            q = 3 - n // 2
            grad_w_down(at_q(q) ^ (1 - n % 2))

            @pl.when(n % 2 == 0)
            def _():
                for p in (4, 5):
                    for h in range(2):
                        core_send(p, h, q)

            return carry

        lax.fori_loop(lo, hi, body, 0)

    def grad_act(lo, hi):
        def body(t, carry):
            c, n = t // 3, t % 3
            to = pl.multiple_of(t * 256, 256)
            work[:, 0:256] = dot_nt(y_low[...], w_down[c, pl.ds(pl.multiple_of(n * 256, 256), 256), :])

            def rows_of(i, total):
                rows = pl.ds(pl.multiple_of(i * 64, 64), 64)
                low = (work[rows, 0:256] * slope[rows, pl.ds(to, 256)].astype(f32)).astype(bf16)
                act[rows, pl.ds(to, 256)] = low
                return total + jnp.sum(low.astype(f32), axis=0, keepdims=True)

            sums = lax.fori_loop(0, 8, rows_of, jnp.zeros((1, 256), f32))
            vec_grad[0:1, pl.ds(pl.multiple_of(bias_up_at + to, 256), 256)] = sums
            return carry

        lax.fori_loop(lo, hi, body, 0)

    def store_units(p, h, m, out):
        ref, base = g_places[p]
        for d in range(16):
            rows = out[24 * d : 24 * d + 24]
            both = jnp.concatenate([rows[:, :half], rows[:, half:]], axis=0)
            ref[base + m, 48 * d : 48 * d + 48, lanes(h)] = both.astype(bf16)

    def grad_w_rows(p, halves=(0, 1)):
        def body(n, carry):
            m = (b // 4) ^ (1 - n)
            rows = pl.ds(pl.multiple_of(m * 384, 128), 384)
            for h in halves:
                if p >= 2:
                    out = dot_nn(y_t[rows, :], act[:, (2 * p - 4 + h) * width : (2 * p - 3 + h) * width])
                elif (p, h) == (1, 1):
                    out = dot_nn(ctx_t[rows, :], y_low[...])
                else:
                    out = dot_nn(x_t[rows, :], qkv[2 * p + h])
                store_units(p, h, m, out)
                for q in (1, 0):
                    core_send(p, h, 2 * (1 - n) + q)
            return carry

        lax.fori_loop(0, 2, body, 0)

    def grad_y():
        def body(n, carry):
            at = pl.multiple_of(n * 256, 256)
            total = xhat2[:, pl.ds(at, 256)]
            for c in range(4):
                total = total + dot_nt(act[:, c * width : (c + 1) * width], w_up[c, pl.ds(at, 256), :])
            work[:, pl.ds(at, 256)] = total
            return carry

        lax.fori_loop(0, 3, body, 0)

    def norm_one_back():
        def body(i, carry):
            rows = pl.ds(pl.multiple_of(i * 64, 64), 64)
            dy = work[rows, :]
            xh = xhat1[rows, :]
            dg = dy * (1.0 + vec(gain1_at))
            m1 = jnp.mean(dg, axis=1, keepdims=True)
            m2 = jnp.mean(dg * xh, axis=1, keepdims=True)
            dh = rstd1[rows, 0:1] * (dg - m1 - xh * m2)
            low = dh.astype(bf16)
            work[rows, :] = dh
            y_low[rows, :] = low
            gain, shift, bias = carry
            return (
                gain + jnp.sum(dy * xh, axis=0, keepdims=True),
                shift + jnp.sum(dy, axis=0, keepdims=True),
                bias + jnp.sum(low.astype(f32), axis=0, keepdims=True),
            )

        zero = jnp.zeros((1, width), f32)
        gain, shift, bias = lax.fori_loop(0, 8, body, (zero, zero, zero), unroll=2)
        vec_grad[0:1, gain1_at : gain1_at + width] = gain
        vec_grad[0:1, shift1_at : shift1_at + width] = shift
        vec_grad[0:1, bias_o : bias_o + width] = bias

    def grad_ctx():
        def body(n, carry):
            at = pl.multiple_of(n * 256, 256)
            ctx[:, pl.ds(at, 256)] = dot_nt(y_low[...], w_attn[3, pl.ds(at, 256), :]).astype(bf16)
            return carry

        lax.fori_loop(0, 3, body, 0)

    def attend_back(group, lo, hi):
        def body(p, carry):
            rows = pl.ds(pl.multiple_of(p * 128, 128), 128)
            for hp in range(4) if group == 0 else range(4, 6):
                places = head_places(hp)
                q2, k2, v2 = [qkv[c, rows, at : at + 128] for c, at in places]
                dc = split_heads(ctx[rows, 128 * hp : 128 * hp + 128])
                a = probs[p * 6 + hp]
                af = a.astype(f32)
                da = dot_nt(dc, v2)
                ds = (af * (da - jnp.sum(af * da, axis=1, keepdims=True))).astype(bf16)
                dv = dot_tn(a, dc)
                wide = jnp.concatenate([ds[:128], ds[128:]], axis=1)
                dq = dot_nn(wide, split_heads(k2)) * HEAD ** (-0.5)
                dk = dot_tn(ds, split_heads(q2)) * HEAD ** (-0.5)
                for (c, at), d in zip(places, (dq, dk, dv)):
                    qkv[c, rows, at : at + 128] = d.astype(bf16)
            return carry

        lax.fori_loop(lo, hi, body, 0, unroll=1 + group)

    def grad_bias_in():
        def body(i, carry):
            rows = pl.ds(pl.multiple_of(i * 64, 64), 64)
            return tuple(have + jnp.sum(qkv[c, rows, :].astype(f32), axis=0, keepdims=True) for c, have in enumerate(carry))

        zero = jnp.zeros((1, width), f32)
        first_sum, second_sum, third_sum = lax.fori_loop(0, 8, body, (zero, zero, zero))
        vec_grad[0:1, bias_q : bias_q + 512] = first_sum[:, 0:512]
        vec_grad[0:1, bias_q + 512 : bias_q + 768] = third_sum[:, 0:256]
        vec_grad[0:1, bias_v : bias_v + 512] = second_sum[:, 256:768]
        vec_grad[0:1, bias_v + 512 : bias_v + 768] = third_sum[:, 512:768]

    def dx_copy(n):
        at = pl.ds(pl.multiple_of(n * 256, 256), 256)
        return pltpu.make_async_copy(work.at[:, at], dx_hbm.at[:, at], local_sem.at[3])

    def grad_x(lo, hi):
        def body(n, carry):
            at = pl.multiple_of(n * 256, 256)
            total = work[:, pl.ds(at, 256)]
            for c in range(3):
                total = total + dot_nt(qkv[c], w_attn[c, pl.ds(at, 256), :])
            work[:, pl.ds(at, 256)] = total
            return carry

        lax.fori_loop(lo, hi, body, 0)
        for n in range(lo, hi):
            dx_copy(n).start()

    def spot(p, run, u, h):
        ref, base = box_places[p]
        return ref.at[base + run // 4, pl.ds((run % 4) * 192 + 48 * u, 48), lanes(h)]

    def core_send(p, h, q):
        remote(
            quad(g_places[p], at_q(q) ^ 1, h), quad(box_places[p], q, h), rs_send.at[p, 0], rc_sem.at[p, h, q], comm.C
        ).start()

    def run_wait(p, run, h, sem):
        ref = quad(box_places[p], run, h)
        remote(ref, ref, rs_send.at[p, 0], sem, comm.C).wait_recv()

    def spot_wait(p, run, u, h, sem):
        ref = spot(p, run, u, h)
        remote(ref, ref, rs_send.at[p, 0], sem, comm.C).wait_recv()

    def add_in(p, h, q, runs):
        target, base = g_places[p]
        box, box_base = box_places[p]
        blk = at_q(q)

        def body(i, carry):
            at = pl.multiple_of((blk % 4) * 192 + i * 48, 16)
            total = target[base + blk // 4, pl.ds(at, 48), lanes(h)].astype(f32)
            for run in runs:
                from_at = pl.multiple_of((run % 4) * 192 + i * 48, 16)
                total = total + box[box_base + run // 4, pl.ds(from_at, 48), lanes(h)].astype(f32)
            target[base + blk // 4, pl.ds(at, 48), lanes(h)] = total.astype(bf16)
            return carry

        lax.fori_loop(0, 4, body, 0)

    def read_unit(p, i, h):
        ref, base = g_places[p]
        return ref[base + i // 16, pl.ds((i % 16) * 48, 48), lanes(h)].astype(f32)

    def read_spot(p, run, u, h):
        ref, base = box_places[p]
        return ref[base + run // 4, (run % 4) * 192 + 48 * u : (run % 4) * 192 + 48 * u + 48, lanes(h)].astype(f32)

    def write_unit(p, i, h, total):
        ref, base = g_places[p]
        ref[base + i // 16, pl.ds((i % 16) * 48, 48), lanes(h)] = total.astype(bf16)

    def pass_run(p, h, q, run, sem):
        along_y = (run < 6) == (h == 0)
        device, way = (comm.Y, 2) if along_y else (comm.X, 1)
        remote(quad(g_places[p], at_q(q), h), quad(box_places[p], run, h), rs_send.at[p, way], sem, device).start()

    def pass_unit(p, i, run, u, h, device, way, sem):
        remote(unit(g_places[p], i, h), spot(p, run, u, h), rs_send.at[p, way], sem, device).start()

    def s1(p, side, halves=(0, 1)):
        for h in halves:
            q = 3 if side == 1 else 2 - h
            run_wait(p, q, h, rc_sem.at[p, h, q])
            add_in(p, h, q, (q,))
            pass_run(p, h, q, 4 + side, r1_sem.at[p, h, side])

    def s2(p, halves=(0, 1)):
        if REDUCE_MODE[p] == Z_FIRST:
            for h in halves:
                q = 1 + h
                run_wait(p, q, h, rc_sem.at[p, h, q])
                run_wait(p, 5, h, r1_sem.at[p, h, 1])
                add_in(p, h, q, (q, 5))
                pass_run(p, h, q, 6, r2_sem.at[p, h])
            return
        for h in halves:
            for j, q in enumerate((0, 1 + h)):
                run_wait(p, q, h, rc_sem.at[p, h, q])
                run_wait(p, 4 + j, h, r1_sem.at[p, h, j])
                add_in(p, h, q, (q, 4 + j))
                pass_unit(p, dev(q, 1), 6, 2 * j, h, comm.Z[1], 3, rz_sem.at[p, h, 2 * j])
                pass_unit(p, dev(q, 3), 6, 2 * j + 1, h, comm.Z[1], 3, rz_sem.at[p, h, 2 * j + 1])

    def s3(p, halves=(0, 1)):
        if REDUCE_MODE[p] == Z_FIRST:
            for h in halves:
                run_wait(p, 0, h, rc_sem.at[p, h, 0])
                run_wait(p, 4, h, r1_sem.at[p, h, 0])
                run_wait(p, 6, h, r2_sem.at[p, h])
                add_in(p, h, 0, (0, 4, 6))
                pass_unit(p, dev(0, 1), 7, 0, h, comm.Z[1], 3, rz_sem.at[p, h, 0])
                pass_unit(p, dev(0, 3), 7, 1, h, comm.Z[1], 3, rz_sem.at[p, h, 1])
            return
        for h in halves:
            for j, q in enumerate((0, 1 + h)):
                spot_wait(p, 6, 2 * j + 1, h, rz_sem.at[p, h, 2 * j + 1])
                write_unit(p, dev(q, 2), h, read_unit(p, dev(q, 2), h) + read_spot(p, 6, 2 * j + 1, h))
                pass_unit(p, dev(q, 2), 7, j, h, comm.Z[2], 3, ry_sem.at[p, h, j])

    def s4(p, halves=(0, 1)):
        if REDUCE_MODE[p] == Z_FIRST:
            for h in halves:
                spot_wait(p, 7, 1, h, rz_sem.at[p, h, 1])
                write_unit(p, dev(0, 2), h, read_unit(p, dev(0, 2), h) + read_spot(p, 7, 1, h))
                pass_unit(p, dev(0, 2), 7, 2, h, comm.Z[2], 3, ry_sem.at[p, h, 0])
            return
        for h in halves:
            q = 1 + h
            spot_wait(p, 6, 2, h, rz_sem.at[p, h, 2])
            spot_wait(p, 7, 1, h, ry_sem.at[p, h, 1])
            write_unit(p, dev(q, 0), h, read_unit(p, dev(q, 0), h) + read_spot(p, 6, 2, h) + read_spot(p, 7, 1, h))
            device, way = (comm.X, 1) if h == 0 else (comm.Y, 2)
            pass_unit(p, dev(q, 0), 7, 2, h, device, way, rf_sem.at[p, h])

    def s5(p, halves=(0, 1)):
        for h in halves:
            total = read_unit(p, me, h)
            if REDUCE_MODE[p] == Z_FIRST:
                spot_wait(p, 7, 0, h, rz_sem.at[p, h, 0])
                spot_wait(p, 7, 2, h, ry_sem.at[p, h, 0])
                total = total + read_spot(p, 7, 0, h) + read_spot(p, 7, 2, h)
            else:
                spot_wait(p, 6, 0, h, rz_sem.at[p, h, 0])
                spot_wait(p, 7, 0, h, ry_sem.at[p, h, 0])
                spot_wait(p, 7, 2, h, rf_sem.at[p, h])
                total = total + read_spot(p, 6, 0, h) + read_spot(p, 7, 0, h) + read_spot(p, 7, 2, h)
            if p >= 4:
                grad_down_ref[48 * h : 48 * h + 48, half * (p - 4) : half * (p - 3)] = total
            else:
                row = jnp.concatenate([total[0:24], total[24:48]], axis=1)
                at = 0
                for c, n in PIECES[p][h]:
                    grad_rows_ref[:, c : c + n] = row[:, at : at + n]
                    at = at + n

    def sums_sent(p):
        z_first = REDUCE_MODE[p] == Z_FIRST
        for way, n in ((0, 32), (1, 12 if z_first else 9), (2, 12 if z_first else 9), (3, 6 if z_first else 12)):
            remote(bulk(n), bulk(n), rs_send.at[p, way], rc_sem.at[p, 0, 0], comm.C).wait_send()

    def vec_pack():
        vec_out[...] = jnp.zeros_like(vec_out)
        for i in range(32):
            for r, n in ((0, 128), (1, 128), (2, share_v - 256)):
                at = share_v * i + 128 * r
                vec_out[i // 4, 3 * (i % 4) + r : 3 * (i % 4) + r + 1, 0:n] = vec_grad[0:1, at : at + n]

    def vec_copy(src, dst, n, device):
        return remote(vec_out.at[src], vec_in.at[dst], vs_sem.at[n], vr_sem.at[dst], device)

    def vec_core():
        for q in range(4):
            vec_copy(at_q(q) ^ 1, q, q, comm.C).start()

    def vec_take(dst, target):
        vec_copy(target, dst, 0, comm.C).wait_recv()
        vec_out[target] = vec_out[target] + vec_in[dst]

    def vec_y():
        for q in range(4):
            vec_take(q, at_q(q))
        vec_copy(at_q(3), 5, 4, comm.Y).start()
        vec_copy(at_q(2), 4, 5, comm.Y).start()

    def vec_x():
        vec_take(5, at_q(1))
        vec_copy(at_q(1), 6, 6, comm.X).start()

    def vec_z():
        vec_take(4, b)
        vec_take(6, b)
        vec_copy(b, 8, 7, comm.Z[2]).start()

    def vec_w():
        vec_copy(b, 8, 0, comm.C).wait_recv()
        vec_in[10] = vec_out[b] + vec_in[8]
        remote(vec_in.at[10], vec_in.at[9], vs_sem.at[8], vr_sem.at[9], comm.Z[1]).start()

    def vec_end():
        vec_copy(b, 9, 0, comm.C).wait_recv()
        total = vec_in[9] + vec_in[10]
        mine = total[0:3]
        for zz in range(1, 4):
            mine = jnp.where(z == zz, total[3 * zz : 3 * zz + 3], mine)
        whole = jnp.concatenate([mine[0:1], mine[1:2], mine[2:3, 0 : share_v - 256]], axis=1)
        grad_vec_ref[...] = whole.reshape(share_v)
        for n in range(9):
            vec_copy(b, 0, n, comm.C).wait_send()

    def load(n):
        src, dst = ((rows_hbm, rows_ref), (down_hbm, down_ref), (x_hbm, x_ref))[n]
        return pltpu.make_async_copy(src, dst, local_sem.at[n])

    def start():
        for n in range(3):
            load(n).start()
        place_vectors()
        token_weights()
        comm.barrier()
        load(0).wait()

    def loaded(n):
        load(n).wait()

    def pair_gather():
        for p in range(6):
            sent(p)
        small_own(pairs, 1)
        transpose_into(y_low, y_t)
        transpose_into(ctx, ctx_t)
        small_z(pairs, 1)
        transpose_into(act, act_t, 0, 6)
        small_cross(pairs, 1)
        transpose_into(act, act_t, 6, 12)
        small_end(pairs, 1)

    def finish():
        for p in range(6):
            sums_sent(p)
        pltpu.make_async_copy(work, dx_hbm, local_sem.at[3]).wait()

    def vectors(n):
        (small_own, small_z, small_cross, small_end)[n](vec_all, 0)

    start()
    cast(0)
    ownz(0)
    col(0, 0)
    cast(1)
    cast(2)
    fin(2, 0, 0)
    cast(3)
    own1(2)
    across(0, 0)
    ownz(1)
    ownz(2)
    col(1, 0)
    col(3, 0)
    across(1, 0)
    fold(0)
    col(0, 2)
    first(2)
    col(0, 1)
    vectors(0)
    fold(1)
    across(0, 2)
    col(1, 2)
    across(0, 1)
    col(1, 1)
    vectors(1)
    last(0, 2)
    fin(2, 1, 0)
    ownz(3)
    col(0, 3)
    across(1, 2)
    vectors(2)
    loaded(1)
    cast(4)
    across(1, 1)
    last(0, 0)
    last(0, 1)
    across(0, 3)
    vectors(3)
    fin(2, 0, 1)
    col(1, 3)
    fold(2, 1)
    fold(2, 0)
    last(0, 3)
    last(1, 2)
    fin(2, 1, 1)
    own1(4)
    ownz(4)
    fin(2, 2, 1)
    last(1, 0)
    across(1, 3)
    loaded(2)
    transpose_into(x_ref, x_t)
    gathered(0)
    relayout(0)
    last(1, 1)
    col(3, 1)
    fin(4, 0, 0)
    fold(3)
    cast(5)
    spread_vectors()
    col(3, 2)
    first(4)
    project(0, 3)
    fin(2, 3, 1)
    last(1, 3)
    col(5, 0)
    project(3, 6)
    fin(4, 0, 1)
    last(2, 1)
    ownz(5)
    attend(0, 0, 2)
    attend(0, 2, 4)
    across(3, 0)
    fin(2, 2, 0)
    col(3, 3)
    across(3, 1)
    gathered(1)
    relayout(1)
    last(4, 0)
    fold(4, 0)
    fin(2, 3, 0)
    fin(4, 2, 0)
    last(2, 2)
    across(3, 2)
    fin(4, 1, 1)
    across(5, 0)
    fin(4, 1, 0)
    project(6, 9)
    across(3, 3)
    fold(4, 1)
    fold(5)
    attend(1, 0, 4)
    fin(4, 3, 0)
    attn_out()
    fin(4, 2, 1)
    fin(4, 3, 1)
    last(2, 0)
    last(2, 3)
    last(3, 1)
    col(5, 1)
    attn_norm()
    col(5, 3)
    last(4, 1)
    last(3, 0)
    gathered(2)
    relayout(2)
    last(3, 2)
    col(5, 2)
    feed_up(0, 3)
    last(3, 3)
    feed_up(3, 6)
    across(5, 1)
    last(5, 0)
    gathered(3)
    last(4, 3)
    last(4, 2)
    relayout(3)
    across(5, 3)
    feed_up(6, 9)
    across(5, 2)
    feed_up(9, 12)
    last(5, 1)
    last(5, 3)
    gathered(4)
    last(5, 2)
    feed_down(0)
    gathered(5)
    feed_down(1)
    down_norm()
    pool()
    pair_gather()
    contrast()
    norm_two_back()
    down_grads(0, 2)
    down_grads(2, 6)
    s1(4, 1)
    down_grads(6, 8)
    grad_act(0, 4)
    s1(4, 0)
    s1(5, 0)
    grad_act(4, 8)
    grad_act(8, 12)
    s2(4)
    s1(5, 1)
    grad_w_rows(2)
    s1(2, 1)
    grad_w_rows(3)
    s1(2, 0)
    s2(5)
    grad_y()
    s2(2)
    norm_one_back()
    grad_w_rows(1, (1,))
    s3(4)
    grad_ctx()
    s1(1, 1, (1,))
    s1(3, 1)
    attend_back(0, 0, 2)
    s3(2)
    s1(3, 0)
    s1(1, 0, (1,))
    attend_back(0, 2, 4)
    s3(5)
    grad_w_rows(0)
    s2(1, (1,))
    attend_back(1, 0, 4)
    s1(0, 1)
    s2(3)
    grad_w_rows(1, (0,))
    s1(1, 1, (0,))
    grad_bias_in()
    vec_pack()
    vec_core()
    s4(2)
    s1(0, 0)
    s1(1, 0, (0,))
    s3(1, (1,))
    s3(3)
    s2(1, (0,))
    grad_x(0, 1)
    vec_y()
    s2(0)
    s4(5)
    grad_x(1, 2)
    vec_x()
    s5(2)
    s3(1, (0,))
    s4(1, (1,))
    s3(0)
    s4(1, (0,))
    s4(4)
    s4(3)
    s5(5)
    grad_x(2, 3)
    vec_z()
    s5(4)
    s4(0)
    vec_w()
    s5(1, (1,))
    s5(1, (0,))
    s5(3)
    vec_end()
    s5(0)
    finish()


def fused_layer(x, tok, groups, counts, rows, down, vec):
    def big(n):
        return pltpu.VMEM((n, 768, 768), bf16)

    scratch = [
        pltpu.VMEM((512, 768), bf16),
        pltpu.VMEM((24, 6144), f32),
        pltpu.VMEM((96, 768), f32),
        big(8),
        big(4),
        big(4),
        big(4),
        big(8),
        pltpu.VMEM((3, 512, 768), bf16),
        pltpu.VMEM((24, 256, 128), bf16),
        pltpu.VMEM((512, 768), bf16),
        pltpu.VMEM((768, 512), bf16),
        pltpu.VMEM((768, 512), bf16),
        pltpu.VMEM((512, 768), bf16),
        pltpu.VMEM((768, 512), bf16),
        pltpu.VMEM((512, 3072), bf16),
        pltpu.VMEM((3072, 512), bf16),
        pltpu.VMEM((512, 3072), bf16),
        pltpu.VMEM((512, 768), f32),
        pltpu.VMEM((512, 768), f32),
        pltpu.VMEM((512, 768), f32),
        pltpu.VMEM((512, 128), f32),
        pltpu.VMEM((512, 128), f32),
        pltpu.VMEM((512, 128), f32),
        pltpu.VMEM((8, 128), f32),
        pltpu.VMEM((8, 128), f32),
        pltpu.VMEM((32, 16, 128), bf16),
        pltpu.VMEM((8, 9216), f32),
        pltpu.VMEM((8, 2304), f32),
        pltpu.VMEM((32, 16, 512), bf16),
        pltpu.VMEM((8, 768), f32),
        pltpu.VMEM((8, 768), f32),
        pltpu.VMEM((8, 128), f32),
        pltpu.VMEM((2, 256, 256), f32),
        pltpu.VMEM((8, 9216), f32),
        pltpu.VMEM((8, 16, 128), f32),
        pltpu.VMEM((12, 16, 128), f32),
    ]
    dma = pltpu.SemaphoreType.DMA
    scratch += [
        dma((4,)), dma((6, 4, 4)), dma((6, 4, 2)), dma((6, 4, 2)), dma((6, 4, 2)), dma((6,)), dma((6, 4)),
        dma((2, 16)), dma((2,)),
        dma((6, 2, 4)), dma((6, 2, 2)), dma((6, 2)), dma((6, 2, 4)), dma((6, 2, 2)), dma((6, 2)), dma((6, 4)),
        dma((12,)), dma((9,)),
    ]
    vmem = pl.BlockSpec(memory_space=pltpu.VMEM)
    smem = pl.BlockSpec(memory_space=pltpu.SMEM)
    anywhere = pl.BlockSpec(memory_space=pl.ANY)
    return pl.pallas_call(
        layer_kernel,
        out_shape=(
            jax.ShapeDtypeStruct((1, 1), f32),
            jax.ShapeDtypeStruct(x.shape, f32),
            jax.ShapeDtypeStruct(rows.shape, f32),
            jax.ShapeDtypeStruct(down.shape, f32),
            jax.ShapeDtypeStruct(vec.shape, f32),
        ),
        in_specs=[anywhere, vmem, smem, smem, anywhere, anywhere, vmem],
        out_specs=(smem, anywhere, vmem, vmem, vmem),
        scratch_shapes=scratch,
        compiler_params=pltpu.CompilerParams(collective_id=0, has_side_effects=True, vmem_limit_bytes=vmem_bytes),
    )(x, tok, groups, counts, rows, down, vec)


def adam_step(master, gradient, moment_one, moment_two, decay, rate):
    mean_new = beta_one * moment_one + (1.0 - beta_one) * gradient
    square_new = beta_two * moment_two + (1.0 - beta_two) * gradient * gradient
    mean_hat = mean_new / (1.0 - beta_one**STEP)
    square_hat = square_new / (1.0 - beta_two**STEP)
    updated = master - rate * (mean_hat / (jnp.sqrt(square_hat) + adam_epsilon) + decay * master)
    return (updated, mean_new, square_new)


def update_kernel(*refs):
    ins, outs, in_bufs, out_bufs = refs[:13], refs[13:23], refs[23:36], refs[36:45]
    in_sem, out_sem = refs[45:]
    loads = [pltpu.make_async_copy(ref, buf, in_sem.at[n]) for n, (ref, buf) in enumerate(zip(ins, in_bufs))]
    stores = [pltpu.make_async_copy(buf, ref, out_sem.at[n]) for n, (buf, ref) in enumerate(zip(in_bufs[:1] + out_bufs, outs))]
    for load in loads:
        load.start()
    loads[0].wait()
    stores[0].start()
    for group, (decay, rate) in enumerate(((decay_rate, learn_rate), (decay_rate, learn_rate), (0.0, vector_rate))):
        for load in loads[1 + 4 * group : 5 + 4 * group]:
            load.wait()
        sources = in_bufs[1 + 4 * group : 5 + 4 * group]
        targets = out_bufs[3 * group : 3 * group + 3]
        if len(sources[0].shape) == 1:
            for target, value in zip(targets, adam_step(*[ref[...] for ref in sources], decay, rate)):
                target[...] = value
        else:

            def body(n, carry, sources=sources, targets=targets, decay=decay, rate=rate):
                part = pl.ds(pl.multiple_of(n * 8, 8), 8)
                for target, value in zip(targets, adam_step(*[ref[part, :] for ref in sources], decay, rate)):
                    target[part, :] = value
                return carry

            lax.fori_loop(0, sources[0].shape[0] // 8, body, 0)
        for store in stores[1 + 3 * group : 4 + 3 * group]:
            store.start()
    for store in stores:
        store.wait()


def update(dx, rows, down, vec):
    news = [jax.ShapeDtypeStruct(dx.shape, f32)]
    for group in (rows, down, vec):
        news += [jax.ShapeDtypeStruct(group[0].shape, f32)] * 3
    anywhere = pl.BlockSpec(memory_space=pl.ANY)
    return pl.pallas_call(
        update_kernel,
        out_shape=tuple(news),
        in_specs=[anywhere] * 13,
        out_specs=(anywhere,) * 10,
        scratch_shapes=[pltpu.VMEM(a.shape, f32) for a in (dx, *rows, *down, *vec)]
        + [pltpu.VMEM(a.shape, f32) for a in news[1:]]
        + [pltpu.SemaphoreType.DMA((13,)), pltpu.SemaphoreType.DMA((10,))],
        compiler_params=pltpu.CompilerParams(vmem_limit_bytes=vmem_bytes),
    )(dx, *rows, *down, *vec)


def on_device_fused(
    embeds, token_mask, groups, counts,
    rows_master, rows_mean, rows_square, down_master, down_mean, down_square,
    vector_master, vector_mean, vector_square,
):
    x = embeds.reshape(-1, embeds.shape[-1])
    loss, dx, rows_grad, down_grad, vec_grad = fused_layer(x, token_mask, groups, counts, rows_master, down_master, vector_master)
    dx, *new = update(
        dx,
        (rows_master, rows_grad, rows_mean, rows_square),
        (down_master, down_grad, down_mean, down_square),
        (vector_master, vec_grad, vector_mean, vector_square),
    )
    return (loss[0, 0], dx.reshape(embeds.shape), *new)


def layer_norm(values, scale_vec, shift_vec):
    centre = values - jnp.mean(values, axis=-1, keepdims=True)
    spread = jnp.mean(centre * centre, axis=-1, keepdims=True)
    return centre * lax.rsqrt(spread + norm_epsilon) * scale_vec + shift_vec


def pool_unit(weights, output):
    summed = jnp.sum(output * weights[:, :, None], axis=1) / jnp.sum(weights, axis=1, keepdims=True)
    return summed * lax.rsqrt(jnp.sum(summed * summed, axis=1, keepdims=True) + unit_epsilon)


def exact_gelu(values):
    return jax.nn.gelu(values, approximate=False)


def softmax_last(values):
    return jax.nn.softmax(values, axis=-1)


def split_vectors(vectors, model_width, hidden):
    extents = [model_width] * 5 + [hidden] + [model_width] * 3
    pieces_out = []
    offset = 0
    for extent in extents:
        pieces_out.append(vectors[offset : offset + extent])
        offset = offset + extent
    return pieces_out


def pair_exps(left_rows, right_rows, left_group, right_group, left_start, right_start):
    scores = score_scale * jnp.dot(left_rows, right_rows.T, precision=highest)
    left_index = left_start + jnp.arange(left_rows.shape[0])
    right_index = right_start + jnp.arange(right_rows.shape[0])
    diagonal = left_index[:, None] == right_index[None, :]
    scores = scores - score_scale * margin * diagonal.astype(jnp.float32)
    same = (left_group[:, None] == right_group[None, :]) & (left_group[:, None] >= 0.0)
    return (jnp.where(same, jnp.exp(scores), 0.0), (diagonal & same).astype(jnp.float32))


def add_sums(own_data, arrived, offset):
    sources, targets, group_own, own_start = own_data
    other_src, other_tgt, other_group = arrived
    row_exp, unused_row = pair_exps(sources, other_tgt, group_own, other_group, own_start, offset)
    col_exp, unused_col = pair_exps(other_src, targets, other_group, group_own, offset, own_start)
    return (jnp.sum(row_exp, axis=1), jnp.sum(col_exp, axis=0))


def add_grads(own_data, loss_coef, arrived, offset):
    sources, targets, group_own, own_start, row_own, col_own = own_data
    other_src, other_tgt, other_group, other_row, other_col = arrived
    row_exp, row_diag = pair_exps(sources, other_tgt, group_own, other_group, own_start, offset)
    row_coef = (
        row_exp / row_own[:, None] + row_exp / other_col[None, :] - 2.0 * row_diag
    ) * loss_coef
    col_exp, col_diag = pair_exps(other_src, targets, other_group, group_own, offset, own_start)
    col_coef = (
        col_exp / other_row[:, None] + col_exp / col_own[None, :] - 2.0 * col_diag
    ) * loss_coef
    grad_src = score_scale * jnp.dot(row_coef, other_tgt, precision=highest)
    grad_tgt = score_scale * jnp.dot(col_coef.T, other_src, precision=highest)
    return (grad_src, grad_tgt)


def on_device_general(
    embeds,
    token_mask,
    groups,
    counts,
    rows_master,
    rows_mean,
    rows_square,
    down_master,
    down_mean,
    down_square,
    vector_master,
    vector_mean,
    vector_square,
):
    slot_count = embeds.shape[0]
    length = embeds.shape[2]
    model_width = embeds.shape[3]
    row_all, down_all, vector_all = (
        lax.all_gather(rows_master.astype(jnp.bfloat16), ("blk", "dp"), axis=0, tiled=True),
        lax.all_gather(down_master.astype(jnp.bfloat16), ("blk", "dp"), axis=0, tiled=True),
        lax.all_gather(vector_master.astype(jnp.bfloat16), ("blk", "dp"), axis=0, tiled=True),
    )
    hidden = down_all.shape[0]
    vectors = vector_all.astype(jnp.float32)
    bias_q, bias_v, bias_o, gain_one, shift_one, bias_up, bias_down, gain_two, shift_two = (
        split_vectors(vectors, model_width, hidden)
    )
    w_attn_in = row_all[:, : 3 * model_width]
    w_attn_out = row_all[:, 3 * model_width : 4 * model_width]
    w_up = row_all[:, 4 * model_width :]
    seq_count = 2 * slot_count
    tokens = seq_count * length
    head_count = model_width // HEAD
    inputs = embeds.reshape(tokens, model_width)
    weights = token_mask.reshape(seq_count, length).astype(jnp.float32)
    key_valid = token_mask.reshape(seq_count, length) > 0
    joined = jnp.concatenate([bias_q, jnp.zeros_like(bias_q), bias_v])
    projected = (jnp.dot(inputs, w_attn_in, preferred_element_type=jnp.float32) + joined).astype(
        jnp.bfloat16
    )
    queries = projected[:, :model_width].reshape(seq_count, length, head_count, HEAD)
    key_part = projected[:, model_width : 2 * model_width].reshape(
        seq_count, length, head_count, HEAD
    )
    values = projected[:, 2 * model_width :].reshape(seq_count, length, head_count, HEAD)
    scores = jnp.einsum(
        "nihe,njhe->nhij", queries, key_part, preferred_element_type=jnp.float32
    ) * HEAD ** (-0.5)
    scores = jnp.where(key_valid[:, None, None, :], scores, -1e30)
    attention, soft_back = jax.vjp(softmax_last, scores)
    attention_low = attention.astype(jnp.bfloat16)
    context = (
        jnp.einsum("nhij,njhe->nihe", attention_low, values, preferred_element_type=jnp.float32)
        .astype(jnp.bfloat16)
        .reshape(tokens, model_width)
    )
    resid_one = (
        inputs.astype(jnp.float32)
        + jnp.dot(context, w_attn_out, preferred_element_type=jnp.float32)
        + bias_o
    )
    normed_full, norm_one_back = jax.vjp(layer_norm, resid_one, 1.0 + gain_one, shift_one)
    normed_one = normed_full.astype(jnp.bfloat16)
    up_pre = jnp.dot(normed_one, w_up, preferred_element_type=jnp.float32) + bias_up
    activated_full, gelu_back = jax.vjp(exact_gelu, up_pre)
    activated = activated_full.astype(jnp.bfloat16)
    resid_two = (
        normed_one.astype(jnp.float32)
        + jnp.dot(activated, down_all, preferred_element_type=jnp.float32)
        + bias_down
    )
    output, norm_two_back = jax.vjp(layer_norm, resid_two, 1.0 + gain_two, shift_two)
    pooled, pool_back = jax.vjp(
        partial(pool_unit, weights), output.reshape(seq_count, length, model_width)
    )
    pooled = pooled.reshape(slot_count, 2, model_width)
    sources = pooled[:, 0]
    targets = pooled[:, 1]
    own_start = lax.axis_index(("blk", "dp")) * slot_count
    valid_slot = jnp.arange(slot_count) < counts[0]
    group_own = jnp.where(valid_slot, groups, -1).astype(jnp.float32)
    pair_total = lax.psum(counts[0].astype(jnp.float32), ("blk", "dp"))
    loss_coef = 0.5 / pair_total
    own_sums = (sources, targets, group_own, own_start)
    row_sum, col_sum = add_sums(
        own_sums,
        (
            lax.all_gather(sources, ("blk", "dp"), axis=0, tiled=True),
            lax.all_gather(targets, ("blk", "dp"), axis=0, tiled=True),
            lax.all_gather(group_own, ("blk", "dp"), axis=0, tiled=True),
        ),
        jnp.int32(0),
    )
    row_safe = jnp.where(valid_slot, row_sum, 1.0)
    col_safe = jnp.where(valid_slot, col_sum, 1.0)
    own_grads = (sources, targets, group_own, own_start, row_safe, col_safe)
    grad_src, grad_tgt = add_grads(
        own_grads,
        loss_coef,
        (
            lax.all_gather(sources, ("blk", "dp"), axis=0, tiled=True),
            lax.all_gather(targets, ("blk", "dp"), axis=0, tiled=True),
            lax.all_gather(group_own, ("blk", "dp"), axis=0, tiled=True),
            lax.all_gather(row_safe, ("blk", "dp"), axis=0, tiled=True),
            lax.all_gather(col_safe, ("blk", "dp"), axis=0, tiled=True),
        ),
        jnp.int32(0),
    )
    positive = score_scale * jnp.sum(sources * targets, axis=1) - score_scale * margin
    loss_terms = jnp.sum(
        jnp.where(valid_slot, jnp.log(row_safe) + jnp.log(col_safe) - 2.0 * positive, 0.0)
    )
    pair_loss = lax.psum(loss_terms, ("blk", "dp")) * loss_coef
    grad_pooled = jnp.stack([grad_src, grad_tgt], axis=1).reshape(seq_count, model_width)
    grad_output = pool_back(grad_pooled)[0].reshape(tokens, model_width)
    grad_resid_two, grad_gain_two, grad_shift_two = norm_two_back(grad_output)
    grad_down_low = grad_resid_two.astype(jnp.bfloat16)
    grad_w_down = jnp.einsum(
        "tf,td->fd", activated, grad_down_low, preferred_element_type=jnp.float32
    )
    grad_bias_down = jnp.sum(grad_down_low.astype(jnp.float32), axis=0)
    grad_act = jnp.einsum("td,fd->tf", grad_down_low, down_all, preferred_element_type=jnp.float32)
    grad_up = gelu_back(grad_act)[0].astype(jnp.bfloat16)
    grad_w_up = jnp.einsum("td,tf->df", normed_one, grad_up, preferred_element_type=jnp.float32)
    grad_bias_up = jnp.sum(grad_up.astype(jnp.float32), axis=0)
    grad_normed = grad_resid_two + jnp.einsum(
        "tf,df->td", grad_up, w_up, preferred_element_type=jnp.float32
    )
    grad_resid_one, grad_gain_one, grad_shift_one = norm_one_back(grad_normed)
    grad_attn_low = grad_resid_one.astype(jnp.bfloat16)
    grad_w_out = jnp.einsum("td,te->de", context, grad_attn_low, preferred_element_type=jnp.float32)
    grad_bias_out = jnp.sum(grad_attn_low.astype(jnp.float32), axis=0)
    grad_context = jnp.einsum(
        "te,de->td", grad_attn_low, w_attn_out, preferred_element_type=jnp.float32
    ).astype(jnp.bfloat16)
    grad_context = grad_context.reshape(seq_count, length, head_count, HEAD)
    grad_attention = jnp.einsum(
        "nihe,njhe->nhij", grad_context, values, preferred_element_type=jnp.float32
    )
    grad_values = jnp.einsum(
        "nhij,nihe->njhe", attention_low, grad_context, preferred_element_type=jnp.float32
    )
    grad_scores = soft_back(grad_attention)[0].astype(jnp.bfloat16)
    grad_queries = jnp.einsum(
        "nhij,njhe->nihe", grad_scores, key_part, preferred_element_type=jnp.float32
    ) * HEAD ** (-0.5)
    grad_keys = jnp.einsum(
        "nhij,nihe->njhe", grad_scores, queries, preferred_element_type=jnp.float32
    ) * HEAD ** (-0.5)
    grad_projected = jnp.concatenate(
        [
            grad_queries.reshape(tokens, model_width),
            grad_keys.reshape(tokens, model_width),
            grad_values.reshape(tokens, model_width),
        ],
        axis=1,
    ).astype(jnp.bfloat16)
    grad_w_in = jnp.einsum("td,te->de", inputs, grad_projected, preferred_element_type=jnp.float32)
    grad_bias_q = jnp.sum(grad_projected[:, :model_width].astype(jnp.float32), axis=0)
    grad_bias_v = jnp.sum(grad_projected[:, 2 * model_width :].astype(jnp.float32), axis=0)
    grad_inputs = grad_resid_one + jnp.einsum(
        "te,de->td", grad_projected, w_attn_in, preferred_element_type=jnp.float32
    )
    grad_vector = jnp.concatenate(
        [
            grad_bias_q,
            grad_bias_v,
            grad_bias_out,
            grad_gain_one,
            grad_shift_one,
            grad_bias_up,
            grad_bias_down,
            grad_gain_two,
            grad_shift_two,
        ]
    )
    rows_share, down_share, vector_share = (
        lax.psum_scatter(
            jnp.concatenate([grad_w_in, grad_w_out, grad_w_up], axis=1),
            ("blk", "dp"),
            scatter_dimension=0,
            tiled=True,
        ),
        lax.psum_scatter(grad_w_down, ("blk", "dp"), scatter_dimension=0, tiled=True),
        lax.psum_scatter(grad_vector, ("blk", "dp"), scatter_dimension=0, tiled=True),
    )
    rows_new = adam_step(rows_master, rows_share, rows_mean, rows_square, decay_rate, learn_rate)
    down_new = adam_step(down_master, down_share, down_mean, down_square, decay_rate, learn_rate)
    vector_new = adam_step(
        vector_master, vector_share, vector_mean, vector_square, 0.0, vector_rate
    )
    embeds_grad = grad_inputs.reshape(slot_count, 2, length, model_width)
    return (
        pair_loss,
        embeds_grad,
        rows_new[0],
        rows_new[1],
        rows_new[2],
        down_new[0],
        down_new[1],
        down_new[2],
        vector_new[0],
        vector_new[1],
        vector_new[2],
    )


def solution(mesh):
    in_specs = (
        P(("blk", "dp"), None, None, None),
        P(("blk", "dp"), None, None),
        P(("blk", "dp")),
        P(("blk", "dp")),
        P(("blk", "dp"), None),
        P(("blk", "dp"), None),
        P(("blk", "dp"), None),
        P(("blk", "dp"), None),
        P(("blk", "dp"), None),
        P(("blk", "dp"), None),
        P(("blk", "dp")),
        P(("blk", "dp")),
        P(("blk", "dp")),
    )
    out_specs = (
        P(),
        P(("blk", "dp"), None, None, None),
        P(("blk", "dp"), None),
        P(("blk", "dp"), None),
        P(("blk", "dp"), None),
        P(("blk", "dp"), None),
        P(("blk", "dp"), None),
        P(("blk", "dp"), None),
        P(("blk", "dp")),
        P(("blk", "dp")),
        P(("blk", "dp")),
    )
    fits = dict(mesh.shape) == {"blk": 8, "dp": 4}
    return jax.shard_map(
        on_device_fused if fits else on_device_general, mesh=mesh, in_specs=in_specs, out_specs=out_specs, check_vma=False
    )
```

```python
from functools import partial

import jax
import jax.numpy as jnp
from jax import lax
from jax.experimental import pallas as pl
from jax.experimental.pallas import tpu as pltpu
from jax.sharding import PartitionSpec as P

HEAD = 64
STEP = 10


score_scale = 32.0
margin = 0.3
beta_one = 0.9
beta_two = 0.999
learn_rate = 0.03
vector_rate = 0.06
decay_rate = 0.01
adam_epsilon = 1e-08
norm_epsilon = 1e-12
unit_epsilon = 1e-06
highest = lax.Precision.HIGHEST

vmem_bytes = 64 * 1024 * 1024 - 65536

f32 = jnp.float32
bf16 = jnp.bfloat16


def dot_nn(a, b, precision=None):
    return lax.dot_general(a, b, (((1,), (0,)), ((), ())), precision=precision, preferred_element_type=f32)


def dot_nt(a, b, precision=None):
    return lax.dot_general(a, b, (((1,), (1,)), ((), ())), precision=precision, preferred_element_type=f32)


def dot_tn(a, b):
    return lax.dot_general(a, b, (((0,), (0,)), ((), ())), preferred_element_type=f32)


Z_FIRST, Z_MID = 0, 1
GATHER_MODE = (Z_FIRST, Z_MID, Z_MID, Z_FIRST, Z_FIRST, Z_MID)
REDUCE_MODE = (Z_FIRST, Z_FIRST, Z_FIRST, Z_MID, Z_MID, Z_MID)

PIECES = (
    (((0, 512), (768, 256)), ((1024, 256), (1536, 512))),
    (((512, 256), (1280, 256), (2048, 256)), ((2304, 768),)),
    (((3072, 768),), ((3840, 768),)),
    (((4608, 768),), ((5376, 768),)),
)


class Comm:
    def __init__(self, depth):
        self.depth = depth
        self.b = lax.axis_index("blk")
        self.z = lax.axis_index("dp")
        b, z = self.b, self.z
        self.X, self.Y, self.C, self.D = (b ^ 2, z), (b ^ 4, z), (b ^ 1, z), (b ^ 6, z)
        self.Z = [(b, z ^ k) for k in range(depth)]
        self.up, self.down = (b, z + 1), (b, z - 1)

    def barrier(self):
        sem = pltpu.get_barrier_semaphore()
        friends = [self.X, self.Y, self.C] + self.Z[1:3]
        for friend in friends:
            pl.semaphore_signal(sem, inc=1, device_id=friend, device_id_type=pl.DeviceIdType.MESH)
        pl.semaphore_wait(sem, len(friends))


def remote(src, dst, send_sem, recv_sem, device):
    return pltpu.make_async_remote_copy(
        src_ref=src,
        dst_ref=dst,
        send_sem=send_sem,
        recv_sem=recv_sem,
        device_id=device,
        device_id_type=pl.DeviceIdType.MESH,
    )


def layer_kernel(
    x_hbm, tok_ref, group_ref, count_ref, rows_hbm, down_hbm, vec_ref,
    loss_ref, dx_hbm, grad_rows_ref, grad_down_ref, grad_vec_ref,
    x_ref, rows_ref, down_ref,
    raw, w_attn, w_up, w_down, g_rest,
    qkv, probs, ctx, ctx_t, x_t, y_low, y_t, act, act_t, slope, xhat1, xhat2, work,
    rstd1, rstd2, tok_w, tok_f, tags, vec_all, vec_row, bias_in, pairs, pooled_hat, own_unit, unit_rs, pair_k, vec_grad, vec_out, vec_in,
    local_sem, zsem, xsem, ysem, dsem, csem, ssem,
    small_recv, small_send,
    rc_sem, r1_sem, r2_sem, rz_sem, ry_sem, rf_sem, rs_send,
    vr_sem, vs_sem,
):
    comm = Comm(4)
    b, z = comm.b, comm.z
    me = b * 4 + z
    width = 768
    half = 384
    def at_q(q):
        return b ^ (2 * q)

    def lanes(h):
        return pl.ds(half * h, half)

    def unit(place, i, h):
        ref, base = place
        return ref.at[base + i // 16, pl.ds((i % 16) * 48, 48), lanes(h)]

    def quad(place, n, h):
        ref, base = place
        return ref.at[base + n // 4, pl.ds((n % 4) * 192, 192), lanes(h)]

    def share(p, i, h):
        if p < 4:
            return unit((raw, 2 * p), i, h)
        return w_down.at[i // 8, pl.ds((i % 8) * 96 + 48 * h, 48), lanes(p - 4)]

    def bulk(n):
        return raw.at[0] if n == 32 else raw.at[0, pl.ds(0, 48 * n), pl.ds(0, half)]

    def send(p, i, h, device, way, rsem):
        ref = share(p, i, h)
        remote(ref, ref, ssem.at[p, way], rsem, device).start()

    def arrived(p, i, h, rsem):
        ref = share(p, i, h)
        remote(ref, ref, ssem.at[p, 0], rsem, comm.X).wait_recv()

    def to_core(p, i, h):
        send(p, i, h, comm.C, 2, csem.at[p])

    def both_to_core(p, i):
        if p < 4:
            ref = raw.at[2 * p + i // 16, pl.ds((i % 16) * 48, 48), :]
        else:
            ref = w_down.at[i // 8, pl.ds((i % 8) * 96, 96), lanes(p - 4)]
        remote(ref, ref, ssem.at[p, 2], csem.at[p], comm.C).start()

    def dev(q, k):
        return at_q(q) * 4 + (z ^ k)

    def cast(p):
        for h in range(2):
            if p < 4:
                row = jnp.concatenate([rows_ref[:, c : c + n] for c, n in PIECES[p][h]], axis=1)
                both = jnp.concatenate([row[:, :half], row[:, half:]], axis=0)
            else:
                both = down_ref[48 * h : 48 * h + 48, half * (p - 4) : half * (p - 3)]
            if p < 4:
                raw[2 * p + me // 16, pl.ds((me % 16) * 48, 48), lanes(h)] = both.astype(bf16)
            else:
                w_down[me // 8, pl.ds((me % 8) * 96 + 48 * h, 48), lanes(p - 4)] = both.astype(bf16)

    def along_z(p, q, k, j, h):
        i = dev(q, k)
        if k == 0:
            send(p, i, h, comm.Z[2], 3, zsem.at[p, 2, 2 * j + h])
            send(p, i, h, comm.Z[1], 3, zsem.at[p, 1, 2 * j + h])
        else:
            send(p, i, h, comm.Z[1], 3, zsem.at[p, 3, 2 * j + h])

    def place(j, h):
        return 0 if j == 0 else (1 if h == 0 else 2)

    def ownz(p):
        for h in range(2):
            along_z(p, 0, 0, 0, h)

    def own1(p):
        send(p, dev(0, 0), 0, comm.X, 0, dsem.at[p, 0, 0])
        send(p, dev(0, 0), 1, comm.Y, 1, dsem.at[p, 0, 1])

    def first(p):
        for h in range(2):
            q = place(1, h)
            arrived(p, dev(q, 0), h, dsem.at[p, 0, h])
            along_z(p, q, 0, 1, h)

    def fold(p, j=0):
        for h in range(2):
            q = place(j, h)
            arrived(p, dev(q, 2), h, zsem.at[p, 2, 2 * j + h])
            along_z(p, q, 2, j, h)

    def z_wait(p, k, j):
        if k in (1, 3):
            for h in range(2):
                arrived(p, dev(place(j, h), k), h, zsem.at[p, k, 2 * j + h])

    def col(p, k):
        z_wait(p, k, 0)
        i = dev(0, k)
        send(p, i, 0, comm.X, 0, xsem.at[p, k, 0])
        send(p, i, 1, comm.Y, 1, ysem.at[p, k, 1])
        send(p, i, 1, comm.X, 0, xsem.at[p, k, 1])
        send(p, i, 0, comm.Y, 1, ysem.at[p, k, 0])
        both_to_core(p, i)

    def across(p, k):
        i = dev(1, k)
        arrived(p, i, 0, xsem.at[p, k, 0])
        send(p, i, 0, comm.Y, 1, dsem.at[p, k, 0])
        to_core(p, i, 0)
        i = dev(2, k)
        arrived(p, i, 1, ysem.at[p, k, 1])
        send(p, i, 1, comm.X, 0, dsem.at[p, k, 1])
        to_core(p, i, 1)

    def fin(p, k, j):
        z_wait(p, k, j)
        i = dev(place(j, 0), k)
        send(p, i, 0, comm.Y, 1, ysem.at[p, k, j])
        to_core(p, i, 0)
        i = dev(place(j, 1), k)
        send(p, i, 1, comm.X, 0, xsem.at[p, k, j])
        to_core(p, i, 1)

    def last(p, k):
        if GATHER_MODE[p] == Z_FIRST:
            rest = ((1, 1, xsem.at[p, k, 1]), (2, 0, ysem.at[p, k, 0]), (3, 0, dsem.at[p, k, 0]), (3, 1, dsem.at[p, k, 1]))
        else:
            rest = ((2, 0, ysem.at[p, k, 0]), (1, 1, xsem.at[p, k, 0]), (3, 0, ysem.at[p, k, 1]), (3, 1, xsem.at[p, k, 1]))
        for q, h, sem in rest:
            arrived(p, dev(q, k), h, sem)
            if q < 3:
                to_core(p, dev(q, k), h)
        both_to_core(p, dev(3, k))

    def gathered(p):
        remote(bulk(32), bulk(32), ssem.at[p, 0], csem.at[p], comm.X).wait_recv()

    def sent(p):
        z_first = GATHER_MODE[p] == Z_FIRST
        for way, n in ((0, 12 if z_first else 9), (1, 12 if z_first else 9), (2, 32), (3, 6 if z_first else 12)):
            remote(bulk(n), bulk(n), ssem.at[p, way], csem.at[p], comm.X).wait_send()

    def small_send_one(ref, n, i, device, rsem):
        block = ref.at[pl.ds(i, 1)]
        remote(block, block, small_send.at[n], rsem, device).start()

    def small_wait(ref, n, i, rsem):
        block = ref.at[pl.ds(i, 1)]
        remote(block, block, small_send.at[n], rsem, comm.X).wait_recv()

    def small_plane(ref, n, k):
        i = dev(0, k)
        small_send_one(ref, n, i, comm.D, small_recv.at[n, 12 + k])
        small_send_one(ref, n, i, comm.X, small_recv.at[n, 4 + k])
        small_send_one(ref, n, i, comm.Y, small_recv.at[n, 8 + k])
        small_send_one(ref, n, i, comm.C, small_recv.at[n, 0])

    def small_own(ref, n):
        for k in (3, 2, 1):
            small_send_one(ref, n, me, comm.Z[k], small_recv.at[n, k])
        small_plane(ref, n, 0)

    def small_z(ref, n):
        for k in (1, 2, 3):
            small_wait(ref, n, dev(0, k), small_recv.at[n, k])
            small_plane(ref, n, k)

    def small_cross(ref, n):
        for k in range(4):
            for q in (1, 2, 3):
                small_wait(ref, n, dev(q, k), small_recv.at[n, 4 * q + k])
                small_send_one(ref, n, dev(q, k), comm.C, small_recv.at[n, 0])

    def small_end(ref, n):
        many = ref.at[pl.ds(0, 16)]
        remote(many, many, small_send.at[n], small_recv.at[n, 0], comm.X).wait_recv()
        many = ref.at[pl.ds(0, 31)]
        remote(many, many, small_send.at[n], small_recv.at[n, 0], comm.X).wait_send()

    def vec(offset, size=width):
        return vec_row[0:1, offset : offset + size]

    bias_q, bias_v, bias_o, gain1_at, shift1_at, bias_up_at = 0, width, 2 * width, 3 * width, 4 * width, 5 * width
    bias_down_at, gain2_at, shift2_at = 9 * width, 10 * width, 11 * width

    share_v = 288

    def place_vectors():
        v = vec_ref[...].reshape(1, share_v)
        tail = jnp.concatenate([v[:, 256:share_v], jnp.zeros((1, 384 - share_v), f32)], axis=1)
        tile = jnp.concatenate([v[:, 0:128], v[:, 128:256], tail, jnp.zeros((13, 128), f32)], axis=0)
        vec_all[pl.ds(me, 1)] = tile.astype(bf16).reshape(1, 16, 128)

    def spread_vectors():
        for i in range(32):
            tile = vec_all[i].astype(f32)
            for r, n in ((0, 128), (1, 128), (2, share_v - 256)):
                at = share_v * i + 128 * r
                vec_row[0:1, at : at + n] = tile[r : r + 1, 0:n]
        bias_in[...] = jnp.zeros_like(bias_in)
        bias_in[0:1, 0:512] = vec(bias_q, 512)
        bias_in[0:1, 1024:1536] = vec(bias_v, 512)
        bias_in[0:1, 1536:1792] = vec(bias_q + 512, 256)
        bias_in[0:1, 2048:2304] = vec(bias_v + 512, 256)

    def relayout(p):
        target, chunk = (w_attn, 2 * p) if p < 2 else (w_up, 2 * p - 4)

        def body(j, carry):
            for h in range(2):
                even = raw[2 * p + j // 8, pl.ds((j % 8) * 96, 48), lanes(h)].astype(f32)
                odd = raw[2 * p + j // 8, pl.ds((j % 8) * 96 + 48, 48), lanes(h)].astype(f32)
                for q in range(2):
                    rows = jnp.concatenate([even[24 * q : 24 * q + 24], odd[24 * q : 24 * q + 24]], axis=0)
                    target[chunk + h, pl.ds(j * 48, 48), lanes(q)] = rows.astype(bf16)
            return carry

        lax.fori_loop(0, 16, body, 0)

    def transpose_into(source, target, lo=0, hi=3):
        def body(j, carry):
            at = pl.multiple_of(j * 256, 256)
            target[pl.ds(at, 256), :] = jnp.transpose(source[:, pl.ds(at, 256)])
            return carry

        lax.fori_loop(lo, hi, body, 0)

    def token_weights():
        lane = lax.broadcasted_iota(jnp.int32, (1, 128), 1)
        left = (lane < 64).astype(f32)
        tok = tok_ref[...].astype(f32)
        tok_f[0:4, :] = jnp.concatenate([tok[:, 0, :], tok[:, 1, :]], axis=1)
        for p in range(4):
            m = tok_f[p : p + 1, :]
            n0 = jnp.sum(m * left, axis=1, keepdims=True)
            n1 = jnp.sum(m * (1.0 - left), axis=1, keepdims=True)
            w = m / (left * n0 + (1.0 - left) * n1)
            tok_w[128 * p : 128 * p + 128, :] = jnp.transpose(jnp.broadcast_to(w, (128, 128)))
        row = lax.broadcasted_iota(jnp.int32, (8, 128), 0) % 4
        tag = jnp.full((8, 128), -1.0, f32)
        for s in range(4):
            tag = jnp.where((row == s) & (count_ref[0] > s), group_ref[s].astype(f32), tag)
        tags[...] = tag

    def project(lo, hi):
        def body(t, carry):
            c, n = t // 3, t % 3
            at = pl.multiple_of(n * 256, 256)
            bias = bias_in[0:1, pl.ds(pl.multiple_of(t * 256, 256), 256)]
            out = dot_nn(x_ref[...], w_attn[c, :, pl.ds(at, 256)]) + bias
            qkv[c, :, pl.ds(at, 256)] = out.astype(bf16)
            return carry

        lax.fori_loop(lo, hi, body, 0)

    def head_places(hp):
        if hp < 4:
            key = (0, 512 + 128 * hp) if hp < 2 else (1, 128 * hp - 256)
            return (0, 128 * hp), key, (1, 256 + 128 * hp)
        return (2, 128 * hp - 512), (2, 128 * hp - 256), (2, 128 * hp)

    lane128 = lax.broadcasted_iota(jnp.int32, (128, 128), 1)
    row128 = lax.broadcasted_iota(jnp.int32, (128, 128), 0)
    even_half = lane128 < 64

    def split_heads(v):
        zero = jnp.zeros_like(v)
        return jnp.concatenate([jnp.where(even_half, v, zero), jnp.where(even_half, zero, v)], axis=0)

    def attend(group, lo, hi):
        def body(p, carry):
            rows = pl.ds(pl.multiple_of(p * 128, 128), 128)
            m = tok_f[pl.ds(p, 1), :]
            same = (row128 < 64) == (lane128 < 64)
            open_one = same & (jnp.broadcast_to(m, (128, 128)) > 0.0)
            block = jnp.where(open_one, 0.0, -1e30)
            block = jnp.concatenate([block, block], axis=0)
            for hp in range(4) if group == 0 else range(4, 6):
                q2, k2, v2 = [qkv[c, rows, at : at + 128] for c, at in head_places(hp)]
                s = dot_nt(split_heads(q2), k2) * HEAD ** (-0.5) + block
                e = jnp.exp(s - jnp.max(s, axis=1, keepdims=True))
                a = (e * (1.0 / jnp.sum(e, axis=1, keepdims=True))).astype(bf16)
                probs[p * 6 + hp] = a
                wide = jnp.concatenate([a[:128], a[128:]], axis=1)
                ctx[rows, 128 * hp : 128 * hp + 128] = dot_nn(wide, split_heads(v2)).astype(bf16)
            return carry

        lax.fori_loop(lo, hi, body, 0, unroll=1 + group)

    def norm_rows(i, source_fn, hat, rstd, emit):
        rows = pl.ds(pl.multiple_of(i * 64, 64), 64)
        h = source_fn(rows)
        centre = h - jnp.mean(h, axis=1, keepdims=True)
        r = lax.rsqrt(jnp.mean(centre * centre, axis=1, keepdims=True) + norm_epsilon)
        xh = centre * r
        hat[rows, :] = xh
        rstd[rows, :] = jnp.broadcast_to(r, (64, 128))
        if emit is not None:
            emit(rows, xh)

    def attn_out():
        def body(n, carry):
            at = pl.multiple_of(n * 256, 256)
            work[:, pl.ds(at, 256)] = dot_nn(ctx[...], w_attn[3, :, pl.ds(at, 256)])
            return carry

        lax.fori_loop(0, 3, body, 0)

    def attn_norm():
        def source(rows):
            return x_ref[rows, :].astype(f32) + work[rows, :] + vec(bias_o)

        def emit(rows, xh):
            y_low[rows, :] = (xh * (1.0 + vec(gain1_at)) + vec(shift1_at)).astype(bf16)

        def norm(i, carry):
            norm_rows(i, source, xhat1, rstd1, emit)
            return carry

        lax.fori_loop(0, 8, norm, 0, unroll=2)

    def feed_up(lo, hi):
        def body(t, carry):
            c, n = t // 3, t % 3
            at = pl.multiple_of(n * 256, 256)
            to = pl.multiple_of(t * 256, 256)
            work[:, pl.ds(0, 256)] = dot_nn(y_low[...], w_up[c, :, pl.ds(at, 256)])
            bias = vec_row[0:1, pl.ds(pl.multiple_of(bias_up_at + to, 256), 256)]

            def rows_of(i, inner):
                rows = pl.ds(pl.multiple_of(i * 32, 32), 32)
                v = work[rows, 0:256] + bias
                cdf = 0.5 * (1.0 + lax.erf(v * 0.7071067811865476))
                dens = jnp.exp(v * v * -0.5) * 0.3989422804014327
                act[rows, pl.ds(to, 256)] = (v * cdf).astype(bf16)
                slope[rows, pl.ds(to, 256)] = (cdf + v * dens).astype(bf16)
                return inner

            lax.fori_loop(0, 16, rows_of, 0, unroll=4)
            return carry

        lax.fori_loop(lo, hi, body, 0)

    def feed_down(s):
        def body(n, carry):
            at = pl.multiple_of(n * 256, 256)
            total = dot_nn(act[:, 0:width], w_down[0, :, pl.ds(at, 256)])
            for c in range(1, 4):
                total = total + dot_nn(act[:, c * width : (c + 1) * width], w_down[c, :, pl.ds(at, 256)])
            work[:, pl.ds(at, 256)] = total
            return carry

        lax.fori_loop(s, 2 * s + 1, body, 0)

    def down_norm():
        def source(rows):
            return y_low[rows, :].astype(f32) + work[rows, :] + vec(bias_down_at)

        def norm(i, carry):
            norm_rows(i, source, xhat2, rstd2, None)
            rows = pl.ds(pl.multiple_of(i * 64, 64), 64)
            got = jnp.sum(xhat2[rows, :] * tok_w[rows, 0:1], axis=0, keepdims=True)
            at = i // 2 + 4 * (i % 2)
            pooled_hat[pl.ds(at, 1), :] = got
            return carry

        lax.fori_loop(0, 8, norm, 0, unroll=2)

    def pool():
        e = pooled_hat[...] * (1.0 + vec(gain2_at)) + vec(shift2_at)
        r = lax.rsqrt(jnp.sum(e * e, axis=1, keepdims=True) + unit_epsilon)
        unit_rs[...] = jnp.broadcast_to(r, (8, 128))
        n = e * r
        own_unit[...] = n
        packed = jnp.concatenate([n[:, :half], n[:, half:]], axis=0)
        tag = jnp.concatenate([tags[...], tags[...]], axis=0)
        pairs[pl.ds(me, 1)] = jnp.concatenate([packed, tag], axis=1).astype(bf16).reshape(1, 16, 512)

    def contrast():
        total = 256
        every = pairs[...].astype(f32)
        left = every[:, 0:8, 0:half].reshape(total, half).astype(bf16)
        right = every[:, 8:16, 0:half].reshape(total, half).astype(bf16)
        tag = every[:, 0:8, half : half + 128].reshape(total, 128)
        tag_row = jnp.concatenate([jnp.transpose(tag[0:128])[0:1], jnp.transpose(tag[128:256])[0:1]], axis=1)
        s = (dot_nt(left, left) + dot_nt(right, right)) * score_scale
        i = lax.broadcasted_iota(jnp.int32, (total, total), 0)
        j = lax.broadcasted_iota(jnp.int32, (total, total), 1)
        opposite = (i & 4) != (j & 4)
        diagonal = (i ^ j) == 4
        s = s - jnp.where(diagonal, score_scale * margin, 0.0)
        same = (tag[:, 0:1] == tag_row) & (tag_row >= 0.0) & opposite
        e = jnp.where(same, jnp.exp(jnp.where(same, s, 0.0)), 0.0)
        valid = tag_row >= 0.0
        sums = jnp.where(valid, jnp.sum(e, axis=0, keepdims=True), 1.0)
        coef = 1.0 / jnp.sum(valid.astype(f32))
        positive = jnp.sum(jnp.where(diagonal & same, s, 0.0))
        loss = (jnp.sum(jnp.where(valid, jnp.log(sums), 0.0)) - positive) * coef
        loss_ref[0, 0] = loss
        pair_k[0] = e
        pair_k[1] = jnp.where(diagonal & same, 2.0, 0.0)
        own_rows = pl.ds(pl.multiple_of(me * 8, 8), 8)
        e_own = pair_k[0, own_rows, :]
        r_own = jnp.sum(e_own, axis=1, keepdims=True)
        r_own = jnp.where(tags[:, 0:1] >= 0.0, r_own, 1.0)
        k = (e_own / r_own + e_own / sums - pair_k[1, own_rows, :]) * (coef * score_scale)
        high = k.astype(bf16)
        low = (k - high.astype(f32)).astype(bf16)
        both = jnp.concatenate([high, low], axis=0)
        dn = jnp.concatenate([dot_nn(both, left), dot_nn(both, right)], axis=1)
        dn = dn[0:8] + dn[8:16]
        n = own_unit[...]
        de = unit_rs[:, 0:1] * (dn - n * jnp.sum(n * dn, axis=1, keepdims=True))
        vec_grad[0:1, gain2_at : gain2_at + width] = jnp.sum(de * pooled_hat[...], axis=0, keepdims=True)
        vec_grad[0:1, shift2_at : shift2_at + width] = jnp.sum(de, axis=0, keepdims=True)
        pooled_hat[...] = de

    def norm_two_back():
        def body(i, carry):
            rows = pl.ds(pl.multiple_of(i * 64, 64), 64)
            de = pooled_hat[pl.ds(i // 2 + 4 * (i % 2), 1), :]
            dg = de * (1.0 + vec(gain2_at))
            xh = xhat2[rows, :]
            m1 = jnp.mean(dg, axis=1, keepdims=True)
            m2 = jnp.mean(dg * xh, axis=1, keepdims=True)
            dz = (rstd2[rows, 0:1] * tok_w[rows, 0:1]) * (dg - m1 - xh * m2)
            low = dz.astype(bf16)
            xhat2[rows, :] = dz
            y_low[rows, :] = low
            return carry + jnp.sum(low.astype(f32), axis=0, keepdims=True)

        vec_grad[0:1, bias_down_at : bias_down_at + width] = lax.fori_loop(0, 8, body, jnp.zeros((1, width), f32), unroll=2)

    g_places = ((w_up, 0), (w_up, 2), (g_rest, 4), (g_rest, 6), (g_rest, 0), (g_rest, 2))
    box_places = ((w_down, 0), (w_down, 2), (raw, 4), (raw, 6), (raw, 0), (raw, 2))

    def grad_w_down(blk):
        out = dot_nn(act_t[pl.ds(pl.multiple_of(blk * 384, 128), 384), :], y_low[...])
        for part in range(2):
            for zz in range(4):
                for h in range(2):
                    rows = out[96 * zz + 48 * h : 96 * zz + 48 * h + 48, half * part : half * part + half]
                    at = pl.multiple_of((blk % 4) * 192 + 48 * zz, 16)
                    g_rest[2 * part + blk // 4, pl.ds(at, 48), lanes(h)] = rows.astype(bf16)

    def down_grads(lo, hi):
        def body(n, carry):
            q = 3 - n // 2
            grad_w_down(at_q(q) ^ (1 - n % 2))

            @pl.when(n % 2 == 0)
            def _():
                for p in (4, 5):
                    for h in range(2):
                        core_send(p, h, q)

            return carry

        lax.fori_loop(lo, hi, body, 0)

    def grad_act(lo, hi):
        def body(t, carry):
            c, n = t // 3, t % 3
            to = pl.multiple_of(t * 256, 256)
            work[:, 0:256] = dot_nt(y_low[...], w_down[c, pl.ds(pl.multiple_of(n * 256, 256), 256), :])

            def rows_of(i, total):
                rows = pl.ds(pl.multiple_of(i * 64, 64), 64)
                low = (work[rows, 0:256] * slope[rows, pl.ds(to, 256)].astype(f32)).astype(bf16)
                act[rows, pl.ds(to, 256)] = low
                return total + jnp.sum(low.astype(f32), axis=0, keepdims=True)

            sums = lax.fori_loop(0, 8, rows_of, jnp.zeros((1, 256), f32), unroll=2)
            vec_grad[0:1, pl.ds(pl.multiple_of(bias_up_at + to, 256), 256)] = sums
            return carry

        lax.fori_loop(lo, hi, body, 0)

    def store_units(p, h, m, out):
        ref, base = g_places[p]
        for d in range(16):
            rows = out[24 * d : 24 * d + 24]
            both = jnp.concatenate([rows[:, :half], rows[:, half:]], axis=0)
            ref[base + m, 48 * d : 48 * d + 48, lanes(h)] = both.astype(bf16)

    def grad_w_rows(p, halves=(0, 1)):
        def body(n, carry):
            m = (b // 4) ^ (1 - n)
            rows = pl.ds(pl.multiple_of(m * 384, 128), 384)
            for h in halves:
                if p >= 2:
                    out = dot_nn(y_t[rows, :], act[:, (2 * p - 4 + h) * width : (2 * p - 3 + h) * width])
                elif (p, h) == (1, 1):
                    out = dot_nn(ctx_t[rows, :], y_low[...])
                else:
                    out = dot_nn(x_t[rows, :], qkv[2 * p + h])
                store_units(p, h, m, out)
                for q in (1, 0):
                    core_send(p, h, 2 * (1 - n) + q)
            return carry

        lax.fori_loop(0, 2, body, 0)

    def grad_y():
        def body(n, carry):
            at = pl.multiple_of(n * 256, 256)
            total = xhat2[:, pl.ds(at, 256)]
            for c in range(4):
                total = total + dot_nt(act[:, c * width : (c + 1) * width], w_up[c, pl.ds(at, 256), :])
            work[:, pl.ds(at, 256)] = total
            return carry

        lax.fori_loop(0, 3, body, 0)

    def norm_one_back():
        def body(i, carry):
            rows = pl.ds(pl.multiple_of(i * 64, 64), 64)
            dy = work[rows, :]
            xh = xhat1[rows, :]
            dg = dy * (1.0 + vec(gain1_at))
            m1 = jnp.mean(dg, axis=1, keepdims=True)
            m2 = jnp.mean(dg * xh, axis=1, keepdims=True)
            dh = rstd1[rows, 0:1] * (dg - m1 - xh * m2)
            low = dh.astype(bf16)
            work[rows, :] = dh
            y_low[rows, :] = low
            gain, shift, bias = carry
            return (
                gain + jnp.sum(dy * xh, axis=0, keepdims=True),
                shift + jnp.sum(dy, axis=0, keepdims=True),
                bias + jnp.sum(low.astype(f32), axis=0, keepdims=True),
            )

        zero = jnp.zeros((1, width), f32)
        gain, shift, bias = lax.fori_loop(0, 8, body, (zero, zero, zero), unroll=2)
        vec_grad[0:1, gain1_at : gain1_at + width] = gain
        vec_grad[0:1, shift1_at : shift1_at + width] = shift
        vec_grad[0:1, bias_o : bias_o + width] = bias

    def grad_ctx():
        def body(n, carry):
            at = pl.multiple_of(n * 256, 256)
            ctx[:, pl.ds(at, 256)] = dot_nt(y_low[...], w_attn[3, pl.ds(at, 256), :]).astype(bf16)
            return carry

        lax.fori_loop(0, 3, body, 0)

    def attend_back(group, lo, hi):
        def body(p, carry):
            rows = pl.ds(pl.multiple_of(p * 128, 128), 128)
            for hp in range(4) if group == 0 else range(4, 6):
                places = head_places(hp)
                q2, k2, v2 = [qkv[c, rows, at : at + 128] for c, at in places]
                dc = split_heads(ctx[rows, 128 * hp : 128 * hp + 128])
                a = probs[p * 6 + hp]
                af = a.astype(f32)
                da = dot_nt(dc, v2)
                ds = (af * (da - jnp.sum(af * da, axis=1, keepdims=True))).astype(bf16)
                dv = dot_tn(a, dc)
                wide = jnp.concatenate([ds[:128], ds[128:]], axis=1)
                dq = dot_nn(wide, split_heads(k2)) * HEAD ** (-0.5)
                dk = dot_tn(ds, split_heads(q2)) * HEAD ** (-0.5)
                for (c, at), d in zip(places, (dq, dk, dv)):
                    qkv[c, rows, at : at + 128] = d.astype(bf16)
            return carry

        lax.fori_loop(lo, hi, body, 0, unroll=1 + group)

    def grad_bias_in():
        def body(i, carry):
            rows = pl.ds(pl.multiple_of(i * 64, 64), 64)
            return tuple(have + jnp.sum(qkv[c, rows, :].astype(f32), axis=0, keepdims=True) for c, have in enumerate(carry))

        zero = jnp.zeros((1, width), f32)
        first_sum, second_sum, third_sum = lax.fori_loop(0, 8, body, (zero, zero, zero))
        vec_grad[0:1, bias_q : bias_q + 512] = first_sum[:, 0:512]
        vec_grad[0:1, bias_q + 512 : bias_q + 768] = third_sum[:, 0:256]
        vec_grad[0:1, bias_v : bias_v + 512] = second_sum[:, 256:768]
        vec_grad[0:1, bias_v + 512 : bias_v + 768] = third_sum[:, 512:768]

    def dx_copy(n):
        at = pl.ds(pl.multiple_of(n * 256, 256), 256)
        return pltpu.make_async_copy(work.at[:, at], dx_hbm.at[:, at], local_sem.at[3])

    def grad_x(lo, hi):
        def body(n, carry):
            at = pl.multiple_of(n * 256, 256)
            total = work[:, pl.ds(at, 256)]
            for c in range(3):
                total = total + dot_nt(qkv[c], w_attn[c, pl.ds(at, 256), :])
            work[:, pl.ds(at, 256)] = total
            return carry

        lax.fori_loop(lo, hi, body, 0)
        for n in range(lo, hi):
            dx_copy(n).start()

    def spot(p, run, u, h):
        ref, base = box_places[p]
        return ref.at[base + run // 4, pl.ds((run % 4) * 192 + 48 * u, 48), lanes(h)]

    def core_send(p, h, q):
        remote(
            quad(g_places[p], at_q(q) ^ 1, h), quad(box_places[p], q, h), rs_send.at[p, 0], rc_sem.at[p, h, q], comm.C
        ).start()

    def run_wait(p, run, h, sem):
        ref = quad(box_places[p], run, h)
        remote(ref, ref, rs_send.at[p, 0], sem, comm.C).wait_recv()

    def spot_wait(p, run, u, h, sem):
        ref = spot(p, run, u, h)
        remote(ref, ref, rs_send.at[p, 0], sem, comm.C).wait_recv()

    def add_in(p, h, q, runs, lo=0, hi=4):
        target, base = g_places[p]
        box, box_base = box_places[p]
        blk = at_q(q)

        def body(i, carry):
            at = pl.multiple_of((blk % 4) * 192 + i * 48, 16)
            total = target[base + blk // 4, pl.ds(at, 48), lanes(h)].astype(f32)
            for run in runs:
                from_at = pl.multiple_of((run % 4) * 192 + i * 48, 16)
                total = total + box[box_base + run // 4, pl.ds(from_at, 48), lanes(h)].astype(f32)
            target[base + blk // 4, pl.ds(at, 48), lanes(h)] = total.astype(bf16)
            return carry

        lax.fori_loop(lo, hi, body, 0)

    def read_unit(p, i, h):
        ref, base = g_places[p]
        return ref[base + i // 16, pl.ds((i % 16) * 48, 48), lanes(h)].astype(f32)

    def read_spot(p, run, u, h):
        ref, base = box_places[p]
        return ref[base + run // 4, (run % 4) * 192 + 48 * u : (run % 4) * 192 + 48 * u + 48, lanes(h)].astype(f32)

    def write_unit(p, i, h, total):
        ref, base = g_places[p]
        ref[base + i // 16, pl.ds((i % 16) * 48, 48), lanes(h)] = total.astype(bf16)

    def pass_run(p, h, q, run, sem):
        along_y = (run < 6) == (h == 0)
        device, way = (comm.Y, 2) if along_y else (comm.X, 1)
        remote(quad(g_places[p], at_q(q), h), quad(box_places[p], run, h), rs_send.at[p, way], sem, device).start()

    def pass_unit(p, i, run, u, h, device, way, sem):
        remote(unit(g_places[p], i, h), spot(p, run, u, h), rs_send.at[p, way], sem, device).start()

    def pair_of(place, n, u, h):
        ref, base = place
        return ref.at[base + n // 4, pl.ds((n % 4) * 192 + 96 * u, 96), lanes(h)]

    def pair_wait(p, run, u, sem):
        ref = pair_of(box_places[p], run, u, 0)
        remote(ref, ref, rs_send.at[p, 0], sem, comm.C).wait_recv()

    def pass_pair(p, q, u, run, along_y, sem):
        device, way = (comm.Y, 2) if along_y else (comm.X, 1)
        remote(pair_of(g_places[p], at_q(q), u, 0), pair_of(box_places[p], run, u, 0), rs_send.at[p, way], sem, device).start()

    def split_s1(p, side):
        for q in (3,) if side == 1 else (2, 1):
            run_wait(p, q, 0, rc_sem.at[p, 0, q])
        for u in range(2):
            q = 3 if side == 1 else 2 - u
            add_in(p, 0, q, (q,), 2 * u, 2 * u + 2)
            pass_pair(p, q, u, 4 + side, u == 0, r1_sem.at[6, u, side])

    def split_s2(p):
        for u in range(2):
            pair_wait(p, 5, u, r1_sem.at[6, u, 1])
            add_in(p, 0, 1 + u, (1 + u, 5), 2 * u, 2 * u + 2)
            pass_pair(p, 1 + u, u, 6, u == 1, r2_sem.at[6, u])

    def split_s3(p):
        run_wait(p, 0, 0, rc_sem.at[p, 0, 0])
        for u in range(2):
            pair_wait(p, 4, u, r1_sem.at[6, u, 0])
            pair_wait(p, 6, u, r2_sem.at[6, u])
        add_in(p, 0, 0, (0, 4, 6))
        pass_unit(p, dev(0, 1), 7, 0, 0, comm.Z[1], 3, rz_sem.at[p, 0, 0])
        pass_unit(p, dev(0, 3), 7, 1, 0, comm.Z[1], 3, rz_sem.at[p, 0, 1])

    def s1(p, side, halves=(0, 1)):
        if halves == (0,):
            return split_s1(p, side)
        for h in halves:
            q = 3 if side == 1 else 2 - h
            run_wait(p, q, h, rc_sem.at[p, h, q])
            add_in(p, h, q, (q,))
            pass_run(p, h, q, 4 + side, r1_sem.at[p, h, side])

    def s2(p, halves=(0, 1)):
        if halves == (0,):
            return split_s2(p)
        if REDUCE_MODE[p] == Z_FIRST:
            for h in halves:
                q = 1 + h
                run_wait(p, q, h, rc_sem.at[p, h, q])
                run_wait(p, 5, h, r1_sem.at[p, h, 1])
                add_in(p, h, q, (q, 5))
                pass_run(p, h, q, 6, r2_sem.at[p, h])
            return
        for h in halves:
            for j, q in enumerate((0, 1 + h)):
                run_wait(p, q, h, rc_sem.at[p, h, q])
                run_wait(p, 4 + j, h, r1_sem.at[p, h, j])
                add_in(p, h, q, (q, 4 + j))
                pass_unit(p, dev(q, 1), 6, 2 * j, h, comm.Z[1], 3, rz_sem.at[p, h, 2 * j])
                pass_unit(p, dev(q, 3), 6, 2 * j + 1, h, comm.Z[1], 3, rz_sem.at[p, h, 2 * j + 1])

    def s3(p, halves=(0, 1)):
        if halves == (0,):
            return split_s3(p)
        if REDUCE_MODE[p] == Z_FIRST:
            for h in halves:
                run_wait(p, 0, h, rc_sem.at[p, h, 0])
                run_wait(p, 4, h, r1_sem.at[p, h, 0])
                run_wait(p, 6, h, r2_sem.at[p, h])
                add_in(p, h, 0, (0, 4, 6))
                pass_unit(p, dev(0, 1), 7, 0, h, comm.Z[1], 3, rz_sem.at[p, h, 0])
                pass_unit(p, dev(0, 3), 7, 1, h, comm.Z[1], 3, rz_sem.at[p, h, 1])
            return
        for h in halves:
            for j, q in enumerate((0, 1 + h)):
                spot_wait(p, 6, 2 * j + 1, h, rz_sem.at[p, h, 2 * j + 1])
                write_unit(p, dev(q, 2), h, read_unit(p, dev(q, 2), h) + read_spot(p, 6, 2 * j + 1, h))
                pass_unit(p, dev(q, 2), 7, j, h, comm.Z[2], 3, ry_sem.at[p, h, j])

    def s4(p, halves=(0, 1)):
        if REDUCE_MODE[p] == Z_FIRST:
            for h in halves:
                spot_wait(p, 7, 1, h, rz_sem.at[p, h, 1])
                write_unit(p, dev(0, 2), h, read_unit(p, dev(0, 2), h) + read_spot(p, 7, 1, h))
                pass_unit(p, dev(0, 2), 7, 2, h, comm.Z[2], 3, ry_sem.at[p, h, 0])
            return
        for h in halves:
            q = 1 + h
            spot_wait(p, 6, 2, h, rz_sem.at[p, h, 2])
            spot_wait(p, 7, 1, h, ry_sem.at[p, h, 1])
            write_unit(p, dev(q, 0), h, read_unit(p, dev(q, 0), h) + read_spot(p, 6, 2, h) + read_spot(p, 7, 1, h))
            device, way = (comm.X, 1) if h == 0 else (comm.Y, 2)
            pass_unit(p, dev(q, 0), 7, 2, h, device, way, rf_sem.at[p, h])

    def s5(p, halves=(0, 1)):
        for h in halves:
            total = read_unit(p, me, h)
            if REDUCE_MODE[p] == Z_FIRST:
                spot_wait(p, 7, 0, h, rz_sem.at[p, h, 0])
                spot_wait(p, 7, 2, h, ry_sem.at[p, h, 0])
                total = total + read_spot(p, 7, 0, h) + read_spot(p, 7, 2, h)
            else:
                spot_wait(p, 6, 0, h, rz_sem.at[p, h, 0])
                spot_wait(p, 7, 0, h, ry_sem.at[p, h, 0])
                spot_wait(p, 7, 2, h, rf_sem.at[p, h])
                total = total + read_spot(p, 6, 0, h) + read_spot(p, 7, 0, h) + read_spot(p, 7, 2, h)
            if p >= 4:
                grad_down_ref[48 * h : 48 * h + 48, half * (p - 4) : half * (p - 3)] = total
            else:
                row = jnp.concatenate([total[0:24], total[24:48]], axis=1)
                at = 0
                for c, n in PIECES[p][h]:
                    grad_rows_ref[:, c : c + n] = row[:, at : at + n]
                    at = at + n

    def sums_sent(p):
        z_first = REDUCE_MODE[p] == Z_FIRST
        along_x = along_y = 12 if z_first else 9
        if p == 1:
            along_x, along_y = 14, 10
        for way, n in ((0, 32), (1, along_x), (2, along_y), (3, 6 if z_first else 12)):
            remote(bulk(n), bulk(n), rs_send.at[p, way], rc_sem.at[p, 0, 0], comm.C).wait_send()

    def vec_pack():
        vec_out[...] = jnp.zeros_like(vec_out)
        for i in range(32):
            for r, n in ((0, 128), (1, 128), (2, share_v - 256)):
                at = share_v * i + 128 * r
                vec_out[i // 4, 3 * (i % 4) + r : 3 * (i % 4) + r + 1, 0:n] = vec_grad[0:1, at : at + n]

    def vec_copy(src, dst, n, device):
        return remote(vec_out.at[src], vec_in.at[dst], vs_sem.at[n], vr_sem.at[dst], device)

    def vec_core():
        for q in range(4):
            vec_copy(at_q(q) ^ 1, q, q, comm.C).start()

    def vec_take(dst, target):
        vec_copy(target, dst, 0, comm.C).wait_recv()
        vec_out[target] = vec_out[target] + vec_in[dst]

    def vec_y():
        for q in range(4):
            vec_take(q, at_q(q))
        vec_copy(at_q(3), 5, 4, comm.Y).start()
        vec_copy(at_q(2), 4, 5, comm.Y).start()

    def vec_x():
        vec_take(5, at_q(1))
        vec_copy(at_q(1), 6, 6, comm.X).start()

    def vec_z():
        vec_take(4, b)
        vec_take(6, b)
        vec_copy(b, 8, 7, comm.Z[2]).start()

    def vec_w():
        vec_copy(b, 8, 0, comm.C).wait_recv()
        vec_in[10] = vec_out[b] + vec_in[8]
        remote(vec_in.at[10], vec_in.at[9], vs_sem.at[8], vr_sem.at[9], comm.Z[1]).start()

    def vec_end():
        vec_copy(b, 9, 0, comm.C).wait_recv()
        total = vec_in[9] + vec_in[10]
        mine = total[0:3]
        for zz in range(1, 4):
            mine = jnp.where(z == zz, total[3 * zz : 3 * zz + 3], mine)
        whole = jnp.concatenate([mine[0:1], mine[1:2], mine[2:3, 0 : share_v - 256]], axis=1)
        grad_vec_ref[...] = whole.reshape(share_v)
        for n in range(9):
            vec_copy(b, 0, n, comm.C).wait_send()

    def load(n):
        src, dst = ((rows_hbm, rows_ref), (down_hbm, down_ref), (x_hbm, x_ref))[n]
        return pltpu.make_async_copy(src, dst, local_sem.at[n])

    def start():
        for n in range(3):
            load(n).start()
        place_vectors()
        token_weights()
        comm.barrier()
        load(0).wait()

    def loaded(n):
        load(n).wait()

    def pair_gather():
        for p in range(6):
            sent(p)
        small_own(pairs, 1)
        transpose_into(y_low, y_t)
        transpose_into(ctx, ctx_t)
        small_z(pairs, 1)
        transpose_into(act, act_t, 0, 6)
        small_cross(pairs, 1)
        transpose_into(act, act_t, 6, 12)
        small_end(pairs, 1)

    def finish():
        for p in range(6):
            sums_sent(p)
        pltpu.make_async_copy(work, dx_hbm, local_sem.at[3]).wait()

    def vectors(n):
        (small_own, small_z, small_cross, small_end)[n](vec_all, 0)

    start()
    loaded(1)
    cast(4)
    cast(0)
    ownz(0)
    col(4, 0)
    cast(1)
    fin(1, 0, 0)
    cast(2)
    fin(2, 0, 0)
    own1(1)
    cast(5)
    col(0, 0)
    ownz(1)
    own1(2)
    first(1)
    col(0, 1)
    vectors(0)
    cast(3)
    fold(0)
    col(0, 2)
    loaded(2)
    transpose_into(x_ref, x_t)
    col(3, 0)
    vectors(1)
    fin(1, 1, 0)
    fold(1, 0)
    own1(5)
    fin(1, 1, 1)
    fold(1, 1)
    vectors(2)
    across(0, 2)
    across(0, 0)
    ownz(2)
    across(4, 0)
    first(2)
    vectors(3)
    col(0, 3)
    fin(1, 0, 1)
    last(1, 1)
    fin(1, 2, 0)
    across(0, 1)
    fin(1, 2, 1)
    last(0, 0)
    ownz(3)
    fold(2, 0)
    fin(1, 3, 1)
    across(0, 3)
    last(0, 2)
    fin(1, 3, 0)
    last(0, 1)
    last(4, 0)
    fin(2, 0, 1)
    last(1, 2)
    fold(2, 1)
    across(3, 0)
    last(0, 3)
    fin(2, 1, 0)
    last(1, 3)
    fin(5, 0, 0)
    fin(2, 1, 1)
    gathered(0)
    relayout(0)
    spread_vectors()
    last(2, 0)
    fold(3)
    fin(2, 2, 1)
    col(3, 2)
    last(1, 0)
    ownz(4)
    col(3, 1)
    fin(2, 2, 0)
    ownz(5)
    project(0, 3)
    project(3, 6)
    fin(2, 3, 0)
    attend(0, 0, 2)
    attend(0, 2, 4)
    across(3, 2)
    last(2, 1)
    fin(2, 3, 1)
    gathered(1)
    across(3, 1)
    first(5)
    relayout(1)
    project(6, 9)
    col(3, 3)
    last(2, 2)
    col(4, 1)
    attend(1, 0, 4)
    last(2, 3)
    fold(4)
    attn_out()
    across(3, 3)
    col(4, 2)
    fold(5, 0)
    attn_norm()
    across(4, 1)
    gathered(2)
    last(3, 2)
    relayout(2)
    fin(5, 1, 0)
    fin(5, 0, 1)
    last(3, 0)
    fold(5, 1)
    feed_up(0, 3)
    across(4, 2)
    last(3, 3)
    col(4, 3)
    feed_up(3, 6)
    fin(5, 3, 0)
    last(3, 1)
    last(4, 2)
    last(4, 1)
    across(4, 3)
    gathered(3)
    fin(5, 1, 1)
    fin(5, 2, 1)
    fin(5, 2, 0)
    relayout(3)
    fin(5, 3, 1)
    feed_up(6, 9)
    last(5, 0)
    last(4, 3)
    last(5, 1)
    feed_up(9, 12)
    last(5, 2)
    gathered(4)
    last(5, 3)
    feed_down(0)
    gathered(5)
    feed_down(1)
    down_norm()
    pool()
    pair_gather()
    contrast()
    norm_two_back()
    down_grads(0, 2)
    down_grads(2, 6)
    s1(4, 1)
    down_grads(6, 8)
    grad_act(0, 4)
    s1(4, 0)
    s1(5, 0)
    grad_act(4, 8)
    grad_act(8, 12)
    s2(4)
    s1(5, 1)
    grad_w_rows(2)
    s1(2, 1)
    grad_w_rows(3)
    s1(2, 0)
    s2(5)
    grad_y()
    s2(2)
    s3(4)
    norm_one_back()
    grad_w_rows(1, (1,))
    grad_ctx()
    s1(1, 1, (1,))
    attend_back(0, 0, 2)
    s1(3, 1)
    s3(2)
    s1(3, 0)
    attend_back(0, 2, 4)
    s3(5)
    grad_w_rows(0)
    s2(1, (1,))
    attend_back(1, 0, 4)
    s1(0, 1)
    grad_w_rows(1, (0,))
    s1(1, 0, (1,))
    s2(3)
    s4(2)
    s1(1, 1, (0,))
    s1(1, 0, (0,))
    grad_bias_in()
    vec_pack()
    vec_core()
    s1(0, 0)
    grad_x(0, 1)
    vec_y()
    s2(1, (0,))
    s3(1, (1,))
    s3(3)
    s2(0)
    s4(5)
    s3(1, (0,))
    s5(2)
    s4(1, (1,))
    grad_x(1, 2)
    vec_x()
    s4(4)
    s3(0)
    s5(1, (1,))
    s4(1, (0,))
    grad_x(2, 3)
    vec_z()
    s5(5)
    s4(3)
    s5(4)
    vec_w()
    s4(0)
    s5(1, (0,))
    s5(3)
    vec_end()
    s5(0)
    finish()


def fused_layer(x, tok, groups, counts, rows, down, vec):
    def big(n):
        return pltpu.VMEM((n, 768, 768), bf16)

    scratch = [
        pltpu.VMEM((512, 768), bf16),
        pltpu.VMEM((24, 6144), f32),
        pltpu.VMEM((96, 768), f32),
        big(8),
        big(4),
        big(4),
        big(4),
        big(8),
        pltpu.VMEM((3, 512, 768), bf16),
        pltpu.VMEM((24, 256, 128), bf16),
        pltpu.VMEM((512, 768), bf16),
        pltpu.VMEM((768, 512), bf16),
        pltpu.VMEM((768, 512), bf16),
        pltpu.VMEM((512, 768), bf16),
        pltpu.VMEM((768, 512), bf16),
        pltpu.VMEM((512, 3072), bf16),
        pltpu.VMEM((3072, 512), bf16),
        pltpu.VMEM((512, 3072), bf16),
        pltpu.VMEM((512, 768), f32),
        pltpu.VMEM((512, 768), f32),
        pltpu.VMEM((512, 768), f32),
        pltpu.VMEM((512, 128), f32),
        pltpu.VMEM((512, 128), f32),
        pltpu.VMEM((512, 128), f32),
        pltpu.VMEM((8, 128), f32),
        pltpu.VMEM((8, 128), f32),
        pltpu.VMEM((32, 16, 128), bf16),
        pltpu.VMEM((8, 9216), f32),
        pltpu.VMEM((8, 2304), f32),
        pltpu.VMEM((32, 16, 512), bf16),
        pltpu.VMEM((8, 768), f32),
        pltpu.VMEM((8, 768), f32),
        pltpu.VMEM((8, 128), f32),
        pltpu.VMEM((2, 256, 256), f32),
        pltpu.VMEM((8, 9216), f32),
        pltpu.VMEM((8, 16, 128), f32),
        pltpu.VMEM((12, 16, 128), f32),
    ]
    dma = pltpu.SemaphoreType.DMA
    scratch += [
        dma((4,)), dma((6, 4, 4)), dma((6, 4, 2)), dma((6, 4, 2)), dma((6, 4, 2)), dma((6,)), dma((6, 4)),
        dma((2, 16)), dma((2,)),
        dma((6, 2, 4)), dma((7, 2, 2)), dma((7, 2)), dma((6, 2, 4)), dma((6, 2, 2)), dma((6, 2)), dma((6, 4)),
        dma((12,)), dma((9,)),
    ]
    vmem = pl.BlockSpec(memory_space=pltpu.VMEM)
    smem = pl.BlockSpec(memory_space=pltpu.SMEM)
    anywhere = pl.BlockSpec(memory_space=pl.ANY)
    return pl.pallas_call(
        layer_kernel,
        out_shape=(
            jax.ShapeDtypeStruct((1, 1), f32),
            jax.ShapeDtypeStruct(x.shape, f32),
            jax.ShapeDtypeStruct(rows.shape, f32),
            jax.ShapeDtypeStruct(down.shape, f32),
            jax.ShapeDtypeStruct(vec.shape, f32),
        ),
        in_specs=[anywhere, vmem, smem, smem, anywhere, anywhere, vmem],
        out_specs=(smem, anywhere, vmem, vmem, vmem),
        scratch_shapes=scratch,
        compiler_params=pltpu.CompilerParams(collective_id=0, has_side_effects=True, vmem_limit_bytes=vmem_bytes),
    )(x, tok, groups, counts, rows, down, vec)


def adam_step(master, gradient, moment_one, moment_two, decay, rate):
    mean_new = beta_one * moment_one + (1.0 - beta_one) * gradient
    square_new = beta_two * moment_two + (1.0 - beta_two) * gradient * gradient
    mean_hat = mean_new / (1.0 - beta_one**STEP)
    square_hat = square_new / (1.0 - beta_two**STEP)
    updated = master - rate * (mean_hat / (jnp.sqrt(square_hat) + adam_epsilon) + decay * master)
    return (updated, mean_new, square_new)


def update_kernel(*refs):
    ins, outs, in_bufs, out_bufs = refs[:13], refs[13:23], refs[23:36], refs[36:45]
    in_sem, out_sem = refs[45:]
    loads = [pltpu.make_async_copy(ref, buf, in_sem.at[n]) for n, (ref, buf) in enumerate(zip(ins, in_bufs))]
    stores = [pltpu.make_async_copy(buf, ref, out_sem.at[n]) for n, (buf, ref) in enumerate(zip(in_bufs[:1] + out_bufs, outs))]
    for load in loads:
        load.start()
    loads[0].wait()
    stores[0].start()
    for group, (decay, rate) in enumerate(((decay_rate, learn_rate), (decay_rate, learn_rate), (0.0, vector_rate))):
        for load in loads[1 + 4 * group : 5 + 4 * group]:
            load.wait()
        sources = in_bufs[1 + 4 * group : 5 + 4 * group]
        targets = out_bufs[3 * group : 3 * group + 3]
        if len(sources[0].shape) == 1:
            for target, value in zip(targets, adam_step(*[ref[...] for ref in sources], decay, rate)):
                target[...] = value
        else:

            def body(n, carry, sources=sources, targets=targets, decay=decay, rate=rate):
                part = pl.ds(pl.multiple_of(n * 8, 8), 8)
                for target, value in zip(targets, adam_step(*[ref[part, :] for ref in sources], decay, rate)):
                    target[part, :] = value
                return carry

            lax.fori_loop(0, sources[0].shape[0] // 8, body, 0)
        for store in stores[1 + 3 * group : 4 + 3 * group]:
            store.start()
    for store in stores:
        store.wait()


def update(dx, rows, down, vec):
    news = [jax.ShapeDtypeStruct(dx.shape, f32)]
    for group in (rows, down, vec):
        news += [jax.ShapeDtypeStruct(group[0].shape, f32)] * 3
    anywhere = pl.BlockSpec(memory_space=pl.ANY)
    return pl.pallas_call(
        update_kernel,
        out_shape=tuple(news),
        in_specs=[anywhere] * 13,
        out_specs=(anywhere,) * 10,
        scratch_shapes=[pltpu.VMEM(a.shape, f32) for a in (dx, *rows, *down, *vec)]
        + [pltpu.VMEM(a.shape, f32) for a in news[1:]]
        + [pltpu.SemaphoreType.DMA((13,)), pltpu.SemaphoreType.DMA((10,))],
        compiler_params=pltpu.CompilerParams(vmem_limit_bytes=vmem_bytes),
    )(dx, *rows, *down, *vec)


def on_device_fused(
    embeds, token_mask, groups, counts,
    rows_master, rows_mean, rows_square, down_master, down_mean, down_square,
    vector_master, vector_mean, vector_square,
):
    x = embeds.reshape(-1, embeds.shape[-1])
    loss, dx, rows_grad, down_grad, vec_grad = fused_layer(x, token_mask, groups, counts, rows_master, down_master, vector_master)
    dx, *new = update(
        dx,
        (rows_master, rows_grad, rows_mean, rows_square),
        (down_master, down_grad, down_mean, down_square),
        (vector_master, vec_grad, vector_mean, vector_square),
    )
    return (loss[0, 0], dx.reshape(embeds.shape), *new)


def layer_norm(values, scale_vec, shift_vec):
    centre = values - jnp.mean(values, axis=-1, keepdims=True)
    spread = jnp.mean(centre * centre, axis=-1, keepdims=True)
    return centre * lax.rsqrt(spread + norm_epsilon) * scale_vec + shift_vec


def pool_unit(weights, output):
    summed = jnp.sum(output * weights[:, :, None], axis=1) / jnp.sum(weights, axis=1, keepdims=True)
    return summed * lax.rsqrt(jnp.sum(summed * summed, axis=1, keepdims=True) + unit_epsilon)


def exact_gelu(values):
    return jax.nn.gelu(values, approximate=False)


def softmax_last(values):
    return jax.nn.softmax(values, axis=-1)


def split_vectors(vectors, model_width, hidden):
    extents = [model_width] * 5 + [hidden] + [model_width] * 3
    pieces_out = []
    offset = 0
    for extent in extents:
        pieces_out.append(vectors[offset : offset + extent])
        offset = offset + extent
    return pieces_out


def pair_exps(left_rows, right_rows, left_group, right_group, left_start, right_start):
    scores = score_scale * jnp.dot(left_rows, right_rows.T, precision=highest)
    left_index = left_start + jnp.arange(left_rows.shape[0])
    right_index = right_start + jnp.arange(right_rows.shape[0])
    diagonal = left_index[:, None] == right_index[None, :]
    scores = scores - score_scale * margin * diagonal.astype(jnp.float32)
    same = (left_group[:, None] == right_group[None, :]) & (left_group[:, None] >= 0.0)
    return (jnp.where(same, jnp.exp(scores), 0.0), (diagonal & same).astype(jnp.float32))


def add_sums(own_data, arrived, offset):
    sources, targets, group_own, own_start = own_data
    other_src, other_tgt, other_group = arrived
    row_exp, unused_row = pair_exps(sources, other_tgt, group_own, other_group, own_start, offset)
    col_exp, unused_col = pair_exps(other_src, targets, other_group, group_own, offset, own_start)
    return (jnp.sum(row_exp, axis=1), jnp.sum(col_exp, axis=0))


def add_grads(own_data, loss_coef, arrived, offset):
    sources, targets, group_own, own_start, row_own, col_own = own_data
    other_src, other_tgt, other_group, other_row, other_col = arrived
    row_exp, row_diag = pair_exps(sources, other_tgt, group_own, other_group, own_start, offset)
    row_coef = (
        row_exp / row_own[:, None] + row_exp / other_col[None, :] - 2.0 * row_diag
    ) * loss_coef
    col_exp, col_diag = pair_exps(other_src, targets, other_group, group_own, offset, own_start)
    col_coef = (
        col_exp / other_row[:, None] + col_exp / col_own[None, :] - 2.0 * col_diag
    ) * loss_coef
    grad_src = score_scale * jnp.dot(row_coef, other_tgt, precision=highest)
    grad_tgt = score_scale * jnp.dot(col_coef.T, other_src, precision=highest)
    return (grad_src, grad_tgt)


def on_device_general(
    embeds,
    token_mask,
    groups,
    counts,
    rows_master,
    rows_mean,
    rows_square,
    down_master,
    down_mean,
    down_square,
    vector_master,
    vector_mean,
    vector_square,
):
    slot_count = embeds.shape[0]
    length = embeds.shape[2]
    model_width = embeds.shape[3]
    row_all, down_all, vector_all = (
        lax.all_gather(rows_master.astype(jnp.bfloat16), ("blk", "dp"), axis=0, tiled=True),
        lax.all_gather(down_master.astype(jnp.bfloat16), ("blk", "dp"), axis=0, tiled=True),
        lax.all_gather(vector_master.astype(jnp.bfloat16), ("blk", "dp"), axis=0, tiled=True),
    )
    hidden = down_all.shape[0]
    vectors = vector_all.astype(jnp.float32)
    bias_q, bias_v, bias_o, gain_one, shift_one, bias_up, bias_down, gain_two, shift_two = (
        split_vectors(vectors, model_width, hidden)
    )
    w_attn_in = row_all[:, : 3 * model_width]
    w_attn_out = row_all[:, 3 * model_width : 4 * model_width]
    w_up = row_all[:, 4 * model_width :]
    seq_count = 2 * slot_count
    tokens = seq_count * length
    head_count = model_width // HEAD
    inputs = embeds.reshape(tokens, model_width)
    weights = token_mask.reshape(seq_count, length).astype(jnp.float32)
    key_valid = token_mask.reshape(seq_count, length) > 0
    joined = jnp.concatenate([bias_q, jnp.zeros_like(bias_q), bias_v])
    projected = (jnp.dot(inputs, w_attn_in, preferred_element_type=jnp.float32) + joined).astype(
        jnp.bfloat16
    )
    queries = projected[:, :model_width].reshape(seq_count, length, head_count, HEAD)
    key_part = projected[:, model_width : 2 * model_width].reshape(
        seq_count, length, head_count, HEAD
    )
    values = projected[:, 2 * model_width :].reshape(seq_count, length, head_count, HEAD)
    scores = jnp.einsum(
        "nihe,njhe->nhij", queries, key_part, preferred_element_type=jnp.float32
    ) * HEAD ** (-0.5)
    scores = jnp.where(key_valid[:, None, None, :], scores, -1e30)
    attention, soft_back = jax.vjp(softmax_last, scores)
    attention_low = attention.astype(jnp.bfloat16)
    context = (
        jnp.einsum("nhij,njhe->nihe", attention_low, values, preferred_element_type=jnp.float32)
        .astype(jnp.bfloat16)
        .reshape(tokens, model_width)
    )
    resid_one = (
        inputs.astype(jnp.float32)
        + jnp.dot(context, w_attn_out, preferred_element_type=jnp.float32)
        + bias_o
    )
    normed_full, norm_one_back = jax.vjp(layer_norm, resid_one, 1.0 + gain_one, shift_one)
    normed_one = normed_full.astype(jnp.bfloat16)
    up_pre = jnp.dot(normed_one, w_up, preferred_element_type=jnp.float32) + bias_up
    activated_full, gelu_back = jax.vjp(exact_gelu, up_pre)
    activated = activated_full.astype(jnp.bfloat16)
    resid_two = (
        normed_one.astype(jnp.float32)
        + jnp.dot(activated, down_all, preferred_element_type=jnp.float32)
        + bias_down
    )
    output, norm_two_back = jax.vjp(layer_norm, resid_two, 1.0 + gain_two, shift_two)
    pooled, pool_back = jax.vjp(
        partial(pool_unit, weights), output.reshape(seq_count, length, model_width)
    )
    pooled = pooled.reshape(slot_count, 2, model_width)
    sources = pooled[:, 0]
    targets = pooled[:, 1]
    own_start = lax.axis_index(("blk", "dp")) * slot_count
    valid_slot = jnp.arange(slot_count) < counts[0]
    group_own = jnp.where(valid_slot, groups, -1).astype(jnp.float32)
    pair_total = lax.psum(counts[0].astype(jnp.float32), ("blk", "dp"))
    loss_coef = 0.5 / pair_total
    own_sums = (sources, targets, group_own, own_start)
    row_sum, col_sum = add_sums(
        own_sums,
        (
            lax.all_gather(sources, ("blk", "dp"), axis=0, tiled=True),
            lax.all_gather(targets, ("blk", "dp"), axis=0, tiled=True),
            lax.all_gather(group_own, ("blk", "dp"), axis=0, tiled=True),
        ),
        jnp.int32(0),
    )
    row_safe = jnp.where(valid_slot, row_sum, 1.0)
    col_safe = jnp.where(valid_slot, col_sum, 1.0)
    own_grads = (sources, targets, group_own, own_start, row_safe, col_safe)
    grad_src, grad_tgt = add_grads(
        own_grads,
        loss_coef,
        (
            lax.all_gather(sources, ("blk", "dp"), axis=0, tiled=True),
            lax.all_gather(targets, ("blk", "dp"), axis=0, tiled=True),
            lax.all_gather(group_own, ("blk", "dp"), axis=0, tiled=True),
            lax.all_gather(row_safe, ("blk", "dp"), axis=0, tiled=True),
            lax.all_gather(col_safe, ("blk", "dp"), axis=0, tiled=True),
        ),
        jnp.int32(0),
    )
    positive = score_scale * jnp.sum(sources * targets, axis=1) - score_scale * margin
    loss_terms = jnp.sum(
        jnp.where(valid_slot, jnp.log(row_safe) + jnp.log(col_safe) - 2.0 * positive, 0.0)
    )
    pair_loss = lax.psum(loss_terms, ("blk", "dp")) * loss_coef
    grad_pooled = jnp.stack([grad_src, grad_tgt], axis=1).reshape(seq_count, model_width)
    grad_output = pool_back(grad_pooled)[0].reshape(tokens, model_width)
    grad_resid_two, grad_gain_two, grad_shift_two = norm_two_back(grad_output)
    grad_down_low = grad_resid_two.astype(jnp.bfloat16)
    grad_w_down = jnp.einsum(
        "tf,td->fd", activated, grad_down_low, preferred_element_type=jnp.float32
    )
    grad_bias_down = jnp.sum(grad_down_low.astype(jnp.float32), axis=0)
    grad_act = jnp.einsum("td,fd->tf", grad_down_low, down_all, preferred_element_type=jnp.float32)
    grad_up = gelu_back(grad_act)[0].astype(jnp.bfloat16)
    grad_w_up = jnp.einsum("td,tf->df", normed_one, grad_up, preferred_element_type=jnp.float32)
    grad_bias_up = jnp.sum(grad_up.astype(jnp.float32), axis=0)
    grad_normed = grad_resid_two + jnp.einsum(
        "tf,df->td", grad_up, w_up, preferred_element_type=jnp.float32
    )
    grad_resid_one, grad_gain_one, grad_shift_one = norm_one_back(grad_normed)
    grad_attn_low = grad_resid_one.astype(jnp.bfloat16)
    grad_w_out = jnp.einsum("td,te->de", context, grad_attn_low, preferred_element_type=jnp.float32)
    grad_bias_out = jnp.sum(grad_attn_low.astype(jnp.float32), axis=0)
    grad_context = jnp.einsum(
        "te,de->td", grad_attn_low, w_attn_out, preferred_element_type=jnp.float32
    ).astype(jnp.bfloat16)
    grad_context = grad_context.reshape(seq_count, length, head_count, HEAD)
    grad_attention = jnp.einsum(
        "nihe,njhe->nhij", grad_context, values, preferred_element_type=jnp.float32
    )
    grad_values = jnp.einsum(
        "nhij,nihe->njhe", attention_low, grad_context, preferred_element_type=jnp.float32
    )
    grad_scores = soft_back(grad_attention)[0].astype(jnp.bfloat16)
    grad_queries = jnp.einsum(
        "nhij,njhe->nihe", grad_scores, key_part, preferred_element_type=jnp.float32
    ) * HEAD ** (-0.5)
    grad_keys = jnp.einsum(
        "nhij,nihe->njhe", grad_scores, queries, preferred_element_type=jnp.float32
    ) * HEAD ** (-0.5)
    grad_projected = jnp.concatenate(
        [
            grad_queries.reshape(tokens, model_width),
            grad_keys.reshape(tokens, model_width),
            grad_values.reshape(tokens, model_width),
        ],
        axis=1,
    ).astype(jnp.bfloat16)
    grad_w_in = jnp.einsum("td,te->de", inputs, grad_projected, preferred_element_type=jnp.float32)
    grad_bias_q = jnp.sum(grad_projected[:, :model_width].astype(jnp.float32), axis=0)
    grad_bias_v = jnp.sum(grad_projected[:, 2 * model_width :].astype(jnp.float32), axis=0)
    grad_inputs = grad_resid_one + jnp.einsum(
        "te,de->td", grad_projected, w_attn_in, preferred_element_type=jnp.float32
    )
    grad_vector = jnp.concatenate(
        [
            grad_bias_q,
            grad_bias_v,
            grad_bias_out,
            grad_gain_one,
            grad_shift_one,
            grad_bias_up,
            grad_bias_down,
            grad_gain_two,
            grad_shift_two,
        ]
    )
    rows_share, down_share, vector_share = (
        lax.psum_scatter(
            jnp.concatenate([grad_w_in, grad_w_out, grad_w_up], axis=1),
            ("blk", "dp"),
            scatter_dimension=0,
            tiled=True,
        ),
        lax.psum_scatter(grad_w_down, ("blk", "dp"), scatter_dimension=0, tiled=True),
        lax.psum_scatter(grad_vector, ("blk", "dp"), scatter_dimension=0, tiled=True),
    )
    rows_new = adam_step(rows_master, rows_share, rows_mean, rows_square, decay_rate, learn_rate)
    down_new = adam_step(down_master, down_share, down_mean, down_square, decay_rate, learn_rate)
    vector_new = adam_step(
        vector_master, vector_share, vector_mean, vector_square, 0.0, vector_rate
    )
    embeds_grad = grad_inputs.reshape(slot_count, 2, length, model_width)
    return (
        pair_loss,
        embeds_grad,
        rows_new[0],
        rows_new[1],
        rows_new[2],
        down_new[0],
        down_new[1],
        down_new[2],
        vector_new[0],
        vector_new[1],
        vector_new[2],
    )


def solution(mesh):
    in_specs = (
        P(("blk", "dp"), None, None, None),
        P(("blk", "dp"), None, None),
        P(("blk", "dp")),
        P(("blk", "dp")),
        P(("blk", "dp"), None),
        P(("blk", "dp"), None),
        P(("blk", "dp"), None),
        P(("blk", "dp"), None),
        P(("blk", "dp"), None),
        P(("blk", "dp"), None),
        P(("blk", "dp")),
        P(("blk", "dp")),
        P(("blk", "dp")),
    )
    out_specs = (
        P(),
        P(("blk", "dp"), None, None, None),
        P(("blk", "dp"), None),
        P(("blk", "dp"), None),
        P(("blk", "dp"), None),
        P(("blk", "dp"), None),
        P(("blk", "dp"), None),
        P(("blk", "dp"), None),
        P(("blk", "dp")),
        P(("blk", "dp")),
        P(("blk", "dp")),
    )
    fits = dict(mesh.shape) == {"blk": 8, "dp": 4}
    return jax.shard_map(
        on_device_fused if fits else on_device_general, mesh=mesh, in_specs=in_specs, out_specs=out_specs, check_vma=False
    )
```

```python
from functools import partial

import jax
import jax.numpy as jnp
from jax import lax
from jax.experimental import pallas as pl
from jax.experimental.pallas import tpu as pltpu
from jax.sharding import PartitionSpec as P

HEAD = 64
STEP = 10


score_scale = 32.0
margin = 0.3
beta_one = 0.9
beta_two = 0.999
learn_rate = 0.03
vector_rate = 0.06
decay_rate = 0.01
adam_epsilon = 1e-08
norm_epsilon = 1e-12
unit_epsilon = 1e-06
highest = lax.Precision.HIGHEST

vmem_bytes = 64 * 1024 * 1024 - 65536

f32 = jnp.float32
bf16 = jnp.bfloat16


def dot_nn(a, b, precision=None):
    return lax.dot_general(a, b, (((1,), (0,)), ((), ())), precision=precision, preferred_element_type=f32)


def dot_nt(a, b, precision=None):
    return lax.dot_general(a, b, (((1,), (1,)), ((), ())), precision=precision, preferred_element_type=f32)


def dot_tn(a, b):
    return lax.dot_general(a, b, (((0,), (0,)), ((), ())), preferred_element_type=f32)


Z_FIRST, Z_MID = 0, 1
GATHER_MODE = (Z_FIRST, Z_MID, Z_MID, Z_FIRST, Z_FIRST, Z_MID)
REDUCE_MODE = (Z_FIRST, Z_FIRST, Z_FIRST, Z_MID, Z_MID, Z_MID)

PIECES = (
    (((0, 512), (768, 256)), ((1024, 256), (1536, 512))),
    (((512, 256), (1280, 256), (2048, 256)), ((2304, 768),)),
    (((3072, 768),), ((3840, 768),)),
    (((4608, 768),), ((5376, 768),)),
)


class Comm:
    def __init__(self, depth):
        self.depth = depth
        self.b = lax.axis_index("blk")
        self.z = lax.axis_index("dp")
        b, z = self.b, self.z
        self.X, self.Y, self.C, self.D = (b ^ 2, z), (b ^ 4, z), (b ^ 1, z), (b ^ 6, z)
        self.Z = [(b, z ^ k) for k in range(depth)]
        self.up, self.down = (b, z + 1), (b, z - 1)

    def greet(self):
        sem = pltpu.get_barrier_semaphore()
        friends = [self.X, self.Y, self.C] + self.Z[1:3]
        for friend in friends:
            pl.semaphore_signal(sem, inc=1, device_id=friend, device_id_type=pl.DeviceIdType.MESH)
        return sem, len(friends)


def remote(src, dst, send_sem, recv_sem, device):
    return pltpu.make_async_remote_copy(
        src_ref=src,
        dst_ref=dst,
        send_sem=send_sem,
        recv_sem=recv_sem,
        device_id=device,
        device_id_type=pl.DeviceIdType.MESH,
    )


def layer_kernel(
    x_hbm, tok_ref, group_ref, count_ref, rows_hbm, down_hbm, vec_ref,
    loss_ref, dx_hbm, grad_rows_hbm, grad_down_hbm, grad_vec_ref,
    x_ref, rows_ref, down_ref, grad_rows_ref, grad_down_ref,
    raw, w_attn, w_up, w_down, g_rest,
    qkv, probs, ctx, ctx_t, x_t, y_low, y_t, act, act_t, slope, xhat1, xhat2, work,
    rstd1, rstd2, tok_w, tok_f, tags, vec_all, vec_row, bias_in, pairs, pooled_hat, own_unit, unit_rs, pair_k, vec_grad, vec_out, vec_in,
    local_sem, zsem, xsem, ysem, dsem, csem, ssem,
    small_recv, small_send,
    rc_sem, r1_sem, r2_sem, rz_sem, ry_sem, rf_sem, rs_send,
    vr_sem, vs_sem,
):
    comm = Comm(4)
    b, z = comm.b, comm.z
    me = b * 4 + z
    width = 768
    half = 384
    def at_q(q):
        return b ^ (2 * q)

    def lanes(h):
        return pl.ds(half * h, half)

    def unit(place, i, h):
        ref, base = place
        return ref.at[base + i // 16, pl.ds((i % 16) * 48, 48), lanes(h)]

    def quad(place, n, h):
        ref, base = place
        return ref.at[base + n // 4, pl.ds((n % 4) * 192, 192), lanes(h)]

    def share(p, i, h):
        if p < 4:
            return unit((raw, 2 * p), i, h)
        return w_down.at[i // 8, pl.ds((i % 8) * 96 + 48 * h, 48), lanes(p - 4)]

    def bulk(n):
        return raw.at[0] if n == 32 else raw.at[0, pl.ds(0, 48 * n), pl.ds(0, half)]

    def send(p, i, h, device, way, rsem):
        ref = share(p, i, h)
        remote(ref, ref, ssem.at[p, way], rsem, device).start()

    def arrived(p, i, h, rsem):
        ref = share(p, i, h)
        remote(ref, ref, ssem.at[p, 0], rsem, comm.X).wait_recv()

    def to_core(p, i, h):
        send(p, i, h, comm.C, 2, csem.at[p])

    def both_to_core(p, i):
        if p < 4:
            ref = raw.at[2 * p + i // 16, pl.ds((i % 16) * 48, 48), :]
        else:
            ref = w_down.at[i // 8, pl.ds((i % 8) * 96, 96), lanes(p - 4)]
        remote(ref, ref, ssem.at[p, 2], csem.at[p], comm.C).start()

    def dev(q, k):
        return at_q(q) * 4 + (z ^ k)

    def cast(p):
        for h in range(2):
            if p < 4:
                row = jnp.concatenate([rows_ref[:, c : c + n] for c, n in PIECES[p][h]], axis=1)
                both = jnp.concatenate([row[:, :half], row[:, half:]], axis=0)
            else:
                both = down_ref[48 * h : 48 * h + 48, half * (p - 4) : half * (p - 3)]
            if p < 4:
                raw[2 * p + me // 16, pl.ds((me % 16) * 48, 48), lanes(h)] = both.astype(bf16)
            else:
                w_down[me // 8, pl.ds((me % 8) * 96 + 48 * h, 48), lanes(p - 4)] = both.astype(bf16)

    def along_z(p, q, k, j, h):
        i = dev(q, k)
        if k == 0:
            send(p, i, h, comm.Z[2], 3, zsem.at[p, 2, 2 * j + h])
            send(p, i, h, comm.Z[1], 3, zsem.at[p, 1, 2 * j + h])
        else:
            send(p, i, h, comm.Z[1], 3, zsem.at[p, 3, 2 * j + h])

    def place(j, h):
        return 0 if j == 0 else (1 if h == 0 else 2)

    def ownz(p):
        for h in range(2):
            along_z(p, 0, 0, 0, h)

    def own1(p):
        send(p, dev(0, 0), 0, comm.X, 0, dsem.at[p, 0, 0])
        send(p, dev(0, 0), 1, comm.Y, 1, dsem.at[p, 0, 1])

    def first(p):
        for h in range(2):
            q = place(1, h)
            arrived(p, dev(q, 0), h, dsem.at[p, 0, h])
            along_z(p, q, 0, 1, h)

    def fold(p, j=0):
        for h in range(2):
            q = place(j, h)
            arrived(p, dev(q, 2), h, zsem.at[p, 2, 2 * j + h])
            along_z(p, q, 2, j, h)

    def z_wait(p, k, j):
        if k in (1, 3):
            for h in range(2):
                arrived(p, dev(place(j, h), k), h, zsem.at[p, k, 2 * j + h])

    def col(p, k):
        z_wait(p, k, 0)
        i = dev(0, k)
        send(p, i, 0, comm.X, 0, xsem.at[p, k, 0])
        send(p, i, 1, comm.Y, 1, ysem.at[p, k, 1])
        send(p, i, 1, comm.X, 0, xsem.at[p, k, 1])
        send(p, i, 0, comm.Y, 1, ysem.at[p, k, 0])
        both_to_core(p, i)

    def across(p, k):
        i = dev(1, k)
        arrived(p, i, 0, xsem.at[p, k, 0])
        send(p, i, 0, comm.Y, 1, dsem.at[p, k, 0])
        to_core(p, i, 0)
        i = dev(2, k)
        arrived(p, i, 1, ysem.at[p, k, 1])
        send(p, i, 1, comm.X, 0, dsem.at[p, k, 1])
        to_core(p, i, 1)

    def fin(p, k, j):
        z_wait(p, k, j)
        i = dev(place(j, 0), k)
        send(p, i, 0, comm.Y, 1, ysem.at[p, k, j])
        to_core(p, i, 0)
        i = dev(place(j, 1), k)
        send(p, i, 1, comm.X, 0, xsem.at[p, k, j])
        to_core(p, i, 1)

    def last(p, k):
        if GATHER_MODE[p] == Z_FIRST:
            rest = ((1, 1, xsem.at[p, k, 1]), (2, 0, ysem.at[p, k, 0]), (3, 0, dsem.at[p, k, 0]), (3, 1, dsem.at[p, k, 1]))
        else:
            rest = ((2, 0, ysem.at[p, k, 0]), (1, 1, xsem.at[p, k, 0]), (3, 0, ysem.at[p, k, 1]), (3, 1, xsem.at[p, k, 1]))
        for q, h, sem in rest:
            arrived(p, dev(q, k), h, sem)
            if q < 3:
                to_core(p, dev(q, k), h)
        both_to_core(p, dev(3, k))

    def gathered(p):
        remote(bulk(32), bulk(32), ssem.at[p, 0], csem.at[p], comm.X).wait_recv()

    def sent(p):
        z_first = GATHER_MODE[p] == Z_FIRST
        for way, n in ((0, 12 if z_first else 9), (1, 12 if z_first else 9), (2, 32), (3, 6 if z_first else 12)):
            remote(bulk(n), bulk(n), ssem.at[p, way], csem.at[p], comm.X).wait_send()

    def small_send_one(ref, n, i, device, rsem):
        block = ref.at[pl.ds(i, 1)]
        remote(block, block, small_send.at[n], rsem, device).start()

    def small_wait(ref, n, i, rsem):
        block = ref.at[pl.ds(i, 1)]
        remote(block, block, small_send.at[n], rsem, comm.X).wait_recv()

    def small_plane(ref, n, k):
        i = dev(0, k)
        small_send_one(ref, n, i, comm.D, small_recv.at[n, 12 + k])
        small_send_one(ref, n, i, comm.X, small_recv.at[n, 4 + k])
        small_send_one(ref, n, i, comm.Y, small_recv.at[n, 8 + k])
        small_send_one(ref, n, i, comm.C, small_recv.at[n, 0])

    def small_own(ref, n):
        for k in (3, 2, 1):
            small_send_one(ref, n, me, comm.Z[k], small_recv.at[n, k])
        small_plane(ref, n, 0)

    def small_z(ref, n):
        for k in (1, 2, 3):
            small_wait(ref, n, dev(0, k), small_recv.at[n, k])
            small_plane(ref, n, k)

    def small_cross(ref, n):
        for k in range(4):
            for q in (1, 2, 3):
                small_wait(ref, n, dev(q, k), small_recv.at[n, 4 * q + k])
                small_send_one(ref, n, dev(q, k), comm.C, small_recv.at[n, 0])

    def small_end(ref, n):
        many = ref.at[pl.ds(0, 16)]
        remote(many, many, small_send.at[n], small_recv.at[n, 0], comm.X).wait_recv()
        many = ref.at[pl.ds(0, 31)]
        remote(many, many, small_send.at[n], small_recv.at[n, 0], comm.X).wait_send()

    def vec(offset, size=width):
        return vec_row[0:1, offset : offset + size]

    bias_q, bias_v, bias_o, gain1_at, shift1_at, bias_up_at = 0, width, 2 * width, 3 * width, 4 * width, 5 * width
    bias_down_at, gain2_at, shift2_at = 9 * width, 10 * width, 11 * width

    share_v = 288

    def place_vectors():
        v = vec_ref[...].reshape(1, share_v)
        tail = jnp.concatenate([v[:, 256:share_v], jnp.zeros((1, 384 - share_v), f32)], axis=1)
        tile = jnp.concatenate([v[:, 0:128], v[:, 128:256], tail, jnp.zeros((13, 128), f32)], axis=0)
        vec_all[pl.ds(me, 1)] = tile.astype(bf16).reshape(1, 16, 128)

    def spread_vectors():
        for i in range(32):
            tile = vec_all[i].astype(f32)
            for r, n in ((0, 128), (1, 128), (2, share_v - 256)):
                at = share_v * i + 128 * r
                vec_row[0:1, at : at + n] = tile[r : r + 1, 0:n]
        bias_in[...] = jnp.zeros_like(bias_in)
        bias_in[0:1, 0:512] = vec(bias_q, 512)
        bias_in[0:1, 1024:1536] = vec(bias_v, 512)
        bias_in[0:1, 1536:1792] = vec(bias_q + 512, 256)
        bias_in[0:1, 2048:2304] = vec(bias_v + 512, 256)

    def relayout(p):
        target, chunk = (w_attn, 2 * p) if p < 2 else (w_up, 2 * p - 4)

        def body(j, carry):
            for h in range(2):
                even = raw[2 * p + j // 8, pl.ds((j % 8) * 96, 48), lanes(h)].astype(f32)
                odd = raw[2 * p + j // 8, pl.ds((j % 8) * 96 + 48, 48), lanes(h)].astype(f32)
                for q in range(2):
                    rows = jnp.concatenate([even[24 * q : 24 * q + 24], odd[24 * q : 24 * q + 24]], axis=0)
                    target[chunk + h, pl.ds(j * 48, 48), lanes(q)] = rows.astype(bf16)
            return carry

        lax.fori_loop(0, 16, body, 0)

    def transpose_into(source, target, lo=0, hi=3):
        def body(j, carry):
            at = pl.multiple_of(j * 256, 256)
            target[pl.ds(at, 256), :] = jnp.transpose(source[:, pl.ds(at, 256)])
            return carry

        lax.fori_loop(lo, hi, body, 0)

    def token_weights():
        lane = lax.broadcasted_iota(jnp.int32, (1, 128), 1)
        left = (lane < 64).astype(f32)
        tok = tok_ref[...].astype(f32)
        tok_f[0:4, :] = jnp.concatenate([tok[:, 0, :], tok[:, 1, :]], axis=1)
        for p in range(4):
            m = tok_f[p : p + 1, :]
            n0 = jnp.sum(m * left, axis=1, keepdims=True)
            n1 = jnp.sum(m * (1.0 - left), axis=1, keepdims=True)
            w = m / (left * n0 + (1.0 - left) * n1)
            tok_w[128 * p : 128 * p + 128, :] = jnp.transpose(jnp.broadcast_to(w, (128, 128)))
        row = lax.broadcasted_iota(jnp.int32, (8, 128), 0) % 4
        tag = jnp.full((8, 128), -1.0, f32)
        for s in range(4):
            tag = jnp.where((row == s) & (count_ref[0] > s), group_ref[s].astype(f32), tag)
        tags[...] = tag

    def project(lo, hi):
        def body(t, carry):
            c, n = t // 3, t % 3
            at = pl.multiple_of(n * 256, 256)
            bias = bias_in[0:1, pl.ds(pl.multiple_of(t * 256, 256), 256)]
            out = dot_nn(x_ref[...], w_attn[c, :, pl.ds(at, 256)]) + bias
            qkv[c, :, pl.ds(at, 256)] = out.astype(bf16)
            return carry

        lax.fori_loop(lo, hi, body, 0)

    def head_places(hp):
        if hp < 4:
            key = (0, 512 + 128 * hp) if hp < 2 else (1, 128 * hp - 256)
            return (0, 128 * hp), key, (1, 256 + 128 * hp)
        return (2, 128 * hp - 512), (2, 128 * hp - 256), (2, 128 * hp)

    lane128 = lax.broadcasted_iota(jnp.int32, (128, 128), 1)
    row128 = lax.broadcasted_iota(jnp.int32, (128, 128), 0)
    even_half = lane128 < 64

    def split_heads(v):
        zero = jnp.zeros_like(v)
        return jnp.concatenate([jnp.where(even_half, v, zero), jnp.where(even_half, zero, v)], axis=0)

    def attend(group, lo, hi):
        def body(p, carry):
            rows = pl.ds(pl.multiple_of(p * 128, 128), 128)
            m = tok_f[pl.ds(p, 1), :]
            same = (row128 < 64) == (lane128 < 64)
            open_one = same & (jnp.broadcast_to(m, (128, 128)) > 0.0)
            block = jnp.where(open_one, 0.0, -1e30)
            block = jnp.concatenate([block, block], axis=0)
            for hp in range(4) if group == 0 else range(4, 6):
                q2, k2, v2 = [qkv[c, rows, at : at + 128] for c, at in head_places(hp)]
                s = dot_nt(split_heads(q2), k2) * HEAD ** (-0.5) + block
                e = jnp.exp(s - jnp.max(s, axis=1, keepdims=True))
                a = (e * (1.0 / jnp.sum(e, axis=1, keepdims=True))).astype(bf16)
                probs[p * 6 + hp] = a
                wide = jnp.concatenate([a[:128], a[128:]], axis=1)
                ctx[rows, 128 * hp : 128 * hp + 128] = dot_nn(wide, split_heads(v2)).astype(bf16)
            return carry

        lax.fori_loop(lo, hi, body, 0, unroll=1 + group)

    def norm_rows(i, source_fn, hat, rstd, emit):
        rows = pl.ds(pl.multiple_of(i * 64, 64), 64)
        h = source_fn(rows)
        centre = h - jnp.mean(h, axis=1, keepdims=True)
        r = lax.rsqrt(jnp.mean(centre * centre, axis=1, keepdims=True) + norm_epsilon)
        xh = centre * r
        hat[rows, :] = xh
        rstd[rows, :] = jnp.broadcast_to(r, (64, 128))
        if emit is not None:
            emit(rows, xh)

    def attn_out():
        def body(n, carry):
            at = pl.multiple_of(n * 256, 256)
            work[:, pl.ds(at, 256)] = dot_nn(ctx[...], w_attn[3, :, pl.ds(at, 256)])
            return carry

        lax.fori_loop(0, 3, body, 0)

    def attn_norm():
        def source(rows):
            return x_ref[rows, :].astype(f32) + work[rows, :] + vec(bias_o)

        def emit(rows, xh):
            y_low[rows, :] = (xh * (1.0 + vec(gain1_at)) + vec(shift1_at)).astype(bf16)

        def norm(i, carry):
            norm_rows(i, source, xhat1, rstd1, emit)
            return carry

        lax.fori_loop(0, 8, norm, 0, unroll=2)

    def feed_up(lo, hi):
        def body(t, carry):
            c, n = t // 3, t % 3
            at = pl.multiple_of(n * 256, 256)
            to = pl.multiple_of(t * 256, 256)
            work[:, pl.ds(0, 256)] = dot_nn(y_low[...], w_up[c, :, pl.ds(at, 256)])
            bias = vec_row[0:1, pl.ds(pl.multiple_of(bias_up_at + to, 256), 256)]

            def rows_of(i, inner):
                rows = pl.ds(pl.multiple_of(i * 32, 32), 32)
                v = work[rows, 0:256] + bias
                cdf = 0.5 * (1.0 + lax.erf(v * 0.7071067811865476))
                dens = jnp.exp(v * v * -0.5) * 0.3989422804014327
                act[rows, pl.ds(to, 256)] = (v * cdf).astype(bf16)
                slope[rows, pl.ds(to, 256)] = (cdf + v * dens).astype(bf16)
                return inner

            lax.fori_loop(0, 16, rows_of, 0, unroll=4)
            return carry

        lax.fori_loop(lo, hi, body, 0)

    def feed_down(s):
        def body(n, carry):
            at = pl.multiple_of(n * 256, 256)
            total = dot_nn(act[:, 0:width], w_down[0, :, pl.ds(at, 256)])
            for c in range(1, 4):
                total = total + dot_nn(act[:, c * width : (c + 1) * width], w_down[c, :, pl.ds(at, 256)])
            work[:, pl.ds(at, 256)] = total
            return carry

        lax.fori_loop(s, 2 * s + 1, body, 0)

    def down_norm():
        def source(rows):
            return y_low[rows, :].astype(f32) + work[rows, :] + vec(bias_down_at)

        def norm(i, carry):
            norm_rows(i, source, xhat2, rstd2, None)
            rows = pl.ds(pl.multiple_of(i * 64, 64), 64)
            got = jnp.sum(xhat2[rows, :] * tok_w[rows, 0:1], axis=0, keepdims=True)
            at = i // 2 + 4 * (i % 2)
            pooled_hat[pl.ds(at, 1), :] = got
            return carry

        lax.fori_loop(0, 8, norm, 0, unroll=2)

    def pool():
        e = pooled_hat[...] * (1.0 + vec(gain2_at)) + vec(shift2_at)
        r = lax.rsqrt(jnp.sum(e * e, axis=1, keepdims=True) + unit_epsilon)
        unit_rs[...] = jnp.broadcast_to(r, (8, 128))
        n = e * r
        own_unit[...] = n
        packed = jnp.concatenate([n[:, :half], n[:, half:]], axis=0)
        tag = jnp.concatenate([tags[...], tags[...]], axis=0)
        pairs[pl.ds(me, 1)] = jnp.concatenate([packed, tag], axis=1).astype(bf16).reshape(1, 16, 512)

    def contrast():
        total = 256
        every = pairs[...].astype(f32)
        left = every[:, 0:8, 0:half].reshape(total, half).astype(bf16)
        right = every[:, 8:16, 0:half].reshape(total, half).astype(bf16)
        tag = every[:, 0:8, half : half + 128].reshape(total, 128)
        tag_row = jnp.concatenate([jnp.transpose(tag[0:128])[0:1], jnp.transpose(tag[128:256])[0:1]], axis=1)
        s = (dot_nt(left, left) + dot_nt(right, right)) * score_scale
        i = lax.broadcasted_iota(jnp.int32, (total, total), 0)
        j = lax.broadcasted_iota(jnp.int32, (total, total), 1)
        opposite = (i & 4) != (j & 4)
        diagonal = (i ^ j) == 4
        s = s - jnp.where(diagonal, score_scale * margin, 0.0)
        same = (tag[:, 0:1] == tag_row) & (tag_row >= 0.0) & opposite
        e = jnp.where(same, jnp.exp(jnp.where(same, s, 0.0)), 0.0)
        valid = tag_row >= 0.0
        sums = jnp.where(valid, jnp.sum(e, axis=0, keepdims=True), 1.0)
        coef = 1.0 / jnp.sum(valid.astype(f32))
        positive = jnp.sum(jnp.where(diagonal & same, s, 0.0))
        loss = (jnp.sum(jnp.where(valid, jnp.log(sums), 0.0)) - positive) * coef
        loss_ref[0, 0] = loss
        pair_k[0] = e
        pair_k[1] = jnp.where(diagonal & same, 2.0, 0.0)
        own_rows = pl.ds(pl.multiple_of(me * 8, 8), 8)
        e_own = pair_k[0, own_rows, :]
        r_own = jnp.sum(e_own, axis=1, keepdims=True)
        r_own = jnp.where(tags[:, 0:1] >= 0.0, r_own, 1.0)
        k = (e_own / r_own + e_own / sums - pair_k[1, own_rows, :]) * (coef * score_scale)
        high = k.astype(bf16)
        low = (k - high.astype(f32)).astype(bf16)
        both = jnp.concatenate([high, low], axis=0)
        dn = jnp.concatenate([dot_nn(both, left), dot_nn(both, right)], axis=1)
        dn = dn[0:8] + dn[8:16]
        n = own_unit[...]
        de = unit_rs[:, 0:1] * (dn - n * jnp.sum(n * dn, axis=1, keepdims=True))
        vec_grad[0:1, gain2_at : gain2_at + width] = jnp.sum(de * pooled_hat[...], axis=0, keepdims=True)
        vec_grad[0:1, shift2_at : shift2_at + width] = jnp.sum(de, axis=0, keepdims=True)
        pooled_hat[...] = de

    def norm_two_back():
        def body(i, carry):
            rows = pl.ds(pl.multiple_of(i * 64, 64), 64)
            de = pooled_hat[pl.ds(i // 2 + 4 * (i % 2), 1), :]
            dg = de * (1.0 + vec(gain2_at))
            xh = xhat2[rows, :]
            m1 = jnp.mean(dg, axis=1, keepdims=True)
            m2 = jnp.mean(dg * xh, axis=1, keepdims=True)
            dz = (rstd2[rows, 0:1] * tok_w[rows, 0:1]) * (dg - m1 - xh * m2)
            low = dz.astype(bf16)
            xhat2[rows, :] = dz
            y_low[rows, :] = low
            return carry + jnp.sum(low.astype(f32), axis=0, keepdims=True)

        vec_grad[0:1, bias_down_at : bias_down_at + width] = lax.fori_loop(0, 8, body, jnp.zeros((1, width), f32), unroll=2)

    g_places = ((w_up, 0), (w_up, 2), (g_rest, 4), (g_rest, 6), (g_rest, 0), (g_rest, 2))
    box_places = ((w_down, 0), (w_down, 2), (raw, 4), (raw, 6), (raw, 0), (raw, 2))

    def grad_w_down(blk):
        out = dot_nn(act_t[pl.ds(pl.multiple_of(blk * 384, 128), 384), :], y_low[...])
        for part in range(2):
            for zz in range(4):
                for h in range(2):
                    rows = out[96 * zz + 48 * h : 96 * zz + 48 * h + 48, half * part : half * part + half]
                    at = pl.multiple_of((blk % 4) * 192 + 48 * zz, 16)
                    g_rest[2 * part + blk // 4, pl.ds(at, 48), lanes(h)] = rows.astype(bf16)

    def down_grads(lo, hi):
        def body(n, carry):
            q = 3 - n // 2
            grad_w_down(at_q(q) ^ (1 - n % 2))

            @pl.when(n % 2 == 0)
            def _():
                for p in (4, 5):
                    for h in range(2):
                        core_send(p, h, q)

            return carry

        lax.fori_loop(lo, hi, body, 0)

    def grad_act(lo, hi):
        def body(t, carry):
            c, n = t // 3, t % 3
            to = pl.multiple_of(t * 256, 256)
            work[:, 0:256] = dot_nt(y_low[...], w_down[c, pl.ds(pl.multiple_of(n * 256, 256), 256), :])

            def rows_of(i, total):
                rows = pl.ds(pl.multiple_of(i * 64, 64), 64)
                low = (work[rows, 0:256] * slope[rows, pl.ds(to, 256)].astype(f32)).astype(bf16)
                act[rows, pl.ds(to, 256)] = low
                return total + jnp.sum(low.astype(f32), axis=0, keepdims=True)

            sums = lax.fori_loop(0, 8, rows_of, jnp.zeros((1, 256), f32), unroll=2)
            vec_grad[0:1, pl.ds(pl.multiple_of(bias_up_at + to, 256), 256)] = sums
            return carry

        lax.fori_loop(lo, hi, body, 0)

    def store_units(p, h, m, out):
        ref, base = g_places[p]
        for d in range(16):
            rows = out[24 * d : 24 * d + 24]
            both = jnp.concatenate([rows[:, :half], rows[:, half:]], axis=0)
            ref[base + m, 48 * d : 48 * d + 48, lanes(h)] = both.astype(bf16)

    def grad_w_rows(p, halves=(0, 1)):
        def body(n, carry):
            m = (b // 4) ^ (1 - n)
            rows = pl.ds(pl.multiple_of(m * 384, 128), 384)
            for h in halves:
                if p >= 2:
                    out = dot_nn(y_t[rows, :], act[:, (2 * p - 4 + h) * width : (2 * p - 3 + h) * width])
                elif (p, h) == (1, 1):
                    out = dot_nn(ctx_t[rows, :], y_low[...])
                else:
                    out = dot_nn(x_t[rows, :], qkv[2 * p + h])
                store_units(p, h, m, out)
                for q in (1, 0):
                    core_send(p, h, 2 * (1 - n) + q)
            return carry

        lax.fori_loop(0, 2, body, 0)

    def grad_y():
        def body(n, carry):
            at = pl.multiple_of(n * 256, 256)
            total = xhat2[:, pl.ds(at, 256)]
            for c in range(4):
                total = total + dot_nt(act[:, c * width : (c + 1) * width], w_up[c, pl.ds(at, 256), :])
            work[:, pl.ds(at, 256)] = total
            return carry

        lax.fori_loop(0, 3, body, 0)

    def norm_one_back():
        def body(i, carry):
            rows = pl.ds(pl.multiple_of(i * 64, 64), 64)
            dy = work[rows, :]
            xh = xhat1[rows, :]
            dg = dy * (1.0 + vec(gain1_at))
            m1 = jnp.mean(dg, axis=1, keepdims=True)
            m2 = jnp.mean(dg * xh, axis=1, keepdims=True)
            dh = rstd1[rows, 0:1] * (dg - m1 - xh * m2)
            low = dh.astype(bf16)
            work[rows, :] = dh
            y_low[rows, :] = low
            gain, shift, bias = carry
            return (
                gain + jnp.sum(dy * xh, axis=0, keepdims=True),
                shift + jnp.sum(dy, axis=0, keepdims=True),
                bias + jnp.sum(low.astype(f32), axis=0, keepdims=True),
            )

        zero = jnp.zeros((1, width), f32)
        gain, shift, bias = lax.fori_loop(0, 8, body, (zero, zero, zero), unroll=2)
        vec_grad[0:1, gain1_at : gain1_at + width] = gain
        vec_grad[0:1, shift1_at : shift1_at + width] = shift
        vec_grad[0:1, bias_o : bias_o + width] = bias

    def grad_ctx():
        def body(n, carry):
            at = pl.multiple_of(n * 256, 256)
            ctx[:, pl.ds(at, 256)] = dot_nt(y_low[...], w_attn[3, pl.ds(at, 256), :]).astype(bf16)
            return carry

        lax.fori_loop(0, 3, body, 0)

    def attend_back(group, lo, hi):
        def body(p, carry):
            rows = pl.ds(pl.multiple_of(p * 128, 128), 128)
            for hp in range(4) if group == 0 else range(4, 6):
                places = head_places(hp)
                q2, k2, v2 = [qkv[c, rows, at : at + 128] for c, at in places]
                dc = split_heads(ctx[rows, 128 * hp : 128 * hp + 128])
                a = probs[p * 6 + hp]
                af = a.astype(f32)
                da = dot_nt(dc, v2)
                ds = (af * (da - jnp.sum(af * da, axis=1, keepdims=True))).astype(bf16)
                dv = dot_tn(a, dc)
                wide = jnp.concatenate([ds[:128], ds[128:]], axis=1)
                dq = dot_nn(wide, split_heads(k2)) * HEAD ** (-0.5)
                dk = dot_tn(ds, split_heads(q2)) * HEAD ** (-0.5)
                for (c, at), d in zip(places, (dq, dk, dv)):
                    qkv[c, rows, at : at + 128] = d.astype(bf16)
            return carry

        lax.fori_loop(lo, hi, body, 0, unroll=1 + group)

    def grad_bias_in():
        def body(i, carry):
            rows = pl.ds(pl.multiple_of(i * 64, 64), 64)
            return tuple(have + jnp.sum(qkv[c, rows, :].astype(f32), axis=0, keepdims=True) for c, have in enumerate(carry))

        zero = jnp.zeros((1, width), f32)
        first_sum, second_sum, third_sum = lax.fori_loop(0, 8, body, (zero, zero, zero))
        vec_grad[0:1, bias_q : bias_q + 512] = first_sum[:, 0:512]
        vec_grad[0:1, bias_q + 512 : bias_q + 768] = third_sum[:, 0:256]
        vec_grad[0:1, bias_v : bias_v + 512] = second_sum[:, 256:768]
        vec_grad[0:1, bias_v + 512 : bias_v + 768] = third_sum[:, 512:768]

    def dx_copy(n):
        at = pl.ds(pl.multiple_of(n * 256, 256), 256)
        return pltpu.make_async_copy(work.at[:, at], dx_hbm.at[:, at], local_sem.at[3])

    def grad_x(lo, hi):
        def body(n, carry):
            at = pl.multiple_of(n * 256, 256)
            total = work[:, pl.ds(at, 256)]
            for c in range(3):
                total = total + dot_nt(qkv[c], w_attn[c, pl.ds(at, 256), :])
            work[:, pl.ds(at, 256)] = total
            return carry

        lax.fori_loop(lo, hi, body, 0)
        for n in range(lo, hi):
            dx_copy(n).start()

    def spot(p, run, u, h):
        ref, base = box_places[p]
        return ref.at[base + run // 4, pl.ds((run % 4) * 192 + 48 * u, 48), lanes(h)]

    def core_send(p, h, q):
        remote(
            quad(g_places[p], at_q(q) ^ 1, h), quad(box_places[p], q, h), rs_send.at[p, 0], rc_sem.at[p, h, q], comm.C
        ).start()

    def run_wait(p, run, h, sem):
        ref = quad(box_places[p], run, h)
        remote(ref, ref, rs_send.at[p, 0], sem, comm.C).wait_recv()

    def spot_wait(p, run, u, h, sem):
        ref = spot(p, run, u, h)
        remote(ref, ref, rs_send.at[p, 0], sem, comm.C).wait_recv()

    def add_in(p, h, q, runs, lo=0, hi=4):
        target, base = g_places[p]
        box, box_base = box_places[p]
        blk = at_q(q)

        def body(i, carry):
            at = pl.multiple_of((blk % 4) * 192 + i * 48, 16)
            total = target[base + blk // 4, pl.ds(at, 48), lanes(h)].astype(f32)
            for run in runs:
                from_at = pl.multiple_of((run % 4) * 192 + i * 48, 16)
                total = total + box[box_base + run // 4, pl.ds(from_at, 48), lanes(h)].astype(f32)
            target[base + blk // 4, pl.ds(at, 48), lanes(h)] = total.astype(bf16)
            return carry

        lax.fori_loop(lo, hi, body, 0)

    def read_unit(p, i, h):
        ref, base = g_places[p]
        return ref[base + i // 16, pl.ds((i % 16) * 48, 48), lanes(h)].astype(f32)

    def read_spot(p, run, u, h):
        ref, base = box_places[p]
        return ref[base + run // 4, (run % 4) * 192 + 48 * u : (run % 4) * 192 + 48 * u + 48, lanes(h)].astype(f32)

    def write_unit(p, i, h, total):
        ref, base = g_places[p]
        ref[base + i // 16, pl.ds((i % 16) * 48, 48), lanes(h)] = total.astype(bf16)

    def pass_run(p, h, q, run, sem):
        along_y = (run < 6) == (h == 0)
        device, way = (comm.Y, 2) if along_y else (comm.X, 1)
        remote(quad(g_places[p], at_q(q), h), quad(box_places[p], run, h), rs_send.at[p, way], sem, device).start()

    def pass_unit(p, i, run, u, h, device, way, sem):
        remote(unit(g_places[p], i, h), spot(p, run, u, h), rs_send.at[p, way], sem, device).start()

    def pair_of(place, n, u, h):
        ref, base = place
        return ref.at[base + n // 4, pl.ds((n % 4) * 192 + 96 * u, 96), lanes(h)]

    def pair_wait(p, run, u, sem):
        ref = pair_of(box_places[p], run, u, 0)
        remote(ref, ref, rs_send.at[p, 0], sem, comm.C).wait_recv()

    def pass_pair(p, q, u, run, along_y, sem):
        device, way = (comm.Y, 2) if along_y else (comm.X, 1)
        remote(pair_of(g_places[p], at_q(q), u, 0), pair_of(box_places[p], run, u, 0), rs_send.at[p, way], sem, device).start()

    def split_s1(p, side):
        for q in (3,) if side == 1 else (2, 1):
            run_wait(p, q, 0, rc_sem.at[p, 0, q])
        for u in range(2):
            q = 3 if side == 1 else 2 - u
            add_in(p, 0, q, (q,), 2 * u, 2 * u + 2)
            pass_pair(p, q, u, 4 + side, u == 0, r1_sem.at[6, u, side])

    def split_s2(p):
        for u in range(2):
            pair_wait(p, 5, u, r1_sem.at[6, u, 1])
            add_in(p, 0, 1 + u, (1 + u, 5), 2 * u, 2 * u + 2)
            pass_pair(p, 1 + u, u, 6, u == 1, r2_sem.at[6, u])

    def split_s3(p):
        run_wait(p, 0, 0, rc_sem.at[p, 0, 0])
        for u in range(2):
            pair_wait(p, 4, u, r1_sem.at[6, u, 0])
            pair_wait(p, 6, u, r2_sem.at[6, u])
        add_in(p, 0, 0, (0, 4, 6))
        pass_unit(p, dev(0, 1), 7, 0, 0, comm.Z[1], 3, rz_sem.at[p, 0, 0])
        pass_unit(p, dev(0, 3), 7, 1, 0, comm.Z[1], 3, rz_sem.at[p, 0, 1])

    def s1(p, side, halves=(0, 1)):
        if halves == (0,):
            return split_s1(p, side)
        for h in halves:
            q = 3 if side == 1 else 2 - h
            run_wait(p, q, h, rc_sem.at[p, h, q])
            add_in(p, h, q, (q,))
            pass_run(p, h, q, 4 + side, r1_sem.at[p, h, side])

    def s2(p, halves=(0, 1)):
        if halves == (0,):
            return split_s2(p)
        if REDUCE_MODE[p] == Z_FIRST:
            for h in halves:
                q = 1 + h
                run_wait(p, q, h, rc_sem.at[p, h, q])
                run_wait(p, 5, h, r1_sem.at[p, h, 1])
                add_in(p, h, q, (q, 5))
                pass_run(p, h, q, 6, r2_sem.at[p, h])
            return
        for h in halves:
            for j, q in enumerate((0, 1 + h)):
                run_wait(p, q, h, rc_sem.at[p, h, q])
                run_wait(p, 4 + j, h, r1_sem.at[p, h, j])
                add_in(p, h, q, (q, 4 + j))
                pass_unit(p, dev(q, 1), 6, 2 * j, h, comm.Z[1], 3, rz_sem.at[p, h, 2 * j])
                pass_unit(p, dev(q, 3), 6, 2 * j + 1, h, comm.Z[1], 3, rz_sem.at[p, h, 2 * j + 1])

    def s3(p, halves=(0, 1)):
        if halves == (0,):
            return split_s3(p)
        if REDUCE_MODE[p] == Z_FIRST:
            for h in halves:
                run_wait(p, 0, h, rc_sem.at[p, h, 0])
                run_wait(p, 4, h, r1_sem.at[p, h, 0])
                run_wait(p, 6, h, r2_sem.at[p, h])
                add_in(p, h, 0, (0, 4, 6))
                pass_unit(p, dev(0, 1), 7, 0, h, comm.Z[1], 3, rz_sem.at[p, h, 0])
                pass_unit(p, dev(0, 3), 7, 1, h, comm.Z[1], 3, rz_sem.at[p, h, 1])
            return
        for h in halves:
            for j, q in enumerate((0, 1 + h)):
                spot_wait(p, 6, 2 * j + 1, h, rz_sem.at[p, h, 2 * j + 1])
                write_unit(p, dev(q, 2), h, read_unit(p, dev(q, 2), h) + read_spot(p, 6, 2 * j + 1, h))
                pass_unit(p, dev(q, 2), 7, j, h, comm.Z[2], 3, ry_sem.at[p, h, j])

    def s4(p, halves=(0, 1)):
        if REDUCE_MODE[p] == Z_FIRST:
            for h in halves:
                spot_wait(p, 7, 1, h, rz_sem.at[p, h, 1])
                write_unit(p, dev(0, 2), h, read_unit(p, dev(0, 2), h) + read_spot(p, 7, 1, h))
                pass_unit(p, dev(0, 2), 7, 2, h, comm.Z[2], 3, ry_sem.at[p, h, 0])
            return
        for h in halves:
            q = 1 + h
            spot_wait(p, 6, 2, h, rz_sem.at[p, h, 2])
            spot_wait(p, 7, 1, h, ry_sem.at[p, h, 1])
            write_unit(p, dev(q, 0), h, read_unit(p, dev(q, 0), h) + read_spot(p, 6, 2, h) + read_spot(p, 7, 1, h))
            device, way = (comm.X, 1) if h == 0 else (comm.Y, 2)
            pass_unit(p, dev(q, 0), 7, 2, h, device, way, rf_sem.at[p, h])

    def s5(p, halves=(0, 1)):
        for h in halves:
            total = read_unit(p, me, h)
            if REDUCE_MODE[p] == Z_FIRST:
                spot_wait(p, 7, 0, h, rz_sem.at[p, h, 0])
                spot_wait(p, 7, 2, h, ry_sem.at[p, h, 0])
                total = total + read_spot(p, 7, 0, h) + read_spot(p, 7, 2, h)
            else:
                spot_wait(p, 6, 0, h, rz_sem.at[p, h, 0])
                spot_wait(p, 7, 0, h, ry_sem.at[p, h, 0])
                spot_wait(p, 7, 2, h, rf_sem.at[p, h])
                total = total + read_spot(p, 6, 0, h) + read_spot(p, 7, 0, h) + read_spot(p, 7, 2, h)
            if p >= 4:
                grad_down_ref[48 * h : 48 * h + 48, half * (p - 4) : half * (p - 3)] = total
                at = (pl.ds(48 * h, 48), lanes(p - 4))
                pltpu.make_async_copy(grad_down_ref.at[at], grad_down_hbm.at[at], local_sem.at[5]).start()
            else:
                row = jnp.concatenate([total[0:24], total[24:48]], axis=1)
                at = 0
                for c, n in PIECES[p][h]:
                    grad_rows_ref[:, c : c + n] = row[:, at : at + n]
                    columns = pl.ds(c, n)
                    pltpu.make_async_copy(grad_rows_ref.at[:, columns], grad_rows_hbm.at[:, columns], local_sem.at[4]).start()
                    at = at + n

    def sums_sent(p):
        z_first = REDUCE_MODE[p] == Z_FIRST
        along_x = along_y = 12 if z_first else 9
        if p == 1:
            along_x, along_y = 14, 10
        for way, n in ((0, 32), (1, along_x), (2, along_y), (3, 6 if z_first else 12)):
            remote(bulk(n), bulk(n), rs_send.at[p, way], rc_sem.at[p, 0, 0], comm.C).wait_send()

    def vec_pack():
        vec_out[...] = jnp.zeros_like(vec_out)
        for i in range(32):
            for r, n in ((0, 128), (1, 128), (2, share_v - 256)):
                at = share_v * i + 128 * r
                vec_out[i // 4, 3 * (i % 4) + r : 3 * (i % 4) + r + 1, 0:n] = vec_grad[0:1, at : at + n]

    def vec_copy(src, dst, n, device):
        return remote(vec_out.at[src], vec_in.at[dst], vs_sem.at[n], vr_sem.at[dst], device)

    def vec_core():
        for q in range(4):
            vec_copy(at_q(q) ^ 1, q, q, comm.C).start()

    def vec_take(dst, target):
        vec_copy(target, dst, 0, comm.C).wait_recv()
        vec_out[target] = vec_out[target] + vec_in[dst]

    def vec_y():
        for q in range(4):
            vec_take(q, at_q(q))
        vec_copy(at_q(3), 5, 4, comm.Y).start()
        vec_copy(at_q(2), 4, 5, comm.Y).start()

    def vec_x():
        vec_take(5, at_q(1))
        vec_copy(at_q(1), 6, 6, comm.X).start()

    def vec_z():
        vec_take(4, b)
        vec_take(6, b)
        vec_copy(b, 8, 7, comm.Z[2]).start()

    def vec_w():
        vec_copy(b, 8, 0, comm.C).wait_recv()
        vec_in[10] = vec_out[b] + vec_in[8]
        remote(vec_in.at[10], vec_in.at[9], vs_sem.at[8], vr_sem.at[9], comm.Z[1]).start()

    def vec_end():
        vec_copy(b, 9, 0, comm.C).wait_recv()
        total = vec_in[9] + vec_in[10]
        mine = total[0:3]
        for zz in range(1, 4):
            mine = jnp.where(z == zz, total[3 * zz : 3 * zz + 3], mine)
        whole = jnp.concatenate([mine[0:1], mine[1:2], mine[2:3, 0 : share_v - 256]], axis=1)
        grad_vec_ref[...] = whole.reshape(share_v)
        for n in range(9):
            vec_copy(b, 0, n, comm.C).wait_send()

    def load(n):
        src, dst = ((rows_hbm, rows_ref), (down_hbm, down_ref), (x_hbm, x_ref))[n]
        return pltpu.make_async_copy(src, dst, local_sem.at[n])

    def start():
        for n in (0, 1, 2):
            load(n).start()
        sem, friends = comm.greet()
        place_vectors()
        token_weights()
        load(0).wait()
        for p in range(4):
            cast(p)
        load(1).wait()
        cast(4)
        cast(5)
        pl.semaphore_wait(sem, friends)

    def loaded(n):
        load(n).wait()

    def pair_gather():
        small_own(pairs, 1)
        transpose_into(y_low, y_t)
        transpose_into(ctx, ctx_t)
        small_z(pairs, 1)
        transpose_into(act, act_t, 0, 6)
        small_cross(pairs, 1)
        transpose_into(act, act_t, 6, 12)
        small_end(pairs, 1)

    def finish():
        for p in range(6):
            sums_sent(p)
        pltpu.make_async_copy(work, dx_hbm, local_sem.at[3]).wait()
        pltpu.make_async_copy(grad_rows_ref, grad_rows_hbm, local_sem.at[4]).wait()
        pltpu.make_async_copy(grad_down_ref, grad_down_hbm, local_sem.at[5]).wait()

    def vectors(n):
        (small_own, small_z, small_cross, small_end)[n](vec_all, 0)

    start()
    ownz(0)
    col(4, 0)
    fin(1, 0, 0)
    fin(2, 0, 0)
    own1(1)
    col(0, 0)
    ownz(1)
    own1(2)
    first(1)
    col(0, 1)
    vectors(0)
    fold(0)
    col(0, 2)
    loaded(2)
    transpose_into(x_ref, x_t)
    col(3, 0)
    vectors(1)
    fin(1, 1, 0)
    fold(1, 0)
    own1(5)
    fin(1, 1, 1)
    fold(1, 1)
    vectors(2)
    across(0, 2)
    across(0, 0)
    ownz(2)
    across(4, 0)
    first(2)
    vectors(3)
    col(0, 3)
    fin(1, 0, 1)
    last(1, 1)
    fin(1, 2, 0)
    across(0, 1)
    fin(1, 2, 1)
    last(0, 0)
    ownz(3)
    fold(2, 0)
    fin(1, 3, 1)
    across(0, 3)
    last(0, 2)
    fin(1, 3, 0)
    last(0, 1)
    last(4, 0)
    fin(2, 0, 1)
    last(1, 2)
    fold(2, 1)
    across(3, 0)
    last(0, 3)
    fin(2, 1, 0)
    last(1, 3)
    fin(5, 0, 0)
    fin(2, 1, 1)
    gathered(0)
    relayout(0)
    spread_vectors()
    last(2, 0)
    fold(3)
    fin(2, 2, 1)
    col(3, 2)
    last(1, 0)
    ownz(4)
    col(3, 1)
    fin(2, 2, 0)
    ownz(5)
    project(0, 3)
    project(3, 6)
    fin(2, 3, 0)
    attend(0, 0, 2)
    attend(0, 2, 4)
    across(3, 2)
    last(2, 1)
    fin(2, 3, 1)
    gathered(1)
    across(3, 1)
    first(5)
    relayout(1)
    project(6, 9)
    col(3, 3)
    last(2, 2)
    col(4, 1)
    attend(1, 0, 4)
    last(2, 3)
    fold(4)
    attn_out()
    across(3, 3)
    col(4, 2)
    fold(5, 0)
    attn_norm()
    across(4, 1)
    gathered(2)
    last(3, 2)
    relayout(2)
    fin(5, 1, 0)
    fin(5, 0, 1)
    last(3, 0)
    fold(5, 1)
    feed_up(0, 3)
    across(4, 2)
    last(3, 3)
    col(4, 3)
    feed_up(3, 6)
    fin(5, 3, 0)
    last(3, 1)
    last(4, 2)
    last(4, 1)
    across(4, 3)
    gathered(3)
    fin(5, 1, 1)
    fin(5, 2, 1)
    fin(5, 2, 0)
    relayout(3)
    fin(5, 3, 1)
    feed_up(6, 9)
    last(5, 0)
    last(4, 3)
    last(5, 1)
    feed_up(9, 12)
    sent(0)
    sent(1)
    sent(2)
    sent(3)
    last(5, 2)
    gathered(4)
    last(5, 3)
    feed_down(0)
    gathered(5)
    sent(4)
    feed_down(1)
    down_norm()
    sent(5)
    pool()
    pair_gather()
    contrast()
    norm_two_back()
    down_grads(0, 2)
    down_grads(2, 6)
    s1(4, 1)
    down_grads(6, 8)
    grad_act(0, 4)
    s1(4, 0)
    s1(5, 0)
    grad_act(4, 8)
    grad_act(8, 12)
    s2(4)
    s1(5, 1)
    grad_w_rows(2)
    s1(2, 1)
    grad_w_rows(3)
    s1(2, 0)
    s2(5)
    grad_y()
    s2(2)
    s3(4)
    norm_one_back()
    grad_w_rows(1, (1,))
    grad_ctx()
    s1(1, 1, (1,))
    attend_back(0, 0, 2)
    s1(3, 1)
    s3(2)
    s1(3, 0)
    attend_back(0, 2, 4)
    s3(5)
    grad_w_rows(0)
    s2(1, (1,))
    attend_back(1, 0, 4)
    s1(0, 1)
    grad_w_rows(1, (0,))
    s1(1, 0, (1,))
    s1(1, 1, (0,))
    s2(3)
    s4(2)
    s1(1, 0, (0,))
    grad_bias_in()
    vec_pack()
    vec_core()
    s1(0, 0)
    grad_x(0, 1)
    vec_y()
    s2(1, (0,))
    s3(1, (1,))
    s3(3)
    s2(0)
    s4(5)
    s3(1, (0,))
    s5(2)
    s4(1, (1,))
    grad_x(1, 2)
    vec_x()
    s4(4)
    s3(0)
    grad_x(2, 3)
    vec_z()
    s5(5)
    s4(3)
    s5(4)
    s5(1, (1,))
    s4(1, (0,))
    vec_w()
    s4(0)
    s5(1, (0,))
    s5(3)
    vec_end()
    s5(0)
    finish()


def fused_layer(x, tok, groups, counts, rows, down, vec):
    def big(n):
        return pltpu.VMEM((n, 768, 768), bf16)

    scratch = [
        pltpu.VMEM((512, 768), bf16),
        pltpu.VMEM((24, 6144), f32),
        pltpu.VMEM((96, 768), f32),
        pltpu.VMEM((24, 6144), f32),
        pltpu.VMEM((96, 768), f32),
        big(8),
        big(4),
        big(4),
        big(4),
        big(8),
        pltpu.VMEM((3, 512, 768), bf16),
        pltpu.VMEM((24, 256, 128), bf16),
        pltpu.VMEM((512, 768), bf16),
        pltpu.VMEM((768, 512), bf16),
        pltpu.VMEM((768, 512), bf16),
        pltpu.VMEM((512, 768), bf16),
        pltpu.VMEM((768, 512), bf16),
        pltpu.VMEM((512, 3072), bf16),
        pltpu.VMEM((3072, 512), bf16),
        pltpu.VMEM((512, 3072), bf16),
        pltpu.VMEM((512, 768), f32),
        pltpu.VMEM((512, 768), f32),
        pltpu.VMEM((512, 768), f32),
        pltpu.VMEM((512, 128), f32),
        pltpu.VMEM((512, 128), f32),
        pltpu.VMEM((512, 128), f32),
        pltpu.VMEM((8, 128), f32),
        pltpu.VMEM((8, 128), f32),
        pltpu.VMEM((32, 16, 128), bf16),
        pltpu.VMEM((8, 9216), f32),
        pltpu.VMEM((8, 2304), f32),
        pltpu.VMEM((32, 16, 512), bf16),
        pltpu.VMEM((8, 768), f32),
        pltpu.VMEM((8, 768), f32),
        pltpu.VMEM((8, 128), f32),
        pltpu.VMEM((2, 256, 256), f32),
        pltpu.VMEM((8, 9216), f32),
        pltpu.VMEM((8, 16, 128), f32),
        pltpu.VMEM((12, 16, 128), f32),
    ]
    dma = pltpu.SemaphoreType.DMA
    scratch += [
        dma((6,)), dma((6, 4, 4)), dma((6, 4, 2)), dma((6, 4, 2)), dma((6, 4, 2)), dma((6,)), dma((6, 4)),
        dma((2, 16)), dma((2,)),
        dma((6, 2, 4)), dma((7, 2, 2)), dma((7, 2)), dma((6, 2, 4)), dma((6, 2, 2)), dma((6, 2)), dma((6, 4)),
        dma((12,)), dma((9,)),
    ]
    vmem = pl.BlockSpec(memory_space=pltpu.VMEM)
    smem = pl.BlockSpec(memory_space=pltpu.SMEM)
    anywhere = pl.BlockSpec(memory_space=pl.ANY)
    return pl.pallas_call(
        layer_kernel,
        out_shape=(
            jax.ShapeDtypeStruct((1, 1), f32),
            jax.ShapeDtypeStruct(x.shape, f32),
            jax.ShapeDtypeStruct(rows.shape, f32),
            jax.ShapeDtypeStruct(down.shape, f32),
            jax.ShapeDtypeStruct(vec.shape, f32),
        ),
        in_specs=[anywhere, vmem, smem, smem, anywhere, anywhere, vmem],
        out_specs=(smem, anywhere, anywhere, anywhere, vmem),
        scratch_shapes=scratch,
        compiler_params=pltpu.CompilerParams(collective_id=0, has_side_effects=True, vmem_limit_bytes=vmem_bytes),
    )(x, tok, groups, counts, rows, down, vec)


def adam_step(master, gradient, moment_one, moment_two, decay, rate):
    mean_new = beta_one * moment_one + (1.0 - beta_one) * gradient
    square_new = beta_two * moment_two + (1.0 - beta_two) * gradient * gradient
    mean_hat = mean_new / (1.0 - beta_one**STEP)
    square_hat = square_new / (1.0 - beta_two**STEP)
    updated = master - rate * (mean_hat / (jnp.sqrt(square_hat) + adam_epsilon) + decay * master)
    return (updated, mean_new, square_new)


def update_kernel(*refs):
    ins, outs, in_bufs, out_bufs = refs[:13], refs[13:23], refs[23:36], refs[36:45]
    in_sem, out_sem = refs[45:]
    loads = [pltpu.make_async_copy(ref, buf, in_sem.at[n]) for n, (ref, buf) in enumerate(zip(ins, in_bufs))]
    stores = [pltpu.make_async_copy(buf, ref, out_sem.at[n]) for n, (buf, ref) in enumerate(zip(in_bufs[:1] + out_bufs, outs))]
    for load in loads:
        load.start()
    loads[0].wait()
    stores[0].start()
    for group, (decay, rate) in enumerate(((decay_rate, learn_rate), (decay_rate, learn_rate), (0.0, vector_rate))):
        for load in loads[1 + 4 * group : 5 + 4 * group]:
            load.wait()
        sources = in_bufs[1 + 4 * group : 5 + 4 * group]
        targets = out_bufs[3 * group : 3 * group + 3]
        if len(sources[0].shape) == 1:
            for target, value in zip(targets, adam_step(*[ref[...] for ref in sources], decay, rate)):
                target[...] = value
        else:

            def body(n, carry, sources=sources, targets=targets, decay=decay, rate=rate):
                part = pl.ds(pl.multiple_of(n * 8, 8), 8)
                for target, value in zip(targets, adam_step(*[ref[part, :] for ref in sources], decay, rate)):
                    target[part, :] = value
                return carry

            lax.fori_loop(0, sources[0].shape[0] // 8, body, 0)
        for store in stores[1 + 3 * group : 4 + 3 * group]:
            store.start()
    for store in stores:
        store.wait()


def update(dx, rows, down, vec):
    news = [jax.ShapeDtypeStruct(dx.shape, f32)]
    for group in (rows, down, vec):
        news += [jax.ShapeDtypeStruct(group[0].shape, f32)] * 3
    anywhere = pl.BlockSpec(memory_space=pl.ANY)
    return pl.pallas_call(
        update_kernel,
        out_shape=tuple(news),
        in_specs=[anywhere] * 13,
        out_specs=(anywhere,) * 10,
        scratch_shapes=[pltpu.VMEM(a.shape, f32) for a in (dx, *rows, *down, *vec)]
        + [pltpu.VMEM(a.shape, f32) for a in news[1:]]
        + [pltpu.SemaphoreType.DMA((13,)), pltpu.SemaphoreType.DMA((10,))],
        compiler_params=pltpu.CompilerParams(vmem_limit_bytes=vmem_bytes),
    )(dx, *rows, *down, *vec)


def on_device_fused(
    embeds, token_mask, groups, counts,
    rows_master, rows_mean, rows_square, down_master, down_mean, down_square,
    vector_master, vector_mean, vector_square,
):
    x = embeds.reshape(-1, embeds.shape[-1])
    loss, dx, rows_grad, down_grad, vec_grad = fused_layer(x, token_mask, groups, counts, rows_master, down_master, vector_master)
    dx, *new = update(
        dx,
        (rows_master, rows_grad, rows_mean, rows_square),
        (down_master, down_grad, down_mean, down_square),
        (vector_master, vec_grad, vector_mean, vector_square),
    )
    return (loss[0, 0], dx.reshape(embeds.shape), *new)


def layer_norm(values, scale_vec, shift_vec):
    centre = values - jnp.mean(values, axis=-1, keepdims=True)
    spread = jnp.mean(centre * centre, axis=-1, keepdims=True)
    return centre * lax.rsqrt(spread + norm_epsilon) * scale_vec + shift_vec


def pool_unit(weights, output):
    summed = jnp.sum(output * weights[:, :, None], axis=1) / jnp.sum(weights, axis=1, keepdims=True)
    return summed * lax.rsqrt(jnp.sum(summed * summed, axis=1, keepdims=True) + unit_epsilon)


def exact_gelu(values):
    return jax.nn.gelu(values, approximate=False)


def softmax_last(values):
    return jax.nn.softmax(values, axis=-1)


def split_vectors(vectors, model_width, hidden):
    extents = [model_width] * 5 + [hidden] + [model_width] * 3
    pieces_out = []
    offset = 0
    for extent in extents:
        pieces_out.append(vectors[offset : offset + extent])
        offset = offset + extent
    return pieces_out


def pair_exps(left_rows, right_rows, left_group, right_group, left_start, right_start):
    scores = score_scale * jnp.dot(left_rows, right_rows.T, precision=highest)
    left_index = left_start + jnp.arange(left_rows.shape[0])
    right_index = right_start + jnp.arange(right_rows.shape[0])
    diagonal = left_index[:, None] == right_index[None, :]
    scores = scores - score_scale * margin * diagonal.astype(jnp.float32)
    same = (left_group[:, None] == right_group[None, :]) & (left_group[:, None] >= 0.0)
    return (jnp.where(same, jnp.exp(scores), 0.0), (diagonal & same).astype(jnp.float32))


def add_sums(own_data, arrived, offset):
    sources, targets, group_own, own_start = own_data
    other_src, other_tgt, other_group = arrived
    row_exp, unused_row = pair_exps(sources, other_tgt, group_own, other_group, own_start, offset)
    col_exp, unused_col = pair_exps(other_src, targets, other_group, group_own, offset, own_start)
    return (jnp.sum(row_exp, axis=1), jnp.sum(col_exp, axis=0))


def add_grads(own_data, loss_coef, arrived, offset):
    sources, targets, group_own, own_start, row_own, col_own = own_data
    other_src, other_tgt, other_group, other_row, other_col = arrived
    row_exp, row_diag = pair_exps(sources, other_tgt, group_own, other_group, own_start, offset)
    row_coef = (
        row_exp / row_own[:, None] + row_exp / other_col[None, :] - 2.0 * row_diag
    ) * loss_coef
    col_exp, col_diag = pair_exps(other_src, targets, other_group, group_own, offset, own_start)
    col_coef = (
        col_exp / other_row[:, None] + col_exp / col_own[None, :] - 2.0 * col_diag
    ) * loss_coef
    grad_src = score_scale * jnp.dot(row_coef, other_tgt, precision=highest)
    grad_tgt = score_scale * jnp.dot(col_coef.T, other_src, precision=highest)
    return (grad_src, grad_tgt)


def on_device_general(
    embeds,
    token_mask,
    groups,
    counts,
    rows_master,
    rows_mean,
    rows_square,
    down_master,
    down_mean,
    down_square,
    vector_master,
    vector_mean,
    vector_square,
):
    slot_count = embeds.shape[0]
    length = embeds.shape[2]
    model_width = embeds.shape[3]
    row_all, down_all, vector_all = (
        lax.all_gather(rows_master.astype(jnp.bfloat16), ("blk", "dp"), axis=0, tiled=True),
        lax.all_gather(down_master.astype(jnp.bfloat16), ("blk", "dp"), axis=0, tiled=True),
        lax.all_gather(vector_master.astype(jnp.bfloat16), ("blk", "dp"), axis=0, tiled=True),
    )
    hidden = down_all.shape[0]
    vectors = vector_all.astype(jnp.float32)
    bias_q, bias_v, bias_o, gain_one, shift_one, bias_up, bias_down, gain_two, shift_two = (
        split_vectors(vectors, model_width, hidden)
    )
    w_attn_in = row_all[:, : 3 * model_width]
    w_attn_out = row_all[:, 3 * model_width : 4 * model_width]
    w_up = row_all[:, 4 * model_width :]
    seq_count = 2 * slot_count
    tokens = seq_count * length
    head_count = model_width // HEAD
    inputs = embeds.reshape(tokens, model_width)
    weights = token_mask.reshape(seq_count, length).astype(jnp.float32)
    key_valid = token_mask.reshape(seq_count, length) > 0
    joined = jnp.concatenate([bias_q, jnp.zeros_like(bias_q), bias_v])
    projected = (jnp.dot(inputs, w_attn_in, preferred_element_type=jnp.float32) + joined).astype(
        jnp.bfloat16
    )
    queries = projected[:, :model_width].reshape(seq_count, length, head_count, HEAD)
    key_part = projected[:, model_width : 2 * model_width].reshape(
        seq_count, length, head_count, HEAD
    )
    values = projected[:, 2 * model_width :].reshape(seq_count, length, head_count, HEAD)
    scores = jnp.einsum(
        "nihe,njhe->nhij", queries, key_part, preferred_element_type=jnp.float32
    ) * HEAD ** (-0.5)
    scores = jnp.where(key_valid[:, None, None, :], scores, -1e30)
    attention, soft_back = jax.vjp(softmax_last, scores)
    attention_low = attention.astype(jnp.bfloat16)
    context = (
        jnp.einsum("nhij,njhe->nihe", attention_low, values, preferred_element_type=jnp.float32)
        .astype(jnp.bfloat16)
        .reshape(tokens, model_width)
    )
    resid_one = (
        inputs.astype(jnp.float32)
        + jnp.dot(context, w_attn_out, preferred_element_type=jnp.float32)
        + bias_o
    )
    normed_full, norm_one_back = jax.vjp(layer_norm, resid_one, 1.0 + gain_one, shift_one)
    normed_one = normed_full.astype(jnp.bfloat16)
    up_pre = jnp.dot(normed_one, w_up, preferred_element_type=jnp.float32) + bias_up
    activated_full, gelu_back = jax.vjp(exact_gelu, up_pre)
    activated = activated_full.astype(jnp.bfloat16)
    resid_two = (
        normed_one.astype(jnp.float32)
        + jnp.dot(activated, down_all, preferred_element_type=jnp.float32)
        + bias_down
    )
    output, norm_two_back = jax.vjp(layer_norm, resid_two, 1.0 + gain_two, shift_two)
    pooled, pool_back = jax.vjp(
        partial(pool_unit, weights), output.reshape(seq_count, length, model_width)
    )
    pooled = pooled.reshape(slot_count, 2, model_width)
    sources = pooled[:, 0]
    targets = pooled[:, 1]
    own_start = lax.axis_index(("blk", "dp")) * slot_count
    valid_slot = jnp.arange(slot_count) < counts[0]
    group_own = jnp.where(valid_slot, groups, -1).astype(jnp.float32)
    pair_total = lax.psum(counts[0].astype(jnp.float32), ("blk", "dp"))
    loss_coef = 0.5 / pair_total
    own_sums = (sources, targets, group_own, own_start)
    row_sum, col_sum = add_sums(
        own_sums,
        (
            lax.all_gather(sources, ("blk", "dp"), axis=0, tiled=True),
            lax.all_gather(targets, ("blk", "dp"), axis=0, tiled=True),
            lax.all_gather(group_own, ("blk", "dp"), axis=0, tiled=True),
        ),
        jnp.int32(0),
    )
    row_safe = jnp.where(valid_slot, row_sum, 1.0)
    col_safe = jnp.where(valid_slot, col_sum, 1.0)
    own_grads = (sources, targets, group_own, own_start, row_safe, col_safe)
    grad_src, grad_tgt = add_grads(
        own_grads,
        loss_coef,
        (
            lax.all_gather(sources, ("blk", "dp"), axis=0, tiled=True),
            lax.all_gather(targets, ("blk", "dp"), axis=0, tiled=True),
            lax.all_gather(group_own, ("blk", "dp"), axis=0, tiled=True),
            lax.all_gather(row_safe, ("blk", "dp"), axis=0, tiled=True),
            lax.all_gather(col_safe, ("blk", "dp"), axis=0, tiled=True),
        ),
        jnp.int32(0),
    )
    positive = score_scale * jnp.sum(sources * targets, axis=1) - score_scale * margin
    loss_terms = jnp.sum(
        jnp.where(valid_slot, jnp.log(row_safe) + jnp.log(col_safe) - 2.0 * positive, 0.0)
    )
    pair_loss = lax.psum(loss_terms, ("blk", "dp")) * loss_coef
    grad_pooled = jnp.stack([grad_src, grad_tgt], axis=1).reshape(seq_count, model_width)
    grad_output = pool_back(grad_pooled)[0].reshape(tokens, model_width)
    grad_resid_two, grad_gain_two, grad_shift_two = norm_two_back(grad_output)
    grad_down_low = grad_resid_two.astype(jnp.bfloat16)
    grad_w_down = jnp.einsum(
        "tf,td->fd", activated, grad_down_low, preferred_element_type=jnp.float32
    )
    grad_bias_down = jnp.sum(grad_down_low.astype(jnp.float32), axis=0)
    grad_act = jnp.einsum("td,fd->tf", grad_down_low, down_all, preferred_element_type=jnp.float32)
    grad_up = gelu_back(grad_act)[0].astype(jnp.bfloat16)
    grad_w_up = jnp.einsum("td,tf->df", normed_one, grad_up, preferred_element_type=jnp.float32)
    grad_bias_up = jnp.sum(grad_up.astype(jnp.float32), axis=0)
    grad_normed = grad_resid_two + jnp.einsum(
        "tf,df->td", grad_up, w_up, preferred_element_type=jnp.float32
    )
    grad_resid_one, grad_gain_one, grad_shift_one = norm_one_back(grad_normed)
    grad_attn_low = grad_resid_one.astype(jnp.bfloat16)
    grad_w_out = jnp.einsum("td,te->de", context, grad_attn_low, preferred_element_type=jnp.float32)
    grad_bias_out = jnp.sum(grad_attn_low.astype(jnp.float32), axis=0)
    grad_context = jnp.einsum(
        "te,de->td", grad_attn_low, w_attn_out, preferred_element_type=jnp.float32
    ).astype(jnp.bfloat16)
    grad_context = grad_context.reshape(seq_count, length, head_count, HEAD)
    grad_attention = jnp.einsum(
        "nihe,njhe->nhij", grad_context, values, preferred_element_type=jnp.float32
    )
    grad_values = jnp.einsum(
        "nhij,nihe->njhe", attention_low, grad_context, preferred_element_type=jnp.float32
    )
    grad_scores = soft_back(grad_attention)[0].astype(jnp.bfloat16)
    grad_queries = jnp.einsum(
        "nhij,njhe->nihe", grad_scores, key_part, preferred_element_type=jnp.float32
    ) * HEAD ** (-0.5)
    grad_keys = jnp.einsum(
        "nhij,nihe->njhe", grad_scores, queries, preferred_element_type=jnp.float32
    ) * HEAD ** (-0.5)
    grad_projected = jnp.concatenate(
        [
            grad_queries.reshape(tokens, model_width),
            grad_keys.reshape(tokens, model_width),
            grad_values.reshape(tokens, model_width),
        ],
        axis=1,
    ).astype(jnp.bfloat16)
    grad_w_in = jnp.einsum("td,te->de", inputs, grad_projected, preferred_element_type=jnp.float32)
    grad_bias_q = jnp.sum(grad_projected[:, :model_width].astype(jnp.float32), axis=0)
    grad_bias_v = jnp.sum(grad_projected[:, 2 * model_width :].astype(jnp.float32), axis=0)
    grad_inputs = grad_resid_one + jnp.einsum(
        "te,de->td", grad_projected, w_attn_in, preferred_element_type=jnp.float32
    )
    grad_vector = jnp.concatenate(
        [
            grad_bias_q,
            grad_bias_v,
            grad_bias_out,
            grad_gain_one,
            grad_shift_one,
            grad_bias_up,
            grad_bias_down,
            grad_gain_two,
            grad_shift_two,
        ]
    )
    rows_share, down_share, vector_share = (
        lax.psum_scatter(
            jnp.concatenate([grad_w_in, grad_w_out, grad_w_up], axis=1),
            ("blk", "dp"),
            scatter_dimension=0,
            tiled=True,
        ),
        lax.psum_scatter(grad_w_down, ("blk", "dp"), scatter_dimension=0, tiled=True),
        lax.psum_scatter(grad_vector, ("blk", "dp"), scatter_dimension=0, tiled=True),
    )
    rows_new = adam_step(rows_master, rows_share, rows_mean, rows_square, decay_rate, learn_rate)
    down_new = adam_step(down_master, down_share, down_mean, down_square, decay_rate, learn_rate)
    vector_new = adam_step(
        vector_master, vector_share, vector_mean, vector_square, 0.0, vector_rate
    )
    embeds_grad = grad_inputs.reshape(slot_count, 2, length, model_width)
    return (
        pair_loss,
        embeds_grad,
        rows_new[0],
        rows_new[1],
        rows_new[2],
        down_new[0],
        down_new[1],
        down_new[2],
        vector_new[0],
        vector_new[1],
        vector_new[2],
    )


def solution(mesh):
    in_specs = (
        P(("blk", "dp"), None, None, None),
        P(("blk", "dp"), None, None),
        P(("blk", "dp")),
        P(("blk", "dp")),
        P(("blk", "dp"), None),
        P(("blk", "dp"), None),
        P(("blk", "dp"), None),
        P(("blk", "dp"), None),
        P(("blk", "dp"), None),
        P(("blk", "dp"), None),
        P(("blk", "dp")),
        P(("blk", "dp")),
        P(("blk", "dp")),
    )
    out_specs = (
        P(),
        P(("blk", "dp"), None, None, None),
        P(("blk", "dp"), None),
        P(("blk", "dp"), None),
        P(("blk", "dp"), None),
        P(("blk", "dp"), None),
        P(("blk", "dp"), None),
        P(("blk", "dp"), None),
        P(("blk", "dp")),
        P(("blk", "dp")),
        P(("blk", "dp")),
    )
    fits = dict(mesh.shape) == {"blk": 8, "dp": 4}
    return jax.shard_map(
        on_device_fused if fits else on_device_general, mesh=mesh, in_specs=in_specs, out_specs=out_specs, check_vma=False
    )
```

```python
from functools import partial

import jax
import jax.numpy as jnp
from jax import lax
from jax.experimental import pallas as pl
from jax.experimental.pallas import tpu as pltpu
from jax.sharding import PartitionSpec as P

HEAD = 64
STEP = 10


score_scale = 32.0
margin = 0.3
beta_one = 0.9
beta_two = 0.999
learn_rate = 0.03
vector_rate = 0.06
decay_rate = 0.01
adam_epsilon = 1e-08
norm_epsilon = 1e-12
unit_epsilon = 1e-06
highest = lax.Precision.HIGHEST

vmem_bytes = 64 * 1024 * 1024 - 65536

f32 = jnp.float32
bf16 = jnp.bfloat16


def dot_nn(a, b, precision=None):
    return lax.dot_general(a, b, (((1,), (0,)), ((), ())), precision=precision, preferred_element_type=f32)


def dot_nt(a, b, precision=None):
    return lax.dot_general(a, b, (((1,), (1,)), ((), ())), precision=precision, preferred_element_type=f32)


def dot_tn(a, b):
    return lax.dot_general(a, b, (((0,), (0,)), ((), ())), preferred_element_type=f32)


Z_FIRST, Z_MID = 0, 1
GATHER_MODE = (Z_FIRST, Z_MID, Z_MID, Z_FIRST, Z_FIRST, Z_MID)
REDUCE_MODE = (Z_FIRST, Z_FIRST, Z_FIRST, Z_MID, Z_MID, Z_MID)

PIECES = (
    (((0, 512), (768, 256)), ((1024, 256), (1536, 512))),
    (((512, 256), (1280, 256), (2048, 256)), ((2304, 768),)),
    (((3072, 768),), ((3840, 768),)),
    (((4608, 768),), ((5376, 768),)),
)


class Comm:
    def __init__(self, depth):
        self.depth = depth
        self.b = lax.axis_index("blk")
        self.z = lax.axis_index("dp")
        b, z = self.b, self.z
        self.X, self.Y, self.C, self.D = (b ^ 2, z), (b ^ 4, z), (b ^ 1, z), (b ^ 6, z)
        self.Z = [(b, z ^ k) for k in range(depth)]
        self.up, self.down = (b, z + 1), (b, z - 1)

    def greet(self):
        sem = pltpu.get_barrier_semaphore()
        friends = [self.X, self.Y, self.C] + self.Z[1:3]
        for friend in friends:
            pl.semaphore_signal(sem, inc=1, device_id=friend, device_id_type=pl.DeviceIdType.MESH)
        return sem, len(friends)


def remote(src, dst, send_sem, recv_sem, device):
    return pltpu.make_async_remote_copy(
        src_ref=src,
        dst_ref=dst,
        send_sem=send_sem,
        recv_sem=recv_sem,
        device_id=device,
        device_id_type=pl.DeviceIdType.MESH,
    )


def layer_kernel(
    x_hbm, tok_ref, group_ref, count_ref, rows_hbm, down_hbm, vec_ref,
    loss_ref, dx_hbm, grad_rows_hbm, grad_down_hbm, grad_vec_ref,
    x_ref, rows_ref, down_ref, grad_rows_ref, grad_down_ref,
    raw, w_attn, w_up, w_down, g_rest,
    qkv, probs, ctx, ctx_t, x_t, y_low, y_t, act, act_t, slope, xhat1, xhat2, work,
    rstd1, rstd2, tok_w, tok_f, tags, vec_all, vec_row, bias_in, pairs, pooled_hat, own_unit, unit_rs, pair_k, vec_grad, vec_out, vec_in,
    local_sem, zsem, xsem, ysem, dsem, csem, ssem,
    small_recv, small_send,
    rc_sem, r1_sem, r2_sem, rz_sem, ry_sem, rf_sem, rs_send,
    vr_sem, vs_sem,
):
    comm = Comm(4)
    b, z = comm.b, comm.z
    me = b * 4 + z
    width = 768
    half = 384
    def at_q(q):
        return b ^ (2 * q)

    def lanes(h):
        return pl.ds(half * h, half)

    def unit(place, i, h):
        ref, base = place
        return ref.at[base + i // 16, pl.ds((i % 16) * 48, 48), lanes(h)]

    def quad(place, n, h):
        ref, base = place
        return ref.at[base + n // 4, pl.ds((n % 4) * 192, 192), lanes(h)]

    def share(p, i, h):
        if p < 4:
            return unit((raw, 2 * p), i, h)
        return w_down.at[i // 8, pl.ds((i % 8) * 96 + 48 * h, 48), lanes(p - 4)]

    def bulk(n):
        return raw.at[0] if n == 32 else raw.at[0, pl.ds(0, 48 * n), pl.ds(0, half)]

    def send(p, i, h, device, way, rsem):
        ref = share(p, i, h)
        remote(ref, ref, ssem.at[p, way], rsem, device).start()

    def arrived(p, i, h, rsem):
        ref = share(p, i, h)
        remote(ref, ref, ssem.at[p, 0], rsem, comm.X).wait_recv()

    def to_core(p, i, h):
        send(p, i, h, comm.C, 2, csem.at[p])

    def both_to_core(p, i):
        if p < 4:
            ref = raw.at[2 * p + i // 16, pl.ds((i % 16) * 48, 48), :]
        else:
            ref = w_down.at[i // 8, pl.ds((i % 8) * 96, 96), lanes(p - 4)]
        remote(ref, ref, ssem.at[p, 2], csem.at[p], comm.C).start()

    def dev(q, k):
        return at_q(q) * 4 + (z ^ k)

    def cast(p):
        for h in range(2):
            if p < 4:
                row = jnp.concatenate([rows_ref[:, c : c + n] for c, n in PIECES[p][h]], axis=1)
                both = jnp.concatenate([row[:, :half], row[:, half:]], axis=0)
            else:
                both = down_ref[48 * h : 48 * h + 48, half * (p - 4) : half * (p - 3)]
            if p < 4:
                raw[2 * p + me // 16, pl.ds((me % 16) * 48, 48), lanes(h)] = both.astype(bf16)
            else:
                w_down[me // 8, pl.ds((me % 8) * 96 + 48 * h, 48), lanes(p - 4)] = both.astype(bf16)

    def along_z(p, q, k, j, h):
        i = dev(q, k)
        if k == 0:
            send(p, i, h, comm.Z[2], 3, zsem.at[p, 2, 2 * j + h])
            send(p, i, h, comm.Z[1], 3, zsem.at[p, 1, 2 * j + h])
        else:
            send(p, i, h, comm.Z[1], 3, zsem.at[p, 3, 2 * j + h])

    def place(j, h):
        return 0 if j == 0 else (1 if h == 0 else 2)

    def ownz(p):
        for h in range(2):
            along_z(p, 0, 0, 0, h)

    def own1(p):
        send(p, dev(0, 0), 0, comm.X, 0, dsem.at[p, 0, 0])
        send(p, dev(0, 0), 1, comm.Y, 1, dsem.at[p, 0, 1])

    def first(p):
        for h in range(2):
            q = place(1, h)
            arrived(p, dev(q, 0), h, dsem.at[p, 0, h])
            along_z(p, q, 0, 1, h)

    def fold(p, j=0):
        for h in range(2):
            q = place(j, h)
            arrived(p, dev(q, 2), h, zsem.at[p, 2, 2 * j + h])
            along_z(p, q, 2, j, h)

    def z_wait(p, k, j):
        if k in (1, 3):
            for h in range(2):
                arrived(p, dev(place(j, h), k), h, zsem.at[p, k, 2 * j + h])

    def col(p, k):
        z_wait(p, k, 0)
        i = dev(0, k)
        send(p, i, 0, comm.X, 0, xsem.at[p, k, 0])
        send(p, i, 1, comm.Y, 1, ysem.at[p, k, 1])
        send(p, i, 1, comm.X, 0, xsem.at[p, k, 1])
        send(p, i, 0, comm.Y, 1, ysem.at[p, k, 0])
        both_to_core(p, i)

    def across(p, k):
        i = dev(1, k)
        arrived(p, i, 0, xsem.at[p, k, 0])
        send(p, i, 0, comm.Y, 1, dsem.at[p, k, 0])
        to_core(p, i, 0)
        i = dev(2, k)
        arrived(p, i, 1, ysem.at[p, k, 1])
        send(p, i, 1, comm.X, 0, dsem.at[p, k, 1])
        to_core(p, i, 1)

    def fin(p, k, j):
        z_wait(p, k, j)
        i = dev(place(j, 0), k)
        send(p, i, 0, comm.Y, 1, ysem.at[p, k, j])
        to_core(p, i, 0)
        i = dev(place(j, 1), k)
        send(p, i, 1, comm.X, 0, xsem.at[p, k, j])
        to_core(p, i, 1)

    def last(p, k):
        if GATHER_MODE[p] == Z_FIRST:
            rest = ((1, 1, xsem.at[p, k, 1]), (2, 0, ysem.at[p, k, 0]), (3, 0, dsem.at[p, k, 0]), (3, 1, dsem.at[p, k, 1]))
        else:
            rest = ((2, 0, ysem.at[p, k, 0]), (1, 1, xsem.at[p, k, 0]), (3, 0, ysem.at[p, k, 1]), (3, 1, xsem.at[p, k, 1]))
        for q, h, sem in rest:
            arrived(p, dev(q, k), h, sem)
            if q < 3:
                to_core(p, dev(q, k), h)
        both_to_core(p, dev(3, k))

    def gathered(p):
        remote(bulk(32), bulk(32), ssem.at[p, 0], csem.at[p], comm.X).wait_recv()

    def sent(p):
        z_first = GATHER_MODE[p] == Z_FIRST
        for way, n in ((0, 12 if z_first else 9), (1, 12 if z_first else 9), (2, 32), (3, 6 if z_first else 12)):
            remote(bulk(n), bulk(n), ssem.at[p, way], csem.at[p], comm.X).wait_send()

    def small_send_one(ref, n, i, device, rsem):
        block = ref.at[pl.ds(i, 1)]
        remote(block, block, small_send.at[n], rsem, device).start()

    def small_wait(ref, n, i, rsem):
        block = ref.at[pl.ds(i, 1)]
        remote(block, block, small_send.at[n], rsem, comm.X).wait_recv()

    def small_plane(ref, n, k):
        i = dev(0, k)
        small_send_one(ref, n, i, comm.D, small_recv.at[n, 12 + k])
        small_send_one(ref, n, i, comm.X, small_recv.at[n, 4 + k])
        small_send_one(ref, n, i, comm.Y, small_recv.at[n, 8 + k])
        small_send_one(ref, n, i, comm.C, small_recv.at[n, 0])

    def small_own(ref, n):
        for k in (3, 2, 1):
            small_send_one(ref, n, me, comm.Z[k], small_recv.at[n, k])
        small_plane(ref, n, 0)

    def small_z(ref, n):
        for k in (1, 2, 3):
            small_wait(ref, n, dev(0, k), small_recv.at[n, k])
            small_plane(ref, n, k)

    def small_cross(ref, n):
        for k in range(4):
            for q in (1, 2, 3):
                small_wait(ref, n, dev(q, k), small_recv.at[n, 4 * q + k])
                small_send_one(ref, n, dev(q, k), comm.C, small_recv.at[n, 0])

    def small_end(ref, n):
        many = ref.at[pl.ds(0, 16)]
        remote(many, many, small_send.at[n], small_recv.at[n, 0], comm.X).wait_recv()
        many = ref.at[pl.ds(0, 31)]
        remote(many, many, small_send.at[n], small_recv.at[n, 0], comm.X).wait_send()

    def vec(offset, size=width):
        return vec_row[0:1, offset : offset + size]

    bias_q, bias_v, bias_o, gain1_at, shift1_at, bias_up_at = 0, width, 2 * width, 3 * width, 4 * width, 5 * width
    bias_down_at, gain2_at, shift2_at = 9 * width, 10 * width, 11 * width

    share_v = 288

    def place_vectors():
        v = vec_ref[...].reshape(1, share_v)
        tail = jnp.concatenate([v[:, 256:share_v], jnp.zeros((1, 384 - share_v), f32)], axis=1)
        tile = jnp.concatenate([v[:, 0:128], v[:, 128:256], tail, jnp.zeros((13, 128), f32)], axis=0)
        vec_all[pl.ds(me, 1)] = tile.astype(bf16).reshape(1, 16, 128)

    def spread_vectors():
        for i in range(32):
            tile = vec_all[i].astype(f32)
            for r, n in ((0, 128), (1, 128), (2, share_v - 256)):
                at = share_v * i + 128 * r
                vec_row[0:1, at : at + n] = tile[r : r + 1, 0:n]
        bias_in[...] = jnp.zeros_like(bias_in)
        bias_in[0:1, 0:512] = vec(bias_q, 512)
        bias_in[0:1, 1024:1536] = vec(bias_v, 512)
        bias_in[0:1, 1536:1792] = vec(bias_q + 512, 256)
        bias_in[0:1, 2048:2304] = vec(bias_v + 512, 256)

    def relayout(p):
        target, chunk = (w_attn, 2 * p) if p < 2 else (w_up, 2 * p - 4)

        def body(j, carry):
            for h in range(2):
                even = raw[2 * p + j // 8, pl.ds((j % 8) * 96, 48), lanes(h)].astype(f32)
                odd = raw[2 * p + j // 8, pl.ds((j % 8) * 96 + 48, 48), lanes(h)].astype(f32)
                for q in range(2):
                    rows = jnp.concatenate([even[24 * q : 24 * q + 24], odd[24 * q : 24 * q + 24]], axis=0)
                    target[chunk + h, pl.ds(j * 48, 48), lanes(q)] = rows.astype(bf16)
            return carry

        lax.fori_loop(0, 16, body, 0)

    def transpose_into(source, target, lo=0, hi=3):
        def body(j, carry):
            at = pl.multiple_of(j * 256, 256)
            target[pl.ds(at, 256), :] = jnp.transpose(source[:, pl.ds(at, 256)])
            return carry

        lax.fori_loop(lo, hi, body, 0)

    def token_weights():
        lane = lax.broadcasted_iota(jnp.int32, (1, 128), 1)
        left = (lane < 64).astype(f32)
        tok = tok_ref[...].astype(f32)
        tok_f[0:4, :] = jnp.concatenate([tok[:, 0, :], tok[:, 1, :]], axis=1)
        for p in range(4):
            m = tok_f[p : p + 1, :]
            n0 = jnp.sum(m * left, axis=1, keepdims=True)
            n1 = jnp.sum(m * (1.0 - left), axis=1, keepdims=True)
            w = m / (left * n0 + (1.0 - left) * n1)
            tok_w[128 * p : 128 * p + 128, :] = jnp.transpose(jnp.broadcast_to(w, (128, 128)))
        row = lax.broadcasted_iota(jnp.int32, (8, 128), 0) % 4
        tag = jnp.full((8, 128), -1.0, f32)
        for s in range(4):
            tag = jnp.where((row == s) & (count_ref[0] > s), group_ref[s].astype(f32), tag)
        tags[...] = tag

    def project(lo, hi):
        def body(t, carry):
            c, n = t // 3, t % 3
            at = pl.multiple_of(n * 256, 256)
            bias = bias_in[0:1, pl.ds(pl.multiple_of(t * 256, 256), 256)]
            out = dot_nn(x_ref[...], w_attn[c, :, pl.ds(at, 256)]) + bias
            qkv[c, :, pl.ds(at, 256)] = out.astype(bf16)
            return carry

        lax.fori_loop(lo, hi, body, 0)

    def head_places(hp):
        if hp < 4:
            key = (0, 512 + 128 * hp) if hp < 2 else (1, 128 * hp - 256)
            return (0, 128 * hp), key, (1, 256 + 128 * hp)
        return (2, 128 * hp - 512), (2, 128 * hp - 256), (2, 128 * hp)

    lane128 = lax.broadcasted_iota(jnp.int32, (128, 128), 1)
    row128 = lax.broadcasted_iota(jnp.int32, (128, 128), 0)
    even_half = lane128 < 64

    def split_heads(v):
        zero = jnp.zeros_like(v)
        return jnp.concatenate([jnp.where(even_half, v, zero), jnp.where(even_half, zero, v)], axis=0)

    def attend(group, lo, hi):
        def body(p, carry):
            rows = pl.ds(pl.multiple_of(p * 128, 128), 128)
            m = tok_f[pl.ds(p, 1), :]
            same = (row128 < 64) == (lane128 < 64)
            open_one = same & (jnp.broadcast_to(m, (128, 128)) > 0.0)
            block = jnp.where(open_one, 0.0, -1e30)
            block = jnp.concatenate([block, block], axis=0)
            for hp in range(4) if group == 0 else range(4, 6):
                q2, k2, v2 = [qkv[c, rows, at : at + 128] for c, at in head_places(hp)]
                s = dot_nt(split_heads(q2), k2) * HEAD ** (-0.5) + block
                e = jnp.exp(s - jnp.max(s, axis=1, keepdims=True))
                a = (e * (1.0 / jnp.sum(e, axis=1, keepdims=True))).astype(bf16)
                probs[p * 6 + hp] = a
                wide = jnp.concatenate([a[:128], a[128:]], axis=1)
                ctx[rows, 128 * hp : 128 * hp + 128] = dot_nn(wide, split_heads(v2)).astype(bf16)
            return carry

        lax.fori_loop(lo, hi, body, 0, unroll=1 + group)

    def norm_rows(i, source_fn, hat, rstd, emit):
        rows = pl.ds(pl.multiple_of(i * 64, 64), 64)
        h = source_fn(rows)
        centre = h - jnp.mean(h, axis=1, keepdims=True)
        r = lax.rsqrt(jnp.mean(centre * centre, axis=1, keepdims=True) + norm_epsilon)
        xh = centre * r
        hat[rows, :] = xh
        rstd[rows, :] = jnp.broadcast_to(r, (64, 128))
        if emit is not None:
            emit(rows, xh)

    def attn_out():
        def body(n, carry):
            at = pl.multiple_of(n * 256, 256)
            work[:, pl.ds(at, 256)] = dot_nn(ctx[...], w_attn[3, :, pl.ds(at, 256)])
            return carry

        lax.fori_loop(0, 3, body, 0)

    def attn_norm():
        def source(rows):
            return x_ref[rows, :].astype(f32) + work[rows, :] + vec(bias_o)

        def emit(rows, xh):
            y_low[rows, :] = (xh * (1.0 + vec(gain1_at)) + vec(shift1_at)).astype(bf16)

        def norm(i, carry):
            norm_rows(i, source, xhat1, rstd1, emit)
            return carry

        lax.fori_loop(0, 8, norm, 0, unroll=2)

    def feed_up(lo, hi):
        def body(t, carry):
            c, n = t // 3, t % 3
            at = pl.multiple_of(n * 256, 256)
            to = pl.multiple_of(t * 256, 256)
            work[:, pl.ds(0, 256)] = dot_nn(y_low[...], w_up[c, :, pl.ds(at, 256)])
            bias = vec_row[0:1, pl.ds(pl.multiple_of(bias_up_at + to, 256), 256)]

            def rows_of(i, inner):
                rows = pl.ds(pl.multiple_of(i * 32, 32), 32)
                v = work[rows, 0:256] + bias
                cdf = 0.5 * (1.0 + lax.erf(v * 0.7071067811865476))
                dens = jnp.exp(v * v * -0.5) * 0.3989422804014327
                act[rows, pl.ds(to, 256)] = (v * cdf).astype(bf16)
                slope[rows, pl.ds(to, 256)] = (cdf + v * dens).astype(bf16)
                return inner

            lax.fori_loop(0, 16, rows_of, 0, unroll=4)
            return carry

        lax.fori_loop(lo, hi, body, 0)

    def feed_down(s):
        def body(n, carry):
            at = pl.multiple_of(n * 256, 256)
            total = dot_nn(act[:, 0:width], w_down[0, :, pl.ds(at, 256)])
            for c in range(1, 4):
                total = total + dot_nn(act[:, c * width : (c + 1) * width], w_down[c, :, pl.ds(at, 256)])
            work[:, pl.ds(at, 256)] = total
            return carry

        lax.fori_loop(s, 2 * s + 1, body, 0)

    def down_norm():
        def source(rows):
            return y_low[rows, :].astype(f32) + work[rows, :] + vec(bias_down_at)

        def norm(i, carry):
            norm_rows(i, source, xhat2, rstd2, None)
            rows = pl.ds(pl.multiple_of(i * 64, 64), 64)
            got = jnp.sum(xhat2[rows, :] * tok_w[rows, 0:1], axis=0, keepdims=True)
            at = i // 2 + 4 * (i % 2)
            pooled_hat[pl.ds(at, 1), :] = got
            return carry

        lax.fori_loop(0, 8, norm, 0, unroll=2)

    def pool():
        e = pooled_hat[...] * (1.0 + vec(gain2_at)) + vec(shift2_at)
        r = lax.rsqrt(jnp.sum(e * e, axis=1, keepdims=True) + unit_epsilon)
        unit_rs[...] = jnp.broadcast_to(r, (8, 128))
        n = e * r
        own_unit[...] = n
        packed = jnp.concatenate([n[:, :half], n[:, half:]], axis=0)
        tag = jnp.concatenate([tags[...], tags[...]], axis=0)
        pairs[pl.ds(me, 1)] = jnp.concatenate([packed, tag], axis=1).astype(bf16).reshape(1, 16, 512)

    def contrast():
        total = 256
        every = pairs[...].astype(f32)
        left = every[:, 0:8, 0:half].reshape(total, half).astype(bf16)
        right = every[:, 8:16, 0:half].reshape(total, half).astype(bf16)
        tag = every[:, 0:8, half : half + 128].reshape(total, 128)
        tag_row = jnp.concatenate([jnp.transpose(tag[0:128])[0:1], jnp.transpose(tag[128:256])[0:1]], axis=1)
        s = (dot_nt(left, left) + dot_nt(right, right)) * score_scale
        i = lax.broadcasted_iota(jnp.int32, (total, total), 0)
        j = lax.broadcasted_iota(jnp.int32, (total, total), 1)
        opposite = (i & 4) != (j & 4)
        diagonal = (i ^ j) == 4
        s = s - jnp.where(diagonal, score_scale * margin, 0.0)
        same = (tag[:, 0:1] == tag_row) & (tag_row >= 0.0) & opposite
        e = jnp.where(same, jnp.exp(jnp.where(same, s, 0.0)), 0.0)
        valid = tag_row >= 0.0
        sums = jnp.where(valid, jnp.sum(e, axis=0, keepdims=True), 1.0)
        coef = 1.0 / jnp.sum(valid.astype(f32))
        positive = jnp.sum(jnp.where(diagonal & same, s, 0.0))
        loss = (jnp.sum(jnp.where(valid, jnp.log(sums), 0.0)) - positive) * coef
        loss_ref[0, 0] = loss
        pair_k[0] = e
        pair_k[1] = jnp.where(diagonal & same, 2.0, 0.0)
        own_rows = pl.ds(pl.multiple_of(me * 8, 8), 8)
        e_own = pair_k[0, own_rows, :]
        r_own = jnp.sum(e_own, axis=1, keepdims=True)
        r_own = jnp.where(tags[:, 0:1] >= 0.0, r_own, 1.0)
        k = (e_own / r_own + e_own / sums - pair_k[1, own_rows, :]) * (coef * score_scale)
        high = k.astype(bf16)
        low = (k - high.astype(f32)).astype(bf16)
        both = jnp.concatenate([high, low], axis=0)
        dn = jnp.concatenate([dot_nn(both, left), dot_nn(both, right)], axis=1)
        dn = dn[0:8] + dn[8:16]
        n = own_unit[...]
        de = unit_rs[:, 0:1] * (dn - n * jnp.sum(n * dn, axis=1, keepdims=True))
        vec_grad[0:1, gain2_at : gain2_at + width] = jnp.sum(de * pooled_hat[...], axis=0, keepdims=True)
        vec_grad[0:1, shift2_at : shift2_at + width] = jnp.sum(de, axis=0, keepdims=True)
        pooled_hat[...] = de

    def norm_two_back():
        def body(i, carry):
            rows = pl.ds(pl.multiple_of(i * 64, 64), 64)
            de = pooled_hat[pl.ds(i // 2 + 4 * (i % 2), 1), :]
            dg = de * (1.0 + vec(gain2_at))
            xh = xhat2[rows, :]
            m1 = jnp.mean(dg, axis=1, keepdims=True)
            m2 = jnp.mean(dg * xh, axis=1, keepdims=True)
            dz = (rstd2[rows, 0:1] * tok_w[rows, 0:1]) * (dg - m1 - xh * m2)
            low = dz.astype(bf16)
            xhat2[rows, :] = dz
            y_low[rows, :] = low
            return carry + jnp.sum(low.astype(f32), axis=0, keepdims=True)

        vec_grad[0:1, bias_down_at : bias_down_at + width] = lax.fori_loop(0, 8, body, jnp.zeros((1, width), f32), unroll=2)

    g_places = ((w_up, 0), (w_up, 2), (g_rest, 4), (g_rest, 6), (g_rest, 0), (g_rest, 2))
    box_places = ((w_down, 0), (w_down, 2), (raw, 4), (raw, 6), (raw, 0), (raw, 2))

    def grad_w_down(blk):
        out = dot_nn(act_t[pl.ds(pl.multiple_of(blk * 384, 128), 384), :], y_low[...])
        for part in range(2):
            for zz in range(4):
                for h in range(2):
                    rows = out[96 * zz + 48 * h : 96 * zz + 48 * h + 48, half * part : half * part + half]
                    at = pl.multiple_of((blk % 4) * 192 + 48 * zz, 16)
                    g_rest[2 * part + blk // 4, pl.ds(at, 48), lanes(h)] = rows.astype(bf16)

    def down_grads(lo, hi):
        def body(n, carry):
            q = 3 - n // 2
            grad_w_down(at_q(q) ^ (1 - n % 2))

            @pl.when(n % 2 == 0)
            def _():
                for p in (4, 5):
                    for h in range(2):
                        core_send(p, h, q)

            return carry

        lax.fori_loop(lo, hi, body, 0)

    def grad_act(lo, hi):
        def body(t, carry):
            c, n = t // 3, t % 3
            to = pl.multiple_of(t * 256, 256)
            work[:, 0:256] = dot_nt(y_low[...], w_down[c, pl.ds(pl.multiple_of(n * 256, 256), 256), :])

            def rows_of(i, total):
                rows = pl.ds(pl.multiple_of(i * 64, 64), 64)
                low = (work[rows, 0:256] * slope[rows, pl.ds(to, 256)].astype(f32)).astype(bf16)
                act[rows, pl.ds(to, 256)] = low
                return total + jnp.sum(low.astype(f32), axis=0, keepdims=True)

            sums = lax.fori_loop(0, 8, rows_of, jnp.zeros((1, 256), f32), unroll=2)
            vec_grad[0:1, pl.ds(pl.multiple_of(bias_up_at + to, 256), 256)] = sums
            return carry

        lax.fori_loop(lo, hi, body, 0)

    def store_units(p, h, m, out):
        ref, base = g_places[p]
        for d in range(16):
            rows = out[24 * d : 24 * d + 24]
            both = jnp.concatenate([rows[:, :half], rows[:, half:]], axis=0)
            ref[base + m, 48 * d : 48 * d + 48, lanes(h)] = both.astype(bf16)

    def grad_w_rows(p, halves=(0, 1)):
        def body(n, carry):
            m = (b // 4) ^ (1 - n)
            rows = pl.ds(pl.multiple_of(m * 384, 128), 384)
            for h in halves:
                if p >= 2:
                    out = dot_nn(y_t[rows, :], act[:, (2 * p - 4 + h) * width : (2 * p - 3 + h) * width])
                elif (p, h) == (1, 1):
                    out = dot_nn(ctx_t[rows, :], y_low[...])
                else:
                    out = dot_nn(x_t[rows, :], qkv[2 * p + h])
                store_units(p, h, m, out)
                for q in (1, 0):
                    core_send(p, h, 2 * (1 - n) + q)
            return carry

        lax.fori_loop(0, 2, body, 0)

    def grad_y():
        def body(n, carry):
            at = pl.multiple_of(n * 256, 256)
            total = xhat2[:, pl.ds(at, 256)]
            for c in range(4):
                total = total + dot_nt(act[:, c * width : (c + 1) * width], w_up[c, pl.ds(at, 256), :])
            work[:, pl.ds(at, 256)] = total
            return carry

        lax.fori_loop(0, 3, body, 0)

    def norm_one_back():
        def body(i, carry):
            rows = pl.ds(pl.multiple_of(i * 64, 64), 64)
            dy = work[rows, :]
            xh = xhat1[rows, :]
            dg = dy * (1.0 + vec(gain1_at))
            m1 = jnp.mean(dg, axis=1, keepdims=True)
            m2 = jnp.mean(dg * xh, axis=1, keepdims=True)
            dh = rstd1[rows, 0:1] * (dg - m1 - xh * m2)
            low = dh.astype(bf16)
            work[rows, :] = dh
            y_low[rows, :] = low
            gain, shift, bias = carry
            return (
                gain + jnp.sum(dy * xh, axis=0, keepdims=True),
                shift + jnp.sum(dy, axis=0, keepdims=True),
                bias + jnp.sum(low.astype(f32), axis=0, keepdims=True),
            )

        zero = jnp.zeros((1, width), f32)
        gain, shift, bias = lax.fori_loop(0, 8, body, (zero, zero, zero), unroll=2)
        vec_grad[0:1, gain1_at : gain1_at + width] = gain
        vec_grad[0:1, shift1_at : shift1_at + width] = shift
        vec_grad[0:1, bias_o : bias_o + width] = bias

    def grad_ctx():
        def body(n, carry):
            at = pl.multiple_of(n * 256, 256)
            ctx[:, pl.ds(at, 256)] = dot_nt(y_low[...], w_attn[3, pl.ds(at, 256), :]).astype(bf16)
            return carry

        lax.fori_loop(0, 3, body, 0)

    def attend_back(group, lo, hi):
        def body(p, carry):
            rows = pl.ds(pl.multiple_of(p * 128, 128), 128)
            for hp in range(4) if group == 0 else range(4, 6):
                places = head_places(hp)
                q2, k2, v2 = [qkv[c, rows, at : at + 128] for c, at in places]
                dc = split_heads(ctx[rows, 128 * hp : 128 * hp + 128])
                a = probs[p * 6 + hp]
                af = a.astype(f32)
                da = dot_nt(dc, v2)
                ds = (af * (da - jnp.sum(af * da, axis=1, keepdims=True))).astype(bf16)
                dv = dot_tn(a, dc)
                wide = jnp.concatenate([ds[:128], ds[128:]], axis=1)
                dq = dot_nn(wide, split_heads(k2)) * HEAD ** (-0.5)
                dk = dot_tn(ds, split_heads(q2)) * HEAD ** (-0.5)
                for (c, at), d in zip(places, (dq, dk, dv)):
                    qkv[c, rows, at : at + 128] = d.astype(bf16)
            return carry

        lax.fori_loop(lo, hi, body, 0, unroll=1 + group)

    def grad_bias_in():
        def body(i, carry):
            rows = pl.ds(pl.multiple_of(i * 64, 64), 64)
            return tuple(have + jnp.sum(qkv[c, rows, :].astype(f32), axis=0, keepdims=True) for c, have in enumerate(carry))

        zero = jnp.zeros((1, width), f32)
        first_sum, second_sum, third_sum = lax.fori_loop(0, 8, body, (zero, zero, zero))
        vec_grad[0:1, bias_q : bias_q + 512] = first_sum[:, 0:512]
        vec_grad[0:1, bias_q + 512 : bias_q + 768] = third_sum[:, 0:256]
        vec_grad[0:1, bias_v : bias_v + 512] = second_sum[:, 256:768]
        vec_grad[0:1, bias_v + 512 : bias_v + 768] = third_sum[:, 512:768]

    def dx_copy(n):
        at = pl.ds(pl.multiple_of(n * 256, 256), 256)
        return pltpu.make_async_copy(work.at[:, at], dx_hbm.at[:, at], local_sem.at[3])

    def grad_x(lo, hi):
        def body(n, carry):
            at = pl.multiple_of(n * 256, 256)
            total = work[:, pl.ds(at, 256)]
            for c in range(3):
                total = total + dot_nt(qkv[c], w_attn[c, pl.ds(at, 256), :])
            work[:, pl.ds(at, 256)] = total
            return carry

        lax.fori_loop(lo, hi, body, 0)
        for n in range(lo, hi):
            dx_copy(n).start()

    def spot(p, run, u, h):
        ref, base = box_places[p]
        return ref.at[base + run // 4, pl.ds((run % 4) * 192 + 48 * u, 48), lanes(h)]

    def core_send(p, h, q):
        remote(
            quad(g_places[p], at_q(q) ^ 1, h), quad(box_places[p], q, h), rs_send.at[p, 0], rc_sem.at[p, h, q], comm.C
        ).start()

    def run_wait(p, run, h, sem):
        ref = quad(box_places[p], run, h)
        remote(ref, ref, rs_send.at[p, 0], sem, comm.C).wait_recv()

    def spot_wait(p, run, u, h, sem):
        ref = spot(p, run, u, h)
        remote(ref, ref, rs_send.at[p, 0], sem, comm.C).wait_recv()

    def add_in(p, h, q, runs, lo=0, hi=4):
        target, base = g_places[p]
        box, box_base = box_places[p]
        blk = at_q(q)

        def body(i, carry):
            at = pl.multiple_of((blk % 4) * 192 + i * 48, 16)
            total = target[base + blk // 4, pl.ds(at, 48), lanes(h)].astype(f32)
            for run in runs:
                from_at = pl.multiple_of((run % 4) * 192 + i * 48, 16)
                total = total + box[box_base + run // 4, pl.ds(from_at, 48), lanes(h)].astype(f32)
            target[base + blk // 4, pl.ds(at, 48), lanes(h)] = total.astype(bf16)
            return carry

        lax.fori_loop(lo, hi, body, 0, unroll=2)

    def read_unit(p, i, h):
        ref, base = g_places[p]
        return ref[base + i // 16, pl.ds((i % 16) * 48, 48), lanes(h)].astype(f32)

    def read_spot(p, run, u, h):
        ref, base = box_places[p]
        return ref[base + run // 4, (run % 4) * 192 + 48 * u : (run % 4) * 192 + 48 * u + 48, lanes(h)].astype(f32)

    def write_unit(p, i, h, total):
        ref, base = g_places[p]
        ref[base + i // 16, pl.ds((i % 16) * 48, 48), lanes(h)] = total.astype(bf16)

    def pass_run(p, h, q, run, sem):
        along_y = (run < 6) == (h == 0)
        device, way = (comm.Y, 2) if along_y else (comm.X, 1)
        remote(quad(g_places[p], at_q(q), h), quad(box_places[p], run, h), rs_send.at[p, way], sem, device).start()

    def pass_unit(p, i, run, u, h, device, way, sem):
        remote(unit(g_places[p], i, h), spot(p, run, u, h), rs_send.at[p, way], sem, device).start()

    def pair_of(place, n, u, h):
        ref, base = place
        return ref.at[base + n // 4, pl.ds((n % 4) * 192 + 96 * u, 96), lanes(h)]

    def pair_wait(p, run, u, sem):
        ref = pair_of(box_places[p], run, u, 0)
        remote(ref, ref, rs_send.at[p, 0], sem, comm.C).wait_recv()

    def pass_pair(p, q, u, run, along_y, sem):
        device, way = (comm.Y, 2) if along_y else (comm.X, 1)
        remote(pair_of(g_places[p], at_q(q), u, 0), pair_of(box_places[p], run, u, 0), rs_send.at[p, way], sem, device).start()

    def split_s1(p, side):
        for q in (3,) if side == 1 else (2, 1):
            run_wait(p, q, 0, rc_sem.at[p, 0, q])
        for u in range(2):
            q = 3 if side == 1 else 2 - u
            add_in(p, 0, q, (q,), 2 * u, 2 * u + 2)
            pass_pair(p, q, u, 4 + side, u == 0, r1_sem.at[6, u, side])

    def split_s2(p):
        for u in range(2):
            pair_wait(p, 5, u, r1_sem.at[6, u, 1])
            add_in(p, 0, 1 + u, (1 + u, 5), 2 * u, 2 * u + 2)
            pass_pair(p, 1 + u, u, 6, u == 1, r2_sem.at[6, u])

    def split_s3(p):
        run_wait(p, 0, 0, rc_sem.at[p, 0, 0])
        for u in range(2):
            pair_wait(p, 4, u, r1_sem.at[6, u, 0])
            pair_wait(p, 6, u, r2_sem.at[6, u])
        add_in(p, 0, 0, (0, 4, 6))
        pass_unit(p, dev(0, 1), 7, 0, 0, comm.Z[1], 3, rz_sem.at[p, 0, 0])
        pass_unit(p, dev(0, 3), 7, 1, 0, comm.Z[1], 3, rz_sem.at[p, 0, 1])

    def s1(p, side, halves=(0, 1)):
        if halves == (0,):
            return split_s1(p, side)
        for h in halves:
            q = 3 if side == 1 else 2 - h
            run_wait(p, q, h, rc_sem.at[p, h, q])
            add_in(p, h, q, (q,))
            pass_run(p, h, q, 4 + side, r1_sem.at[p, h, side])

    def s2(p, halves=(0, 1)):
        if halves == (0,):
            return split_s2(p)
        if REDUCE_MODE[p] == Z_FIRST:
            for h in halves:
                q = 1 + h
                run_wait(p, q, h, rc_sem.at[p, h, q])
                run_wait(p, 5, h, r1_sem.at[p, h, 1])
                add_in(p, h, q, (q, 5))
                pass_run(p, h, q, 6, r2_sem.at[p, h])
            return
        for h in halves:
            for j, q in enumerate((0, 1 + h)):
                run_wait(p, q, h, rc_sem.at[p, h, q])
                run_wait(p, 4 + j, h, r1_sem.at[p, h, j])
                add_in(p, h, q, (q, 4 + j))
                pass_unit(p, dev(q, 1), 6, 2 * j, h, comm.Z[1], 3, rz_sem.at[p, h, 2 * j])
                pass_unit(p, dev(q, 3), 6, 2 * j + 1, h, comm.Z[1], 3, rz_sem.at[p, h, 2 * j + 1])

    def s3(p, halves=(0, 1)):
        if halves == (0,):
            return split_s3(p)
        if REDUCE_MODE[p] == Z_FIRST:
            for h in halves:
                run_wait(p, 0, h, rc_sem.at[p, h, 0])
                run_wait(p, 4, h, r1_sem.at[p, h, 0])
                run_wait(p, 6, h, r2_sem.at[p, h])
                add_in(p, h, 0, (0, 4, 6))
                pass_unit(p, dev(0, 1), 7, 0, h, comm.Z[1], 3, rz_sem.at[p, h, 0])
                pass_unit(p, dev(0, 3), 7, 1, h, comm.Z[1], 3, rz_sem.at[p, h, 1])
            return
        for h in halves:
            for j, q in enumerate((0, 1 + h)):
                spot_wait(p, 6, 2 * j + 1, h, rz_sem.at[p, h, 2 * j + 1])
                write_unit(p, dev(q, 2), h, read_unit(p, dev(q, 2), h) + read_spot(p, 6, 2 * j + 1, h))
                pass_unit(p, dev(q, 2), 7, j, h, comm.Z[2], 3, ry_sem.at[p, h, j])

    def s4(p, halves=(0, 1)):
        if REDUCE_MODE[p] == Z_FIRST:
            for h in halves:
                spot_wait(p, 7, 1, h, rz_sem.at[p, h, 1])
                write_unit(p, dev(0, 2), h, read_unit(p, dev(0, 2), h) + read_spot(p, 7, 1, h))
                pass_unit(p, dev(0, 2), 7, 2, h, comm.Z[2], 3, ry_sem.at[p, h, 0])
            return
        for h in halves:
            q = 1 + h
            spot_wait(p, 6, 2, h, rz_sem.at[p, h, 2])
            spot_wait(p, 7, 1, h, ry_sem.at[p, h, 1])
            write_unit(p, dev(q, 0), h, read_unit(p, dev(q, 0), h) + read_spot(p, 6, 2, h) + read_spot(p, 7, 1, h))
            device, way = (comm.X, 1) if h == 0 else (comm.Y, 2)
            pass_unit(p, dev(q, 0), 7, 2, h, device, way, rf_sem.at[p, h])

    def s5(p, halves=(0, 1)):
        for h in halves:
            total = read_unit(p, me, h)
            if REDUCE_MODE[p] == Z_FIRST:
                spot_wait(p, 7, 0, h, rz_sem.at[p, h, 0])
                spot_wait(p, 7, 2, h, ry_sem.at[p, h, 0])
                total = total + read_spot(p, 7, 0, h) + read_spot(p, 7, 2, h)
            else:
                spot_wait(p, 6, 0, h, rz_sem.at[p, h, 0])
                spot_wait(p, 7, 0, h, ry_sem.at[p, h, 0])
                spot_wait(p, 7, 2, h, rf_sem.at[p, h])
                total = total + read_spot(p, 6, 0, h) + read_spot(p, 7, 0, h) + read_spot(p, 7, 2, h)
            if p >= 4:
                grad_down_ref[48 * h : 48 * h + 48, half * (p - 4) : half * (p - 3)] = total
                at = (pl.ds(48 * h, 48), lanes(p - 4))
                pltpu.make_async_copy(grad_down_ref.at[at], grad_down_hbm.at[at], local_sem.at[5]).start()
            else:
                row = jnp.concatenate([total[0:24], total[24:48]], axis=1)
                at = 0
                for c, n in PIECES[p][h]:
                    grad_rows_ref[:, c : c + n] = row[:, at : at + n]
                    columns = pl.ds(c, n)
                    pltpu.make_async_copy(grad_rows_ref.at[:, columns], grad_rows_hbm.at[:, columns], local_sem.at[4]).start()
                    at = at + n

    def sums_sent(p):
        z_first = REDUCE_MODE[p] == Z_FIRST
        along_x = along_y = 12 if z_first else 9
        if p == 1:
            along_x, along_y = 14, 10
        for way, n in ((0, 32), (1, along_x), (2, along_y), (3, 6 if z_first else 12)):
            remote(bulk(n), bulk(n), rs_send.at[p, way], rc_sem.at[p, 0, 0], comm.C).wait_send()

    def vec_pack():
        vec_out[...] = jnp.zeros_like(vec_out)
        for i in range(32):
            for r, n in ((0, 128), (1, 128), (2, share_v - 256)):
                at = share_v * i + 128 * r
                vec_out[i // 4, 3 * (i % 4) + r : 3 * (i % 4) + r + 1, 0:n] = vec_grad[0:1, at : at + n]

    def vec_copy(src, dst, n, device):
        return remote(vec_out.at[src], vec_in.at[dst], vs_sem.at[n], vr_sem.at[dst], device)

    def vec_core():
        for q in range(4):
            vec_copy(at_q(q) ^ 1, q, q, comm.C).start()

    def vec_take(dst, target):
        vec_copy(target, dst, 0, comm.C).wait_recv()
        vec_out[target] = vec_out[target] + vec_in[dst]

    def vec_y():
        for q in range(4):
            vec_take(q, at_q(q))
        vec_copy(at_q(3), 5, 4, comm.Y).start()
        vec_copy(at_q(2), 4, 5, comm.Y).start()

    def vec_x():
        vec_take(5, at_q(1))
        vec_copy(at_q(1), 6, 6, comm.X).start()

    def vec_z():
        vec_take(4, b)
        vec_take(6, b)
        vec_copy(b, 8, 7, comm.Z[2]).start()

    def vec_w():
        vec_copy(b, 8, 0, comm.C).wait_recv()
        vec_in[10] = vec_out[b] + vec_in[8]
        remote(vec_in.at[10], vec_in.at[9], vs_sem.at[8], vr_sem.at[9], comm.Z[1]).start()

    def vec_end():
        vec_copy(b, 9, 0, comm.C).wait_recv()
        total = vec_in[9] + vec_in[10]
        mine = total[0:3]
        for zz in range(1, 4):
            mine = jnp.where(z == zz, total[3 * zz : 3 * zz + 3], mine)
        whole = jnp.concatenate([mine[0:1], mine[1:2], mine[2:3, 0 : share_v - 256]], axis=1)
        grad_vec_ref[...] = whole.reshape(share_v)
        for n in range(9):
            vec_copy(b, 0, n, comm.C).wait_send()

    def load(n):
        src, dst = ((rows_hbm, rows_ref), (down_hbm, down_ref), (x_hbm, x_ref))[n]
        return pltpu.make_async_copy(src, dst, local_sem.at[n])

    def start():
        for n in (0, 1, 2):
            load(n).start()
        sem, friends = comm.greet()
        place_vectors()
        token_weights()
        load(0).wait()
        for p in range(4):
            cast(p)
        load(1).wait()
        cast(4)
        cast(5)
        pl.semaphore_wait(sem, friends)

    def loaded(n):
        load(n).wait()

    def pair_gather():
        small_own(pairs, 1)
        transpose_into(y_low, y_t)
        transpose_into(ctx, ctx_t)
        small_z(pairs, 1)
        transpose_into(act, act_t, 0, 6)
        small_cross(pairs, 1)
        transpose_into(act, act_t, 6, 12)
        small_end(pairs, 1)

    def finish():
        for p in range(6):
            sums_sent(p)
        pltpu.make_async_copy(work, dx_hbm, local_sem.at[3]).wait()
        pltpu.make_async_copy(grad_rows_ref, grad_rows_hbm, local_sem.at[4]).wait()
        pltpu.make_async_copy(grad_down_ref, grad_down_hbm, local_sem.at[5]).wait()

    def vectors(n):
        (small_own, small_z, small_cross, small_end)[n](vec_all, 0)

    start()
    ownz(0)
    col(4, 0)
    fin(1, 0, 0)
    fin(2, 0, 0)
    own1(1)
    col(0, 0)
    ownz(1)
    own1(2)
    first(1)
    col(0, 1)
    vectors(0)
    fold(0)
    col(0, 2)
    loaded(2)
    transpose_into(x_ref, x_t)
    col(3, 0)
    vectors(1)
    fin(1, 1, 0)
    fold(1, 0)
    own1(5)
    fin(1, 1, 1)
    fold(1, 1)
    vectors(2)
    across(0, 2)
    across(0, 0)
    ownz(2)
    across(4, 0)
    first(2)
    vectors(3)
    col(0, 3)
    fin(1, 0, 1)
    last(1, 1)
    fin(1, 2, 0)
    across(0, 1)
    fin(1, 2, 1)
    last(0, 0)
    ownz(3)
    fold(2, 0)
    fin(1, 3, 1)
    across(0, 3)
    last(0, 2)
    fin(1, 3, 0)
    last(0, 1)
    last(4, 0)
    fin(2, 0, 1)
    last(1, 2)
    fold(2, 1)
    across(3, 0)
    last(0, 3)
    fin(2, 1, 0)
    last(1, 3)
    fin(5, 0, 0)
    fin(2, 1, 1)
    gathered(0)
    relayout(0)
    spread_vectors()
    last(2, 0)
    fold(3)
    fin(2, 2, 1)
    col(3, 2)
    last(1, 0)
    ownz(4)
    col(3, 1)
    fin(2, 2, 0)
    ownz(5)
    project(0, 3)
    project(3, 6)
    fin(2, 3, 0)
    attend(0, 0, 2)
    attend(0, 2, 4)
    across(3, 2)
    last(2, 1)
    fin(2, 3, 1)
    gathered(1)
    across(3, 1)
    first(5)
    relayout(1)
    project(6, 9)
    col(3, 3)
    last(2, 2)
    col(4, 1)
    attend(1, 0, 4)
    last(2, 3)
    fold(4)
    attn_out()
    across(3, 3)
    col(4, 2)
    fold(5, 0)
    attn_norm()
    across(4, 1)
    gathered(2)
    last(3, 2)
    relayout(2)
    fin(5, 1, 0)
    fin(5, 0, 1)
    last(3, 0)
    fold(5, 1)
    feed_up(0, 3)
    across(4, 2)
    last(3, 3)
    col(4, 3)
    feed_up(3, 6)
    fin(5, 3, 0)
    last(3, 1)
    last(4, 2)
    last(4, 1)
    across(4, 3)
    gathered(3)
    fin(5, 1, 1)
    fin(5, 2, 1)
    fin(5, 2, 0)
    relayout(3)
    fin(5, 3, 1)
    feed_up(6, 9)
    last(5, 0)
    last(4, 3)
    last(5, 1)
    feed_up(9, 12)
    sent(0)
    sent(1)
    sent(2)
    sent(3)
    last(5, 2)
    gathered(4)
    last(5, 3)
    feed_down(0)
    gathered(5)
    sent(4)
    feed_down(1)
    down_norm()
    sent(5)
    pool()
    pair_gather()
    contrast()
    norm_two_back()
    down_grads(0, 2)
    down_grads(2, 6)
    s1(4, 1)
    down_grads(6, 8)
    grad_act(0, 4)
    s1(4, 0)
    s1(5, 0)
    grad_act(4, 8)
    grad_act(8, 12)
    s2(4)
    s1(5, 1)
    grad_w_rows(2)
    s1(2, 1)
    grad_w_rows(3)
    s1(2, 0)
    s2(5)
    grad_y()
    s2(2)
    s3(4)
    norm_one_back()
    grad_w_rows(1, (1,))
    grad_ctx()
    s1(1, 1, (1,))
    attend_back(0, 0, 2)
    s1(3, 1)
    s3(2)
    s1(3, 0)
    attend_back(0, 2, 4)
    s3(5)
    grad_w_rows(0)
    s2(1, (1,))
    attend_back(1, 0, 4)
    s1(0, 1)
    grad_w_rows(1, (0,))
    s1(1, 0, (1,))
    s1(1, 1, (0,))
    s2(3)
    s4(2)
    s1(1, 0, (0,))
    grad_bias_in()
    vec_pack()
    vec_core()
    s1(0, 0)
    grad_x(0, 1)
    vec_y()
    s2(1, (0,))
    s3(1, (1,))
    s3(3)
    s2(0)
    s4(5)
    s3(1, (0,))
    s5(2)
    s4(1, (1,))
    grad_x(1, 2)
    vec_x()
    s4(4)
    s3(0)
    grad_x(2, 3)
    vec_z()
    s5(5)
    s4(3)
    s5(4)
    s5(1, (1,))
    s4(1, (0,))
    vec_w()
    s4(0)
    s5(1, (0,))
    s5(3)
    vec_end()
    s5(0)
    finish()


def fused_layer(x, tok, groups, counts, rows, down, vec):
    def big(n):
        return pltpu.VMEM((n, 768, 768), bf16)

    scratch = [
        pltpu.VMEM((512, 768), bf16),
        pltpu.VMEM((24, 6144), f32),
        pltpu.VMEM((96, 768), f32),
        pltpu.VMEM((24, 6144), f32),
        pltpu.VMEM((96, 768), f32),
        big(8),
        big(4),
        big(4),
        big(4),
        big(8),
        pltpu.VMEM((3, 512, 768), bf16),
        pltpu.VMEM((24, 256, 128), bf16),
        pltpu.VMEM((512, 768), bf16),
        pltpu.VMEM((768, 512), bf16),
        pltpu.VMEM((768, 512), bf16),
        pltpu.VMEM((512, 768), bf16),
        pltpu.VMEM((768, 512), bf16),
        pltpu.VMEM((512, 3072), bf16),
        pltpu.VMEM((3072, 512), bf16),
        pltpu.VMEM((512, 3072), bf16),
        pltpu.VMEM((512, 768), f32),
        pltpu.VMEM((512, 768), f32),
        pltpu.VMEM((512, 768), f32),
        pltpu.VMEM((512, 128), f32),
        pltpu.VMEM((512, 128), f32),
        pltpu.VMEM((512, 128), f32),
        pltpu.VMEM((8, 128), f32),
        pltpu.VMEM((8, 128), f32),
        pltpu.VMEM((32, 16, 128), bf16),
        pltpu.VMEM((8, 9216), f32),
        pltpu.VMEM((8, 2304), f32),
        pltpu.VMEM((32, 16, 512), bf16),
        pltpu.VMEM((8, 768), f32),
        pltpu.VMEM((8, 768), f32),
        pltpu.VMEM((8, 128), f32),
        pltpu.VMEM((2, 256, 256), f32),
        pltpu.VMEM((8, 9216), f32),
        pltpu.VMEM((8, 16, 128), f32),
        pltpu.VMEM((12, 16, 128), f32),
    ]
    dma = pltpu.SemaphoreType.DMA
    scratch += [
        dma((6,)), dma((6, 4, 4)), dma((6, 4, 2)), dma((6, 4, 2)), dma((6, 4, 2)), dma((6,)), dma((6, 4)),
        dma((2, 16)), dma((2,)),
        dma((6, 2, 4)), dma((7, 2, 2)), dma((7, 2)), dma((6, 2, 4)), dma((6, 2, 2)), dma((6, 2)), dma((6, 4)),
        dma((12,)), dma((9,)),
    ]
    vmem = pl.BlockSpec(memory_space=pltpu.VMEM)
    smem = pl.BlockSpec(memory_space=pltpu.SMEM)
    anywhere = pl.BlockSpec(memory_space=pl.ANY)
    return pl.pallas_call(
        layer_kernel,
        out_shape=(
            jax.ShapeDtypeStruct((1, 1), f32),
            jax.ShapeDtypeStruct(x.shape, f32),
            jax.ShapeDtypeStruct(rows.shape, f32),
            jax.ShapeDtypeStruct(down.shape, f32),
            jax.ShapeDtypeStruct(vec.shape, f32),
        ),
        in_specs=[anywhere, vmem, smem, smem, anywhere, anywhere, vmem],
        out_specs=(smem, anywhere, anywhere, anywhere, vmem),
        scratch_shapes=scratch,
        compiler_params=pltpu.CompilerParams(collective_id=0, has_side_effects=True, vmem_limit_bytes=vmem_bytes),
    )(x, tok, groups, counts, rows, down, vec)


def adam_step(master, gradient, moment_one, moment_two, decay, rate):
    mean_new = beta_one * moment_one + (1.0 - beta_one) * gradient
    square_new = beta_two * moment_two + (1.0 - beta_two) * gradient * gradient
    mean_hat = mean_new / (1.0 - beta_one**STEP)
    square_hat = square_new / (1.0 - beta_two**STEP)
    updated = master - rate * (mean_hat / (jnp.sqrt(square_hat) + adam_epsilon) + decay * master)
    return (updated, mean_new, square_new)


def update_kernel(*refs):
    ins, outs, in_bufs, out_bufs = refs[:13], refs[13:23], refs[23:36], refs[36:45]
    in_sem, out_sem = refs[45:]
    loads = [pltpu.make_async_copy(ref, buf, in_sem.at[n]) for n, (ref, buf) in enumerate(zip(ins, in_bufs))]
    stores = [pltpu.make_async_copy(buf, ref, out_sem.at[n]) for n, (buf, ref) in enumerate(zip(in_bufs[:1] + out_bufs, outs))]
    for load in loads:
        load.start()
    loads[0].wait()
    stores[0].start()
    for group, (decay, rate) in enumerate(((decay_rate, learn_rate), (decay_rate, learn_rate), (0.0, vector_rate))):
        for load in loads[1 + 4 * group : 5 + 4 * group]:
            load.wait()
        sources = in_bufs[1 + 4 * group : 5 + 4 * group]
        targets = out_bufs[3 * group : 3 * group + 3]
        if len(sources[0].shape) == 1:
            for target, value in zip(targets, adam_step(*[ref[...] for ref in sources], decay, rate)):
                target[...] = value
        else:

            def body(n, carry, sources=sources, targets=targets, decay=decay, rate=rate):
                part = pl.ds(pl.multiple_of(n * 8, 8), 8)
                for target, value in zip(targets, adam_step(*[ref[part, :] for ref in sources], decay, rate)):
                    target[part, :] = value
                return carry

            lax.fori_loop(0, sources[0].shape[0] // 8, body, 0)
        for store in stores[1 + 3 * group : 4 + 3 * group]:
            store.start()
    for store in stores:
        store.wait()


def update(dx, rows, down, vec):
    news = [jax.ShapeDtypeStruct(dx.shape, f32)]
    for group in (rows, down, vec):
        news += [jax.ShapeDtypeStruct(group[0].shape, f32)] * 3
    anywhere = pl.BlockSpec(memory_space=pl.ANY)
    return pl.pallas_call(
        update_kernel,
        out_shape=tuple(news),
        in_specs=[anywhere] * 13,
        out_specs=(anywhere,) * 10,
        scratch_shapes=[pltpu.VMEM(a.shape, f32) for a in (dx, *rows, *down, *vec)]
        + [pltpu.VMEM(a.shape, f32) for a in news[1:]]
        + [pltpu.SemaphoreType.DMA((13,)), pltpu.SemaphoreType.DMA((10,))],
        compiler_params=pltpu.CompilerParams(vmem_limit_bytes=vmem_bytes),
    )(dx, *rows, *down, *vec)


def on_device_fused(
    embeds, token_mask, groups, counts,
    rows_master, rows_mean, rows_square, down_master, down_mean, down_square,
    vector_master, vector_mean, vector_square,
):
    x = embeds.reshape(-1, embeds.shape[-1])
    loss, dx, rows_grad, down_grad, vec_grad = fused_layer(x, token_mask, groups, counts, rows_master, down_master, vector_master)
    dx, *new = update(
        dx,
        (rows_master, rows_grad, rows_mean, rows_square),
        (down_master, down_grad, down_mean, down_square),
        (vector_master, vec_grad, vector_mean, vector_square),
    )
    return (loss[0, 0], dx.reshape(embeds.shape), *new)


def layer_norm(values, scale_vec, shift_vec):
    centre = values - jnp.mean(values, axis=-1, keepdims=True)
    spread = jnp.mean(centre * centre, axis=-1, keepdims=True)
    return centre * lax.rsqrt(spread + norm_epsilon) * scale_vec + shift_vec


def pool_unit(weights, output):
    summed = jnp.sum(output * weights[:, :, None], axis=1) / jnp.sum(weights, axis=1, keepdims=True)
    return summed * lax.rsqrt(jnp.sum(summed * summed, axis=1, keepdims=True) + unit_epsilon)


def exact_gelu(values):
    return jax.nn.gelu(values, approximate=False)


def softmax_last(values):
    return jax.nn.softmax(values, axis=-1)


def split_vectors(vectors, model_width, hidden):
    extents = [model_width] * 5 + [hidden] + [model_width] * 3
    pieces_out = []
    offset = 0
    for extent in extents:
        pieces_out.append(vectors[offset : offset + extent])
        offset = offset + extent
    return pieces_out


def pair_exps(left_rows, right_rows, left_group, right_group, left_start, right_start):
    scores = score_scale * jnp.dot(left_rows, right_rows.T, precision=highest)
    left_index = left_start + jnp.arange(left_rows.shape[0])
    right_index = right_start + jnp.arange(right_rows.shape[0])
    diagonal = left_index[:, None] == right_index[None, :]
    scores = scores - score_scale * margin * diagonal.astype(jnp.float32)
    same = (left_group[:, None] == right_group[None, :]) & (left_group[:, None] >= 0.0)
    return (jnp.where(same, jnp.exp(scores), 0.0), (diagonal & same).astype(jnp.float32))


def add_sums(own_data, arrived, offset):
    sources, targets, group_own, own_start = own_data
    other_src, other_tgt, other_group = arrived
    row_exp, unused_row = pair_exps(sources, other_tgt, group_own, other_group, own_start, offset)
    col_exp, unused_col = pair_exps(other_src, targets, other_group, group_own, offset, own_start)
    return (jnp.sum(row_exp, axis=1), jnp.sum(col_exp, axis=0))


def add_grads(own_data, loss_coef, arrived, offset):
    sources, targets, group_own, own_start, row_own, col_own = own_data
    other_src, other_tgt, other_group, other_row, other_col = arrived
    row_exp, row_diag = pair_exps(sources, other_tgt, group_own, other_group, own_start, offset)
    row_coef = (
        row_exp / row_own[:, None] + row_exp / other_col[None, :] - 2.0 * row_diag
    ) * loss_coef
    col_exp, col_diag = pair_exps(other_src, targets, other_group, group_own, offset, own_start)
    col_coef = (
        col_exp / other_row[:, None] + col_exp / col_own[None, :] - 2.0 * col_diag
    ) * loss_coef
    grad_src = score_scale * jnp.dot(row_coef, other_tgt, precision=highest)
    grad_tgt = score_scale * jnp.dot(col_coef.T, other_src, precision=highest)
    return (grad_src, grad_tgt)


def on_device_general(
    embeds,
    token_mask,
    groups,
    counts,
    rows_master,
    rows_mean,
    rows_square,
    down_master,
    down_mean,
    down_square,
    vector_master,
    vector_mean,
    vector_square,
):
    slot_count = embeds.shape[0]
    length = embeds.shape[2]
    model_width = embeds.shape[3]
    row_all, down_all, vector_all = (
        lax.all_gather(rows_master.astype(jnp.bfloat16), ("blk", "dp"), axis=0, tiled=True),
        lax.all_gather(down_master.astype(jnp.bfloat16), ("blk", "dp"), axis=0, tiled=True),
        lax.all_gather(vector_master.astype(jnp.bfloat16), ("blk", "dp"), axis=0, tiled=True),
    )
    hidden = down_all.shape[0]
    vectors = vector_all.astype(jnp.float32)
    bias_q, bias_v, bias_o, gain_one, shift_one, bias_up, bias_down, gain_two, shift_two = (
        split_vectors(vectors, model_width, hidden)
    )
    w_attn_in = row_all[:, : 3 * model_width]
    w_attn_out = row_all[:, 3 * model_width : 4 * model_width]
    w_up = row_all[:, 4 * model_width :]
    seq_count = 2 * slot_count
    tokens = seq_count * length
    head_count = model_width // HEAD
    inputs = embeds.reshape(tokens, model_width)
    weights = token_mask.reshape(seq_count, length).astype(jnp.float32)
    key_valid = token_mask.reshape(seq_count, length) > 0
    joined = jnp.concatenate([bias_q, jnp.zeros_like(bias_q), bias_v])
    projected = (jnp.dot(inputs, w_attn_in, preferred_element_type=jnp.float32) + joined).astype(
        jnp.bfloat16
    )
    queries = projected[:, :model_width].reshape(seq_count, length, head_count, HEAD)
    key_part = projected[:, model_width : 2 * model_width].reshape(
        seq_count, length, head_count, HEAD
    )
    values = projected[:, 2 * model_width :].reshape(seq_count, length, head_count, HEAD)
    scores = jnp.einsum(
        "nihe,njhe->nhij", queries, key_part, preferred_element_type=jnp.float32
    ) * HEAD ** (-0.5)
    scores = jnp.where(key_valid[:, None, None, :], scores, -1e30)
    attention, soft_back = jax.vjp(softmax_last, scores)
    attention_low = attention.astype(jnp.bfloat16)
    context = (
        jnp.einsum("nhij,njhe->nihe", attention_low, values, preferred_element_type=jnp.float32)
        .astype(jnp.bfloat16)
        .reshape(tokens, model_width)
    )
    resid_one = (
        inputs.astype(jnp.float32)
        + jnp.dot(context, w_attn_out, preferred_element_type=jnp.float32)
        + bias_o
    )
    normed_full, norm_one_back = jax.vjp(layer_norm, resid_one, 1.0 + gain_one, shift_one)
    normed_one = normed_full.astype(jnp.bfloat16)
    up_pre = jnp.dot(normed_one, w_up, preferred_element_type=jnp.float32) + bias_up
    activated_full, gelu_back = jax.vjp(exact_gelu, up_pre)
    activated = activated_full.astype(jnp.bfloat16)
    resid_two = (
        normed_one.astype(jnp.float32)
        + jnp.dot(activated, down_all, preferred_element_type=jnp.float32)
        + bias_down
    )
    output, norm_two_back = jax.vjp(layer_norm, resid_two, 1.0 + gain_two, shift_two)
    pooled, pool_back = jax.vjp(
        partial(pool_unit, weights), output.reshape(seq_count, length, model_width)
    )
    pooled = pooled.reshape(slot_count, 2, model_width)
    sources = pooled[:, 0]
    targets = pooled[:, 1]
    own_start = lax.axis_index(("blk", "dp")) * slot_count
    valid_slot = jnp.arange(slot_count) < counts[0]
    group_own = jnp.where(valid_slot, groups, -1).astype(jnp.float32)
    pair_total = lax.psum(counts[0].astype(jnp.float32), ("blk", "dp"))
    loss_coef = 0.5 / pair_total
    own_sums = (sources, targets, group_own, own_start)
    row_sum, col_sum = add_sums(
        own_sums,
        (
            lax.all_gather(sources, ("blk", "dp"), axis=0, tiled=True),
            lax.all_gather(targets, ("blk", "dp"), axis=0, tiled=True),
            lax.all_gather(group_own, ("blk", "dp"), axis=0, tiled=True),
        ),
        jnp.int32(0),
    )
    row_safe = jnp.where(valid_slot, row_sum, 1.0)
    col_safe = jnp.where(valid_slot, col_sum, 1.0)
    own_grads = (sources, targets, group_own, own_start, row_safe, col_safe)
    grad_src, grad_tgt = add_grads(
        own_grads,
        loss_coef,
        (
            lax.all_gather(sources, ("blk", "dp"), axis=0, tiled=True),
            lax.all_gather(targets, ("blk", "dp"), axis=0, tiled=True),
            lax.all_gather(group_own, ("blk", "dp"), axis=0, tiled=True),
            lax.all_gather(row_safe, ("blk", "dp"), axis=0, tiled=True),
            lax.all_gather(col_safe, ("blk", "dp"), axis=0, tiled=True),
        ),
        jnp.int32(0),
    )
    positive = score_scale * jnp.sum(sources * targets, axis=1) - score_scale * margin
    loss_terms = jnp.sum(
        jnp.where(valid_slot, jnp.log(row_safe) + jnp.log(col_safe) - 2.0 * positive, 0.0)
    )
    pair_loss = lax.psum(loss_terms, ("blk", "dp")) * loss_coef
    grad_pooled = jnp.stack([grad_src, grad_tgt], axis=1).reshape(seq_count, model_width)
    grad_output = pool_back(grad_pooled)[0].reshape(tokens, model_width)
    grad_resid_two, grad_gain_two, grad_shift_two = norm_two_back(grad_output)
    grad_down_low = grad_resid_two.astype(jnp.bfloat16)
    grad_w_down = jnp.einsum(
        "tf,td->fd", activated, grad_down_low, preferred_element_type=jnp.float32
    )
    grad_bias_down = jnp.sum(grad_down_low.astype(jnp.float32), axis=0)
    grad_act = jnp.einsum("td,fd->tf", grad_down_low, down_all, preferred_element_type=jnp.float32)
    grad_up = gelu_back(grad_act)[0].astype(jnp.bfloat16)
    grad_w_up = jnp.einsum("td,tf->df", normed_one, grad_up, preferred_element_type=jnp.float32)
    grad_bias_up = jnp.sum(grad_up.astype(jnp.float32), axis=0)
    grad_normed = grad_resid_two + jnp.einsum(
        "tf,df->td", grad_up, w_up, preferred_element_type=jnp.float32
    )
    grad_resid_one, grad_gain_one, grad_shift_one = norm_one_back(grad_normed)
    grad_attn_low = grad_resid_one.astype(jnp.bfloat16)
    grad_w_out = jnp.einsum("td,te->de", context, grad_attn_low, preferred_element_type=jnp.float32)
    grad_bias_out = jnp.sum(grad_attn_low.astype(jnp.float32), axis=0)
    grad_context = jnp.einsum(
        "te,de->td", grad_attn_low, w_attn_out, preferred_element_type=jnp.float32
    ).astype(jnp.bfloat16)
    grad_context = grad_context.reshape(seq_count, length, head_count, HEAD)
    grad_attention = jnp.einsum(
        "nihe,njhe->nhij", grad_context, values, preferred_element_type=jnp.float32
    )
    grad_values = jnp.einsum(
        "nhij,nihe->njhe", attention_low, grad_context, preferred_element_type=jnp.float32
    )
    grad_scores = soft_back(grad_attention)[0].astype(jnp.bfloat16)
    grad_queries = jnp.einsum(
        "nhij,njhe->nihe", grad_scores, key_part, preferred_element_type=jnp.float32
    ) * HEAD ** (-0.5)
    grad_keys = jnp.einsum(
        "nhij,nihe->njhe", grad_scores, queries, preferred_element_type=jnp.float32
    ) * HEAD ** (-0.5)
    grad_projected = jnp.concatenate(
        [
            grad_queries.reshape(tokens, model_width),
            grad_keys.reshape(tokens, model_width),
            grad_values.reshape(tokens, model_width),
        ],
        axis=1,
    ).astype(jnp.bfloat16)
    grad_w_in = jnp.einsum("td,te->de", inputs, grad_projected, preferred_element_type=jnp.float32)
    grad_bias_q = jnp.sum(grad_projected[:, :model_width].astype(jnp.float32), axis=0)
    grad_bias_v = jnp.sum(grad_projected[:, 2 * model_width :].astype(jnp.float32), axis=0)
    grad_inputs = grad_resid_one + jnp.einsum(
        "te,de->td", grad_projected, w_attn_in, preferred_element_type=jnp.float32
    )
    grad_vector = jnp.concatenate(
        [
            grad_bias_q,
            grad_bias_v,
            grad_bias_out,
            grad_gain_one,
            grad_shift_one,
            grad_bias_up,
            grad_bias_down,
            grad_gain_two,
            grad_shift_two,
        ]
    )
    rows_share, down_share, vector_share = (
        lax.psum_scatter(
            jnp.concatenate([grad_w_in, grad_w_out, grad_w_up], axis=1),
            ("blk", "dp"),
            scatter_dimension=0,
            tiled=True,
        ),
        lax.psum_scatter(grad_w_down, ("blk", "dp"), scatter_dimension=0, tiled=True),
        lax.psum_scatter(grad_vector, ("blk", "dp"), scatter_dimension=0, tiled=True),
    )
    rows_new = adam_step(rows_master, rows_share, rows_mean, rows_square, decay_rate, learn_rate)
    down_new = adam_step(down_master, down_share, down_mean, down_square, decay_rate, learn_rate)
    vector_new = adam_step(
        vector_master, vector_share, vector_mean, vector_square, 0.0, vector_rate
    )
    embeds_grad = grad_inputs.reshape(slot_count, 2, length, model_width)
    return (
        pair_loss,
        embeds_grad,
        rows_new[0],
        rows_new[1],
        rows_new[2],
        down_new[0],
        down_new[1],
        down_new[2],
        vector_new[0],
        vector_new[1],
        vector_new[2],
    )


def solution(mesh):
    in_specs = (
        P(("blk", "dp"), None, None, None),
        P(("blk", "dp"), None, None),
        P(("blk", "dp")),
        P(("blk", "dp")),
        P(("blk", "dp"), None),
        P(("blk", "dp"), None),
        P(("blk", "dp"), None),
        P(("blk", "dp"), None),
        P(("blk", "dp"), None),
        P(("blk", "dp"), None),
        P(("blk", "dp")),
        P(("blk", "dp")),
        P(("blk", "dp")),
    )
    out_specs = (
        P(),
        P(("blk", "dp"), None, None, None),
        P(("blk", "dp"), None),
        P(("blk", "dp"), None),
        P(("blk", "dp"), None),
        P(("blk", "dp"), None),
        P(("blk", "dp"), None),
        P(("blk", "dp"), None),
        P(("blk", "dp")),
        P(("blk", "dp")),
        P(("blk", "dp")),
    )
    fits = dict(mesh.shape) == {"blk": 8, "dp": 4}
    return jax.shard_map(
        on_device_fused if fits else on_device_general, mesh=mesh, in_specs=in_specs, out_specs=out_specs, check_vma=False
    )
```
